32 devices in a mesh: dp: 4 (over z), fsdp: 8 (over y, x, core).
Axes of the slice: x: 2, y: 2, z: 4, core: 2. Of those that a mesh axis runs over, the one named last changes fastest.
Arguments:
- features: bfloat16 [256, 64, 2048], P(('dp', 'fsdp')), may hold values from -6 to 6
- crop_ids: int32 [256, 64], P(('dp', 'fsdp')), may hold values from -1 to 15, as said below
- labels: int32 [256, 64], P(('dp', 'fsdp')), may hold values from 0 to 18
- w_reduce: bfloat16 [2048, 512], P(None, 'fsdp'), may hold values from -0.125 to 0.125
- gain_reduce: float32 [512], replicated, may hold values from 0.5 to 1.5
- bias_reduce: float32 [512], replicated, may hold values from -1 to 1
- w_dilated: bfloat16 [3, 3, 512, 512], P(None, None, None, 'fsdp'), may hold values from -0.09375 to 0.09375
- gain_dilated: float32 [512], replicated, may hold values from 0.5 to 1.5
- bias_dilated: float32 [512], replicated, may hold values from -1 to 1
- w_expand: bfloat16 [512, 2048], P(None, 'fsdp'), may hold values from -0.25 to 0.25
- gain_expand: float32 [2048], replicated, may hold values from 0.5 to 1.5
- bias_expand: float32 [2048], replicated, may hold values from -1 to 1
- w_point: bfloat16 [2048, 256], P(None, 'fsdp'), may hold values from -0.125 to 0.125
- gain_point: float32 [256], replicated, may hold values from 0.5 to 1.5
- bias_point: float32 [256], replicated, may hold values from -1 to 1
- w_rate: bfloat16 [3, 3, 2048, 256], P(None, None, None, 'fsdp'), may hold values from -0.046875 to 0.046875
- gain_rate: float32 [256], replicated, may hold values from 0.5 to 1.5
- bias_rate: float32 [256], replicated, may hold values from -1 to 1
- w_rate_double: bfloat16 [3, 3, 2048, 256], P(None, None, None, 'fsdp'), may hold values from -0.046875 to 0.046875
- gain_rate_double: float32 [256], replicated, may hold values from 0.5 to 1.5
- bias_rate_double: float32 [256], replicated, may hold values from -1 to 1
- w_rate_triple: bfloat16 [3, 3, 2048, 256], P(None, None, None, 'fsdp'), may hold values from -0.046875 to 0.046875
- gain_rate_triple: float32 [256], replicated, may hold values from 0.5 to 1.5
- bias_rate_triple: float32 [256], replicated, may hold values from -1 to 1
- w_pool: bfloat16 [2048, 256], P(None, 'fsdp'), may hold values from -0.125 to 0.125
- w_merge: bfloat16 [1280, 256], P(None, 'fsdp'), may hold values from -0.15625 to 0.15625
- gain_merge: float32 [256], replicated, may hold values from 0.5 to 1.5
- bias_merge: float32 [256], replicated, may hold values from -1 to 1
- w_classes: bfloat16 [256, 19], P('fsdp'), may hold values from -0.75 to 0.75
Outputs:
- class_logits: bfloat16 [256, 64, 19], P(('dp', 'fsdp'))
- grad_features: float32 [256, 64, 2048], P(('dp', 'fsdp'))
- grad_reduce: float32 [2048, 512], P(None, 'fsdp')
- grad_gain_reduce: float32 [512], replicated
- grad_bias_reduce: float32 [512], replicated
- grad_dilated: float32 [3, 3, 512, 512], P(None, None, None, 'fsdp')
- grad_gain_dilated: float32 [512], replicated
- grad_bias_dilated: float32 [512], replicated
- grad_expand: float32 [512, 2048], P(None, 'fsdp')
- grad_gain_expand: float32 [2048], replicated
- grad_bias_expand: float32 [2048], replicated
- grad_point: float32 [2048, 256], P(None, 'fsdp')
- grad_gain_point: float32 [256], replicated
- grad_bias_point: float32 [256], replicated
- grad_rate: float32 [3, 3, 2048, 256], P(None, None, None, 'fsdp')
- grad_gain_rate: float32 [256], replicated
- grad_bias_rate: float32 [256], replicated
- grad_rate_double: float32 [3, 3, 2048, 256], P(None, None, None, 'fsdp')
- grad_gain_rate_double: float32 [256], replicated
- grad_bias_rate_double: float32 [256], replicated
- grad_rate_triple: float32 [3, 3, 2048, 256], P(None, None, None, 'fsdp')
- grad_gain_rate_triple: float32 [256], replicated
- grad_bias_rate_triple: float32 [256], replicated
- grad_pool: float32 [2048, 256], P(None, 'fsdp')
- grad_merge: float32 [1280, 256], P(None, 'fsdp')
- grad_gain_merge: float32 [256], replicated
- grad_bias_merge: float32 [256], replicated
- grad_classes: float32 [256, 19], P('fsdp')
The draws below stay inside these ranges and needn't reach their ends.
Inputs may be any that keep to these rules, and one draw needn't show every extreme that they name: `crop_ids`: each aligned tile of 64 rows holds 4 rectangular crops numbered tile * 4 + 0 to 3; two of them span all the tile's rows; -1 marks padding pixels; every crop has pixels.
All inputs are finite; a program needn't handle non-finite values.
Results may differ from the reference program's by a relative error of at most 0.04.
Values may be sent and summed in bfloat16 or wider, within the bound.
A program may use at most 448 MiB of HBM per device.

```python
import jax
import jax.numpy as jnp
from jax import lax

CIN = 2048
NECK_CHANNELS = 512
ASPP = 256
CLASSES = 19
TILE_COLUMNS = 64
CROPS_TILE = 4
DILATION_SPAN = 4
RATE = 12
TILE_ROWS = 64
TOTAL_ROWS = 256
CROPS = 16


def draw_crop_ids(key, part):
    key = jax.random.fold_in(key, 7)
    tile_count = TOTAL_ROWS // TILE_ROWS
    key_col, key_left, key_split, key_pad = jax.random.split(key, 4)
    cut_col = jax.random.randint(key_col, (tile_count,), TILE_COLUMNS // 4, 3 * TILE_COLUMNS // 4 + 1)
    cut_left = jax.random.randint(key_left, (tile_count,), TILE_ROWS // 4, 3 * TILE_ROWS // 4 + 1)
    split_draw = jax.random.randint(key_split, (tile_count,), 0, TILE_COLUMNS)
    cut_split = cut_col + 1 + split_draw % (TILE_COLUMNS - 1 - cut_col)
    padding = jax.random.randint(key_pad, (tile_count,), 1, TILE_ROWS // 8 + 1)
    row_index = jnp.arange(TOTAL_ROWS)
    tile_index = row_index // TILE_ROWS
    inner = (row_index % TILE_ROWS)[:, None]
    col_index = jnp.arange(TILE_COLUMNS)[None, :]
    right_side = col_index >= cut_col[tile_index][:, None]
    far_right = col_index >= cut_split[tile_index][:, None]
    lower_part = inner >= cut_left[tile_index][:, None]
    local_id = jnp.where(right_side, 2 + far_right.astype(jnp.int32), lower_part.astype(jnp.int32))
    crop_number = tile_index[:, None] * CROPS_TILE + local_id
    padded_input = jnp.logical_not(right_side) & (inner >= TILE_ROWS - padding[tile_index][:, None])
    return jnp.where(padded_input, -1, crop_number).astype(jnp.int32)


def plant(entries, own_key, smallest, high):
    shape = entries.shape
    place = [jax.random.randint(jax.random.fold_in(own_key, axis), (), 0, shape[axis]) for axis in range(len(shape))]
    entries = entries.at[tuple(place)].set(smallest)
    longest = shape.index(max(shape))
    place[longest] = (place[longest] + 1) % shape[longest]
    return entries.at[tuple(place)].set(high)


def block_scale(own_key, shape, cuts, least, largest):
    def one(dim, shards_of):
        steps = jax.random.uniform(jax.random.fold_in(jax.random.fold_in(own_key, 6), dim), (shards_of,), jnp.float32, least / len(cuts), largest / len(cuts))
        return jnp.repeat(jnp.exp(steps), shape[dim] // shards_of).reshape((-1,) + (1,) * (len(shape) - dim - 1))

    gain = one(*cuts[0])
    for cut in cuts[1:]:
        gain = gain * one(*cut)
    return gain


def noise(rng, dims, width, bound, cuts=(), held_as=jnp.bfloat16):
    entries = jax.random.normal(rng, dims, jnp.float32) * width
    if len(cuts) > 0:
        entries = block_scale(rng, dims, cuts, -0.22, 0.18) * entries
    return jnp.clip(entries, min=-bound, max=bound).astype(held_as)


def setup_inputs(seed: int = 0) -> dict:
    streams_of = jax.random.split(jax.random.key(seed), 30)
    features = noise(streams_of[0], (TOTAL_ROWS, TILE_COLUMNS, CIN), 1.0, 6.0, ((0, 32),))
    crop_ids = draw_crop_ids(jax.random.fold_in(streams_of[29], 71), 0)
    labels = plant(jax.random.randint(streams_of[2], (TOTAL_ROWS, TILE_COLUMNS), 0, CLASSES), jax.random.fold_in(streams_of[2], 1), 0, CLASSES - 1).astype(jnp.int32)
    w_reduce = noise(streams_of[3], (CIN, NECK_CHANNELS), CIN ** -0.5, 0.125, ((1, 8),))
    gain_reduce = jnp.clip(jax.random.uniform(streams_of[4], (NECK_CHANNELS,), jnp.float32, 0.5, 1.5), 0.5, 1.5)
    bias_reduce = noise(streams_of[5], (NECK_CHANNELS,), 0.3, 1.0, (), jnp.float32)
    w_dilated = noise(streams_of[6], (3, 3, NECK_CHANNELS, NECK_CHANNELS), (9 * NECK_CHANNELS) ** -0.5, 0.09375, ((3, 8),))
    gain_dilated = jnp.clip(jax.random.uniform(streams_of[7], (NECK_CHANNELS,), jnp.float32, 0.5, 1.5), 0.5, 1.5)
    bias_dilated = noise(streams_of[8], (NECK_CHANNELS,), 0.3, 1.0, (), jnp.float32)
    w_expand = noise(streams_of[9], (NECK_CHANNELS, CIN), NECK_CHANNELS ** -0.5, 0.25, ((1, 8),))
    gain_expand = jnp.clip(jax.random.uniform(streams_of[10], (CIN,), jnp.float32, 0.5, 1.5), 0.5, 1.5)
    bias_expand = noise(streams_of[11], (CIN,), 0.3, 1.0, (), jnp.float32)
    w_point = noise(streams_of[12], (CIN, ASPP), CIN ** -0.5, 0.125, ((1, 8),))
    gain_point = jnp.clip(jax.random.uniform(streams_of[13], (ASPP,), jnp.float32, 0.5, 1.5), 0.5, 1.5)
    bias_point = noise(streams_of[14], (ASPP,), 0.3, 1.0, (), jnp.float32)
    w_rate = noise(streams_of[15], (3, 3, CIN, ASPP), (9 * CIN) ** -0.5, 0.046875, ((3, 8),))
    gain_rate = jnp.clip(jax.random.uniform(streams_of[16], (ASPP,), jnp.float32, 0.5, 1.5), 0.5, 1.5)
    bias_rate = noise(streams_of[17], (ASPP,), 0.3, 1.0, (), jnp.float32)
    w_rate_double = noise(streams_of[18], (3, 3, CIN, ASPP), (9 * CIN) ** -0.5, 0.046875, ((3, 8),))
    gain_rate_double = jnp.clip(jax.random.uniform(streams_of[19], (ASPP,), jnp.float32, 0.5, 1.5), 0.5, 1.5)
    bias_rate_double = noise(streams_of[20], (ASPP,), 0.3, 1.0, (), jnp.float32)
    w_rate_triple = noise(streams_of[21], (3, 3, CIN, ASPP), (9 * CIN) ** -0.5, 0.046875, ((3, 8),))
    gain_rate_triple = jnp.clip(jax.random.uniform(streams_of[22], (ASPP,), jnp.float32, 0.5, 1.5), 0.5, 1.5)
    bias_rate_triple = noise(streams_of[23], (ASPP,), 0.3, 1.0, (), jnp.float32)
    w_pool = noise(streams_of[24], (CIN, ASPP), CIN ** -0.5, 0.125, ((1, 8),))
    w_merge = noise(streams_of[25], (5 * ASPP, ASPP), (5 * ASPP) ** -0.5, 0.15625, ((1, 8),))
    gain_merge = jnp.clip(jax.random.uniform(streams_of[26], (ASPP,), jnp.float32, 0.5, 1.5), 0.5, 1.5)
    bias_merge = noise(streams_of[27], (ASPP,), 0.3, 1.0, (), jnp.float32)
    w_classes = noise(streams_of[28], (ASPP, CLASSES), 0.125, 0.75, ((0, 8),))
    return {"features": features, "crop_ids": crop_ids, "labels": labels, "w_reduce": w_reduce, "gain_reduce": gain_reduce, "bias_reduce": bias_reduce, "w_dilated": w_dilated, "gain_dilated": gain_dilated, "bias_dilated": bias_dilated, "w_expand": w_expand, "gain_expand": gain_expand, "bias_expand": bias_expand, "w_point": w_point, "gain_point": gain_point, "bias_point": bias_point, "w_rate": w_rate, "gain_rate": gain_rate, "bias_rate": bias_rate, "w_rate_double": w_rate_double, "gain_rate_double": gain_rate_double, "bias_rate_double": bias_rate_double, "w_rate_triple": w_rate_triple, "gain_rate_triple": gain_rate_triple, "bias_rate_triple": bias_rate_triple, "w_pool": w_pool, "w_merge": w_merge, "gain_merge": gain_merge, "bias_merge": bias_merge, "w_classes": w_classes}


eps = 1e-05

@jax.custom_vjp
def low(v):
    return lax.optimization_barrier(v.astype(jnp.bfloat16)).astype(jnp.float32)

@jax.custom_vjp
def low_back(v):
    return v

def low_keep(v):
    return (low(v), None)

def low_pass(kept, grad):
    return (grad,)

def back_keep(v):
    return (v, None)

def back_low(kept, grad):
    return (low(grad),)
low.defvjp(low_keep, low_pass)
low_back.defvjp(back_keep, back_low)

def matmul(first_op, second_op):
    return jnp.dot(first_op, second_op, precision=lax.Precision.HIGHEST, preferred_element_type=jnp.float32)

def offset_table(crop_random_keys, spacing):
    extended = jnp.pad(crop_random_keys, spacing)
    height, breadth = crop_random_keys.shape
    tables = []
    for row_tap in range(3):
        for col_tap in range(3):
            nearby = extended[row_tap * spacing:row_tap * spacing + height, col_tap * spacing:col_tap * spacing + breadth]
            tables.append(((nearby == crop_random_keys) & (crop_random_keys > 0)).astype(jnp.float32))
    return tables

def dilated_conv(inputs, kernel, tables, spacing):
    height, breadth, channels = inputs.shape
    extended = jnp.pad(inputs, ((spacing, spacing), (spacing, spacing), (0, 0)))
    summed = jnp.zeros((height, breadth, kernel.shape[3]), jnp.float32)
    for row_tap in range(3):
        for col_tap in range(3):
            nearby = extended[row_tap * spacing:row_tap * spacing + height, col_tap * spacing:col_tap * spacing + breadth]
            product = matmul(nearby.reshape(height * breadth, channels), kernel[row_tap, col_tap])
            summed = summed + tables[3 * row_tap + col_tap][:, :, None] * product.reshape(height, breadth, kernel.shape[3])
    return summed

def normalize(values, inside, pixel_count, factor, offset):
    average = lax.optimization_barrier(jnp.sum(values * inside, axis=0)) / pixel_count
    squares = lax.optimization_barrier(jnp.sum(values * values * inside, axis=0)) / pixel_count
    inverse = lax.rsqrt(squares - average * average + eps)
    return (values - average) * inverse * factor + offset

def reference(features, crop_ids, labels, w_reduce, gain_reduce, bias_reduce, w_dilated, gain_dilated, bias_dilated, w_expand, gain_expand, bias_expand, w_point, gain_point, bias_point, w_rate, gain_rate, bias_rate, w_rate_double, gain_rate_double, bias_rate_double, w_rate_triple, gain_rate_triple, bias_rate_triple, w_pool, w_merge, gain_merge, bias_merge, w_classes):
    pixel_values = TOTAL_ROWS * TILE_COLUMNS
    crop_random_keys = crop_ids + 1
    inner_neck = offset_table(crop_random_keys, DILATION_SPAN)
    spacings = (RATE, 2 * RATE, 3 * RATE)
    near_rates = [offset_table(crop_random_keys, spacing) for spacing in spacings]
    inside = (crop_random_keys > 0).astype(jnp.float32).reshape(pixel_values, 1)
    pixel_count = jnp.sum(inside)
    members = (crop_ids.reshape(pixel_values, 1) == jnp.arange(CROPS)[None, :]).astype(jnp.float32)
    crop_sizes = lax.optimization_barrier(jnp.sum(members, axis=0))
    targets = (labels.reshape(pixel_values, 1) == jnp.arange(CLASSES)[None, :]).astype(jnp.float32)
    verified_convolution = jax.checkpoint(dilated_conv, static_argnums=(3,))

    def bottleneck(inputs_flat, reduce_w, reduce_g, reduce_b, dilated_weight, dilated_g, dilated_b, expand_w, expand_g, expand_b):
        act_one = low_back(matmul(inputs_flat, reduce_w))
        first_hidden = low(jax.nn.silu(normalize(act_one, inside, pixel_count, reduce_g, reduce_b)))
        second_activation = low_back(verified_convolution(first_hidden.reshape(TOTAL_ROWS, TILE_COLUMNS, NECK_CHANNELS), dilated_weight, inner_neck, DILATION_SPAN).reshape(pixel_values, NECK_CHANNELS))
        hidden_two = low(jax.nn.silu(normalize(second_activation, inside, pixel_count, dilated_g, dilated_b)))
        act_three = low_back(matmul(hidden_two, expand_w))
        return low(jax.nn.silu(normalize(act_three, inside, pixel_count, expand_g, expand_b) + inputs_flat))
    saved_bottleneck = jax.checkpoint(bottleneck)

    def forward(parameters):
        inputs_all, reduce_w, reduce_g, reduce_b, dilated_weight, dilated_g, dilated_b, expand_w, expand_g, expand_b, point_w, point_g, point_b, rate_w, rate_g, rate_b, double_w, double_g, double_b, triple_w, triple_g, triple_b, pool_w, merge_w, merge_g, merge_b, classes_w = parameters
        inputs_flat = inputs_all.reshape(pixel_values, CIN)
        block_out = saved_bottleneck(inputs_flat, reduce_w, reduce_g, reduce_b, dilated_weight, dilated_g, dilated_b, expand_w, expand_g, expand_b)
        point_act = low_back(matmul(block_out, point_w))
        branches = [low(jax.nn.silu(normalize(point_act, inside, pixel_count, point_g, point_b)))]
        block_grid = block_out.reshape(TOTAL_ROWS, TILE_COLUMNS, CIN)
        for kernel, factor, offset, spacing, tables in zip((rate_w, double_w, triple_w), (rate_g, double_g, triple_g), (rate_b, double_b, triple_b), spacings, near_rates):
            rate_act = low_back(verified_convolution(block_grid, kernel, tables, spacing).reshape(pixel_values, ASPP))
            branches.append(low(jax.nn.silu(normalize(rate_act, inside, pixel_count, factor, offset))))
        pooled = low(matmul(members.T, block_out) / crop_sizes[:, None])
        pool_low = low(jax.nn.silu(low_back(matmul(pooled, pool_w))))
        branches.append(matmul(members, pool_low))
        joined = jnp.concatenate(branches, axis=1)
        merge_act = low_back(matmul(joined, merge_w))
        merged = low(jax.nn.silu(normalize(merge_act, inside, pixel_count, merge_g, merge_b)))
        logits = low_back(matmul(merged, classes_w))
        spread = jax.nn.logsumexp(logits, axis=1, keepdims=True)
        loss = jnp.sum(inside * targets * (spread - logits)) / pixel_count
        return (loss, logits)
    floats = (features.astype(jnp.float32), w_reduce.astype(jnp.float32), gain_reduce, bias_reduce, w_dilated.astype(jnp.float32), gain_dilated, bias_dilated, w_expand.astype(jnp.float32), gain_expand, bias_expand, w_point.astype(jnp.float32), gain_point, bias_point, w_rate.astype(jnp.float32), gain_rate, bias_rate, w_rate_double.astype(jnp.float32), gain_rate_double, bias_rate_double, w_rate_triple.astype(jnp.float32), gain_rate_triple, bias_rate_triple, w_pool.astype(jnp.float32), w_merge.astype(jnp.float32), gain_merge, bias_merge, w_classes.astype(jnp.float32))
    loss, pullback, logits = jax.vjp(forward, floats, has_aux=True)
    grads = pullback(jnp.ones((), loss.dtype))[0]
    class_logits = logits.reshape(TOTAL_ROWS, TILE_COLUMNS, CLASSES).astype(jnp.bfloat16)
    return (class_logits, grads[0], grads[1], grads[2], grads[3], grads[4], grads[5], grads[6], grads[7], grads[8], grads[9], grads[10], grads[11], grads[12], grads[13], grads[14], grads[15], grads[16], grads[17], grads[18], grads[19], grads[20], grads[21], grads[22], grads[23], grads[24], grads[25], grads[26])
```

```python
import functools
import jax
import jax.numpy as jnp
from jax import lax
from jax.experimental import pallas as pl
from jax.experimental.pallas import tpu as pltpu
from jax.sharding import PartitionSpec as P


CLASSES = 19
CROPS_TILE = 4
DILATION_SPAN = 4
RATE = 12

eps = 1e-05

MESH = pl.DeviceIdType.MESH
ANY = pl.BlockSpec(memory_space=pl.ANY)
VM = pl.BlockSpec(memory_space=pltpu.VMEM)
DMA = pltpu.SemaphoreType.DMA
PAD = 144
VLIM = 60 * 2**20


def greet(fs, ds):
    f = lax.axis_index("fsdp")
    d = lax.axis_index("dp")
    bar = pltpu.get_barrier_semaphore()
    for k in fs:
        pl.semaphore_signal(bar, inc=1, device_id=(d, f ^ k), device_id_type=MESH)
    for k in ds:
        pl.semaphore_signal(bar, inc=1, device_id=(d ^ k, f), device_id_type=MESH)
    pl.semaphore_wait(bar, len(fs) + len(ds))
    return f, d


def remote(src, dst, ss, rs, d, f):
    c = pltpu.make_async_remote_copy(
        src_ref=src, dst_ref=dst, send_sem=ss, recv_sem=rs, device_id=(d, f), device_id_type=MESH
    )
    c.start()
    return c


def sum_kernel(x_ref, o_ref, b1, b2, s1, r1, s2, r2):
    f, d = greet(range(1, 8), range(1, 4))
    b1[f] = x_ref[...]
    cps = [remote(x_ref, b1.at[f], s1.at[k], r1.at[k], d, f ^ k) for k in range(1, 8)]
    for c in cps:
        c.wait()
    tot = b1[0]
    for k in range(1, 8):
        tot = tot + b1[k]
    b2[d] = tot
    cps = [remote(b2.at[d], b2.at[d], s2.at[k], r2.at[k], d ^ k, f) for k in range(1, 4)]
    for c in cps:
        c.wait()
    tot = b2[0]
    for k in range(1, 4):
        tot = tot + b2[k]
    o_ref[...] = tot


def total_sum(rows, cid):
    x = jnp.stack(rows)
    R, C = x.shape
    return pl.pallas_call(
        sum_kernel,
        out_shape=jax.ShapeDtypeStruct((R, C), jnp.float32),
        in_specs=[VM],
        out_specs=VM,
        scratch_shapes=[
            pltpu.VMEM((8, R, C), jnp.float32),
            pltpu.VMEM((4, R, C), jnp.float32),
            DMA((8,)),
            DMA((8,)),
            DMA((4,)),
            DMA((4,)),
        ],
        compiler_params=pltpu.CompilerParams(collective_id=cid, has_side_effects=True),
        name=f"total_sum_{cid}",
    )(x)


def spread_kernel(x_ref, o_ref, ss, rs, ls):
    f, d = greet(range(1, 8), ())
    w = o_ref.shape[2]
    h = x_ref.shape[1]
    dst = o_ref.at[:, pl.ds(pl.multiple_of(PAD + h * f, 16), h), :]

    def part(g):
        return x_ref.at[:, :, pl.ds(pl.multiple_of(g * w, 128), w)]

    cps = [remote(part(f ^ k), dst, ss.at[k], rs.at[k], d, f ^ k) for k in (6, 7, 2, 3, 4, 5, 1)]
    own = pltpu.make_async_copy(part(f), dst, ls)
    own.start()
    for c in cps:
        c.wait()
    own.wait()


def spread_channels(x, cid):
    q, h, C = x.shape
    return pl.pallas_call(
        spread_kernel,
        out_shape=jax.ShapeDtypeStruct((q, 8 * h + 2 * PAD, C // 8), x.dtype),
        in_specs=[VM],
        out_specs=ANY,
        scratch_shapes=[DMA((8,)), DMA((8,)), DMA(())],
        compiler_params=pltpu.CompilerParams(collective_id=cid, has_side_effects=True, vmem_limit_bytes=VLIM),
        name=f"spread_{cid}",
    )(x)


def collect_kernel(x_ref, o_ref, ss, rs, ls):
    f, d = greet(range(1, 8), ())
    w = x_ref.shape[2]
    h = o_ref.shape[1]
    dst = o_ref.at[:, :, pl.ds(pl.multiple_of(f * w, 128), w)]

    def part(g):
        return x_ref.at[:, pl.ds(pl.multiple_of(h * g, 16), h), :]

    cps = [remote(part(f ^ k), dst, ss.at[k], rs.at[k], d, f ^ k) for k in (6, 7, 2, 3, 4, 5, 1)]
    own = pltpu.make_async_copy(part(f), dst, ls)
    own.start()
    for c in cps:
        c.wait()
    own.wait()


def collect_channels(x, cid):
    q, t, w = x.shape
    return pl.pallas_call(
        collect_kernel,
        out_shape=jax.ShapeDtypeStruct((q, t // 8, 8 * w), x.dtype),
        in_specs=[VM],
        out_specs=ANY,
        scratch_shapes=[DMA((8,)), DMA((8,)), DMA(())],
        compiler_params=pltpu.CompilerParams(collective_id=cid, has_side_effects=True, vmem_limit_bytes=VLIM),
        name=f"collect_{cid}",
    )(x)


def gather_kernel(x_ref, o_ref, ss, rs, ps, pr, ls):
    f, d = greet((1, 2, 4, 6), ())
    h = x_ref.shape[1]

    def slot(g):
        return o_ref.at[:, pl.ds(pl.multiple_of(PAD + h * g, 16), h), :]

    cps = [remote(x_ref, slot(f), ss.at[k], rs.at[k], d, f ^ (2 * k)) for k in (3, 1, 2)]
    own = pltpu.make_async_copy(x_ref, slot(f), ls)
    own.start()
    pair = [remote(x_ref, slot(f), ps.at[0], pr.at[0], d, f ^ 1)]
    for k, c in zip((3, 1, 2), cps):
        c.wait_recv()
        got = slot(f ^ (2 * k))
        pair.append(remote(got, got, ps.at[k], pr.at[k], d, f ^ 1))
    for c in cps:
        c.wait_send()
    for c in pair:
        c.wait()
    own.wait()


def gather_rows(x, cid):
    q, h, C = x.shape
    return pl.pallas_call(
        gather_kernel,
        out_shape=jax.ShapeDtypeStruct((q, 8 * h + 2 * PAD, C), x.dtype),
        in_specs=[VM],
        out_specs=ANY,
        scratch_shapes=[DMA((4,)), DMA((4,)), DMA((4,)), DMA((4,)), DMA(())],
        compiler_params=pltpu.CompilerParams(collective_id=cid, has_side_effects=True, vmem_limit_bytes=VLIM),
        name=f"gather_{cid}",
    )(x)


def scatter_kernel(x_ref, o_ref, near, mine, far, ps, pr, ss, rs):
    f, d = greet((1, 2, 4, 6), ())
    c0 = f & 1
    pair = [
        remote(x_ref.at[2 * k + 1 - c0], near.at[k], ps.at[k], pr.at[k], d, f ^ 1) for k in range(4)
    ]
    me = lax.shift_right_logical(f, 1)
    cps = []
    for c in pair:
        c.wait()
    for k in (3, 1, 2, 0):
        g = me ^ k
        val = x_ref[2 * g + c0].astype(jnp.float32) + near[g].astype(jnp.float32)
        if k:
            mine[k] = val.astype(mine.dtype)
            cps.append(remote(mine.at[k], far.at[k], ss.at[k], rs.at[k], d, f ^ (2 * k)))
        else:
            o_ref[...] = val
    for c in cps:
        c.wait()
    o_ref[...] += far[1].astype(jnp.float32) + far[2].astype(jnp.float32) + far[3].astype(jnp.float32)


def scatter_sum(x, cid):
    n, R, C = x.shape
    return pl.pallas_call(
        scatter_kernel,
        out_shape=jax.ShapeDtypeStruct((R, C), jnp.float32),
        in_specs=[VM],
        out_specs=VM,
        scratch_shapes=[
            pltpu.VMEM((4, R, C), x.dtype),
            pltpu.VMEM((4, R, C), x.dtype),
            pltpu.VMEM((4, R, C), x.dtype),
            DMA((4,)),
            DMA((4,)),
            DMA((4,)),
            DMA((4,)),
        ],
        compiler_params=pltpu.CompilerParams(collective_id=cid, has_side_effects=True, vmem_limit_bytes=VLIM),
        name=f"scatter_{cid}",
    )(x)


def nt_dot(a, b):
    return lax.dot_general(a, b, (((1,), (1,)), ((), ())), preferred_element_type=jnp.float32)


def nn_dot(a, b):
    return lax.dot_general(a, b, (((1,), (0,)), ((), ())), preferred_element_type=jnp.float32)


def tn_dot(a, b):
    return lax.dot_general(a, b, (((0,), (0,)), ((), ())), preferred_element_type=jnp.float32)


def span(shift, count):
    return max(0, -shift), min(count, count - shift)


def conv_forward_kernel(steps, y_ref, key_ref, k_ref, o_ref, acc):
    Q = y_ref.shape[0]
    h = o_ref.shape[2]
    w = y_ref.shape[2]
    out = k_ref.shape[1]
    dest = pl.program_id(0)
    base = PAD + h * dest
    T = 8 * h
    for b, s in enumerate(steps):
        acc[...] = jnp.zeros_like(acc)
        for i in (-1, 0, 1):
            first = h * dest + 16 * s * i

            @pl.when((first + h > 0) & (first < T))
            def _():
                at = pl.multiple_of(base + 16 * s * i, 16)
                for j in (-1, 0, 1):
                    lo, hi = span(s * j, Q)
                    here = key_ref[lo:hi, pl.ds(pl.multiple_of(base, 16), h), :]
                    there = key_ref[lo + s * j : hi + s * j, pl.ds(at, h), :]
                    ok = (here == there) & (here > 0)
                    ok = jnp.concatenate([ok] * (w // 128), axis=2)
                    x = jnp.where(ok, y_ref[lo + s * j : hi + s * j, pl.ds(at, h), :], 0)
                    x = x.reshape((hi - lo) * h, w)
                    acc[lo * h : hi * h] += nt_dot(x, k_ref[9 * b + 3 * (i + 1) + j + 1])

        o_ref[0, :, :, b * out : (b + 1) * out] = acc[...].reshape(Q, h, out).astype(o_ref.dtype)


def conv_forward(y, key, k, steps):
    Q, TT, w = y.shape
    h = (TT - 2 * PAD) // 8
    out = k.shape[1]
    return pl.pallas_call(
        functools.partial(conv_forward_kernel, steps),
        out_shape=jax.ShapeDtypeStruct((8, Q, h, 3 * out), jnp.bfloat16),
        grid=(8,),
        in_specs=[VM, VM, VM],
        out_specs=pl.BlockSpec((1, Q, h, 3 * out), lambda i: (i, 0, 0, 0)),
        scratch_shapes=[pltpu.VMEM((Q * h, out), jnp.float32)],
        compiler_params=pltpu.CompilerParams(vmem_limit_bytes=VLIM),
        name="conv_forward",
    )(y, key, k)


def conv_data_kernel(steps, g_ref, key_ref, k_ref, o_ref, acc):
    Q = g_ref.shape[0]
    h = o_ref.shape[1]
    w = o_ref.shape[2]
    out = k_ref.shape[1]
    dest = pl.program_id(0)
    base = PAD + h * dest
    T = 8 * h
    acc[...] = jnp.zeros_like(acc)
    for b, s in enumerate(steps):
        for i in (-1, 0, 1):
            first = h * dest - 16 * s * i

            @pl.when((first + h > 0) & (first < T))
            def _():
                at = pl.multiple_of(base - 16 * s * i, 16)
                for j in (-1, 0, 1):
                    lo, hi = span(-s * j, Q)
                    here = key_ref[lo:hi, pl.ds(pl.multiple_of(base, 16), h), :]
                    there = key_ref[lo - s * j : hi - s * j, pl.ds(at, h), :]
                    ok = (here == there) & (here > 0)
                    ok = jnp.concatenate([ok] * (out // 128), axis=2)
                    x = jnp.where(
                        ok, g_ref[lo - s * j : hi - s * j, pl.ds(at, h), b * out : (b + 1) * out], 0
                    )
                    x = x.reshape((hi - lo) * h, out)
                    acc[lo * h : hi * h] += nn_dot(x, k_ref[9 * b + 3 * (i + 1) + j + 1])

    o_ref[...] = acc[...].reshape(Q, h, w).astype(o_ref.dtype)


def conv_data(g, key, k, steps):
    Q, TT, _ = g.shape
    h = (TT - 2 * PAD) // 8
    w = k.shape[2]
    return pl.pallas_call(
        functools.partial(conv_data_kernel, steps),
        out_shape=jax.ShapeDtypeStruct((Q, 8 * h, w), jnp.bfloat16),
        grid=(8,),
        in_specs=[VM, VM, VM],
        out_specs=pl.BlockSpec((Q, h, w), lambda i: (0, i, 0)),
        scratch_shapes=[pltpu.VMEM((Q * h, w), jnp.float32)],
        compiler_params=pltpu.CompilerParams(vmem_limit_bytes=VLIM),
        name="conv_data",
    )(g, key, k)


def conv_weight_kernel(steps, y_ref, key_ref, g_ref, o_ref, x_ref):
    Q = y_ref.shape[0]
    w = y_ref.shape[2]
    out = o_ref.shape[1]
    TT = y_ref.shape[1]
    T = TT - 2 * PAD
    b = pl.program_id(0)
    for n, s in enumerate(steps):

        @pl.when(b == n)
        def _():
            for i in (-1, 0, 1):
                r0, r1 = span(16 * s * i, T)
                r0, r1 = r0 // 128 * 128, -(-r1 // 128) * 128
                for j in (-1, 0, 1):
                    lo, hi = span(s * j, Q)
                    L = r1 - r0

                    def one(q, _):
                        here = key_ref[q, PAD + r0 : PAD + r1, :]
                        a = PAD + r0 + 16 * s * i
                        there = key_ref[q + s * j, a : a + L, :]
                        ok = (here == there) & (here > 0)
                        ok = jnp.concatenate([ok] * (w // 128), axis=1)
                        x = jnp.where(ok, y_ref[q + s * j, a : a + L, :], 0)
                        x_ref[pl.ds(pl.multiple_of((q - lo) * L, 128), L), :] = x
                        return 0

                    lax.fori_loop(lo, hi, one, 0)
                    d = g_ref[lo:hi, PAD + r0 : PAD + r1, n * out : (n + 1) * out]
                    d = d.reshape((hi - lo) * L, out)
                    o_ref[3 * (i + 1) + j + 1] = tn_dot(d, x_ref[: (hi - lo) * L, :]).astype(o_ref.dtype)


def conv_weight(y, key, g, steps, out):
    Q, TT, w = y.shape
    T = TT - 2 * PAD
    return pl.pallas_call(
        functools.partial(conv_weight_kernel, steps),
        out_shape=jax.ShapeDtypeStruct((27, out, w), jnp.bfloat16),
        grid=(3,),
        in_specs=[VM, VM, VM],
        out_specs=pl.BlockSpec((9, out, w), lambda i: (i, 0, 0)),
        scratch_shapes=[pltpu.VMEM((Q * T, w), jnp.bfloat16)],
        compiler_params=pltpu.CompilerParams(vmem_limit_bytes=VLIM),
        name="conv_weight",
    )(y, key, g)


def norm_coeffs(totals, squares, count):
    average = totals / count
    return average, lax.rsqrt(squares / count - average * average + eps)


def fast_body(
    features, crop_ids, labels, w_reduce, gain_reduce, bias_reduce, w_dilated, gain_dilated, bias_dilated,
    w_expand, gain_expand, bias_expand, w_point, gain_point, bias_point, w_rate, gain_rate, bias_rate,
    w_rate_double, gain_rate_double, bias_rate_double, w_rate_triple, gain_rate_triple, bias_rate_triple,
    w_pool, w_merge, gain_merge, bias_merge, w_classes,
):
    rows, cols, C = features.shape
    Q = cols // 4
    h = rows * 4
    N = rows * cols
    nf = lax.axis_size("fsdp")
    W = gain_point.shape[0]
    steps = (RATE // 4, 2 * RATE // 4, 3 * RATE // 4)
    place = lax.axis_index("fsdp")

    def perm(a):
        a = a.reshape((rows, Q, 4) + a.shape[2:])
        return jnp.swapaxes(a, 0, 1).reshape((N,) + a.shape[3:])

    def unperm(a):
        a = a.reshape((Q, rows, 4) + a.shape[1:])
        return jnp.swapaxes(a, 0, 1).reshape((rows, cols) + a.shape[3:])

    kt = jnp.concatenate([jnp.swapaxes(w.reshape(9, C, -1), 1, 2) for w in (w_rate, w_rate_double, w_rate_triple)])
    full_reduce = lax.all_gather(w_reduce, "fsdp", axis=1, tiled=True)
    full_dilated = lax.all_gather(w_dilated, "fsdp", axis=3, tiled=True)
    full_expand = lax.all_gather(w_expand, "fsdp", axis=1, tiled=True)
    kernel = lax.all_to_all(kt, "fsdp", split_axis=2, concat_axis=1, tiled=True)
    full_point = lax.all_gather(w_point, "fsdp", axis=1, tiled=True)
    full_merge = lax.all_gather(w_merge, "fsdp", axis=1, tiled=True)
    full_pool = lax.all_gather(w_pool, "fsdp", axis=1, tiled=True)
    full_classes = lax.all_gather(w_classes, "fsdp", axis=0, tiled=True)

    x0 = perm(features)
    local_crop = perm(crop_ids) - lax.axis_index("dp") * CROPS_TILE
    in_crop = perm(crop_ids) >= 0
    inside = in_crop.astype(jnp.float32)[:, None]
    key_loc = jnp.where(in_crop, local_crop + 1, 0).astype(jnp.bfloat16)
    key_all = lax.all_gather(key_loc.reshape(Q, h), "fsdp", axis=1, tiled=True)
    key_pad = jnp.pad(key_all, ((0, 0), (PAD, PAD)))
    key = jnp.broadcast_to(key_pad[:, :, None], key_pad.shape + (128,))

    a_one = flat_dot(x0, full_reduce)
    neck = a_one.shape[1]
    st = total_sum(
        [jnp.sum(a_one * inside, axis=0), jnp.sum(a_one * a_one * inside, axis=0), jnp.full((neck,), jnp.sum(inside))], 1
    )
    count = st[2, 0]
    m_one, s_one = norm_coeffs(st[0], st[1], count)
    n_one = (a_one - m_one) * s_one
    p_one = n_one * gain_reduce + bias_reduce
    h_one = jax.nn.silu(p_one).astype(jnp.bfloat16)

    def halo(a):
        a = a.reshape(Q, h, -1)
        e = 4 * DILATION_SPAN
        up = passed_along(a[:, h - e :], "fsdp", 1)
        down = passed_along(a[:, :e], "fsdp", -1)
        return jnp.concatenate([up, a, down], axis=1)

    e = 4 * DILATION_SPAN
    key_near = lax.dynamic_slice_in_dim(key_pad, PAD - e + h * place, h + 2 * e, axis=1)
    key_here = key_near[:, e : e + h]

    def taps(a):
        a = jnp.pad(a, ((1, 1), (0, 0), (0, 0)))
        kn = jnp.pad(key_near, ((1, 1), (0, 0)))
        pieces = []
        for i in range(3):
            for j in range(3):
                ok = (kn[j : j + Q, e * i : e * i + h] == key_here) & (key_here > 0)
                pieces.append(jnp.where(ok[:, :, None], a[j : j + Q, e * i : e * i + h], 0).reshape(N, -1))
        return pieces

    x_taps = taps(halo(h_one))
    a_two = sum(flat_dot(x_taps[t], full_dilated[t // 3, t % 3]) for t in range(9))
    st = total_sum([jnp.sum(a_two * inside, axis=0), jnp.sum(a_two * a_two * inside, axis=0)], 2)
    m_two, s_two = norm_coeffs(st[0], st[1], count)
    n_two = (a_two - m_two) * s_two
    p_two = n_two * gain_dilated + bias_dilated
    h_two = jax.nn.silu(p_two).astype(jnp.bfloat16)
    a_three = flat_dot(h_two, full_expand)
    st = total_sum([jnp.sum(a_three * inside, axis=0), jnp.sum(a_three * a_three * inside, axis=0)], 3)
    m_three, s_three = norm_coeffs(st[0], st[1], count)
    n_three = (a_three - m_three) * s_three
    p_three = n_three * gain_expand + bias_expand + x0
    y = jax.nn.silu(p_three).astype(jnp.bfloat16)

    y_own = spread_channels(y.reshape(Q, h, C), 4)
    part = conv_forward(y_own, key, kernel, steps)
    a_rates = scatter_sum(part.reshape(nf, N, 3 * W), 5)
    a_point = flat_dot(y, full_point)
    a_br = jnp.concatenate([a_point, a_rates], axis=1)
    member = local_crop[:, None] == jnp.arange(CROPS_TILE)[None, :]
    member = (member & in_crop[:, None]).astype(jnp.bfloat16)
    crop_sums = inner_dot(member, y)
    crop_sizes = jnp.sum(member.astype(jnp.float32), axis=0)
    crop_sums, crop_sizes = lax.psum((crop_sums, crop_sizes), "fsdp")
    st = total_sum([jnp.sum(a_br * inside, axis=0), jnp.sum(a_br * a_br * inside, axis=0)], 6)
    m_br, s_br = norm_coeffs(st[0], st[1], count)
    g_br = jnp.concatenate([gain_point, gain_rate, gain_rate_double, gain_rate_triple])
    b_br = jnp.concatenate([bias_point, bias_rate, bias_rate_double, bias_rate_triple])
    n_br = (a_br - m_br) * s_br
    p_br = n_br * g_br + b_br
    u_br = jax.nn.silu(p_br).astype(jnp.bfloat16)
    pooled = (crop_sums / crop_sizes[:, None]).astype(jnp.bfloat16)
    pool_act = flat_dot(pooled, full_pool)
    pool_low = jax.nn.silu(pool_act).astype(jnp.bfloat16)
    u_pool = flat_dot(member, pool_low).astype(jnp.bfloat16)
    joined = jnp.concatenate([u_br, u_pool], axis=1)
    a_merge = flat_dot(joined, full_merge)
    st = total_sum([jnp.sum(a_merge * inside, axis=0), jnp.sum(a_merge * a_merge * inside, axis=0)], 7)
    m_merge, s_merge = norm_coeffs(st[0], st[1], count)
    n_merge = (a_merge - m_merge) * s_merge
    p_merge = n_merge * gain_merge + bias_merge
    merged = jax.nn.silu(p_merge).astype(jnp.bfloat16)
    logits = flat_dot(merged, full_classes)
    class_logits = unperm(logits.astype(jnp.bfloat16))

    probability = jax.nn.softmax(logits, axis=1)
    targets = (perm(labels)[:, None] == jnp.arange(CLASSES)[None, :]).astype(jnp.float32)
    d_logits = (inside * (probability - targets) / count).astype(jnp.bfloat16)
    grad_classes = inner_dot(merged, d_logits)

    def back(up, n, s, gain, cid):
        st = total_sum([jnp.sum(up * inside, axis=0), jnp.sum(up * n * inside, axis=0)], cid)
        d = inside * gain * s * (up - st[0] / count - n * st[1] / count)
        return d.astype(jnp.bfloat16), st[1], st[0]

    d_merge, gg_merge, gb_merge = back(outer_dot(d_logits, full_classes) * slope(p_merge), n_merge, s_merge, gain_merge, 8)
    grad_merge = inner_dot(joined, d_merge)
    d_joined = outer_dot(d_merge, full_merge)
    d_br, gg_br, gb_br = back(d_joined[:, : 4 * W] * slope(p_br), n_br, s_br, g_br, 9)
    crop_grad = lax.dot_general(
        member.astype(jnp.float32), d_joined[:, 4 * W :], (((0,), (0,)), ((), ())),
        precision=lax.Precision.HIGHEST, preferred_element_type=jnp.float32,
    )
    crop_grad = lax.psum(crop_grad, "fsdp")
    d_pool = (crop_grad * slope(pool_act)).astype(jnp.bfloat16)
    owned = (jnp.arange(CROPS_TILE) % nf == place).astype(jnp.float32)[:, None]
    grad_pool = inner_dot(pooled, (d_pool * owned).astype(jnp.bfloat16))
    grad_pooled = outer_dot(d_pool, full_pool) / crop_sizes[:, None]
    g_all = gather_rows(d_br[:, W:].reshape(Q, h, 3 * W), 10)
    d_y_own = conv_data(g_all, key, kernel, steps)
    d_y = collect_channels(d_y_own, 11).reshape(N, C).astype(jnp.float32)
    grad_k = conv_weight(y_own, key, g_all, steps, W)
    grad_k = lax.all_to_all(grad_k, "fsdp", split_axis=1, concat_axis=2, tiled=True)
    grad_k = lax.psum(grad_k, "dp").astype(jnp.float32)
    grad_point = inner_dot(y, d_br[:, :W])
    d_y = d_y + outer_dot(d_br[:, :W], full_point)
    d_y = d_y + lax.dot_general(
        member.astype(jnp.float32), grad_pooled, (((1,), (0,)), ((), ())),
        precision=lax.Precision.HIGHEST, preferred_element_type=jnp.float32,
    )
    d_p3 = d_y * slope(p_three)
    d_three, gg_expand, gb_expand = back(d_p3, n_three, s_three, gain_expand, 12)
    grad_expand = inner_dot(h_two, d_three)
    d_h2 = outer_dot(d_three, full_expand)
    d_two, gg_dilated, gb_dilated = back(d_h2 * slope(p_two), n_two, s_two, gain_dilated, 13)
    grad_dilated = jnp.stack([inner_dot(x_taps[t], d_two) for t in range(9)])
    d_taps = taps(halo(d_two))
    d_h1 = sum(outer_dot(d_taps[8 - t], full_dilated[t // 3, t % 3]) for t in range(9))
    d_one, gg_reduce, gb_reduce = back(d_h1 * slope(p_one), n_one, s_one, gain_reduce, 14)
    grad_reduce = inner_dot(x0, d_one)
    grad_features = unperm(d_p3 + outer_dot(d_one, full_reduce))

    def shard(g, dim):
        g = lax.psum_scatter(g, "fsdp", scatter_dimension=dim, tiled=True)
        return lax.psum(g.astype(jnp.bfloat16), "dp").astype(jnp.float32)

    grad_k = jnp.swapaxes(grad_k.reshape(3, 3, 3, -1, C), 3, 4)
    return (
        class_logits,
        grad_features,
        shard(grad_reduce, 1), gg_reduce, gb_reduce,
        shard(grad_dilated, 2).reshape(3, 3, neck, -1), gg_dilated, gb_dilated,
        shard(grad_expand, 1), gg_expand, gb_expand,
        shard(grad_point, 1), gg_br[:W], gb_br[:W],
        grad_k[0], gg_br[W : 2 * W], gb_br[W : 2 * W],
        grad_k[1], gg_br[2 * W : 3 * W], gb_br[2 * W : 3 * W],
        grad_k[2], gg_br[3 * W :], gb_br[3 * W :],
        shard(grad_pool, 1),
        shard(grad_merge, 1), gg_merge, gb_merge,
        shard(grad_classes, 0),
    )


def passed_along(value, axis, by):
    count = lax.axis_size(axis)
    pairs = [(i, i + by) for i in range(count) if 0 <= i + by < count]
    return lax.ppermute(value, axis, pairs)


def padded(cells, sides, width):
    for axis, dim in sides:
        count = lax.axis_size(axis)
        ends = count - 1
        head = lax.slice_in_dim(cells, 0, width, axis=dim)
        tail = lax.slice_in_dim(cells, cells.shape[dim] - width, cells.shape[dim], axis=dim)
        cells = jnp.concatenate(
            [
                lax.ppermute(tail, axis, [(i, (i + 1) % count) for i in range(ends)]),
                cells,
                lax.ppermute(head, axis, [((i + 1) % count, i) for i in range(ends)]),
            ],
            axis=dim,
        )
    return cells


def flat_dot(first_op, second_op):
    return jnp.dot(first_op, second_op, preferred_element_type=jnp.float32)


def inner_dot(first_op, second_op):
    return lax.dot_general(
        first_op, second_op, (((0,), (0,)), ((), ())), preferred_element_type=jnp.float32
    )


def outer_dot(first_op, second_op):
    return lax.dot_general(
        first_op, second_op, (((1,), (1,)), ((), ())), preferred_element_type=jnp.float32
    )


def slope(values):
    gate_value = jax.nn.sigmoid(values)
    return gate_value * (1.0 + values * (1.0 - gate_value))


def widen_rows(values, extent, mover):
    row_count = values.shape[0]
    neighbours = -(-extent // row_count)
    above = [mover(values, distance) for distance in range(neighbours, 0, -1)]
    below = [mover(values, -distance) for distance in range(1, neighbours + 1)]
    stacked = jnp.concatenate(above + [values] + below, axis=0)
    start_row = neighbours * row_count - extent
    return stacked[start_row : start_row + row_count + 2 * extent]


def rim_slice(widened, spacing, margin, height):
    return widened[margin - spacing : margin + height + spacing]


def offset_table(broad_key_rows, crop_random_keys, spacing, margin):
    height, breadth = crop_random_keys.shape
    first_row = margin - spacing
    extended = jnp.pad(
        broad_key_rows[first_row : first_row + height + 2 * spacing], ((0, 0), (spacing, spacing))
    )
    tables = []
    for row_tap in range(3):
        for col_tap in range(3):
            nearby = extended[
                row_tap * spacing : row_tap * spacing + height,
                col_tap * spacing : col_tap * spacing + breadth,
            ]
            tables.append(
                ((nearby == crop_random_keys) & (crop_random_keys > 0))
                .astype(jnp.float32)
                .reshape(height * breadth, 1)
            )
    return tables


def spread_offsets(widened, kernel, tables, spacing, height, breadth):
    channels = widened.shape[2]
    extended = jnp.pad(widened, ((0, 0), (spacing, spacing), (0, 0)))
    summed = jnp.zeros((height * breadth, kernel.shape[3]), jnp.float32)
    for row_tap in range(3):
        for col_tap in range(3):
            nearby = extended[
                row_tap * spacing : row_tap * spacing + height,
                col_tap * spacing : col_tap * spacing + breadth,
            ]
            summed = summed + tables[3 * row_tap + col_tap] * flat_dot(
                nearby.reshape(height * breadth, channels), kernel[row_tap, col_tap]
            )
    return summed


def collect_taps(widened, kernel, tables, spacing, height, breadth):
    channels = widened.shape[2]
    extended = jnp.pad(widened, ((0, 0), (spacing, spacing), (0, 0)))
    summed = jnp.zeros((height * breadth, kernel.shape[2]), jnp.float32)
    for row_tap in range(3):
        for col_tap in range(3):
            back_row = 2 - row_tap
            back_col = 2 - col_tap
            nearby = extended[
                back_row * spacing : back_row * spacing + height,
                back_col * spacing : back_col * spacing + breadth,
            ]
            summed = summed + tables[3 * back_row + back_col] * outer_dot(
                nearby.reshape(height * breadth, channels), kernel[row_tap, col_tap]
            )
    return summed


def kernel_offsets(widened, grads_low, tables, spacing, height, breadth):
    channels = widened.shape[2]
    extended = jnp.pad(widened, ((0, 0), (spacing, spacing), (0, 0)))
    pieces = []
    for row_tap in range(3):
        for col_tap in range(3):
            nearby = extended[
                row_tap * spacing : row_tap * spacing + height,
                col_tap * spacing : col_tap * spacing + breadth,
            ]
            masked = (tables[3 * row_tap + col_tap] * grads_low).astype(jnp.bfloat16)
            pieces.append(inner_dot(nearby.reshape(height * breadth, channels), masked))
    return pieces


def statistics(partial_value):
    return lax.psum(partial_value, ("dp", "fsdp"))


def norm_apply(values, totals, squares, pixel_count, factor, offset):
    average = totals / pixel_count
    inverse = lax.rsqrt(squares / pixel_count - average * average + eps)
    normed = (values - average) * inverse
    return (normed * factor + offset, normed, inverse)


def norm_forward(values, inside, pixel_count, factor, offset):
    totals, squares = statistics(
        (jnp.sum(values * inside, axis=0), jnp.sum(values * values * inside, axis=0))
    )
    return norm_apply(values, totals, squares, pixel_count, factor, offset)


def norm_backward(upstream, normed, inverse, factor, inside, pixel_count):
    totals, crossed = lax.psum(
        (jnp.sum(upstream * inside, axis=0), jnp.sum(upstream * normed * inside, axis=0)),
        ("dp", "fsdp"),
    )
    passed = (
        inside
        * factor
        * inverse
        * (upstream - totals / pixel_count - normed * crossed / pixel_count)
    )
    return (passed, crossed, totals)


def body(
    features,
    crop_ids,
    labels,
    w_reduce,
    gain_reduce,
    bias_reduce,
    w_dilated,
    gain_dilated,
    bias_dilated,
    w_expand,
    gain_expand,
    bias_expand,
    w_point,
    gain_point,
    bias_point,
    w_rate,
    gain_rate,
    bias_rate,
    w_rate_double,
    gain_rate_double,
    bias_rate_double,
    w_rate_triple,
    gain_rate_triple,
    bias_rate_triple,
    w_pool,
    w_merge,
    gain_merge,
    bias_merge,
    w_classes,
):
    local_rows, local_columns, channels = features.shape
    pixel_values = local_rows * local_columns
    inputs_flat = features.reshape(pixel_values, channels)
    crop_random_keys = crop_ids + 1
    outer_extent = 3 * RATE
    spacings = (RATE, 2 * RATE, 3 * RATE)
    broad_key_rows = widen_rows(
        crop_random_keys,
        outer_extent,
        lambda piece, distance: passed_along(piece, "fsdp", distance),
    )
    inside = (crop_random_keys > 0).astype(jnp.float32).reshape(pixel_values, 1)
    inner_neck = offset_table(broad_key_rows, crop_random_keys, DILATION_SPAN, outer_extent)
    near_rates = [
        offset_table(broad_key_rows, crop_random_keys, spacing, outer_extent)
        for spacing in spacings
    ]
    (
        full_reduce,
        complete_dilated,
        full_expand,
        full_point,
        full_rate,
        full_double,
        full_triple,
        full_pool,
        full_merge,
        full_classes,
    ) = (
        lax.all_gather(w_reduce, "fsdp", axis=1, tiled=True),
        lax.all_gather(w_dilated, "fsdp", axis=3, tiled=True),
        lax.all_gather(w_expand, "fsdp", axis=1, tiled=True),
        lax.all_gather(w_point, "fsdp", axis=1, tiled=True),
        lax.all_gather(w_rate, "fsdp", axis=3, tiled=True),
        lax.all_gather(w_rate_double, "fsdp", axis=3, tiled=True),
        lax.all_gather(w_rate_triple, "fsdp", axis=3, tiled=True),
        lax.all_gather(w_pool, "fsdp", axis=1, tiled=True),
        lax.all_gather(w_merge, "fsdp", axis=1, tiled=True),
        lax.all_gather(w_classes, "fsdp", axis=0, tiled=True),
    )
    rate_kernels = (full_rate, full_double, full_triple)
    rate_gains = (gain_rate, gain_rate_double, gain_rate_triple)
    rate_biases = (bias_rate, bias_rate_double, bias_rate_triple)
    act_one = flat_dot(inputs_flat, full_reduce)
    totals, squares, pixel_count = statistics(
        (
            jnp.sum(act_one * inside, axis=0),
            jnp.sum(act_one * act_one * inside, axis=0),
            jnp.sum(inside),
        )
    )
    pre_one, normed_one, inverse_one = norm_apply(
        act_one, totals, squares, pixel_count, gain_reduce, bias_reduce
    )
    first_hidden = jax.nn.silu(pre_one).astype(jnp.bfloat16)
    first_broad = padded(
        first_hidden.reshape(local_rows, local_columns, -1), (("fsdp", 0),), DILATION_SPAN
    )
    second_activation = spread_offsets(
        first_broad, complete_dilated, inner_neck, DILATION_SPAN, local_rows, local_columns
    )
    pre_two, normed_two, inverse_two = norm_forward(
        second_activation, inside, pixel_count, gain_dilated, bias_dilated
    )
    hidden_two = jax.nn.silu(pre_two).astype(jnp.bfloat16)
    act_three = flat_dot(hidden_two, full_expand)
    pre_three, normed_three, inverse_three = norm_forward(
        act_three, inside, pixel_count, gain_expand, bias_expand
    )
    pre_three = pre_three + inputs_flat
    block_out = jax.nn.silu(pre_three).astype(jnp.bfloat16)
    wide_block = widen_rows(
        block_out.reshape(local_rows, local_columns, channels),
        outer_extent,
        lambda piece, distance: passed_along(piece, "fsdp", distance),
    )
    point_act = flat_dot(block_out, full_point)
    pre_point, normed_point, inverse_point = norm_forward(
        point_act, inside, pixel_count, gain_point, bias_point
    )
    branch_point = jax.nn.silu(pre_point).astype(jnp.bfloat16)
    rate_states = []
    rate_branches = []
    for kernel, factor, offset, spacing, tables in zip(
        rate_kernels, rate_gains, rate_biases, spacings, near_rates
    ):
        rate_act = spread_offsets(
            rim_slice(wide_block, spacing, outer_extent, local_rows),
            kernel,
            tables,
            spacing,
            local_rows,
            local_columns,
        )
        pre_rate, normed_rate, inverse_rate = norm_forward(
            rate_act, inside, pixel_count, factor, offset
        )
        rate_states.append((pre_rate, normed_rate, inverse_rate))
        rate_branches.append(jax.nn.silu(pre_rate).astype(jnp.bfloat16))
    crop_flat = crop_ids.reshape(pixel_values)
    crop_total = CROPS_TILE
    first_crop = lax.axis_index("dp") * crop_total
    owner_group = lax.axis_size("fsdp")
    owner_place = lax.axis_index("fsdp")
    local_crop = crop_flat - first_crop
    member = local_crop[:, None] == jnp.arange(crop_total)[None, :]
    member_low = member.astype(jnp.bfloat16)
    crop_sums = inner_dot(member_low, block_out)
    crop_sizes = jnp.sum(member.astype(jnp.float32), axis=0)
    crop_sums, crop_sizes = lax.psum((crop_sums, crop_sizes), "fsdp")
    pooled = (crop_sums / crop_sizes[:, None]).astype(jnp.bfloat16)
    pool_act = flat_dot(pooled, full_pool)
    pool_low = jax.nn.silu(pool_act).astype(jnp.bfloat16)
    branch_pool = flat_dot(member_low, pool_low).astype(jnp.bfloat16)
    joined = jnp.concatenate([branch_point] + rate_branches + [branch_pool], axis=1)
    merge_act = flat_dot(joined, full_merge)
    pre_merge, normed_merge, inverse_merge = norm_forward(
        merge_act, inside, pixel_count, gain_merge, bias_merge
    )
    merged = jax.nn.silu(pre_merge).astype(jnp.bfloat16)
    logits_full = flat_dot(merged, full_classes)
    class_logits = logits_full.astype(jnp.bfloat16).reshape(local_rows, local_columns, -1)
    (
        full_reduce,
        complete_dilated,
        full_expand,
        full_point,
        full_rate,
        full_double,
        full_triple,
        full_pool,
        full_merge,
        full_classes,
    ) = (
        lax.all_gather(w_reduce, "fsdp", axis=1, tiled=True),
        lax.all_gather(w_dilated, "fsdp", axis=3, tiled=True),
        lax.all_gather(w_expand, "fsdp", axis=1, tiled=True),
        lax.all_gather(w_point, "fsdp", axis=1, tiled=True),
        lax.all_gather(w_rate, "fsdp", axis=3, tiled=True),
        lax.all_gather(w_rate_double, "fsdp", axis=3, tiled=True),
        lax.all_gather(w_rate_triple, "fsdp", axis=3, tiled=True),
        lax.all_gather(w_pool, "fsdp", axis=1, tiled=True),
        lax.all_gather(w_merge, "fsdp", axis=1, tiled=True),
        lax.all_gather(w_classes, "fsdp", axis=0, tiled=True),
    )
    rate_kernels = (full_rate, full_double, full_triple)
    highest = jnp.max(logits_full, axis=1, keepdims=True)
    shifted = jnp.exp(logits_full - highest)
    probability = shifted / jnp.sum(shifted, axis=1, keepdims=True)
    targets = (labels.reshape(pixel_values, 1) == jnp.arange(CLASSES)[None, :]).astype(jnp.float32)
    grad_logits = (inside * (probability - targets) / pixel_count).astype(jnp.bfloat16)
    grad_classes = inner_dot(merged, grad_logits)
    grad_merged = outer_dot(grad_logits, full_classes)
    passed, grad_gain_merge, grad_bias_merge = norm_backward(
        grad_merged * slope(pre_merge), normed_merge, inverse_merge, gain_merge, inside, pixel_count
    )
    grad_merge_act = passed.astype(jnp.bfloat16)
    grad_merge = inner_dot(joined, grad_merge_act)
    grad_joined = outer_dot(grad_merge_act, full_merge)
    branch_width = full_merge.shape[1]
    passed, grad_gain_point, grad_bias_point = norm_backward(
        grad_joined[:, :branch_width] * slope(pre_point),
        normed_point,
        inverse_point,
        gain_point,
        inside,
        pixel_count,
    )
    grad_point_act = passed.astype(jnp.bfloat16)
    grad_point = inner_dot(block_out, grad_point_act)
    grad_block = outer_dot(grad_point_act, full_point)
    rate_grads = []
    rate_weight_grads = []
    rate_gain_grads = []
    rate_bias_grads = []
    for branch in range(3):
        column = (1 + branch) * branch_width
        pre_rate, normed_rate, inverse_rate = rate_states[branch]
        passed, gain_grad, bias_grad = norm_backward(
            grad_joined[:, column : column + branch_width] * slope(pre_rate),
            normed_rate,
            inverse_rate,
            rate_gains[branch],
            inside,
            pixel_count,
        )
        grad_rate_act = passed.astype(jnp.bfloat16)
        pieces = kernel_offsets(
            rim_slice(wide_block, spacings[branch], outer_extent, local_rows),
            grad_rate_act,
            near_rates[branch],
            spacings[branch],
            local_rows,
            local_columns,
        )
        rate_weight_grads.append(jnp.stack(pieces).reshape(3, 3, channels, branch_width))
        rate_grads.append(grad_rate_act)
        rate_gain_grads.append(gain_grad)
        rate_bias_grads.append(bias_grad)
    rate_grads_low = jnp.concatenate(rate_grads, axis=1).reshape(local_rows, local_columns, -1)
    wide_grad_rate = widen_rows(
        rate_grads_low, outer_extent, lambda piece, distance: passed_along(piece, "fsdp", distance)
    )
    for branch in range(3):
        grad_slab = wide_grad_rate[:, :, branch * branch_width : (branch + 1) * branch_width]
        grad_block = grad_block + collect_taps(
            rim_slice(grad_slab, spacings[branch], outer_extent, local_rows),
            rate_kernels[branch],
            near_rates[branch],
            spacings[branch],
            local_rows,
            local_columns,
        )
    crop_grad = lax.dot_general(
        member.astype(jnp.float32),
        grad_joined[:, 4 * branch_width :],
        (((0,), (0,)), ((), ())),
        precision=lax.Precision.HIGHEST,
        preferred_element_type=jnp.float32,
    )
    crop_grad = lax.psum(crop_grad, "fsdp")
    grad_pool_act = (crop_grad * slope(pool_act)).astype(jnp.bfloat16)
    owned_crops = (jnp.arange(crop_total) % owner_group == owner_place).astype(jnp.float32)[:, None]
    grad_pool = inner_dot(pooled, (grad_pool_act * owned_crops).astype(jnp.bfloat16))
    grad_pooled = outer_dot(grad_pool_act, full_pool) / crop_sizes[:, None]
    grad_block = grad_block + inside * jnp.take(
        grad_pooled, jnp.clip(local_crop, 0, crop_total - 1), axis=0
    )
    grad_pre_three = grad_block * slope(pre_three)
    passed, grad_gain_expand, grad_bias_expand = norm_backward(
        grad_pre_three, normed_three, inverse_three, gain_expand, inside, pixel_count
    )
    grad_three = passed.astype(jnp.bfloat16)
    grad_expand = inner_dot(hidden_two, grad_three)
    grad_hidden_two = outer_dot(grad_three, full_expand)
    passed, grad_gain_dilated, grad_bias_dilated = norm_backward(
        grad_hidden_two * slope(pre_two), normed_two, inverse_two, gain_dilated, inside, pixel_count
    )
    second_gradient = passed.astype(jnp.bfloat16)
    dilated_fragments = kernel_offsets(
        first_broad, second_gradient, inner_neck, DILATION_SPAN, local_rows, local_columns
    )
    grad_dilated = jnp.stack(dilated_fragments).reshape(
        3, 3, second_gradient.shape[1], second_gradient.shape[1]
    )
    broad_neck_gradient = padded(
        second_gradient.reshape(local_rows, local_columns, -1), (("fsdp", 0),), DILATION_SPAN
    )
    grad_hidden_one = collect_taps(
        broad_neck_gradient, complete_dilated, inner_neck, DILATION_SPAN, local_rows, local_columns
    )
    passed, grad_gain_reduce, grad_bias_reduce = norm_backward(
        grad_hidden_one * slope(pre_one), normed_one, inverse_one, gain_reduce, inside, pixel_count
    )
    grad_one = passed.astype(jnp.bfloat16)
    grad_reduce = inner_dot(inputs_flat, grad_one)
    grad_features = (grad_pre_three + outer_dot(grad_one, full_reduce)).reshape(
        local_rows, local_columns, channels
    )
    shards = (
        lax.psum_scatter(grad_reduce, "fsdp", scatter_dimension=1, tiled=True),
        lax.psum_scatter(grad_dilated, "fsdp", scatter_dimension=3, tiled=True),
        lax.psum_scatter(grad_expand, "fsdp", scatter_dimension=1, tiled=True),
        lax.psum_scatter(grad_point, "fsdp", scatter_dimension=1, tiled=True),
        lax.psum_scatter(rate_weight_grads[0], "fsdp", scatter_dimension=3, tiled=True),
        lax.psum_scatter(rate_weight_grads[1], "fsdp", scatter_dimension=3, tiled=True),
        lax.psum_scatter(rate_weight_grads[2], "fsdp", scatter_dimension=3, tiled=True),
        lax.psum_scatter(grad_pool, "fsdp", scatter_dimension=1, tiled=True),
        lax.psum_scatter(grad_merge, "fsdp", scatter_dimension=1, tiled=True),
        lax.psum_scatter(grad_classes, "fsdp", scatter_dimension=0, tiled=True),
    )
    shards = (
        lax.psum(shards[0].astype(jnp.bfloat16), "dp").astype(jnp.float32),
        lax.psum(shards[1].astype(jnp.bfloat16), "dp").astype(jnp.float32),
        lax.psum(shards[2].astype(jnp.bfloat16), "dp").astype(jnp.float32),
        lax.psum(shards[3].astype(jnp.bfloat16), "dp").astype(jnp.float32),
        lax.psum(shards[4].astype(jnp.bfloat16), "dp").astype(jnp.float32),
        lax.psum(shards[5].astype(jnp.bfloat16), "dp").astype(jnp.float32),
        lax.psum(shards[6].astype(jnp.bfloat16), "dp").astype(jnp.float32),
        lax.psum(shards[7].astype(jnp.bfloat16), "dp").astype(jnp.float32),
        lax.psum(shards[8].astype(jnp.bfloat16), "dp").astype(jnp.float32),
        lax.psum(shards[9].astype(jnp.bfloat16), "dp").astype(jnp.float32),
    )
    return (
        class_logits,
        grad_features,
        shards[0],
        grad_gain_reduce,
        grad_bias_reduce,
        shards[1],
        grad_gain_dilated,
        grad_bias_dilated,
        shards[2],
        grad_gain_expand,
        grad_bias_expand,
        shards[3],
        grad_gain_point,
        grad_bias_point,
        shards[4],
        rate_gain_grads[0],
        rate_bias_grads[0],
        shards[5],
        rate_gain_grads[1],
        rate_bias_grads[1],
        shards[6],
        rate_gain_grads[2],
        rate_bias_grads[2],
        shards[7],
        shards[8],
        grad_gain_merge,
        grad_bias_merge,
        shards[9],
    )


def solution(mesh):
    tiled = mesh.shape["fsdp"] == 8 and mesh.shape["dp"] == 4

    return jax.shard_map(
        fast_body if tiled else body,
        mesh=mesh,
        in_specs=(
            P(("dp", "fsdp"), None, None),
            P(("dp", "fsdp"), None),
            P(("dp", "fsdp"), None),
            P(None, "fsdp"),
            P(),
            P(),
            P(None, None, None, "fsdp"),
            P(),
            P(),
            P(None, "fsdp"),
            P(),
            P(),
            P(None, "fsdp"),
            P(),
            P(),
            P(None, None, None, "fsdp"),
            P(),
            P(),
            P(None, None, None, "fsdp"),
            P(),
            P(),
            P(None, None, None, "fsdp"),
            P(),
            P(),
            P(None, "fsdp"),
            P(None, "fsdp"),
            P(),
            P(),
            P("fsdp", None),
        ),
        out_specs=(
            P(("dp", "fsdp"), None, None),
            P(("dp", "fsdp"), None, None),
            P(None, "fsdp"),
            P(),
            P(),
            P(None, None, None, "fsdp"),
            P(),
            P(),
            P(None, "fsdp"),
            P(),
            P(),
            P(None, "fsdp"),
            P(),
            P(),
            P(None, None, None, "fsdp"),
            P(),
            P(),
            P(None, None, None, "fsdp"),
            P(),
            P(),
            P(None, None, None, "fsdp"),
            P(),
            P(),
            P(None, "fsdp"),
            P(None, "fsdp"),
            P(),
            P(),
            P("fsdp", None),
        ),
        check_vma=False,
    )
```

```python
import functools
import jax
import jax.numpy as jnp
from jax import lax
from jax.experimental import pallas as pl
from jax.experimental.pallas import tpu as pltpu
from jax.sharding import PartitionSpec as P


CLASSES = 19
CROPS_TILE = 4
DILATION_SPAN = 4
RATE = 12

eps = 1e-05

MESH = pl.DeviceIdType.MESH
ANY = pl.BlockSpec(memory_space=pl.ANY)
VM = pl.BlockSpec(memory_space=pltpu.VMEM)
DMA = pltpu.SemaphoreType.DMA
PAD = 144
VLIM = 60 * 2**20


def greet(fs, ds):
    f = lax.axis_index("fsdp")
    d = lax.axis_index("dp")
    bar = pltpu.get_barrier_semaphore()
    for k in fs:
        pl.semaphore_signal(bar, inc=1, device_id=(d, f ^ k), device_id_type=MESH)
    for k in ds:
        pl.semaphore_signal(bar, inc=1, device_id=(d ^ k, f), device_id_type=MESH)
    pl.semaphore_wait(bar, len(fs) + len(ds))
    return f, d


def remote(src, dst, ss, rs, d, f):
    c = pltpu.make_async_remote_copy(
        src_ref=src, dst_ref=dst, send_sem=ss, recv_sem=rs, device_id=(d, f), device_id_type=MESH
    )
    c.start()
    return c


def sum_kernel(x_ref, o_ref, b1, b2, s1, r1, s2, r2):
    f, d = greet(range(1, 8), range(1, 4))
    b1[f] = x_ref[...]
    cps = [remote(x_ref, b1.at[f], s1.at[k], r1.at[k], d, f ^ k) for k in range(1, 8)]
    for c in cps:
        c.wait()
    tot = b1[0]
    for k in range(1, 8):
        tot = tot + b1[k]
    b2[d] = tot
    cps = [remote(b2.at[d], b2.at[d], s2.at[k], r2.at[k], d ^ k, f) for k in range(1, 4)]
    for c in cps:
        c.wait()
    tot = b2[0]
    for k in range(1, 4):
        tot = tot + b2[k]
    o_ref[...] = tot


def total_sum(rows, cid):
    x = jnp.stack(rows)
    R, C = x.shape
    return pl.pallas_call(
        sum_kernel,
        out_shape=jax.ShapeDtypeStruct((R, C), jnp.float32),
        in_specs=[VM],
        out_specs=VM,
        scratch_shapes=[
            pltpu.VMEM((8, R, C), jnp.float32),
            pltpu.VMEM((4, R, C), jnp.float32),
            DMA((8,)),
            DMA((8,)),
            DMA((4,)),
            DMA((4,)),
        ],
        compiler_params=pltpu.CompilerParams(collective_id=cid, has_side_effects=True),
        name=f"total_sum_{cid}",
    )(x)


def spread_kernel(x_ref, o_ref, ss, rs, ls):
    f, d = greet(range(1, 8), ())
    w = o_ref.shape[2]
    h = x_ref.shape[1]
    dst = o_ref.at[:, pl.ds(pl.multiple_of(PAD + h * f, 16), h), :]

    def part(g):
        return x_ref.at[:, :, pl.ds(pl.multiple_of(g * w, 128), w)]

    cps = [remote(part(f ^ k), dst, ss.at[k], rs.at[k], d, f ^ k) for k in (6, 7, 2, 3, 4, 5, 1)]
    own = pltpu.make_async_copy(part(f), dst, ls)
    own.start()
    for c in cps:
        c.wait()
    own.wait()


def spread_channels(x, cid):
    q, h, C = x.shape
    return pl.pallas_call(
        spread_kernel,
        out_shape=jax.ShapeDtypeStruct((q, 8 * h + 2 * PAD, C // 8), x.dtype),
        in_specs=[VM],
        out_specs=ANY,
        scratch_shapes=[DMA((8,)), DMA((8,)), DMA(())],
        compiler_params=pltpu.CompilerParams(collective_id=cid, has_side_effects=True, vmem_limit_bytes=VLIM),
        name=f"spread_{cid}",
    )(x)


def collect_kernel(x_ref, o_ref, ss, rs, ls):
    f, d = greet(range(1, 8), ())
    w = x_ref.shape[2]
    h = o_ref.shape[1]
    dst = o_ref.at[:, :, pl.ds(pl.multiple_of(f * w, 128), w)]

    def part(g):
        return x_ref.at[:, pl.ds(pl.multiple_of(h * g, 16), h), :]

    cps = [remote(part(f ^ k), dst, ss.at[k], rs.at[k], d, f ^ k) for k in (6, 7, 2, 3, 4, 5, 1)]
    own = pltpu.make_async_copy(part(f), dst, ls)
    own.start()
    for c in cps:
        c.wait()
    own.wait()


def collect_channels(x, cid):
    q, t, w = x.shape
    return pl.pallas_call(
        collect_kernel,
        out_shape=jax.ShapeDtypeStruct((q, t // 8, 8 * w), x.dtype),
        in_specs=[VM],
        out_specs=ANY,
        scratch_shapes=[DMA((8,)), DMA((8,)), DMA(())],
        compiler_params=pltpu.CompilerParams(collective_id=cid, has_side_effects=True, vmem_limit_bytes=VLIM),
        name=f"collect_{cid}",
    )(x)


def gather_kernel(x_ref, o_ref, ss, rs, ps, pr, ls):
    f, d = greet((1, 2, 4, 6), ())
    h = x_ref.shape[1]

    def slot(g):
        return o_ref.at[:, pl.ds(pl.multiple_of(PAD + h * g, 16), h), :]

    cps = [remote(x_ref, slot(f), ss.at[k], rs.at[k], d, f ^ (2 * k)) for k in (3, 1, 2)]
    own = pltpu.make_async_copy(x_ref, slot(f), ls)
    own.start()
    pair = [remote(x_ref, slot(f), ps.at[0], pr.at[0], d, f ^ 1)]
    for k, c in zip((3, 1, 2), cps):
        c.wait_recv()
        got = slot(f ^ (2 * k))
        pair.append(remote(got, got, ps.at[k], pr.at[k], d, f ^ 1))
    for c in cps:
        c.wait_send()
    for c in pair:
        c.wait()
    own.wait()


def gather_rows(x, cid):
    q, h, C = x.shape
    return pl.pallas_call(
        gather_kernel,
        out_shape=jax.ShapeDtypeStruct((q, 8 * h + 2 * PAD, C), x.dtype),
        in_specs=[VM],
        out_specs=ANY,
        scratch_shapes=[DMA((4,)), DMA((4,)), DMA((4,)), DMA((4,)), DMA(())],
        compiler_params=pltpu.CompilerParams(collective_id=cid, has_side_effects=True, vmem_limit_bytes=VLIM),
        name=f"gather_{cid}",
    )(x)


def scatter_kernel(x_ref, o_ref, near, mine, far, ps, pr, ss, rs):
    f, d = greet((1, 2, 4, 6), ())
    c0 = f & 1
    pair = [
        remote(x_ref.at[2 * k + 1 - c0], near.at[k], ps.at[k], pr.at[k], d, f ^ 1) for k in range(4)
    ]
    me = lax.shift_right_logical(f, 1)
    cps = []
    for c in pair:
        c.wait()
    for k in (3, 1, 2, 0):
        g = me ^ k
        val = x_ref[2 * g + c0].astype(jnp.float32) + near[g].astype(jnp.float32)
        if k:
            mine[k] = val.astype(mine.dtype)
            cps.append(remote(mine.at[k], far.at[k], ss.at[k], rs.at[k], d, f ^ (2 * k)))
        else:
            o_ref[...] = val
    for c in cps:
        c.wait()
    o_ref[...] += far[1].astype(jnp.float32) + far[2].astype(jnp.float32) + far[3].astype(jnp.float32)


def scatter_sum(x, cid):
    n, R, C = x.shape
    return pl.pallas_call(
        scatter_kernel,
        out_shape=jax.ShapeDtypeStruct((R, C), jnp.float32),
        in_specs=[VM],
        out_specs=VM,
        scratch_shapes=[
            pltpu.VMEM((4, R, C), x.dtype),
            pltpu.VMEM((4, R, C), x.dtype),
            pltpu.VMEM((4, R, C), x.dtype),
            DMA((4,)),
            DMA((4,)),
            DMA((4,)),
            DMA((4,)),
        ],
        compiler_params=pltpu.CompilerParams(collective_id=cid, has_side_effects=True, vmem_limit_bytes=VLIM),
        name=f"scatter_{cid}",
    )(x)


def nt_dot(a, b):
    return lax.dot_general(a, b, (((1,), (1,)), ((), ())), preferred_element_type=jnp.float32)


def nn_dot(a, b):
    return lax.dot_general(a, b, (((1,), (0,)), ((), ())), preferred_element_type=jnp.float32)


def tn_dot(a, b):
    return lax.dot_general(a, b, (((0,), (0,)), ((), ())), preferred_element_type=jnp.float32)


def span(shift, count):
    return max(0, -shift), min(count, count - shift)


def conv_forward_kernel(steps, y_ref, key_ref, k_ref, o_ref, acc):
    Q = y_ref.shape[0]
    h = o_ref.shape[2]
    w = y_ref.shape[2]
    out = k_ref.shape[1]
    dest = pl.program_id(0)
    base = PAD + h * dest
    T = 8 * h
    for b, s in enumerate(steps):
        acc[...] = jnp.zeros_like(acc)
        for i in (-1, 0, 1):
            first = h * dest + 16 * s * i

            @pl.when((first + h > 0) & (first < T))
            def _():
                at = pl.multiple_of(base + 16 * s * i, 16)
                for j in (-1, 0, 1):
                    lo, hi = span(s * j, Q)
                    here = key_ref[lo:hi, pl.ds(pl.multiple_of(base, 16), h), :]
                    there = key_ref[lo + s * j : hi + s * j, pl.ds(at, h), :]
                    ok = (here == there) & (here > 0)
                    ok = jnp.concatenate([ok] * (w // 128), axis=2)
                    x = jnp.where(ok, y_ref[lo + s * j : hi + s * j, pl.ds(at, h), :], 0)
                    x = x.reshape((hi - lo) * h, w)
                    acc[lo * h : hi * h] += nt_dot(x, k_ref[9 * b + 3 * (i + 1) + j + 1])

        o_ref[0, :, :, b * out : (b + 1) * out] = acc[...].reshape(Q, h, out).astype(o_ref.dtype)


def conv_forward(y, key, k, steps):
    Q, TT, w = y.shape
    h = (TT - 2 * PAD) // 8
    out = k.shape[1]
    return pl.pallas_call(
        functools.partial(conv_forward_kernel, steps),
        out_shape=jax.ShapeDtypeStruct((8, Q, h, 3 * out), jnp.bfloat16),
        grid=(8,),
        in_specs=[VM, VM, VM],
        out_specs=pl.BlockSpec((1, Q, h, 3 * out), lambda i: (i, 0, 0, 0)),
        scratch_shapes=[pltpu.VMEM((Q * h, out), jnp.float32)],
        compiler_params=pltpu.CompilerParams(vmem_limit_bytes=VLIM),
        name="conv_forward",
    )(y, key, k)


def conv_data_kernel(steps, g_ref, key_ref, k_ref, o_ref, acc):
    Q = g_ref.shape[0]
    h = o_ref.shape[1]
    w = o_ref.shape[2]
    out = k_ref.shape[1]
    dest = pl.program_id(0)
    base = PAD + h * dest
    T = 8 * h
    acc[...] = jnp.zeros_like(acc)
    for b, s in enumerate(steps):
        for i in (-1, 0, 1):
            first = h * dest - 16 * s * i

            @pl.when((first + h > 0) & (first < T))
            def _():
                at = pl.multiple_of(base - 16 * s * i, 16)
                for j in (-1, 0, 1):
                    lo, hi = span(-s * j, Q)
                    here = key_ref[lo:hi, pl.ds(pl.multiple_of(base, 16), h), :]
                    there = key_ref[lo - s * j : hi - s * j, pl.ds(at, h), :]
                    ok = (here == there) & (here > 0)
                    ok = jnp.concatenate([ok] * (out // 128), axis=2)
                    x = jnp.where(
                        ok, g_ref[lo - s * j : hi - s * j, pl.ds(at, h), b * out : (b + 1) * out], 0
                    )
                    x = x.reshape((hi - lo) * h, out)
                    acc[lo * h : hi * h] += nn_dot(x, k_ref[9 * b + 3 * (i + 1) + j + 1])

    o_ref[...] = acc[...].reshape(Q, h, w).astype(o_ref.dtype)


def conv_data(g, key, k, steps):
    Q, TT, _ = g.shape
    h = (TT - 2 * PAD) // 8
    w = k.shape[2]
    return pl.pallas_call(
        functools.partial(conv_data_kernel, steps),
        out_shape=jax.ShapeDtypeStruct((Q, 8 * h, w), jnp.bfloat16),
        grid=(8,),
        in_specs=[VM, VM, VM],
        out_specs=pl.BlockSpec((Q, h, w), lambda i: (0, i, 0)),
        scratch_shapes=[pltpu.VMEM((Q * h, w), jnp.float32)],
        compiler_params=pltpu.CompilerParams(vmem_limit_bytes=VLIM),
        name="conv_data",
    )(g, key, k)


def conv_weight_kernel(steps, y_ref, key_ref, g_ref, o_ref, x_ref):
    Q = y_ref.shape[0]
    w = y_ref.shape[2]
    out = o_ref.shape[1]
    TT = y_ref.shape[1]
    T = TT - 2 * PAD
    b = pl.program_id(0)
    for n, s in enumerate(steps):

        @pl.when(b == n)
        def _():
            for i in (-1, 0, 1):
                r0, r1 = span(16 * s * i, T)
                r0, r1 = r0 // 128 * 128, -(-r1 // 128) * 128
                for j in (-1, 0, 1):
                    lo, hi = span(s * j, Q)
                    L = r1 - r0

                    def one(q, _):
                        here = key_ref[q, PAD + r0 : PAD + r1, :]
                        a = PAD + r0 + 16 * s * i
                        there = key_ref[q + s * j, a : a + L, :]
                        ok = (here == there) & (here > 0)
                        ok = jnp.concatenate([ok] * (w // 128), axis=1)
                        x = jnp.where(ok, y_ref[q + s * j, a : a + L, :], 0)
                        x_ref[pl.ds(pl.multiple_of((q - lo) * L, 128), L), :] = x
                        return 0

                    lax.fori_loop(lo, hi, one, 0)
                    d = g_ref[lo:hi, PAD + r0 : PAD + r1, n * out : (n + 1) * out]
                    d = d.reshape((hi - lo) * L, out)
                    o_ref[3 * (i + 1) + j + 1] = tn_dot(d, x_ref[: (hi - lo) * L, :]).astype(o_ref.dtype)


def conv_weight(y, key, g, steps, out):
    Q, TT, w = y.shape
    T = TT - 2 * PAD
    return pl.pallas_call(
        functools.partial(conv_weight_kernel, steps),
        out_shape=jax.ShapeDtypeStruct((27, out, w), jnp.bfloat16),
        grid=(3,),
        in_specs=[VM, VM, VM],
        out_specs=pl.BlockSpec((9, out, w), lambda i: (i, 0, 0)),
        scratch_shapes=[pltpu.VMEM((Q * T, w), jnp.bfloat16)],
        compiler_params=pltpu.CompilerParams(vmem_limit_bytes=VLIM),
        name="conv_weight",
    )(y, key, g)


class Gather:
    def __init__(self, src, slot, sems, d, f):
        self.src, self.slot, self.sems, self.d, self.f = src, slot, sems, d, f

    def start(self):
        far_s, far_r, near_s, near_r, local = self.sems
        d, f = self.d, self.f
        mine = self.slot(f)
        self.far = {k: remote(self.src, mine, far_s.at[k], far_r.at[k], d, f ^ (2 * k)) for k in (3, 1, 2)}
        self.near = [remote(self.src, mine, near_s.at[0], near_r.at[0], d, f ^ 1)]
        self.own = pltpu.make_async_copy(self.src, mine, local)
        self.own.start()

    def forward(self):
        far_s, far_r, near_s, near_r, local = self.sems
        for k in (1, 2, 3):
            self.far[k].wait_recv()
            got = self.slot(self.f ^ (2 * k))
            self.near.append(remote(got, got, near_s.at[k], near_r.at[k], self.d, self.f ^ 1))

    def arrive(self):
        self.own.wait()
        for c in self.near:
            c.wait_recv()

    def finish(self):
        for c in list(self.far.values()) + self.near:
            c.wait_send()


def gather_sems():
    return [DMA((4,)), DMA((4,)), DMA((4,)), DMA((4,)), DMA(())]


def sum_sems(R, C):
    return [
        pltpu.VMEM((8, R, C), jnp.float32),
        pltpu.VMEM((4, R, C), jnp.float32),
        DMA((8,)),
        DMA((8,)),
        DMA((4,)),
        DMA((4,)),
    ]


def sum_all(rows, bufs, d, f):
    b1, b2, s1, r1, s2, r2 = bufs
    for n, row in enumerate(rows):
        b1[f, n : n + 1, :] = row
    cps = [remote(b1.at[f], b1.at[f], s1.at[k], r1.at[k], d, f ^ k) for k in (6, 2, 4, 7, 3, 5, 1)]
    for c in cps:
        c.wait()
    tot = b1[0]
    for k in range(1, 8):
        tot = tot + b1[k]
    b2[d] = tot
    cps = [remote(b2.at[d], b2.at[d], s2.at[k], r2.at[k], d ^ k, f) for k in (3, 2, 1)]
    for c in cps:
        c.wait()
    tot = b2[0]
    for k in range(1, 4):
        tot = tot + b2[k]
    return tot


def column_sums(a, ins):
    m = a * jnp.concatenate([ins] * (a.shape[1] // 128), axis=1)
    return jnp.sum(m, axis=0, keepdims=True), jnp.sum(m * a, axis=0, keepdims=True)


def bend(p):
    g = 1.0 / (1.0 + jnp.exp(-p))
    return p * g, g * (1.0 + p * (1.0 - g))


def same_crop(here, there, width):
    ok = (here == there) & (here > 0)
    return jnp.concatenate([ok] * (width // 128), axis=ok.ndim - 1)


def cat_rows(parts):
    return jnp.concatenate(parts, axis=1)


def bottleneck_kernel(
    x_ref, kb_ref, ins_ref, gr, br, gd, bd, ge, be,
    wr_s, wd_s, we_s, wp_s, wm_s, wc_s, k_s0, k_s1, k_s2, kp_s,
    yo_o, y_o, n3_o, l3_o, n1_o, l1_o, n2_o, l2_o, ext_o, h2_o, key_o, k_o, wr_o, wd_o, we_o, wp_o, wm_o, wc_o, cnt_o,
    xp, a1, a2, a3, ext, h2, y, n3, l3, n1, l1, n2, l2, key, wr, wd, we,
    *sems,
):
    sems = list(sems)

    def take(n):
        got = sems[:n]
        del sems[:n]
        return got

    f, d = greet(range(1, 8), range(1, 4))
    N, C = x_ref.shape
    Q, h = ext.shape[0], ext.shape[1] // 2
    e = h // 2
    rows = h // 4
    neck = a1.shape[1]
    T = 8 * h

    def rows_of(ref, n):
        return lambda g: ref.at[pl.ds(pl.multiple_of(n * g, n), n)]

    nr, nd_, ne, np_ = wr_s.shape[0], wd_s.shape[1], we_s.shape[1], wp_s.shape[0]
    g_key = Gather(kb_ref, lambda g: key.at[:, pl.ds(pl.multiple_of(PAD + h * g, 16), h), :], take(5), d, f)
    g_wr = Gather(wr_s, rows_of(wr, nr), take(5), d, f)
    g_wd = Gather(wd_s, lambda g: wd.at[:, pl.ds(pl.multiple_of(nd_ * g, 16), nd_), :], take(5), d, f)
    g_we = Gather(we_s, lambda g: we.at[:, pl.ds(pl.multiple_of(ne * g, 128), ne)], take(5), d, f)
    g_wp = Gather(wp_s, rows_of(wp_o, np_), take(5), d, f)
    g_wm = Gather(wm_s, rows_of(wm_o, np_), take(5), d, f)
    g_wc = Gather(wc_s, rows_of(wc_o, np_), take(5), d, f)
    ks, kr, kl, hs, hr, ys, yr, yl, os_ = take(9)
    sum1, sum2, sum3 = take(6), take(6), take(6)

    g_key.start()
    g_wr.start()
    g_wd.start()
    order = lax.broadcasted_iota(jnp.int32, (N, N), 0)
    m, r, q = order % 4, (order // 4) % rows, order // h
    pick = (r * (N // rows) + q * 4 + m) == lax.broadcasted_iota(jnp.int32, (N, N), 1)
    pick = pick.astype(jnp.float32).astype(jnp.bfloat16)
    for c in range(0, C, 256):
        xp[:, c : c + 256] = nn_dot(pick, x_ref[:, c : c + 256]).astype(jnp.bfloat16)
    key[:, :PAD, :] = jnp.zeros((Q, PAD, 128), jnp.bfloat16)
    key[:, PAD + T :, :] = jnp.zeros((Q, PAD, 128), jnp.bfloat16)
    g_key.forward()
    g_wr.forward()
    g_we.start()
    g_wr.arrive()
    sums, squares = [], []
    for c in range(0, neck, 256):
        a = nt_dot(xp[...], wr[c : c + 256, :])
        a1[:, c : c + 256] = a
        s, t = column_sums(a, ins_ref[...])
        sums.append(s)
        squares.append(t)
    inside = jnp.sum(ins_ref[...], axis=0, keepdims=True)
    st = sum_all([cat_rows(sums), cat_rows(squares), cat_rows([inside] * (neck // 128))], sum1, d, f)
    count = st[2:3, :]
    cnt_o[...] = jnp.zeros_like(cnt_o)
    cnt_o[0:1, :neck] = count
    mean = st[0:1] / count
    inv = lax.rsqrt(st[1:2] / count - mean * mean + eps)
    cnt_o[1:2, :neck] = inv
    for c in range(0, neck, 256):
        w = slice(c, c + 256)
        n = (a1[:, w] - mean[:, w]) * inv[:, w]
        act, lean = bend(n * gr[:, w] + br[:, w])
        ext[:, e : e + h, w] = act.astype(jnp.bfloat16).reshape(Q, h, 256)
        n1[:, w] = n.astype(jnp.bfloat16)
        l1[:, w] = lean.astype(jnp.bfloat16)
    up = remote(ext.at[:, pl.ds(e, e)], ext.at[:, pl.ds(e + h, e)], hs.at[0], hr.at[0], d, lax.rem(f + 7, 8))
    down = remote(ext.at[:, pl.ds(h, e)], ext.at[:, pl.ds(0, e)], hs.at[1], hr.at[1], d, lax.rem(f + 1, 8))
    g_wd.forward()
    kcp = []
    for k in (6, 7, 2, 3, 4, 5, 1):
        for b, src in enumerate((k_s0, k_s1, k_s2, kp_s)):
            n = src.shape[0]
            o = src.shape[1]
            kcp.append(
                remote(
                    src.at[:, :, pl.ds(pl.multiple_of((f ^ k) * 256, 128), 256)],
                    k_o.at[pl.ds(9 * b, n), pl.ds(pl.multiple_of(o * f, 16), o), :],
                    ks.at[b, k], kr.at[b, k], d, f ^ k,
                )
            )
    for b, src in enumerate((k_s0, k_s1, k_s2, kp_s)):
        n = src.shape[0]
        o = src.shape[1]
        c = pltpu.make_async_copy(
            src.at[:, :, pl.ds(pl.multiple_of(f * 256, 128), 256)],
            k_o.at[pl.ds(9 * b, n), pl.ds(pl.multiple_of(o * f, 16), o), :],
            kl.at[b],
        )
        c.start()
        kcp.append(c)
    for g in (g_wp, g_wm, g_wc):
        g.start()
    g_key.arrive()
    outs = [(n1, n1_o), (l1, l1_o), (key, key_o), (wr, wr_o)]
    base = pl.multiple_of(PAD + h * f, 16)
    up.wait()
    down.wait()
    outs.append((ext, ext_o))
    g_wd.arrive()
    outs.append((wd, wd_o))
    a2[...] = jnp.zeros_like(a2)
    for i in range(3):
        for j in (1, 0, 2):
            lo, hi = span(j - 1, Q)
            ok = same_crop(
                key[lo:hi, pl.ds(base, h), :],
                key[lo + j - 1 : hi + j - 1, pl.ds(pl.multiple_of(base + e * (i - 1), 16), h), :],
                neck,
            )
            v = jnp.where(ok, ext[lo + j - 1 : hi + j - 1, e * i : e * i + h, :], 0).reshape((hi - lo) * h, neck)
            for c in range(0, neck, 256):
                a2[lo * h : hi * h, c : c + 256] += nt_dot(v, wd[3 * i + j, c : c + 256, :])
    sums, squares = [], []
    for c in range(0, neck, 256):
        s, t = column_sums(a2[:, c : c + 256], ins_ref[...])
        sums.append(s)
        squares.append(t)
    st = sum_all([cat_rows(sums), cat_rows(squares)], sum2, d, f)
    mean = st[0:1] / count
    inv = lax.rsqrt(st[1:2] / count - mean * mean + eps)
    cnt_o[2:3, :neck] = inv
    for c in range(0, neck, 256):
        w = slice(c, c + 256)
        n = (a2[:, w] - mean[:, w]) * inv[:, w]
        act, lean = bend(n * gd[:, w] + bd[:, w])
        h2[:, w] = act.astype(jnp.bfloat16)
        n2[:, w] = n.astype(jnp.bfloat16)
        l2[:, w] = lean.astype(jnp.bfloat16)
    outs += [(n2, n2_o), (l2, l2_o), (h2, h2_o)]
    g_we.forward()
    g_we.arrive()
    outs.append((we, we_o))
    sums, squares = [], []
    for c in range(0, C, 256):
        a = nn_dot(h2[...], we[:, c : c + 256])
        a3[:, c : c + 256] = a
        s, t = column_sums(a, ins_ref[...])
        sums.append(s)
        squares.append(t)
    st = sum_all([cat_rows(sums), cat_rows(squares)], sum3, d, f)
    total = count[:, :1]
    mean3 = st[0:1] / total
    inv3 = lax.rsqrt(st[1:2] / total - mean3 * mean3 + eps)
    coef = sum3[0]
    coef[0, 0:1, :] = mean3
    coef[0, 1:2, :] = inv3
    cnt_o[3:4, :] = inv3
    sent = []
    dst = yo_o.at[:, pl.ds(base, h), :]
    for k in (6, 7, 2, 3, 4, 5, 1, 0):
        g = f ^ k
        w = pl.ds(pl.multiple_of(g * 256, 256), 256)
        n = (a3[:, w] - coef[0, 0:1, w]) * coef[0, 1:2, w]
        act, lean = bend(n * ge[:, w] + be[:, w] + xp[:, w].astype(jnp.float32))
        y[:, :, w] = act.astype(jnp.bfloat16).reshape(Q, h, 256)
        n3[:, w] = n.astype(jnp.bfloat16)
        l3[:, w] = lean.astype(jnp.bfloat16)
        part = y.at[:, :, w]
        if k:
            sent.append(remote(part, dst, ys.at[k], yr.at[k], d, g))
        else:
            own = pltpu.make_async_copy(part, dst, yl)
            own.start()
            sent.append(own)
    outs += [(y, y_o), (n3, n3_o), (l3, l3_o)]
    saved = []
    for n, (src, to) in enumerate(outs):
        c = pltpu.make_async_copy(src, to, os_.at[n])
        c.start()
        saved.append(c)
    for g in (g_wp, g_wm, g_wc):
        g.forward()
    for g in (g_wp, g_wm, g_wc):
        g.arrive()
    for g in (g_key, g_wr, g_wd, g_we, g_wp, g_wm, g_wc):
        g.finish()
    for c in kcp + sent + saved:
        c.wait()


def bottleneck(x, kb, ins, vecs, shards, kparts):
    N, C = x.shape
    Q, h, _ = kb.shape
    wr, wd, we, wp, wm, wc = shards
    neck = we.shape[0]
    W = 8 * wp.shape[0]
    b16, f32 = jnp.bfloat16, jnp.float32
    S = jax.ShapeDtypeStruct
    TT = 8 * h + 2 * PAD
    outs = [
        S((Q, TT, C // 8), b16), S((Q, h, C), b16), S((N, C), b16), S((N, C), b16),
        S((N, neck), b16), S((N, neck), b16), S((N, neck), b16), S((N, neck), b16),
        S((Q, 2 * h, neck), b16), S((N, neck), b16), S((Q, TT, 128), b16), S((28, W, C // 8), b16),
        S((neck, C), b16), S((9, neck, neck), b16), S((neck, C), b16), S((W, C), b16), S((W, wm.shape[1]), b16),
        S((W, 128), b16), S((8, C), f32),
    ]
    V = pltpu.VMEM
    scratch = [
        V((N, C), b16), V((N, neck), f32), V((N, neck), f32), V((N, C), f32), V((Q, 2 * h, neck), b16), V((N, neck), b16),
        V((Q, h, C), b16), V((N, C), b16), V((N, C), b16),
        V((N, neck), b16), V((N, neck), b16), V((N, neck), b16), V((N, neck), b16), V((Q, TT, 128), b16),
        V((neck, C), b16), V((9, neck, neck), b16), V((neck, C), b16),
    ]
    for _ in range(7):
        scratch += gather_sems()
    scratch += [DMA((4, 8)), DMA((4, 8)), DMA((4,)), DMA((2,)), DMA((2,)), DMA((8,)), DMA((8,)), DMA(()), DMA((16,))]
    scratch += sum_sems(3, neck) + sum_sems(2, neck) + sum_sems(2, C)
    return pl.pallas_call(
        bottleneck_kernel,
        out_shape=outs,
        in_specs=[VM] * 9 + [ANY] * 10,
        out_specs=[ANY] * 18 + [VM],
        scratch_shapes=scratch,
        compiler_params=pltpu.CompilerParams(collective_id=1, has_side_effects=True, vmem_limit_bytes=VLIM),
        name="bottleneck",
    )(x, kb, ins, *vecs, *shards, *kparts)


def branches_back_kernel(
    steps, d_ref, y_ref, key_ref, k_ref, pooled_ref, dr_ref, size_ref, dy_o, gk_o,
    g, gt, x, gk, dyo, acc, gp, *sems,
):
    sems = list(sems)
    f, d = greet(range(1, 8), ())
    Q, h, w = y_ref.shape[0], d_ref.shape[1], y_ref.shape[2]
    W = k_ref.shape[1]
    T = 8 * h
    o = W // 8
    g_d = Gather(d_ref, lambda n: g.at[:, pl.ds(pl.multiple_of(PAD + h * n, 16), h), :], sems[:5], d, f)
    ws, wr, wl, ds_, dr_, dl = sems[5:]
    g_d.start()
    gk[27] = tn_dot(dr_ref[...], pooled_ref[...]).astype(gk.dtype)
    gp[...] = nn_dot(dr_ref[...], k_ref[27]) / size_ref[:, :1]
    g_d.forward()
    g_d.arrive()

    def turn(q, _):
        for b in range(3):
            gt[b * W : (b + 1) * W, pl.ds(pl.multiple_of(q * T, 256), T)] = g[q, PAD : PAD + T, b * W : (b + 1) * W].T
        return 0

    lax.fori_loop(0, Q, turn, 0)
    cps = []
    for b, s in enumerate(steps):
        for i in (-1, 0, 1):
            for j in (-1, 0, 1):
                lo, hi = span(s * j, Q)
                a = PAD + 16 * s * i

                def one(q, _):
                    ok = same_crop(key_ref[q, PAD : PAD + T, :], key_ref[q + s * j, a : a + T, :], w)
                    x[pl.ds(pl.multiple_of((q - lo) * T, 256), T), :] = jnp.where(ok, y_ref[q + s * j, a : a + T, :], 0)
                    return 0

                lax.fori_loop(lo, hi, one, 0)
                gk[9 * b + 3 * (i + 1) + j + 1] = nn_dot(
                    gt[b * W : (b + 1) * W, lo * T : hi * T], x[: (hi - lo) * T, :]
                ).astype(gk.dtype)
        n = 9 if b < 2 else 10
        for k in (6, 7, 2, 3, 4, 5, 1, 0):
            src = gk.at[pl.ds(9 * b, n), pl.ds(pl.multiple_of(o * (f ^ k), 16), o), :]
            dst = gk_o.at[pl.ds(9 * b, n), :, pl.ds(pl.multiple_of(w * f, 128), w)]
            if k:
                cps.append(remote(src, dst, ws.at[b, k], wr.at[b, k], d, f ^ k))
            else:
                c = pltpu.make_async_copy(src, dst, wl.at[b])
                c.start()
                cps.append(c)

    dst = dy_o.at[:, :, pl.ds(pl.multiple_of(w * f, 128), w)]

    def rows_of(k):
        return pl.ds(pl.multiple_of(h * (f ^ k), 16), h)

    def dest_step(m, _):
        k = 7 - m
        dest = f ^ k
        base = pl.multiple_of(PAD + h * dest, 16)
        here = key_ref[:, pl.ds(base, h), :].astype(jnp.float32).reshape(Q * h, 128)
        here = jnp.concatenate([here] * (w // 128), axis=1)
        total = jnp.zeros((Q * h, w), jnp.float32)
        for c in range(CROPS_TILE):
            total = jnp.where(here == c + 1.0, gp[c : c + 1, :], total)
        acc[...] = total
        for b, s in enumerate(steps):
            for i in (-1, 0, 1):
                first = h * dest - 16 * s * i

                @pl.when((first + h > 0) & (first < T))
                def _():
                    at = pl.multiple_of(base - 16 * s * i, 16)
                    for j in (-1, 0, 1):
                        lo, hi = span(-s * j, Q)
                        ok = same_crop(
                            key_ref[lo:hi, pl.ds(base, h), :], key_ref[lo - s * j : hi - s * j, pl.ds(at, h), :], W
                        )
                        v = jnp.where(ok, g[lo - s * j : hi - s * j, pl.ds(at, h), b * W : (b + 1) * W], 0)
                        acc[lo * h : hi * h] += nn_dot(v.reshape((hi - lo) * h, W), k_ref[9 * b + 3 * (i + 1) + j + 1])

        rows = rows_of(k)
        dyo[:, rows, :] = acc[...].reshape(Q, h, w).astype(dyo.dtype)
        src = dyo.at[:, rows, :]

        @pl.when(k > 0)
        def _():
            remote(src, dst, ds_.at[k], dr_.at[k], d, dest)

        @pl.when(k == 0)
        def _():
            pltpu.make_async_copy(src, dst, dl).start()

        return 0

    lax.fori_loop(0, 8, dest_step, 0)
    for k in range(1, 8):
        c = pltpu.make_async_remote_copy(
            src_ref=dyo.at[:, rows_of(k), :], dst_ref=dst, send_sem=ds_.at[k], recv_sem=dr_.at[k],
            device_id=(d, f ^ k), device_id_type=MESH,
        )
        c.wait()
    pltpu.make_async_copy(dyo.at[:, rows_of(0), :], dst, dl).wait()
    g_d.finish()
    for c in cps:
        c.wait()


def branches_back(d, y, key, k, pooled, dr, sizes, steps):
    Q, h, W3 = d.shape
    TT, w = y.shape[1:]
    W = W3 // 3
    T = 8 * h
    b16, f32 = jnp.bfloat16, jnp.float32
    V = pltpu.VMEM
    return pl.pallas_call(
        functools.partial(branches_back_kernel, steps),
        out_shape=[jax.ShapeDtypeStruct((Q, h, 8 * w), b16), jax.ShapeDtypeStruct((28, W // 8, 8 * w), b16)],
        in_specs=[VM] * 7,
        out_specs=[ANY] * 2,
        scratch_shapes=[
            V((Q, TT, W3), b16), V((W3, Q * T), b16), V((Q * T, w), b16), V((28, W, w), b16), V((Q, T, w), b16),
            V((Q * h, w), f32), V((8, w), f32),
        ]
        + gather_sems()
        + [DMA((3, 8)), DMA((3, 8)), DMA((3,)), DMA((8,)), DMA((8,)), DMA(())],
        compiler_params=pltpu.CompilerParams(collective_id=10, has_side_effects=True, vmem_limit_bytes=VLIM),
        name="branches_back",
    )(d, y, key, k, pooled, dr, sizes)


class Sum:
    def __init__(self, bufs, d, f):
        self.b1, self.b2, self.s1, self.r1, self.s2, self.r2 = bufs
        self.d, self.f = d, f

    def start(self, rows):
        b1, d, f = self.b1, self.d, self.f
        for n, row in enumerate(rows):
            b1[f, n : n + 1, :] = row
        self.cps = [remote(b1.at[f], b1.at[f], self.s1.at[k], self.r1.at[k], d, f ^ k) for k in (6, 2, 4, 7, 3, 5, 1)]

    def turn(self):
        b1, b2, d, f = self.b1, self.b2, self.d, self.f
        for c in self.cps:
            c.wait()
        tot = b1[0]
        for k in range(1, 8):
            tot = tot + b1[k]
        b2[d] = tot
        self.cps = [remote(b2.at[d], b2.at[d], self.s2.at[k], self.r2.at[k], d ^ k, f) for k in (3, 2, 1)]

    def result(self):
        for c in self.cps:
            c.wait()
        tot = self.b2[0]
        for k in range(1, 4):
            tot = tot + self.b2[k]
        return tot


class Reduce:
    def __init__(self, full, part, near, far, tot, zr, out, quarter, sems, d, f):
        self.full, self.part, self.near, self.fars, self.tot, self.zr, self.out = full, part, near, far, tot, zr, out
        self.quarter, self.d, self.f = quarter, d, f
        self.sems = sems
        self.c0 = f % 2
        self.me = f // 2
        self.sent = []

    def pair(self):
        ps, pr = self.sems[:2]
        self.cps = [
            remote(self.full.at[self.part(2 * g + 1 - self.c0)], self.near.at[g], ps.at[g], pr.at[g], self.d, self.f ^ 1)
            for g in range(4)
        ]

    def far(self):
        ss, rs = self.sems[2:4]
        for c in self.cps:
            c.wait()
        self.cps = []
        for k in (3, 1, 2, 0):
            g = self.me ^ k
            val = self.full[self.part(2 * g + self.c0)].astype(jnp.float32) + self.near[g].astype(jnp.float32)
            self.near[g] = val.astype(self.near.dtype)
            if k:
                self.cps.append(
                    remote(self.near.at[g], self.fars.at[k], ss.at[k], rs.at[k], self.d, self.f ^ (2 * k))
                )

    def tiles(self):
        ss, rs = self.sems[4:6]
        for c in self.cps:
            c.wait()
        val = self.near[self.me].astype(jnp.float32)
        for k in (1, 2, 3):
            val = val + self.fars[k].astype(jnp.float32)
        self.tot[...] = val.astype(self.tot.dtype)
        self.cps = [
            remote(self.tot.at[self.quarter(self.d ^ k)], self.zr.at[self.d], ss.at[k], rs.at[k], self.d ^ k, self.f)
            for k in (3, 2, 1)
        ]
        self.zr[self.d] = self.tot[self.quarter(self.d)]

    def back(self):
        ss, rs = self.sems[6:8]
        for c in self.cps:
            c.wait()
        val = self.zr[0].astype(jnp.float32)
        for k in (1, 2, 3):
            val = val + self.zr[k].astype(jnp.float32)
        mine = self.quarter(self.d)
        self.out[mine] = val.astype(self.out.dtype)
        self.cps = [
            remote(self.out.at[mine], self.out.at[mine], ss.at[k], rs.at[k], self.d ^ k, self.f) for k in (3, 2, 1)
        ]

    def done(self):
        for c in self.cps:
            c.wait()


def reduce_scratch(block, quarter):
    V, b16 = pltpu.VMEM, jnp.bfloat16
    return [V((4,) + block, b16), V((4,) + block, b16), V(block, b16), V((4,) + quarter, b16)] + [DMA((4,))] * 8


def wide(row, n):
    return jnp.concatenate([row] * n, axis=1)


def bottleneck_back_kernel(
    x_ref, ins_ref, st_ref, gr, gd, ge, dy, dpt, y_ref, pm_in, wp, n3, l3, we, n2, l2, h2, wd, ext, n1, l1, wr, key_any,
    gf_o, pm_o, ex_o, di_o, re_o, s3_o, s2_o, s1_o,
    pm, ex, di, re_, dp3, d3, acc, ext2, d1n, key, gf, pick, ksem, hs, hr, gs,
    *sems,
):
    sems = list(sems)

    def take(n):
        got = sems[:n]
        del sems[:n]
        return got

    f, d = greet(range(1, 8), range(1, 4))
    N, C = x_ref.shape
    Q, h = ext2.shape[0], ext2.shape[1] // 2
    e = h // 2
    rows = h // 4
    neck = acc.shape[1]
    nb = neck // 8
    nw = pm.shape[0] // 8
    PW = pm.shape[1] // 4
    W = dpt.shape[1]

    def ds(i, n):
        return pl.ds(pl.multiple_of(n * i, n), n)

    def reducer(full, part, out, quarter):
        near, far, tot, zr = take(4)
        return Reduce(full, part, near, far, tot, zr, out, quarter, take(8), d, f)

    r_pm = reducer(pm, lambda g: (ds(g, nw),), pm_o, lambda g: (slice(None), ds(g, PW)))
    r_ex = reducer(ex, lambda g: (slice(None), ds(g, C // 8)), ex_o, lambda g: (ds(g, neck // 4),))
    r_di = reducer(
        di, lambda g: (slice(None), ds(g, nb)), di_o, lambda g: (slice(None), ds(g, nb // 4))
    )
    r_re = reducer(re_, lambda g: (ds(g, nb),), re_o, lambda g: (ds(g, nb // 4),))
    sum3, sum2, sum1 = (Sum(take(6), d, f) for _ in range(3))

    kcp = pltpu.make_async_copy(key_any.at[:, pl.ds(pl.multiple_of(PAD - e + h * f, 16), 2 * h), :], key, ksem)
    kcp.start()
    count = st_ref[0:1, 0:1]
    for c in range(0, C, 256):
        pm[:, c : c + 256] = tn_dot(dpt[...], y_ref[:, c : c + 256]).astype(jnp.bfloat16)
    pm[:, C:] = pm_in[...]
    r_pm.pair()
    ones, crossed = [], []
    ins = wide(ins_ref[...], 2)
    for c in range(0, C, 256):
        w = slice(c, c + 256)
        v = dy[:, w].astype(jnp.float32) + nn_dot(dpt[...], wp[:, w])
        v = v * l3[:, w].astype(jnp.float32)
        dp3[:, w] = v.astype(jnp.bfloat16)
        v = v * ins
        ones.append(jnp.sum(v, axis=0, keepdims=True))
        crossed.append(jnp.sum(v * n3[:, w].astype(jnp.float32), axis=0, keepdims=True))
    sum3.start([cat_rows(ones), cat_rows(crossed)])
    order = lax.broadcasted_iota(jnp.int32, (N, N), 1)
    m, r, q = order % 4, (order // 4) % rows, order // h
    hit = (r * (N // rows) + q * 4 + m) == lax.broadcasted_iota(jnp.int32, (N, N), 0)
    pick[...] = hit.astype(jnp.float32).astype(jnp.bfloat16)
    sum3.turn()
    r_pm.far()
    tot = sum3.result()
    s3_o[...] = tot
    for c in range(0, C, 256):
        w = slice(c, c + 256)
        v = dp3[:, w].astype(jnp.float32) - tot[0:1, w] / count - n3[:, w].astype(jnp.float32) * (tot[1:2, w] / count)
        d3[:, w] = (ins * v * (ge[:, w] * st_ref[3:4, w])).astype(jnp.bfloat16)
    ones, crossed = [], []
    for c in range(0, neck, 256):
        w = slice(c, c + 256)
        v = nt_dot(d3[...], we[w, :]) * l2[:, w].astype(jnp.float32)
        acc[:, w] = v
        v = v * ins
        ones.append(jnp.sum(v, axis=0, keepdims=True))
        crossed.append(jnp.sum(v * n2[:, w].astype(jnp.float32), axis=0, keepdims=True))
    sum2.start([cat_rows(ones), cat_rows(crossed)])
    for c in range(0, C, 256):
        ex[:, c : c + 256] = tn_dot(h2[...], d3[:, c : c + 256]).astype(jnp.bfloat16)
    sum2.turn()
    r_ex.pair()
    tot = sum2.result()
    s2_o[...] = tot
    for c in range(0, neck, 256):
        w = slice(c, c + 256)
        v = acc[:, w] - tot[0:1, w] / count - n2[:, w].astype(jnp.float32) * (tot[1:2, w] / count)
        v = ins * v * (gd[:, w] * st_ref[2:3, w])
        ext2[:, e : e + h, w] = v.astype(jnp.bfloat16).reshape(Q, h, 256)
    up = remote(ext2.at[:, pl.ds(e, e)], ext2.at[:, pl.ds(e + h, e)], hs.at[0], hr.at[0], d, lax.rem(f + 7, 8))
    down = remote(ext2.at[:, pl.ds(h, e)], ext2.at[:, pl.ds(0, e)], hs.at[1], hr.at[1], d, lax.rem(f + 1, 8))
    kcp.wait()
    r_pm.tiles()
    r_ex.far()
    for i in range(3):
        for j in range(3):
            lo, hi = span(j - 1, Q)
            ok = same_crop(
                key[lo:hi, e : e + h, :], key[lo + j - 1 : hi + j - 1, e * i : e * i + h, :], neck
            )
            v = jnp.where(ok, ext[lo + j - 1 : hi + j - 1, e * i : e * i + h, :], 0).reshape((hi - lo) * h, neck)
            g = ext2[lo:hi, e : e + h, :].reshape((hi - lo) * h, neck)
            di[3 * i + j] = tn_dot(g, v).astype(jnp.bfloat16)
    r_di.pair()
    up.wait()
    down.wait()
    acc[...] = jnp.zeros_like(acc)
    for i in range(3):
        for j in (1, 0, 2):
            lo, hi = span(1 - j, Q)
            ok = same_crop(
                key[lo:hi, e : e + h, :], key[lo + 1 - j : hi + 1 - j, e * (2 - i) : e * (2 - i) + h, :], neck
            )
            v = jnp.where(ok, ext2[lo + 1 - j : hi + 1 - j, e * (2 - i) : e * (2 - i) + h, :], 0)
            v = v.reshape((hi - lo) * h, neck)
            for c in range(0, neck, 256):
                acc[lo * h : hi * h, c : c + 256] += nn_dot(v, wd[3 * i + j, :, c : c + 256])
    ones, crossed = [], []
    for c in range(0, neck, 256):
        w = slice(c, c + 256)
        v = acc[:, w] * l1[:, w].astype(jnp.float32)
        acc[:, w] = v
        v = v * ins
        ones.append(jnp.sum(v, axis=0, keepdims=True))
        crossed.append(jnp.sum(v * n1[:, w].astype(jnp.float32), axis=0, keepdims=True))
    sum1.start([cat_rows(ones), cat_rows(crossed)])
    r_di.far()
    sum1.turn()
    r_pm.back()
    r_ex.tiles()
    tot = sum1.result()
    s1_o[...] = tot
    for c in range(0, neck, 256):
        w = slice(c, c + 256)
        v = acc[:, w] - tot[0:1, w] / count - n1[:, w].astype(jnp.float32) * (tot[1:2, w] / count)
        v = (ins * v * (gr[:, w] * st_ref[1:2, w])).astype(jnp.bfloat16)
        d1n[:, w] = nn_dot(pick[...], v).astype(jnp.bfloat16)
    for c in range(0, C, 256):
        re_[:, c : c + 256] = tn_dot(d1n[...], x_ref[:, c : c + 256]).astype(jnp.bfloat16)
    r_re.pair()
    out = []
    for n, c in enumerate(range(0, C, 256)):
        w = slice(c, c + 256)
        if n >= 2:
            out[n - 2].wait()
        gf[n % 2] = nn_dot(pick[...], dp3[:, w]) + nn_dot(d1n[...], wr[:, w])
        cp = pltpu.make_async_copy(gf.at[n % 2], gf_o.at[:, pl.ds(c, 256)], gs.at[n % 2])
        cp.start()
        out.append(cp)
        if n == 1:
            r_re.far()
        if n == 3:
            r_ex.back()
        if n == 5:
            r_di.tiles()
    r_re.tiles()
    r_di.back()
    r_re.back()
    out[-2].wait()
    out[-1].wait()
    for r in (r_pm, r_ex, r_di, r_re):
        r.done()


def bottleneck_back(*args):
    x, st, dpt, pm_in, h2 = args[0], args[2], args[7], args[9], args[16]
    N, C = x.shape
    Q, h2_, neck = args[18].shape
    h = h2_ // 2
    W = dpt.shape[1]
    PM = C + pm_in.shape[1]
    b16, f32 = jnp.bfloat16, jnp.float32
    S, V = jax.ShapeDtypeStruct, pltpu.VMEM
    blocks = [
        ((W // 8, PM), (W // 8, PM // 4)),
        ((neck, C // 8), (neck // 4, C // 8)),
        ((9, neck // 8, neck), (9, neck // 32, neck)),
        ((neck // 8, C), (neck // 32, C)),
    ]
    scratch = [
        V((W, PM), b16), V((neck, C), b16), V((9, neck, neck), b16), V((neck, C), b16), V((N, C), b16), V((N, C), b16),
        V((N, neck), f32), V((Q, 2 * h, neck), b16), V((N, neck), b16), V((Q, 2 * h, 128), b16), V((2, N, 256), f32),
        V((N, N), b16), DMA(()), DMA((2,)), DMA((2,)), DMA((2,)),
    ]
    for block, quarter in blocks:
        scratch += reduce_scratch(block, quarter)
    scratch += sum_sems(2, C) + sum_sems(2, neck) + sum_sems(2, neck)
    return pl.pallas_call(
        bottleneck_back_kernel,
        out_shape=[S((N, C), f32)] + [S(b, b16) for b, _ in blocks] + [S((2, C), f32), S((2, neck), f32), S((2, neck), f32)],
        in_specs=[VM] * 22 + [ANY],
        out_specs=[ANY] + [VM] * 7,
        scratch_shapes=scratch,
        compiler_params=pltpu.CompilerParams(collective_id=12, has_side_effects=True, vmem_limit_bytes=VLIM),
        name="bottleneck_back",
    )(*args)


def norm_coeffs(totals, squares, count):
    average = totals / count
    return average, lax.rsqrt(squares / count - average * average + eps)


def fast_body(
    features, crop_ids, labels, w_reduce, gain_reduce, bias_reduce, w_dilated, gain_dilated, bias_dilated,
    w_expand, gain_expand, bias_expand, w_point, gain_point, bias_point, w_rate, gain_rate, bias_rate,
    w_rate_double, gain_rate_double, bias_rate_double, w_rate_triple, gain_rate_triple, bias_rate_triple,
    w_pool, w_merge, gain_merge, bias_merge, w_classes,
):
    rows, cols, C = features.shape
    Q = cols // 4
    h = rows * 4
    N = rows * cols
    nf = lax.axis_size("fsdp")
    W = gain_point.shape[0]
    steps = (RATE // 4, 2 * RATE // 4, 3 * RATE // 4)
    place = lax.axis_index("fsdp")

    def perm(a):
        a = a.reshape((rows, Q, 4) + a.shape[2:])
        return jnp.swapaxes(a, 0, 1).reshape((N,) + a.shape[3:])

    def unperm(a):
        a = a.reshape((Q, rows, 4) + a.shape[1:])
        return jnp.swapaxes(a, 0, 1).reshape((rows, cols) + a.shape[3:])

    local_crop = perm(crop_ids) - lax.axis_index("dp") * CROPS_TILE
    in_crop = perm(crop_ids) >= 0
    inside = in_crop.astype(jnp.float32)[:, None]
    key_loc = jnp.where(in_crop, local_crop + 1, 0)
    kb = jnp.broadcast_to(key_loc.astype(jnp.bfloat16)[:, None], (N, 128)).reshape(Q, h, 128)
    ins = jnp.broadcast_to(inside, (N, 128))
    rates = [jnp.swapaxes(w.reshape(9, C, -1), 1, 2) for w in (w_rate, w_rate_double, w_rate_triple)]
    vecs = [v[None, :] for v in (gain_reduce, bias_reduce, gain_dilated, bias_dilated, gain_expand, bias_expand)]
    (
        y_own, y, n_three, l_three, n_one, l_one, n_two, l_two, ext, h_two, key, kernel,
        wr, wd, full_expand, wp, wm, wc, count,
    ) = bottleneck(
        features.reshape(N, C), kb, ins, vecs,
        [
            w_reduce.T, jnp.swapaxes(w_dilated.reshape(9, w_dilated.shape[2], -1), 1, 2), w_expand, w_point.T, w_merge.T,
            jnp.pad(w_classes, ((0, 0), (0, 128 - CLASSES))),
        ],
        rates + [w_pool.T[None]],
    )
    neck = gain_reduce.shape[0]
    stats = count
    count = count[0, 0]
    y = y.reshape(N, C)
    full_reduce, full_point, full_merge, full_classes = wr.T, wp.T, wm.T, wc[:, :CLASSES]
    neck = gain_reduce.shape[0]
    full_pool = lax.all_gather(w_pool, "fsdp", axis=1, tiled=True)

    part = conv_forward(y_own, key, kernel[:27], steps)
    a_rates = scatter_sum(part.reshape(nf, N, 3 * W), 5)
    a_point = flat_dot(y, full_point)
    a_br = jnp.concatenate([a_point, a_rates], axis=1)
    member = local_crop[:, None] == jnp.arange(CROPS_TILE)[None, :]
    member = (member & in_crop[:, None]).astype(jnp.bfloat16)
    crop_sums = inner_dot(member, y)
    crop_sizes = jnp.sum(member.astype(jnp.float32), axis=0)
    crop_sums, crop_sizes = lax.psum((crop_sums, crop_sizes), "fsdp")
    st = total_sum([jnp.sum(a_br * inside, axis=0), jnp.sum(a_br * a_br * inside, axis=0)], 6)
    m_br, s_br = norm_coeffs(st[0], st[1], count)
    g_br = jnp.concatenate([gain_point, gain_rate, gain_rate_double, gain_rate_triple])
    b_br = jnp.concatenate([bias_point, bias_rate, bias_rate_double, bias_rate_triple])
    n_br = (a_br - m_br) * s_br
    p_br = n_br * g_br + b_br
    u_br = jax.nn.silu(p_br).astype(jnp.bfloat16)
    pooled = (crop_sums / crop_sizes[:, None]).astype(jnp.bfloat16)
    pool_act = flat_dot(pooled, full_pool)
    pool_low = jax.nn.silu(pool_act).astype(jnp.bfloat16)
    u_pool = flat_dot(member, pool_low).astype(jnp.bfloat16)
    joined = jnp.concatenate([u_br, u_pool], axis=1)
    a_merge = flat_dot(joined, full_merge)
    st = total_sum([jnp.sum(a_merge * inside, axis=0), jnp.sum(a_merge * a_merge * inside, axis=0)], 7)
    m_merge, s_merge = norm_coeffs(st[0], st[1], count)
    n_merge = (a_merge - m_merge) * s_merge
    p_merge = n_merge * gain_merge + bias_merge
    merged = jax.nn.silu(p_merge).astype(jnp.bfloat16)
    logits = flat_dot(merged, full_classes)
    class_logits = unperm(logits.astype(jnp.bfloat16))

    probability = jax.nn.softmax(logits, axis=1)
    targets = (perm(labels)[:, None] == jnp.arange(CLASSES)[None, :]).astype(jnp.float32)
    d_logits = (inside * (probability - targets) / count).astype(jnp.bfloat16)
    grad_classes = inner_dot(merged, d_logits)

    def back(up, n, s, gain, cid):
        st = total_sum([jnp.sum(up * inside, axis=0), jnp.sum(up * n * inside, axis=0)], cid)
        d = inside * gain * s * (up - st[0] / count - n * st[1] / count)
        return d.astype(jnp.bfloat16), st[1], st[0]

    d_merge, gg_merge, gb_merge = back(outer_dot(d_logits, full_classes) * slope(p_merge), n_merge, s_merge, gain_merge, 8)
    grad_merge = inner_dot(joined, d_merge)
    d_joined = outer_dot(d_merge, full_merge)
    d_br, gg_br, gb_br = back(d_joined[:, : 4 * W] * slope(p_br), n_br, s_br, g_br, 9)
    crop_grad = lax.dot_general(
        member.astype(jnp.float32), d_joined[:, 4 * W :], (((0,), (0,)), ((), ())),
        precision=lax.Precision.HIGHEST, preferred_element_type=jnp.float32,
    )
    crop_grad = lax.psum(crop_grad, "fsdp")
    d_pool = (crop_grad * slope(pool_act)).astype(jnp.bfloat16)

    def eight(a):
        return jnp.pad(a, ((0, 8 - a.shape[0]), (0, 0)))

    pooled_own = lax.dynamic_slice_in_dim(pooled, place * (C // nf), C // nf, axis=1)
    sizes = jnp.broadcast_to(jnp.pad(crop_sizes, (0, 8 - CROPS_TILE), constant_values=1.0)[:, None], (8, 128))
    d_y, grad_k = branches_back(
        d_br[:, W:].reshape(Q, h, 3 * W), y_own, key, kernel, eight(pooled_own), eight(d_pool), sizes, steps
    )
    grad_k = lax.psum(grad_k, "dp").astype(jnp.float32)
    rest = jnp.concatenate(
        [grad_merge.T, jnp.pad(grad_classes, ((0, 0), (0, 128 - CLASSES)))], axis=1
    ).astype(jnp.bfloat16)
    rest = jnp.pad(rest, ((0, 0), (0, -(C + rest.shape[1]) % 512)))
    grad_features, pm, ex, di, re_, st3, st2, st1 = bottleneck_back(
        features.reshape(N, C), ins, stats, vecs[0], vecs[2], vecs[4], d_y.reshape(N, C), d_br[:, :W], y, rest, wp,
        n_three, l_three, full_expand, n_two, l_two, h_two, wd, ext, n_one, l_one, wr, key,
    )
    pm = pm.astype(jnp.float32)
    grad_point, grad_merge, grad_classes = pm[:, :C].T, pm[:, C : C + 5 * W].T, pm[:, C + 5 * W : C + 5 * W + CLASSES]
    grad_features = grad_features.reshape(rows, cols, C)
    grad_reduce = re_.astype(jnp.float32).T
    grad_dilated = jnp.swapaxes(di.astype(jnp.float32), 1, 2).reshape(3, 3, neck, -1)
    grad_expand = ex.astype(jnp.float32)
    gg_expand, gb_expand, gg_dilated, gb_dilated, gg_reduce, gb_reduce = st3[1], st3[0], st2[1], st2[0], st1[1], st1[0]
    grad_pool = grad_k[27].T
    grad_k = jnp.swapaxes(grad_k[:27].reshape(3, 3, 3, -1, C), 3, 4)
    return (
        class_logits,
        grad_features,
        grad_reduce, gg_reduce, gb_reduce,
        grad_dilated, gg_dilated, gb_dilated,
        grad_expand, gg_expand, gb_expand,
        grad_point, gg_br[:W], gb_br[:W],
        grad_k[0], gg_br[W : 2 * W], gb_br[W : 2 * W],
        grad_k[1], gg_br[2 * W : 3 * W], gb_br[2 * W : 3 * W],
        grad_k[2], gg_br[3 * W :], gb_br[3 * W :],
        grad_pool,
        grad_merge, gg_merge, gb_merge,
        grad_classes,
    )


def passed_along(value, axis, by):
    count = lax.axis_size(axis)
    pairs = [(i, i + by) for i in range(count) if 0 <= i + by < count]
    return lax.ppermute(value, axis, pairs)


def padded(cells, sides, width):
    for axis, dim in sides:
        count = lax.axis_size(axis)
        ends = count - 1
        head = lax.slice_in_dim(cells, 0, width, axis=dim)
        tail = lax.slice_in_dim(cells, cells.shape[dim] - width, cells.shape[dim], axis=dim)
        cells = jnp.concatenate(
            [
                lax.ppermute(tail, axis, [(i, (i + 1) % count) for i in range(ends)]),
                cells,
                lax.ppermute(head, axis, [((i + 1) % count, i) for i in range(ends)]),
            ],
            axis=dim,
        )
    return cells


def flat_dot(first_op, second_op):
    return jnp.dot(first_op, second_op, preferred_element_type=jnp.float32)


def inner_dot(first_op, second_op):
    return lax.dot_general(
        first_op, second_op, (((0,), (0,)), ((), ())), preferred_element_type=jnp.float32
    )


def outer_dot(first_op, second_op):
    return lax.dot_general(
        first_op, second_op, (((1,), (1,)), ((), ())), preferred_element_type=jnp.float32
    )


def slope(values):
    gate_value = jax.nn.sigmoid(values)
    return gate_value * (1.0 + values * (1.0 - gate_value))


def widen_rows(values, extent, mover):
    row_count = values.shape[0]
    neighbours = -(-extent // row_count)
    above = [mover(values, distance) for distance in range(neighbours, 0, -1)]
    below = [mover(values, -distance) for distance in range(1, neighbours + 1)]
    stacked = jnp.concatenate(above + [values] + below, axis=0)
    start_row = neighbours * row_count - extent
    return stacked[start_row : start_row + row_count + 2 * extent]


def rim_slice(widened, spacing, margin, height):
    return widened[margin - spacing : margin + height + spacing]


def offset_table(broad_key_rows, crop_random_keys, spacing, margin):
    height, breadth = crop_random_keys.shape
    first_row = margin - spacing
    extended = jnp.pad(
        broad_key_rows[first_row : first_row + height + 2 * spacing], ((0, 0), (spacing, spacing))
    )
    tables = []
    for row_tap in range(3):
        for col_tap in range(3):
            nearby = extended[
                row_tap * spacing : row_tap * spacing + height,
                col_tap * spacing : col_tap * spacing + breadth,
            ]
            tables.append(
                ((nearby == crop_random_keys) & (crop_random_keys > 0))
                .astype(jnp.float32)
                .reshape(height * breadth, 1)
            )
    return tables


def spread_offsets(widened, kernel, tables, spacing, height, breadth):
    channels = widened.shape[2]
    extended = jnp.pad(widened, ((0, 0), (spacing, spacing), (0, 0)))
    summed = jnp.zeros((height * breadth, kernel.shape[3]), jnp.float32)
    for row_tap in range(3):
        for col_tap in range(3):
            nearby = extended[
                row_tap * spacing : row_tap * spacing + height,
                col_tap * spacing : col_tap * spacing + breadth,
            ]
            summed = summed + tables[3 * row_tap + col_tap] * flat_dot(
                nearby.reshape(height * breadth, channels), kernel[row_tap, col_tap]
            )
    return summed


def collect_taps(widened, kernel, tables, spacing, height, breadth):
    channels = widened.shape[2]
    extended = jnp.pad(widened, ((0, 0), (spacing, spacing), (0, 0)))
    summed = jnp.zeros((height * breadth, kernel.shape[2]), jnp.float32)
    for row_tap in range(3):
        for col_tap in range(3):
            back_row = 2 - row_tap
            back_col = 2 - col_tap
            nearby = extended[
                back_row * spacing : back_row * spacing + height,
                back_col * spacing : back_col * spacing + breadth,
            ]
            summed = summed + tables[3 * back_row + back_col] * outer_dot(
                nearby.reshape(height * breadth, channels), kernel[row_tap, col_tap]
            )
    return summed


def kernel_offsets(widened, grads_low, tables, spacing, height, breadth):
    channels = widened.shape[2]
    extended = jnp.pad(widened, ((0, 0), (spacing, spacing), (0, 0)))
    pieces = []
    for row_tap in range(3):
        for col_tap in range(3):
            nearby = extended[
                row_tap * spacing : row_tap * spacing + height,
                col_tap * spacing : col_tap * spacing + breadth,
            ]
            masked = (tables[3 * row_tap + col_tap] * grads_low).astype(jnp.bfloat16)
            pieces.append(inner_dot(nearby.reshape(height * breadth, channels), masked))
    return pieces


def statistics(partial_value):
    return lax.psum(partial_value, ("dp", "fsdp"))


def norm_apply(values, totals, squares, pixel_count, factor, offset):
    average = totals / pixel_count
    inverse = lax.rsqrt(squares / pixel_count - average * average + eps)
    normed = (values - average) * inverse
    return (normed * factor + offset, normed, inverse)


def norm_forward(values, inside, pixel_count, factor, offset):
    totals, squares = statistics(
        (jnp.sum(values * inside, axis=0), jnp.sum(values * values * inside, axis=0))
    )
    return norm_apply(values, totals, squares, pixel_count, factor, offset)


def norm_backward(upstream, normed, inverse, factor, inside, pixel_count):
    totals, crossed = lax.psum(
        (jnp.sum(upstream * inside, axis=0), jnp.sum(upstream * normed * inside, axis=0)),
        ("dp", "fsdp"),
    )
    passed = (
        inside
        * factor
        * inverse
        * (upstream - totals / pixel_count - normed * crossed / pixel_count)
    )
    return (passed, crossed, totals)


def body(
    features,
    crop_ids,
    labels,
    w_reduce,
    gain_reduce,
    bias_reduce,
    w_dilated,
    gain_dilated,
    bias_dilated,
    w_expand,
    gain_expand,
    bias_expand,
    w_point,
    gain_point,
    bias_point,
    w_rate,
    gain_rate,
    bias_rate,
    w_rate_double,
    gain_rate_double,
    bias_rate_double,
    w_rate_triple,
    gain_rate_triple,
    bias_rate_triple,
    w_pool,
    w_merge,
    gain_merge,
    bias_merge,
    w_classes,
):
    local_rows, local_columns, channels = features.shape
    pixel_values = local_rows * local_columns
    inputs_flat = features.reshape(pixel_values, channels)
    crop_random_keys = crop_ids + 1
    outer_extent = 3 * RATE
    spacings = (RATE, 2 * RATE, 3 * RATE)
    broad_key_rows = widen_rows(
        crop_random_keys,
        outer_extent,
        lambda piece, distance: passed_along(piece, "fsdp", distance),
    )
    inside = (crop_random_keys > 0).astype(jnp.float32).reshape(pixel_values, 1)
    inner_neck = offset_table(broad_key_rows, crop_random_keys, DILATION_SPAN, outer_extent)
    near_rates = [
        offset_table(broad_key_rows, crop_random_keys, spacing, outer_extent)
        for spacing in spacings
    ]
    (
        full_reduce,
        complete_dilated,
        full_expand,
        full_point,
        full_rate,
        full_double,
        full_triple,
        full_pool,
        full_merge,
        full_classes,
    ) = (
        lax.all_gather(w_reduce, "fsdp", axis=1, tiled=True),
        lax.all_gather(w_dilated, "fsdp", axis=3, tiled=True),
        lax.all_gather(w_expand, "fsdp", axis=1, tiled=True),
        lax.all_gather(w_point, "fsdp", axis=1, tiled=True),
        lax.all_gather(w_rate, "fsdp", axis=3, tiled=True),
        lax.all_gather(w_rate_double, "fsdp", axis=3, tiled=True),
        lax.all_gather(w_rate_triple, "fsdp", axis=3, tiled=True),
        lax.all_gather(w_pool, "fsdp", axis=1, tiled=True),
        lax.all_gather(w_merge, "fsdp", axis=1, tiled=True),
        lax.all_gather(w_classes, "fsdp", axis=0, tiled=True),
    )
    rate_kernels = (full_rate, full_double, full_triple)
    rate_gains = (gain_rate, gain_rate_double, gain_rate_triple)
    rate_biases = (bias_rate, bias_rate_double, bias_rate_triple)
    act_one = flat_dot(inputs_flat, full_reduce)
    totals, squares, pixel_count = statistics(
        (
            jnp.sum(act_one * inside, axis=0),
            jnp.sum(act_one * act_one * inside, axis=0),
            jnp.sum(inside),
        )
    )
    pre_one, normed_one, inverse_one = norm_apply(
        act_one, totals, squares, pixel_count, gain_reduce, bias_reduce
    )
    first_hidden = jax.nn.silu(pre_one).astype(jnp.bfloat16)
    first_broad = padded(
        first_hidden.reshape(local_rows, local_columns, -1), (("fsdp", 0),), DILATION_SPAN
    )
    second_activation = spread_offsets(
        first_broad, complete_dilated, inner_neck, DILATION_SPAN, local_rows, local_columns
    )
    pre_two, normed_two, inverse_two = norm_forward(
        second_activation, inside, pixel_count, gain_dilated, bias_dilated
    )
    hidden_two = jax.nn.silu(pre_two).astype(jnp.bfloat16)
    act_three = flat_dot(hidden_two, full_expand)
    pre_three, normed_three, inverse_three = norm_forward(
        act_three, inside, pixel_count, gain_expand, bias_expand
    )
    pre_three = pre_three + inputs_flat
    block_out = jax.nn.silu(pre_three).astype(jnp.bfloat16)
    wide_block = widen_rows(
        block_out.reshape(local_rows, local_columns, channels),
        outer_extent,
        lambda piece, distance: passed_along(piece, "fsdp", distance),
    )
    point_act = flat_dot(block_out, full_point)
    pre_point, normed_point, inverse_point = norm_forward(
        point_act, inside, pixel_count, gain_point, bias_point
    )
    branch_point = jax.nn.silu(pre_point).astype(jnp.bfloat16)
    rate_states = []
    rate_branches = []
    for kernel, factor, offset, spacing, tables in zip(
        rate_kernels, rate_gains, rate_biases, spacings, near_rates
    ):
        rate_act = spread_offsets(
            rim_slice(wide_block, spacing, outer_extent, local_rows),
            kernel,
            tables,
            spacing,
            local_rows,
            local_columns,
        )
        pre_rate, normed_rate, inverse_rate = norm_forward(
            rate_act, inside, pixel_count, factor, offset
        )
        rate_states.append((pre_rate, normed_rate, inverse_rate))
        rate_branches.append(jax.nn.silu(pre_rate).astype(jnp.bfloat16))
    crop_flat = crop_ids.reshape(pixel_values)
    crop_total = CROPS_TILE
    first_crop = lax.axis_index("dp") * crop_total
    owner_group = lax.axis_size("fsdp")
    owner_place = lax.axis_index("fsdp")
    local_crop = crop_flat - first_crop
    member = local_crop[:, None] == jnp.arange(crop_total)[None, :]
    member_low = member.astype(jnp.bfloat16)
    crop_sums = inner_dot(member_low, block_out)
    crop_sizes = jnp.sum(member.astype(jnp.float32), axis=0)
    crop_sums, crop_sizes = lax.psum((crop_sums, crop_sizes), "fsdp")
    pooled = (crop_sums / crop_sizes[:, None]).astype(jnp.bfloat16)
    pool_act = flat_dot(pooled, full_pool)
    pool_low = jax.nn.silu(pool_act).astype(jnp.bfloat16)
    branch_pool = flat_dot(member_low, pool_low).astype(jnp.bfloat16)
    joined = jnp.concatenate([branch_point] + rate_branches + [branch_pool], axis=1)
    merge_act = flat_dot(joined, full_merge)
    pre_merge, normed_merge, inverse_merge = norm_forward(
        merge_act, inside, pixel_count, gain_merge, bias_merge
    )
    merged = jax.nn.silu(pre_merge).astype(jnp.bfloat16)
    logits_full = flat_dot(merged, full_classes)
    class_logits = logits_full.astype(jnp.bfloat16).reshape(local_rows, local_columns, -1)
    (
        full_reduce,
        complete_dilated,
        full_expand,
        full_point,
        full_rate,
        full_double,
        full_triple,
        full_pool,
        full_merge,
        full_classes,
    ) = (
        lax.all_gather(w_reduce, "fsdp", axis=1, tiled=True),
        lax.all_gather(w_dilated, "fsdp", axis=3, tiled=True),
        lax.all_gather(w_expand, "fsdp", axis=1, tiled=True),
        lax.all_gather(w_point, "fsdp", axis=1, tiled=True),
        lax.all_gather(w_rate, "fsdp", axis=3, tiled=True),
        lax.all_gather(w_rate_double, "fsdp", axis=3, tiled=True),
        lax.all_gather(w_rate_triple, "fsdp", axis=3, tiled=True),
        lax.all_gather(w_pool, "fsdp", axis=1, tiled=True),
        lax.all_gather(w_merge, "fsdp", axis=1, tiled=True),
        lax.all_gather(w_classes, "fsdp", axis=0, tiled=True),
    )
    rate_kernels = (full_rate, full_double, full_triple)
    highest = jnp.max(logits_full, axis=1, keepdims=True)
    shifted = jnp.exp(logits_full - highest)
    probability = shifted / jnp.sum(shifted, axis=1, keepdims=True)
    targets = (labels.reshape(pixel_values, 1) == jnp.arange(CLASSES)[None, :]).astype(jnp.float32)
    grad_logits = (inside * (probability - targets) / pixel_count).astype(jnp.bfloat16)
    grad_classes = inner_dot(merged, grad_logits)
    grad_merged = outer_dot(grad_logits, full_classes)
    passed, grad_gain_merge, grad_bias_merge = norm_backward(
        grad_merged * slope(pre_merge), normed_merge, inverse_merge, gain_merge, inside, pixel_count
    )
    grad_merge_act = passed.astype(jnp.bfloat16)
    grad_merge = inner_dot(joined, grad_merge_act)
    grad_joined = outer_dot(grad_merge_act, full_merge)
    branch_width = full_merge.shape[1]
    passed, grad_gain_point, grad_bias_point = norm_backward(
        grad_joined[:, :branch_width] * slope(pre_point),
        normed_point,
        inverse_point,
        gain_point,
        inside,
        pixel_count,
    )
    grad_point_act = passed.astype(jnp.bfloat16)
    grad_point = inner_dot(block_out, grad_point_act)
    grad_block = outer_dot(grad_point_act, full_point)
    rate_grads = []
    rate_weight_grads = []
    rate_gain_grads = []
    rate_bias_grads = []
    for branch in range(3):
        column = (1 + branch) * branch_width
        pre_rate, normed_rate, inverse_rate = rate_states[branch]
        passed, gain_grad, bias_grad = norm_backward(
            grad_joined[:, column : column + branch_width] * slope(pre_rate),
            normed_rate,
            inverse_rate,
            rate_gains[branch],
            inside,
            pixel_count,
        )
        grad_rate_act = passed.astype(jnp.bfloat16)
        pieces = kernel_offsets(
            rim_slice(wide_block, spacings[branch], outer_extent, local_rows),
            grad_rate_act,
            near_rates[branch],
            spacings[branch],
            local_rows,
            local_columns,
        )
        rate_weight_grads.append(jnp.stack(pieces).reshape(3, 3, channels, branch_width))
        rate_grads.append(grad_rate_act)
        rate_gain_grads.append(gain_grad)
        rate_bias_grads.append(bias_grad)
    rate_grads_low = jnp.concatenate(rate_grads, axis=1).reshape(local_rows, local_columns, -1)
    wide_grad_rate = widen_rows(
        rate_grads_low, outer_extent, lambda piece, distance: passed_along(piece, "fsdp", distance)
    )
    for branch in range(3):
        grad_slab = wide_grad_rate[:, :, branch * branch_width : (branch + 1) * branch_width]
        grad_block = grad_block + collect_taps(
            rim_slice(grad_slab, spacings[branch], outer_extent, local_rows),
            rate_kernels[branch],
            near_rates[branch],
            spacings[branch],
            local_rows,
            local_columns,
        )
    crop_grad = lax.dot_general(
        member.astype(jnp.float32),
        grad_joined[:, 4 * branch_width :],
        (((0,), (0,)), ((), ())),
        precision=lax.Precision.HIGHEST,
        preferred_element_type=jnp.float32,
    )
    crop_grad = lax.psum(crop_grad, "fsdp")
    grad_pool_act = (crop_grad * slope(pool_act)).astype(jnp.bfloat16)
    owned_crops = (jnp.arange(crop_total) % owner_group == owner_place).astype(jnp.float32)[:, None]
    grad_pool = inner_dot(pooled, (grad_pool_act * owned_crops).astype(jnp.bfloat16))
    grad_pooled = outer_dot(grad_pool_act, full_pool) / crop_sizes[:, None]
    grad_block = grad_block + inside * jnp.take(
        grad_pooled, jnp.clip(local_crop, 0, crop_total - 1), axis=0
    )
    grad_pre_three = grad_block * slope(pre_three)
    passed, grad_gain_expand, grad_bias_expand = norm_backward(
        grad_pre_three, normed_three, inverse_three, gain_expand, inside, pixel_count
    )
    grad_three = passed.astype(jnp.bfloat16)
    grad_expand = inner_dot(hidden_two, grad_three)
    grad_hidden_two = outer_dot(grad_three, full_expand)
    passed, grad_gain_dilated, grad_bias_dilated = norm_backward(
        grad_hidden_two * slope(pre_two), normed_two, inverse_two, gain_dilated, inside, pixel_count
    )
    second_gradient = passed.astype(jnp.bfloat16)
    dilated_fragments = kernel_offsets(
        first_broad, second_gradient, inner_neck, DILATION_SPAN, local_rows, local_columns
    )
    grad_dilated = jnp.stack(dilated_fragments).reshape(
        3, 3, second_gradient.shape[1], second_gradient.shape[1]
    )
    broad_neck_gradient = padded(
        second_gradient.reshape(local_rows, local_columns, -1), (("fsdp", 0),), DILATION_SPAN
    )
    grad_hidden_one = collect_taps(
        broad_neck_gradient, complete_dilated, inner_neck, DILATION_SPAN, local_rows, local_columns
    )
    passed, grad_gain_reduce, grad_bias_reduce = norm_backward(
        grad_hidden_one * slope(pre_one), normed_one, inverse_one, gain_reduce, inside, pixel_count
    )
    grad_one = passed.astype(jnp.bfloat16)
    grad_reduce = inner_dot(inputs_flat, grad_one)
    grad_features = (grad_pre_three + outer_dot(grad_one, full_reduce)).reshape(
        local_rows, local_columns, channels
    )
    shards = (
        lax.psum_scatter(grad_reduce, "fsdp", scatter_dimension=1, tiled=True),
        lax.psum_scatter(grad_dilated, "fsdp", scatter_dimension=3, tiled=True),
        lax.psum_scatter(grad_expand, "fsdp", scatter_dimension=1, tiled=True),
        lax.psum_scatter(grad_point, "fsdp", scatter_dimension=1, tiled=True),
        lax.psum_scatter(rate_weight_grads[0], "fsdp", scatter_dimension=3, tiled=True),
        lax.psum_scatter(rate_weight_grads[1], "fsdp", scatter_dimension=3, tiled=True),
        lax.psum_scatter(rate_weight_grads[2], "fsdp", scatter_dimension=3, tiled=True),
        lax.psum_scatter(grad_pool, "fsdp", scatter_dimension=1, tiled=True),
        lax.psum_scatter(grad_merge, "fsdp", scatter_dimension=1, tiled=True),
        lax.psum_scatter(grad_classes, "fsdp", scatter_dimension=0, tiled=True),
    )
    shards = (
        lax.psum(shards[0].astype(jnp.bfloat16), "dp").astype(jnp.float32),
        lax.psum(shards[1].astype(jnp.bfloat16), "dp").astype(jnp.float32),
        lax.psum(shards[2].astype(jnp.bfloat16), "dp").astype(jnp.float32),
        lax.psum(shards[3].astype(jnp.bfloat16), "dp").astype(jnp.float32),
        lax.psum(shards[4].astype(jnp.bfloat16), "dp").astype(jnp.float32),
        lax.psum(shards[5].astype(jnp.bfloat16), "dp").astype(jnp.float32),
        lax.psum(shards[6].astype(jnp.bfloat16), "dp").astype(jnp.float32),
        lax.psum(shards[7].astype(jnp.bfloat16), "dp").astype(jnp.float32),
        lax.psum(shards[8].astype(jnp.bfloat16), "dp").astype(jnp.float32),
        lax.psum(shards[9].astype(jnp.bfloat16), "dp").astype(jnp.float32),
    )
    return (
        class_logits,
        grad_features,
        shards[0],
        grad_gain_reduce,
        grad_bias_reduce,
        shards[1],
        grad_gain_dilated,
        grad_bias_dilated,
        shards[2],
        grad_gain_expand,
        grad_bias_expand,
        shards[3],
        grad_gain_point,
        grad_bias_point,
        shards[4],
        rate_gain_grads[0],
        rate_bias_grads[0],
        shards[5],
        rate_gain_grads[1],
        rate_bias_grads[1],
        shards[6],
        rate_gain_grads[2],
        rate_bias_grads[2],
        shards[7],
        shards[8],
        grad_gain_merge,
        grad_bias_merge,
        shards[9],
    )


def solution(mesh):
    tiled = mesh.shape["fsdp"] == 8 and mesh.shape["dp"] == 4

    return jax.shard_map(
        fast_body if tiled else body,
        mesh=mesh,
        in_specs=(
            P(("dp", "fsdp"), None, None),
            P(("dp", "fsdp"), None),
            P(("dp", "fsdp"), None),
            P(None, "fsdp"),
            P(),
            P(),
            P(None, None, None, "fsdp"),
            P(),
            P(),
            P(None, "fsdp"),
            P(),
            P(),
            P(None, "fsdp"),
            P(),
            P(),
            P(None, None, None, "fsdp"),
            P(),
            P(),
            P(None, None, None, "fsdp"),
            P(),
            P(),
            P(None, None, None, "fsdp"),
            P(),
            P(),
            P(None, "fsdp"),
            P(None, "fsdp"),
            P(),
            P(),
            P("fsdp", None),
        ),
        out_specs=(
            P(("dp", "fsdp"), None, None),
            P(("dp", "fsdp"), None, None),
            P(None, "fsdp"),
            P(),
            P(),
            P(None, None, None, "fsdp"),
            P(),
            P(),
            P(None, "fsdp"),
            P(),
            P(),
            P(None, "fsdp"),
            P(),
            P(),
            P(None, None, None, "fsdp"),
            P(),
            P(),
            P(None, None, None, "fsdp"),
            P(),
            P(),
            P(None, None, None, "fsdp"),
            P(),
            P(),
            P(None, "fsdp"),
            P(None, "fsdp"),
            P(),
            P(),
            P("fsdp", None),
        ),
        check_vma=False,
    )
```

```python
import functools
import jax
import jax.numpy as jnp
from jax import lax
from jax.experimental import pallas as pl
from jax.experimental.pallas import tpu as pltpu
from jax.sharding import PartitionSpec as P


CLASSES = 19
CROPS_TILE = 4
DILATION_SPAN = 4
RATE = 12

eps = 1e-05

MESH = pl.DeviceIdType.MESH
ANY = pl.BlockSpec(memory_space=pl.ANY)
VM = pl.BlockSpec(memory_space=pltpu.VMEM)
DMA = pltpu.SemaphoreType.DMA
PAD = 144
VLIM = 60 * 2**20


def greet(fs, ds):
    f = lax.axis_index("fsdp")
    d = lax.axis_index("dp")
    bar = pltpu.get_barrier_semaphore()
    for k in fs:
        pl.semaphore_signal(bar, inc=1, device_id=(d, f ^ k), device_id_type=MESH)
    for k in ds:
        pl.semaphore_signal(bar, inc=1, device_id=(d ^ k, f), device_id_type=MESH)
    pl.semaphore_wait(bar, len(fs) + len(ds))
    return f, d


def remote(src, dst, ss, rs, d, f):
    c = pltpu.make_async_remote_copy(
        src_ref=src, dst_ref=dst, send_sem=ss, recv_sem=rs, device_id=(d, f), device_id_type=MESH
    )
    c.start()
    return c


def sum_kernel(x_ref, o_ref, b1, b2, s1, r1, s2, r2):
    f, d = greet(range(1, 8), range(1, 4))
    b1[f] = x_ref[...]
    cps = [remote(x_ref, b1.at[f], s1.at[k], r1.at[k], d, f ^ k) for k in range(1, 8)]
    for c in cps:
        c.wait()
    tot = b1[0]
    for k in range(1, 8):
        tot = tot + b1[k]
    b2[d] = tot
    cps = [remote(b2.at[d], b2.at[d], s2.at[k], r2.at[k], d ^ k, f) for k in range(1, 4)]
    for c in cps:
        c.wait()
    tot = b2[0]
    for k in range(1, 4):
        tot = tot + b2[k]
    o_ref[...] = tot


def total_sum(rows, cid):
    x = jnp.stack(rows)
    R, C = x.shape
    return pl.pallas_call(
        sum_kernel,
        out_shape=jax.ShapeDtypeStruct((R, C), jnp.float32),
        in_specs=[VM],
        out_specs=VM,
        scratch_shapes=[
            pltpu.VMEM((8, R, C), jnp.float32),
            pltpu.VMEM((4, R, C), jnp.float32),
            DMA((8,)),
            DMA((8,)),
            DMA((4,)),
            DMA((4,)),
        ],
        compiler_params=pltpu.CompilerParams(collective_id=cid, has_side_effects=True),
        name=f"total_sum_{cid}",
    )(x)


def spread_kernel(x_ref, o_ref, ss, rs, ls):
    f, d = greet(range(1, 8), ())
    w = o_ref.shape[2]
    h = x_ref.shape[1]
    dst = o_ref.at[:, pl.ds(pl.multiple_of(PAD + h * f, 16), h), :]

    def part(g):
        return x_ref.at[:, :, pl.ds(pl.multiple_of(g * w, 128), w)]

    cps = [remote(part(f ^ k), dst, ss.at[k], rs.at[k], d, f ^ k) for k in (6, 7, 2, 3, 4, 5, 1)]
    own = pltpu.make_async_copy(part(f), dst, ls)
    own.start()
    for c in cps:
        c.wait()
    own.wait()


def spread_channels(x, cid):
    q, h, C = x.shape
    return pl.pallas_call(
        spread_kernel,
        out_shape=jax.ShapeDtypeStruct((q, 8 * h + 2 * PAD, C // 8), x.dtype),
        in_specs=[VM],
        out_specs=ANY,
        scratch_shapes=[DMA((8,)), DMA((8,)), DMA(())],
        compiler_params=pltpu.CompilerParams(collective_id=cid, has_side_effects=True, vmem_limit_bytes=VLIM),
        name=f"spread_{cid}",
    )(x)


def collect_kernel(x_ref, o_ref, ss, rs, ls):
    f, d = greet(range(1, 8), ())
    w = x_ref.shape[2]
    h = o_ref.shape[1]
    dst = o_ref.at[:, :, pl.ds(pl.multiple_of(f * w, 128), w)]

    def part(g):
        return x_ref.at[:, pl.ds(pl.multiple_of(h * g, 16), h), :]

    cps = [remote(part(f ^ k), dst, ss.at[k], rs.at[k], d, f ^ k) for k in (6, 7, 2, 3, 4, 5, 1)]
    own = pltpu.make_async_copy(part(f), dst, ls)
    own.start()
    for c in cps:
        c.wait()
    own.wait()


def collect_channels(x, cid):
    q, t, w = x.shape
    return pl.pallas_call(
        collect_kernel,
        out_shape=jax.ShapeDtypeStruct((q, t // 8, 8 * w), x.dtype),
        in_specs=[VM],
        out_specs=ANY,
        scratch_shapes=[DMA((8,)), DMA((8,)), DMA(())],
        compiler_params=pltpu.CompilerParams(collective_id=cid, has_side_effects=True, vmem_limit_bytes=VLIM),
        name=f"collect_{cid}",
    )(x)


def gather_kernel(x_ref, o_ref, ss, rs, ps, pr, ls):
    f, d = greet((1, 2, 4, 6), ())
    h = x_ref.shape[1]

    def slot(g):
        return o_ref.at[:, pl.ds(pl.multiple_of(PAD + h * g, 16), h), :]

    cps = [remote(x_ref, slot(f), ss.at[k], rs.at[k], d, f ^ (2 * k)) for k in (3, 1, 2)]
    own = pltpu.make_async_copy(x_ref, slot(f), ls)
    own.start()
    pair = [remote(x_ref, slot(f), ps.at[0], pr.at[0], d, f ^ 1)]
    for k, c in zip((3, 1, 2), cps):
        c.wait_recv()
        got = slot(f ^ (2 * k))
        pair.append(remote(got, got, ps.at[k], pr.at[k], d, f ^ 1))
    for c in cps:
        c.wait_send()
    for c in pair:
        c.wait()
    own.wait()


def gather_rows(x, cid):
    q, h, C = x.shape
    return pl.pallas_call(
        gather_kernel,
        out_shape=jax.ShapeDtypeStruct((q, 8 * h + 2 * PAD, C), x.dtype),
        in_specs=[VM],
        out_specs=ANY,
        scratch_shapes=[DMA((4,)), DMA((4,)), DMA((4,)), DMA((4,)), DMA(())],
        compiler_params=pltpu.CompilerParams(collective_id=cid, has_side_effects=True, vmem_limit_bytes=VLIM),
        name=f"gather_{cid}",
    )(x)


def scatter_kernel(x_ref, o_ref, near, mine, far, ps, pr, ss, rs):
    f, d = greet((1, 2, 4, 6), ())
    c0 = f & 1
    pair = [
        remote(x_ref.at[2 * k + 1 - c0], near.at[k], ps.at[k], pr.at[k], d, f ^ 1) for k in range(4)
    ]
    me = lax.shift_right_logical(f, 1)
    cps = []
    for c in pair:
        c.wait()
    for k in (3, 1, 2, 0):
        g = me ^ k
        val = x_ref[2 * g + c0].astype(jnp.float32) + near[g].astype(jnp.float32)
        if k:
            mine[k] = val.astype(mine.dtype)
            cps.append(remote(mine.at[k], far.at[k], ss.at[k], rs.at[k], d, f ^ (2 * k)))
        else:
            o_ref[...] = val
    for c in cps:
        c.wait()
    o_ref[...] += far[1].astype(jnp.float32) + far[2].astype(jnp.float32) + far[3].astype(jnp.float32)


def scatter_sum(x, cid):
    n, R, C = x.shape
    return pl.pallas_call(
        scatter_kernel,
        out_shape=jax.ShapeDtypeStruct((R, C), jnp.float32),
        in_specs=[VM],
        out_specs=VM,
        scratch_shapes=[
            pltpu.VMEM((4, R, C), x.dtype),
            pltpu.VMEM((4, R, C), x.dtype),
            pltpu.VMEM((4, R, C), x.dtype),
            DMA((4,)),
            DMA((4,)),
            DMA((4,)),
            DMA((4,)),
        ],
        compiler_params=pltpu.CompilerParams(collective_id=cid, has_side_effects=True, vmem_limit_bytes=VLIM),
        name=f"scatter_{cid}",
    )(x)


def nt_dot(a, b):
    return lax.dot_general(a, b, (((1,), (1,)), ((), ())), preferred_element_type=jnp.float32)


def nn_dot(a, b):
    return lax.dot_general(a, b, (((1,), (0,)), ((), ())), preferred_element_type=jnp.float32)


def tn_dot(a, b):
    return lax.dot_general(a, b, (((0,), (0,)), ((), ())), preferred_element_type=jnp.float32)


def span(shift, count):
    return max(0, -shift), min(count, count - shift)


def conv_forward_kernel(steps, y_ref, key_ref, k_ref, o_ref, acc):
    Q = y_ref.shape[0]
    h = o_ref.shape[2]
    w = y_ref.shape[2]
    out = k_ref.shape[1]
    dest = pl.program_id(0)
    base = PAD + h * dest
    T = 8 * h
    for b, s in enumerate(steps):
        acc[...] = jnp.zeros_like(acc)
        for i in (-1, 0, 1):
            first = h * dest + 16 * s * i

            @pl.when((first + h > 0) & (first < T))
            def _():
                at = pl.multiple_of(base + 16 * s * i, 16)
                for j in (-1, 0, 1):
                    lo, hi = span(s * j, Q)
                    here = key_ref[lo:hi, pl.ds(pl.multiple_of(base, 16), h), :]
                    there = key_ref[lo + s * j : hi + s * j, pl.ds(at, h), :]
                    ok = (here == there) & (here > 0)
                    ok = jnp.concatenate([ok] * (w // 128), axis=2)
                    x = jnp.where(ok, y_ref[lo + s * j : hi + s * j, pl.ds(at, h), :], 0)
                    x = x.reshape((hi - lo) * h, w)
                    acc[lo * h : hi * h] += nt_dot(x, k_ref[9 * b + 3 * (i + 1) + j + 1])

        o_ref[0, :, :, b * out : (b + 1) * out] = acc[...].reshape(Q, h, out).astype(o_ref.dtype)


def conv_forward(y, key, k, steps):
    Q, TT, w = y.shape
    h = (TT - 2 * PAD) // 8
    out = k.shape[1]
    return pl.pallas_call(
        functools.partial(conv_forward_kernel, steps),
        out_shape=jax.ShapeDtypeStruct((8, Q, h, 3 * out), jnp.bfloat16),
        grid=(8,),
        in_specs=[VM, VM, VM],
        out_specs=pl.BlockSpec((1, Q, h, 3 * out), lambda i: (i, 0, 0, 0)),
        scratch_shapes=[pltpu.VMEM((Q * h, out), jnp.float32)],
        compiler_params=pltpu.CompilerParams(vmem_limit_bytes=VLIM),
        name="conv_forward",
    )(y, key, k)


def conv_data_kernel(steps, g_ref, key_ref, k_ref, o_ref, acc):
    Q = g_ref.shape[0]
    h = o_ref.shape[1]
    w = o_ref.shape[2]
    out = k_ref.shape[1]
    dest = pl.program_id(0)
    base = PAD + h * dest
    T = 8 * h
    acc[...] = jnp.zeros_like(acc)
    for b, s in enumerate(steps):
        for i in (-1, 0, 1):
            first = h * dest - 16 * s * i

            @pl.when((first + h > 0) & (first < T))
            def _():
                at = pl.multiple_of(base - 16 * s * i, 16)
                for j in (-1, 0, 1):
                    lo, hi = span(-s * j, Q)
                    here = key_ref[lo:hi, pl.ds(pl.multiple_of(base, 16), h), :]
                    there = key_ref[lo - s * j : hi - s * j, pl.ds(at, h), :]
                    ok = (here == there) & (here > 0)
                    ok = jnp.concatenate([ok] * (out // 128), axis=2)
                    x = jnp.where(
                        ok, g_ref[lo - s * j : hi - s * j, pl.ds(at, h), b * out : (b + 1) * out], 0
                    )
                    x = x.reshape((hi - lo) * h, out)
                    acc[lo * h : hi * h] += nn_dot(x, k_ref[9 * b + 3 * (i + 1) + j + 1])

    o_ref[...] = acc[...].reshape(Q, h, w).astype(o_ref.dtype)


def conv_data(g, key, k, steps):
    Q, TT, _ = g.shape
    h = (TT - 2 * PAD) // 8
    w = k.shape[2]
    return pl.pallas_call(
        functools.partial(conv_data_kernel, steps),
        out_shape=jax.ShapeDtypeStruct((Q, 8 * h, w), jnp.bfloat16),
        grid=(8,),
        in_specs=[VM, VM, VM],
        out_specs=pl.BlockSpec((Q, h, w), lambda i: (0, i, 0)),
        scratch_shapes=[pltpu.VMEM((Q * h, w), jnp.float32)],
        compiler_params=pltpu.CompilerParams(vmem_limit_bytes=VLIM),
        name="conv_data",
    )(g, key, k)


def conv_weight_kernel(steps, y_ref, key_ref, g_ref, o_ref, x_ref):
    Q = y_ref.shape[0]
    w = y_ref.shape[2]
    out = o_ref.shape[1]
    TT = y_ref.shape[1]
    T = TT - 2 * PAD
    b = pl.program_id(0)
    for n, s in enumerate(steps):

        @pl.when(b == n)
        def _():
            for i in (-1, 0, 1):
                r0, r1 = span(16 * s * i, T)
                r0, r1 = r0 // 128 * 128, -(-r1 // 128) * 128
                for j in (-1, 0, 1):
                    lo, hi = span(s * j, Q)
                    L = r1 - r0

                    def one(q, _):
                        here = key_ref[q, PAD + r0 : PAD + r1, :]
                        a = PAD + r0 + 16 * s * i
                        there = key_ref[q + s * j, a : a + L, :]
                        ok = (here == there) & (here > 0)
                        ok = jnp.concatenate([ok] * (w // 128), axis=1)
                        x = jnp.where(ok, y_ref[q + s * j, a : a + L, :], 0)
                        x_ref[pl.ds(pl.multiple_of((q - lo) * L, 128), L), :] = x
                        return 0

                    lax.fori_loop(lo, hi, one, 0)
                    d = g_ref[lo:hi, PAD + r0 : PAD + r1, n * out : (n + 1) * out]
                    d = d.reshape((hi - lo) * L, out)
                    o_ref[3 * (i + 1) + j + 1] = tn_dot(d, x_ref[: (hi - lo) * L, :]).astype(o_ref.dtype)


def conv_weight(y, key, g, steps, out):
    Q, TT, w = y.shape
    T = TT - 2 * PAD
    return pl.pallas_call(
        functools.partial(conv_weight_kernel, steps),
        out_shape=jax.ShapeDtypeStruct((27, out, w), jnp.bfloat16),
        grid=(3,),
        in_specs=[VM, VM, VM],
        out_specs=pl.BlockSpec((9, out, w), lambda i: (i, 0, 0)),
        scratch_shapes=[pltpu.VMEM((Q * T, w), jnp.bfloat16)],
        compiler_params=pltpu.CompilerParams(vmem_limit_bytes=VLIM),
        name="conv_weight",
    )(y, key, g)


class Gather:
    def __init__(self, src, slot, sems, d, f):
        self.src, self.slot, self.sems, self.d, self.f = src, slot, sems, d, f

    def start(self):
        far_s, far_r, near_s, near_r, local = self.sems
        d, f = self.d, self.f
        mine = self.slot(f)
        self.far = {k: remote(self.src, mine, far_s.at[k], far_r.at[k], d, f ^ (2 * k)) for k in (3, 1, 2)}
        self.near = [remote(self.src, mine, near_s.at[0], near_r.at[0], d, f ^ 1)]
        self.own = pltpu.make_async_copy(self.src, mine, local)
        self.own.start()

    def forward(self):
        far_s, far_r, near_s, near_r, local = self.sems
        for k in (1, 2, 3):
            self.far[k].wait_recv()
            got = self.slot(self.f ^ (2 * k))
            self.near.append(remote(got, got, near_s.at[k], near_r.at[k], self.d, self.f ^ 1))

    def arrive(self):
        self.own.wait()
        for c in self.near:
            c.wait_recv()

    def finish(self):
        for c in list(self.far.values()) + self.near:
            c.wait_send()


class HalfGather:
    def __init__(self, src, slot, half, sems, d, f):
        self.src, self.slot, self.half, self.sems, self.d, self.f = src, slot, half, sems, d, f

    def start(self):
        far_s, far_r, near_s, near_r, side_s, side_r, local = self.sems
        d, f = self.d, self.f
        mine = self.slot(f)
        a = self.half(d % 2)
        self.far = {
            k: remote(self.src.at[a], mine.at[a], far_s.at[k], far_r.at[k], d, f ^ (2 * k)) for k in (3, 1, 2)
        }
        self.near = [remote(self.src, mine, near_s.at[0], near_r.at[0], d, f ^ 1)]
        self.own = pltpu.make_async_copy(self.src, mine, local)
        self.own.start()

    def forward(self):
        far_s, far_r, near_s, near_r, side_s, side_r, local = self.sems
        d, f = self.d, self.f
        a = self.half(d % 2)
        self.side = {}
        for k in (1, 2, 3):
            self.far[k].wait_recv()
            got = self.slot(f ^ (2 * k)).at[a]
            self.side[k] = remote(got, got, side_s.at[k], side_r.at[k], d ^ 1, f)
            self.near.append(remote(got, got, near_s.at[k], near_r.at[k], d, f ^ 1))

    def arrive(self):
        far_s, far_r, near_s, near_r, side_s, side_r, local = self.sems
        d, f = self.d, self.f
        b = self.half(1 - d % 2)
        for k in (1, 2, 3):
            self.side[k].wait_recv()
            got = self.slot(f ^ (2 * k)).at[b]
            self.near.append(remote(got, got, near_s.at[k + 3], near_r.at[k + 3], d, f ^ 1))
        self.own.wait()
        for c in self.near:
            c.wait_recv()

    def finish(self):
        for c in list(self.far.values()) + self.near + list(self.side.values()):
            c.wait_send()


def half_sems():
    return [DMA((4,)), DMA((4,)), DMA((7,)), DMA((7,)), DMA((4,)), DMA((4,)), DMA(())]


def gather_sems():
    return [DMA((4,)), DMA((4,)), DMA((4,)), DMA((4,)), DMA(())]


def sum_sems(R, C):
    return [
        pltpu.VMEM((8, R, C), jnp.float32),
        pltpu.VMEM((4, R, C), jnp.float32),
        DMA((8,)),
        DMA((8,)),
        DMA((4,)),
        DMA((4,)),
    ]


def sum_all(rows, bufs, d, f):
    b1, b2, s1, r1, s2, r2 = bufs
    for n, row in enumerate(rows):
        b1[f, n : n + 1, :] = row
    cps = [remote(b1.at[f], b1.at[f], s1.at[k], r1.at[k], d, f ^ k) for k in (6, 2, 4, 7, 3, 5, 1)]
    for c in cps:
        c.wait()
    tot = b1[0]
    for k in range(1, 8):
        tot = tot + b1[k]
    b2[d] = tot
    cps = [remote(b2.at[d], b2.at[d], s2.at[k], r2.at[k], d ^ k, f) for k in (3, 2, 1)]
    for c in cps:
        c.wait()
    tot = b2[0]
    for k in range(1, 4):
        tot = tot + b2[k]
    return tot


def column_sums(a, ins):
    m = a * jnp.concatenate([ins] * (a.shape[1] // 128), axis=1)
    return jnp.sum(m, axis=0, keepdims=True), jnp.sum(m * a, axis=0, keepdims=True)


def bend(p):
    g = 1.0 / (1.0 + jnp.exp(-p))
    return p * g, g * (1.0 + p * (1.0 - g))


def same_crop(here, there, width):
    ok = (here == there) & (here > 0)
    return jnp.concatenate([ok] * (width // 128), axis=ok.ndim - 1)


def cat_rows(parts):
    return jnp.concatenate(parts, axis=1)


def bottleneck_kernel(
    x_ref, kb_ref, ins_ref, gr, br, gd, bd, ge, be,
    wr_s, wd_s, we_s, wp_s, wm_s, wc_s, k_s0, k_s1, k_s2, kp_s,
    yo_o, y_o, n3_o, l3_o, n1_o, l1_o, n2_o, l2_o, ext_o, h2_o, key_o, k_o, wr_o, wd_o, we_o, wp_o, wm_o, wc_o, cnt_o,
    xp, a1, a2, a3, ext, h2, y, n3, l3, n1, l1, n2, l2, key, wr, wd, we,
    *sems,
):
    sems = list(sems)

    def take(n):
        got = sems[:n]
        del sems[:n]
        return got

    f, d = greet(range(1, 8), range(1, 4))
    N, C = x_ref.shape
    Q, h = ext.shape[0], ext.shape[1] // 2
    e = h // 2
    rows = h // 4
    neck = a1.shape[1]
    T = 8 * h

    def rows_of(ref, n):
        return lambda g: ref.at[pl.ds(pl.multiple_of(n * g, n), n)]

    nr, nd_, ne, np_ = wr_s.shape[0], wd_s.shape[1], we_s.shape[1], wp_s.shape[0]
    def half(n, lead=()):
        return lambda a: lead + (pl.ds(pl.multiple_of(n * a, n), n),)

    g_wr = Gather(wr_s, rows_of(wr, nr), take(5), d, f)
    g_wd = [
        HalfGather(
            wd_s.at[pl.ds(3 * i, 3)],
            lambda g, i=i: wd.at[pl.ds(3 * i, 3), pl.ds(pl.multiple_of(nd_ * g, 16), nd_), :],
            half(nd_ // 2, (slice(None),)), take(7), d, f,
        )
        for i in range(3)
    ]
    g_we = HalfGather(
        we_s, lambda g: we.at[:, pl.ds(pl.multiple_of(ne * g, 128), ne)], half(we_s.shape[0] // 2), take(7), d, f
    )
    g_wp = Gather(wp_s, rows_of(wp_o, np_), take(5), d, f)
    g_wm = Gather(wm_s, rows_of(wm_o, np_), take(5), d, f)
    g_wc = Gather(wc_s, rows_of(wc_o, np_), take(5), d, f)
    ks, kr, kl, zs, zk, hs, hr, ys, yr, yl, os_, qs, qr, kc = take(14)
    sum1, sum2, sum3 = (Sum(take(6), d, f) for _ in range(3))

    key_sent = [
        remote(kb_ref, kc.at[f], qs.at[k], qr.at[k], d, f ^ k) for k in (6, 7, 2, 3, 4, 5, 1)
    ]
    kc[f] = kb_ref[...]
    g_wr.start()
    g_wd[0].start()
    order = lax.broadcasted_iota(jnp.int32, (N, N), 0)
    m, r, q = order % 4, (order // 4) % rows, order // h
    pick = (r * (N // rows) + q * 4 + m) == lax.broadcasted_iota(jnp.int32, (N, N), 1)
    pick = pick.astype(jnp.float32).astype(jnp.bfloat16)
    for c in range(0, C, 256):
        xp[:, c : c + 256] = nn_dot(pick, x_ref[:, c : c + 256]).astype(jnp.bfloat16)
    key[:, :PAD, :] = jnp.zeros((Q, PAD, 128), jnp.bfloat16)
    key[:, PAD + T :, :] = jnp.zeros((Q, PAD, 128), jnp.bfloat16)
    g_wr.forward()
    g_wd[1].start()
    g_wd[2].start()
    g_wr.arrive()
    g_wd[0].forward()
    sums, squares = [], []
    for c in range(0, neck, 256):
        a = nt_dot(xp[...], wr[c : c + 256, :])
        a1[:, c : c + 256] = a
        s, t = column_sums(a, ins_ref[...])
        sums.append(s)
        squares.append(t)
    inside = jnp.sum(ins_ref[...], axis=0, keepdims=True)
    sum1.start([cat_rows(sums), cat_rows(squares), cat_rows([inside] * (neck // 128))])
    g_we.start()
    g_wd[1].forward()
    g_wd[2].forward()
    kparts = (k_s0, k_s1, k_s2, kp_s)

    def kslot(b, g, lo, n):
        o = kparts[b].shape[1]
        return k_o.at[pl.ds(9 * b, kparts[b].shape[0]), pl.ds(pl.multiple_of(o * g + lo, 16), n), :]

    kcp, kfar = [], {}

    def kernels_out(b):
        src = kparts[b]
        o = src.shape[1] // 2
        lo = pl.multiple_of(o * (d % 2), 16)
        for k in (6, 7, 2, 3, 4, 5):
            to = pl.ds(pl.multiple_of((f ^ k) * 256, 128), 256)
            kfar[b, k] = remote(
                src.at[:, pl.ds(lo, o), to], kslot(b, f, lo, o), ks.at[b, k], kr.at[b, k], d, f ^ k
            )
        to = pl.ds(pl.multiple_of((f ^ 1) * 256, 128), 256)
        kcp.append(remote(src.at[:, :, to], kslot(b, f, 0, 2 * o), ks.at[b, 1], kr.at[b, 1], d, f ^ 1))
        own = pl.ds(pl.multiple_of(f * 256, 128), 256)
        c = pltpu.make_async_copy(src.at[:, :, own], kslot(b, f, 0, 2 * o), kl.at[b])
        c.start()
        kcp.append(c)

    def kernels_aside(b):
        o = kparts[b].shape[1] // 2
        lo = pl.multiple_of(o * (d % 2), 16)
        for k in (2, 3, 4, 5, 6, 7):
            kfar[b, k].wait_recv()
            got = kslot(b, f ^ k, lo, o)
            kcp.append(remote(got, got, zs.at[b, k], zk.at[b, k], d ^ 1, f))

    sum1.turn()
    st = sum1.result()
    g_we.forward()
    count = st[2:3, :]
    cnt_o[...] = jnp.zeros_like(cnt_o)
    cnt_o[0:1, :neck] = count
    mean = st[0:1] / count
    inv = lax.rsqrt(st[1:2] / count - mean * mean + eps)
    cnt_o[1:2, :neck] = inv
    for c in range(0, neck, 256):
        w = slice(c, c + 256)
        n = (a1[:, w] - mean[:, w]) * inv[:, w]
        act, lean = bend(n * gr[:, w] + br[:, w])
        ext[:, e : e + h, w] = act.astype(jnp.bfloat16).reshape(Q, h, 256)
        n1[:, w] = n.astype(jnp.bfloat16)
        l1[:, w] = lean.astype(jnp.bfloat16)
    up = remote(ext.at[:, pl.ds(e, e)], ext.at[:, pl.ds(e + h, e)], hs.at[0], hr.at[0], d, lax.rem(f + 7, 8))
    down = remote(ext.at[:, pl.ds(h, e)], ext.at[:, pl.ds(0, e)], hs.at[1], hr.at[1], d, lax.rem(f + 1, 8))
    for c in key_sent:
        c.wait()
    for g in range(8):
        turned = kc[g].T
        for q in range(Q):
            key[q, PAD + h * g : PAD + h * g + h, :] = jnp.broadcast_to(turned[:h, q : q + 1], (h, 128)).astype(jnp.bfloat16)
    for b in range(4):
        kernels_out(b)
    outs = [(n1, n1_o), (l1, l1_o), (key, key_o), (wr, wr_o)]
    base = pl.multiple_of(PAD + h * f, 16)
    up.wait()
    down.wait()
    outs.append((ext, ext_o))
    outs.append((wd, wd_o))
    a2[...] = jnp.zeros_like(a2)
    for i in range(3):
        g_wd[i].arrive()
        for j in (1, 0, 2):
            lo, hi = span(j - 1, Q)
            ok = same_crop(
                key[lo:hi, pl.ds(base, h), :],
                key[lo + j - 1 : hi + j - 1, pl.ds(pl.multiple_of(base + e * (i - 1), 16), h), :],
                neck,
            )
            v = jnp.where(ok, ext[lo + j - 1 : hi + j - 1, e * i : e * i + h, :], 0).reshape((hi - lo) * h, neck)
            for c in range(0, neck, 256):
                a2[lo * h : hi * h, c : c + 256] += nt_dot(v, wd[3 * i + j, c : c + 256, :])
    sums, squares = [], []
    for c in range(0, neck, 256):
        s, t = column_sums(a2[:, c : c + 256], ins_ref[...])
        sums.append(s)
        squares.append(t)
    sum2.start([cat_rows(sums), cat_rows(squares)])
    kernels_aside(0)
    sum2.turn()
    st = sum2.result()
    mean = st[0:1] / count
    inv = lax.rsqrt(st[1:2] / count - mean * mean + eps)
    cnt_o[2:3, :neck] = inv
    for c in range(0, neck, 256):
        w = slice(c, c + 256)
        n = (a2[:, w] - mean[:, w]) * inv[:, w]
        act, lean = bend(n * gd[:, w] + bd[:, w])
        h2[:, w] = act.astype(jnp.bfloat16)
        n2[:, w] = n.astype(jnp.bfloat16)
        l2[:, w] = lean.astype(jnp.bfloat16)
    outs += [(n2, n2_o), (l2, l2_o), (h2, h2_o)]
    g_we.arrive()
    outs.append((we, we_o))
    sums, squares = [], []
    for c in range(0, C, 256):
        a = nn_dot(h2[...], we[:, c : c + 256])
        a3[:, c : c + 256] = a
        s, t = column_sums(a, ins_ref[...])
        sums.append(s)
        squares.append(t)
    sum3.start([cat_rows(sums), cat_rows(squares)])
    kernels_aside(1)
    sum3.turn()
    for g in (g_wp, g_wm, g_wc):
        g.start()
    st = sum3.result()
    total = count[:, :1]
    mean3 = st[0:1] / total
    inv3 = lax.rsqrt(st[1:2] / total - mean3 * mean3 + eps)
    coef = sum3.b1
    coef[0, 0:1, :] = mean3
    coef[0, 1:2, :] = inv3
    cnt_o[3:4, :] = inv3
    sent = []
    dst = yo_o.at[:, pl.ds(base, h), :]
    for k in (6, 7, 2, 3, 4, 5, 1, 0):
        g = f ^ k
        w = pl.ds(pl.multiple_of(g * 256, 256), 256)
        n = (a3[:, w] - coef[0, 0:1, w]) * coef[0, 1:2, w]
        act, lean = bend(n * ge[:, w] + be[:, w] + xp[:, w].astype(jnp.float32))
        y[:, :, w] = act.astype(jnp.bfloat16).reshape(Q, h, 256)
        n3[:, w] = n.astype(jnp.bfloat16)
        l3[:, w] = lean.astype(jnp.bfloat16)
        part = y.at[:, :, w]
        if k:
            sent.append(remote(part, dst, ys.at[k], yr.at[k], d, g))
        else:
            own = pltpu.make_async_copy(part, dst, yl)
            own.start()
            sent.append(own)
    outs += [(y, y_o), (n3, n3_o), (l3, l3_o)]
    saved = []
    kernels_aside(2)
    kernels_aside(3)
    for n, (src, to) in enumerate(outs):
        c = pltpu.make_async_copy(src, to, os_.at[n])
        c.start()
        saved.append(c)
    for g in (g_wp, g_wm, g_wc):
        g.forward()
    for g in (g_wp, g_wm, g_wc):
        g.arrive()
    for g in [g_wr, g_we, g_wp, g_wm, g_wc] + g_wd:
        g.finish()
    for c in kfar.values():
        c.wait_send()
    for c in kcp + sent + saved:
        c.wait()


def bottleneck(x, kb, ins, vecs, shards, kparts):
    N, C = x.shape
    Q = kb.shape[0]
    h = N // Q
    wr, wd, we, wp, wm, wc = shards
    neck = we.shape[0]
    W = 8 * wp.shape[0]
    b16, f32 = jnp.bfloat16, jnp.float32
    S = jax.ShapeDtypeStruct
    TT = 8 * h + 2 * PAD
    outs = [
        S((Q, TT, C // 8), b16), S((Q, h, C), b16), S((N, C), b16), S((N, C), b16),
        S((N, neck), b16), S((N, neck), b16), S((N, neck), b16), S((N, neck), b16),
        S((Q, 2 * h, neck), b16), S((N, neck), b16), S((Q, TT, 128), b16), S((28, W, C // 8), b16),
        S((neck, C), b16), S((9, neck, neck), b16), S((neck, C), b16), S((W, C), b16), S((W, wm.shape[1]), b16),
        S((W, 128), b16), S((8, C), f32),
    ]
    V = pltpu.VMEM
    scratch = [
        V((N, C), b16), V((N, neck), f32), V((N, neck), f32), V((N, C), f32), V((Q, 2 * h, neck), b16), V((N, neck), b16),
        V((Q, h, C), b16), V((N, C), b16), V((N, C), b16),
        V((N, neck), b16), V((N, neck), b16), V((N, neck), b16), V((N, neck), b16), V((Q, TT, 128), b16),
        V((neck, C), b16), V((9, neck, neck), b16), V((neck, C), b16),
    ]
    scratch += gather_sems() + half_sems() * 4 + gather_sems() * 3
    scratch += [DMA((4, 8)), DMA((4, 8)), DMA((4,)), DMA((4, 8)), DMA((4, 8)), DMA((2,)), DMA((2,)), DMA((8,)), DMA((8,)), DMA(()), DMA((16,))]
    scratch += [DMA((8,)), DMA((8,)), V((8, Q, 128), f32)]
    scratch += sum_sems(3, neck) + sum_sems(2, neck) + sum_sems(2, C)
    return pl.pallas_call(
        bottleneck_kernel,
        out_shape=outs,
        in_specs=[VM] * 9 + [ANY] * 10,
        out_specs=[ANY] * 18 + [VM],
        scratch_shapes=scratch,
        compiler_params=pltpu.CompilerParams(collective_id=1, has_side_effects=True, vmem_limit_bytes=VLIM),
        name="bottleneck",
    )(x, kb, ins, *vecs, *shards, *kparts)


def branches_back_kernel(
    steps, d_ref, y_ref, key_ref, k_ref, pooled_ref, dr_ref, size_ref, dy_o, gk_o,
    g, gt, x, gk, fin, in1, in2, dyo, acc, gp, *sems,
):
    sems = list(sems)
    f, d = greet(range(1, 8), range(1, 4))
    Q, h, w = y_ref.shape[0], d_ref.shape[1], y_ref.shape[2]
    W = k_ref.shape[1]
    T = 8 * h
    o = W // 8
    taps = gk.shape[0]
    gathers = [
        Gather(
            d_ref.at[:, :, pl.ds(b * W, W)],
            lambda n, b=b: g.at[:, pl.ds(pl.multiple_of(PAD + h * n, 16), h), pl.ds(b * W, W)],
            sems[5 * b : 5 * b + 5], d, f,
        )
        for b in range(3)
    ]
    ws, wr, wl, ds_, dr_, dl, s1, r1, s2, r2, s3, r3 = sems[15:]
    for c in gathers:
        c.start()
    outer = d % 3 == 0

    def to_inner(t):
        return pltpu.make_async_remote_copy(
            src_ref=gk.at[t], dst_ref=in1.at[t], send_sem=s1.at[t], recv_sem=r1.at[t],
            device_id=(d ^ 1, f), device_id_type=MESH,
        )

    def across(t):
        return pltpu.make_async_remote_copy(
            src_ref=gk.at[t], dst_ref=in2.at[t], send_sem=s2.at[t], recv_sem=r2.at[t],
            device_id=(d ^ 3, f), device_id_type=MESH,
        )

    def to_outer(t):
        return pltpu.make_async_remote_copy(
            src_ref=fin.at[t], dst_ref=fin.at[t], send_sem=s3.at[t], recv_sem=r3.at[t],
            device_id=(d ^ 1, f), device_id_type=MESH,
        )

    def hand(t):
        @pl.when(outer)
        def _():
            to_inner(t).start()

    def first(t):
        @pl.when(jnp.logical_not(outer))
        def _():
            to_inner(t).wait_recv()
            gk[t] = (gk[t].astype(jnp.float32) + in1[t].astype(jnp.float32)).astype(gk.dtype)
            across(t).start()

    def second(t):
        @pl.when(jnp.logical_not(outer))
        def _():
            across(t).wait_recv()
            fin[t] = (gk[t].astype(jnp.float32) + in2[t].astype(jnp.float32)).astype(fin.dtype)
            to_outer(t).start()

        @pl.when(outer)
        def _():
            to_outer(t).wait_recv()

    gk[27] = tn_dot(dr_ref[...], pooled_ref[...]).astype(gk.dtype)
    gp[...] = nn_dot(dr_ref[...], k_ref[27]) / size_ref[:, :1]
    for b, s in enumerate(steps):
        gathers[b].forward()
        gathers[b].arrive()

        def turn(q, _):
            gt[b * W : (b + 1) * W, pl.ds(pl.multiple_of(q * T, 256), T)] = g[q, PAD : PAD + T, b * W : (b + 1) * W].T
            return 0

        lax.fori_loop(0, Q, turn, 0)
        for i in (-1, 0, 1):
            for j in (-1, 0, 1):
                lo, hi = span(s * j, Q)
                a = PAD + 16 * s * i

                def one(q, _):
                    ok = same_crop(key_ref[q, PAD : PAD + T, :], key_ref[q + s * j, a : a + T, :], w)
                    x[pl.ds(pl.multiple_of((q - lo) * T, 256), T), :] = jnp.where(ok, y_ref[q + s * j, a : a + T, :], 0)
                    return 0

                lax.fori_loop(lo, hi, one, 0)
                t = 9 * b + 3 * (i + 1) + j + 1
                gk[t] = nn_dot(
                    gt[b * W : (b + 1) * W, lo * T : hi * T], x[: (hi - lo) * T, :]
                ).astype(gk.dtype)
                hand(t)
    hand(27)
    cps = []
    ready = 4

    def lead(t, _):
        first(t)
        return 0

    lax.fori_loop(0, ready, lead, 0)

    dst = dy_o.at[:, :, pl.ds(pl.multiple_of(w * f, 128), w)]

    def rows_of(k):
        return pl.ds(pl.multiple_of(h * (f ^ k), 16), h)

    def dest_step(m, _):
        k = 7 - m
        dest = f ^ k
        first(ready + m)
        base = pl.multiple_of(PAD + h * dest, 16)
        here = key_ref[:, pl.ds(base, h), :].astype(jnp.float32).reshape(Q * h, 128)
        here = jnp.concatenate([here] * (w // 128), axis=1)
        total = jnp.zeros((Q * h, w), jnp.float32)
        for c in range(CROPS_TILE):
            total = jnp.where(here == c + 1.0, gp[c : c + 1, :], total)
        acc[...] = total
        for b in range(3):
            spaced_taps(g, key_ref, k_ref, acc, base, h, steps, -1, b * W, nn_dot, b)
        rows = rows_of(k)
        dyo[:, rows, :] = acc[...].reshape(Q, h, w).astype(dyo.dtype)
        src = dyo.at[:, rows, :]

        @pl.when(k > 0)
        def _():
            remote(src, dst, ds_.at[k], dr_.at[k], d, dest)

        @pl.when(k == 0)
        def _():
            pltpu.make_async_copy(src, dst, dl).start()

        return 0

    lax.fori_loop(0, 8, dest_step, 0)
    done = ready + 8

    def first_when(t):
        @pl.when(t < taps)
        def _():
            first(t)

    groups = (9, 9, 5, 5)
    at = 0
    for n, size in enumerate(groups):
        stop = at + size
        lax.fori_loop(at, stop, lambda t, _: (first_when(t + done), second(t), 0)[-1], 0)
        for k in (6, 7, 2, 3, 4, 5, 1, 0):
            src = fin.at[pl.ds(at, size), pl.ds(pl.multiple_of(o * (f ^ k), 16), o), :]
            to = gk_o.at[pl.ds(at, size), :, pl.ds(pl.multiple_of(w * f, 128), w)]
            if k:
                cps.append(remote(src, to, ws.at[n, k], wr.at[n, k], d, f ^ k))
            else:
                c = pltpu.make_async_copy(src, to, wl.at[n])
                c.start()
                cps.append(c)
        at = stop
    for k in range(1, 8):
        c = pltpu.make_async_remote_copy(
            src_ref=dyo.at[:, rows_of(k), :], dst_ref=dst, send_sem=ds_.at[k], recv_sem=dr_.at[k],
            device_id=(d, f ^ k), device_id_type=MESH,
        )
        c.wait()
    pltpu.make_async_copy(dyo.at[:, rows_of(0), :], dst, dl).wait()
    for c in gathers:
        c.finish()
    for c in cps:
        c.wait()

    def sent(t, _):
        @pl.when(outer)
        def _():
            to_inner(t).wait_send()

        @pl.when(jnp.logical_not(outer))
        def _():
            across(t).wait_send()
            to_outer(t).wait_send()

        return 0

    lax.fori_loop(0, taps, sent, 0)


def branches_back(d, y, key, k, pooled, dr, sizes, steps):
    Q, h, W3 = d.shape
    TT, w = y.shape[1:]
    W = W3 // 3
    T = 8 * h
    b16, f32 = jnp.bfloat16, jnp.float32
    V = pltpu.VMEM
    return pl.pallas_call(
        functools.partial(branches_back_kernel, steps),
        out_shape=[jax.ShapeDtypeStruct((Q, h, 8 * w), b16), jax.ShapeDtypeStruct((28, W // 8, 8 * w), b16)],
        in_specs=[VM] * 7,
        out_specs=[ANY] * 2,
        scratch_shapes=[
            V((Q, TT, W3), b16), V((W3, Q * T), b16), V((Q * T, w), b16), V((28, W, w), b16), V((28, W, w), b16),
            V((28, W, w), b16), V((28, W, w), b16), V((Q, T, w), b16),
            V((Q * h, w), f32), V((8, w), f32),
        ]
        + gather_sems() * 3
        + [DMA((4, 8)), DMA((4, 8)), DMA((4,)), DMA((8,)), DMA((8,)), DMA(())]
        + [DMA((28,))] * 6,
        compiler_params=pltpu.CompilerParams(collective_id=10, has_side_effects=True, vmem_limit_bytes=VLIM),
        name="branches_back",
    )(d, y, key, k, pooled, dr, sizes)


class Sum:
    def __init__(self, bufs, d, f):
        self.b1, self.b2, self.s1, self.r1, self.s2, self.r2 = bufs
        self.d, self.f = d, f

    def start(self, rows):
        b1, d, f = self.b1, self.d, self.f
        for n, row in enumerate(rows):
            b1[f, n : n + 1, :] = row
        self.cps = [remote(b1.at[f], b1.at[f], self.s1.at[k], self.r1.at[k], d, f ^ k) for k in (6, 2, 4, 7, 3, 5, 1)]

    def turn(self):
        b1, b2, d, f = self.b1, self.b2, self.d, self.f
        for c in self.cps:
            c.wait()
        tot = b1[0]
        for k in range(1, 8):
            tot = tot + b1[k]
        b2[d] = tot
        self.cps = [remote(b2.at[d], b2.at[d], self.s2.at[k], self.r2.at[k], d ^ k, f) for k in (3, 2, 1)]

    def result(self):
        for c in self.cps:
            c.wait()
        tot = self.b2[0]
        for k in range(1, 4):
            tot = tot + self.b2[k]
        return tot


class Reduce:
    def __init__(self, full, part, near, far, tot, zr, out, quarter, sems, d, f):
        self.full, self.part, self.near, self.fars, self.tot, self.zr, self.out = full, part, near, far, tot, zr, out
        self.quarter, self.d, self.f = quarter, d, f
        self.sems = sems
        self.c0 = f % 2
        self.me = f // 2
        self.sent = []

    def pair(self):
        ps, pr = self.sems[:2]
        self.cps = [
            remote(self.full.at[self.part(2 * g + 1 - self.c0)], self.near.at[g], ps.at[g], pr.at[g], self.d, self.f ^ 1)
            for g in range(4)
        ]

    def far(self):
        ss, rs = self.sems[2:4]
        for c in self.cps:
            c.wait()
        self.cps = []
        for k in (3, 1, 2, 0):
            g = self.me ^ k
            val = self.full[self.part(2 * g + self.c0)].astype(jnp.float32) + self.near[g].astype(jnp.float32)
            self.near[g] = val.astype(self.near.dtype)
            if k:
                self.cps.append(
                    remote(self.near.at[g], self.fars.at[k], ss.at[k], rs.at[k], self.d, self.f ^ (2 * k))
                )

    def tiles(self):
        ss, rs = self.sems[4:6]
        for c in self.cps:
            c.wait()
        val = self.near[self.me].astype(jnp.float32)
        for k in (1, 2, 3):
            val = val + self.fars[k].astype(jnp.float32)
        self.tot[...] = val.astype(self.tot.dtype)
        self.cps = [
            remote(self.tot.at[self.quarter(self.d ^ k)], self.zr.at[self.d], ss.at[k], rs.at[k], self.d ^ k, self.f)
            for k in (3, 2, 1)
        ]
        self.zr[self.d] = self.tot[self.quarter(self.d)]

    def back(self):
        ss, rs = self.sems[6:8]
        for c in self.cps:
            c.wait()
        val = self.zr[0].astype(jnp.float32)
        for k in (1, 2, 3):
            val = val + self.zr[k].astype(jnp.float32)
        mine = self.quarter(self.d)
        self.out[mine] = val.astype(self.out.dtype)
        self.cps = [
            remote(self.out.at[mine], self.out.at[mine], ss.at[k], rs.at[k], self.d ^ k, self.f) for k in (3, 2, 1)
        ]

    def done(self):
        for c in self.cps:
            c.wait()


def reduce_scratch(block, quarter):
    V, b16 = pltpu.VMEM, jnp.bfloat16
    return [V((4,) + block, b16), V((4,) + block, b16), V(block, b16), V((4,) + quarter, b16)] + [DMA((4,))] * 8


def wide(row, n):
    return jnp.concatenate([row] * n, axis=1)


def bottleneck_back_kernel(
    x_ref, ins_ref, st_ref, gr, gd, ge, dy, dpt, y_ref, pm_in, wp, n3, l3, we, n2, l2, h2, wd, ext, n1, l1, wr, key_any,
    gf_o, pm_o, ex_o, di_o, re_o, s3_o, s2_o, s1_o,
    pm, ex, di, re_, dp3, d3, acc, ext2, d1n, key, gf, pick, ksem, hs, hr, gs,
    *sems,
):
    sems = list(sems)

    def take(n):
        got = sems[:n]
        del sems[:n]
        return got

    f, d = greet(range(1, 8), range(1, 4))
    N, C = x_ref.shape
    Q, h = ext2.shape[0], ext2.shape[1] // 2
    e = h // 2
    rows = h // 4
    neck = acc.shape[1]
    nb = neck // 8
    nw = pm.shape[0] // 8
    PW = pm.shape[1] // 4
    W = dpt.shape[1]

    def ds(i, n):
        return pl.ds(pl.multiple_of(n * i, n), n)

    def reducer(full, part, out, quarter):
        near, far, tot, zr = take(4)
        return Reduce(full, part, near, far, tot, zr, out, quarter, take(8), d, f)

    r_pm = reducer(pm, lambda g: (ds(g, nw),), pm_o, lambda g: (slice(None), ds(g, PW)))
    r_ex = reducer(ex, lambda g: (slice(None), ds(g, C // 8)), ex_o, lambda g: (ds(g, neck // 4),))
    r_di = reducer(
        di, lambda g: (slice(None), ds(g, nb)), di_o, lambda g: (slice(None), ds(g, nb // 4))
    )
    r_re = reducer(re_, lambda g: (ds(g, nb),), re_o, lambda g: (ds(g, nb // 4),))
    sum3, sum2, sum1 = (Sum(take(6), d, f) for _ in range(3))

    kcp = pltpu.make_async_copy(key_any.at[:, pl.ds(pl.multiple_of(PAD - e + h * f, 16), 2 * h), :], key, ksem)
    kcp.start()
    count = st_ref[0:1, 0:1]
    for c in range(0, C, 256):
        pm[:, c : c + 256] = tn_dot(dpt[...], y_ref[:, c : c + 256]).astype(jnp.bfloat16)
    pm[:, C:] = pm_in[...]
    r_pm.pair()
    ones, crossed = [], []
    ins = wide(ins_ref[...], 2)
    for c in range(0, C, 256):
        w = slice(c, c + 256)
        v = dy[:, w].astype(jnp.float32) + nn_dot(dpt[...], wp[:, w])
        v = v * l3[:, w].astype(jnp.float32)
        dp3[:, w] = v.astype(jnp.bfloat16)
        v = v * ins
        ones.append(jnp.sum(v, axis=0, keepdims=True))
        crossed.append(jnp.sum(v * n3[:, w].astype(jnp.float32), axis=0, keepdims=True))
    sum3.start([cat_rows(ones), cat_rows(crossed)])
    order = lax.broadcasted_iota(jnp.int32, (N, N), 1)
    m, r, q = order % 4, (order // 4) % rows, order // h
    hit = (r * (N // rows) + q * 4 + m) == lax.broadcasted_iota(jnp.int32, (N, N), 0)
    pick[...] = hit.astype(jnp.float32).astype(jnp.bfloat16)
    sum3.turn()
    r_pm.far()
    tot = sum3.result()
    s3_o[...] = tot
    for c in range(0, C, 256):
        w = slice(c, c + 256)
        v = dp3[:, w].astype(jnp.float32) - tot[0:1, w] / count - n3[:, w].astype(jnp.float32) * (tot[1:2, w] / count)
        d3[:, w] = (ins * v * (ge[:, w] * st_ref[3:4, w])).astype(jnp.bfloat16)
    ones, crossed = [], []
    for c in range(0, neck, 256):
        w = slice(c, c + 256)
        v = nt_dot(d3[...], we[w, :]) * l2[:, w].astype(jnp.float32)
        acc[:, w] = v
        v = v * ins
        ones.append(jnp.sum(v, axis=0, keepdims=True))
        crossed.append(jnp.sum(v * n2[:, w].astype(jnp.float32), axis=0, keepdims=True))
    sum2.start([cat_rows(ones), cat_rows(crossed)])
    for c in range(0, C, 256):
        ex[:, c : c + 256] = tn_dot(h2[...], d3[:, c : c + 256]).astype(jnp.bfloat16)
    sum2.turn()
    r_ex.pair()
    tot = sum2.result()
    s2_o[...] = tot
    for c in range(0, neck, 256):
        w = slice(c, c + 256)
        v = acc[:, w] - tot[0:1, w] / count - n2[:, w].astype(jnp.float32) * (tot[1:2, w] / count)
        v = ins * v * (gd[:, w] * st_ref[2:3, w])
        ext2[:, e : e + h, w] = v.astype(jnp.bfloat16).reshape(Q, h, 256)
    up = remote(ext2.at[:, pl.ds(e, e)], ext2.at[:, pl.ds(e + h, e)], hs.at[0], hr.at[0], d, lax.rem(f + 7, 8))
    down = remote(ext2.at[:, pl.ds(h, e)], ext2.at[:, pl.ds(0, e)], hs.at[1], hr.at[1], d, lax.rem(f + 1, 8))
    kcp.wait()
    r_pm.tiles()
    r_ex.far()
    for i in range(3):
        for j in range(3):
            lo, hi = span(j - 1, Q)
            ok = same_crop(
                key[lo:hi, e : e + h, :], key[lo + j - 1 : hi + j - 1, e * i : e * i + h, :], neck
            )
            v = jnp.where(ok, ext[lo + j - 1 : hi + j - 1, e * i : e * i + h, :], 0).reshape((hi - lo) * h, neck)
            g = ext2[lo:hi, e : e + h, :].reshape((hi - lo) * h, neck)
            di[3 * i + j] = tn_dot(g, v).astype(jnp.bfloat16)
    r_di.pair()
    up.wait()
    down.wait()
    acc[...] = jnp.zeros_like(acc)
    for i in range(3):
        for j in (1, 0, 2):
            lo, hi = span(1 - j, Q)
            ok = same_crop(
                key[lo:hi, e : e + h, :], key[lo + 1 - j : hi + 1 - j, e * (2 - i) : e * (2 - i) + h, :], neck
            )
            v = jnp.where(ok, ext2[lo + 1 - j : hi + 1 - j, e * (2 - i) : e * (2 - i) + h, :], 0)
            v = v.reshape((hi - lo) * h, neck)
            for c in range(0, neck, 256):
                acc[lo * h : hi * h, c : c + 256] += nn_dot(v, wd[3 * i + j, :, c : c + 256])
    ones, crossed = [], []
    for c in range(0, neck, 256):
        w = slice(c, c + 256)
        v = acc[:, w] * l1[:, w].astype(jnp.float32)
        acc[:, w] = v
        v = v * ins
        ones.append(jnp.sum(v, axis=0, keepdims=True))
        crossed.append(jnp.sum(v * n1[:, w].astype(jnp.float32), axis=0, keepdims=True))
    sum1.start([cat_rows(ones), cat_rows(crossed)])
    r_di.far()
    sum1.turn()
    r_pm.back()
    r_ex.tiles()
    tot = sum1.result()
    s1_o[...] = tot
    for c in range(0, neck, 256):
        w = slice(c, c + 256)
        v = acc[:, w] - tot[0:1, w] / count - n1[:, w].astype(jnp.float32) * (tot[1:2, w] / count)
        v = (ins * v * (gr[:, w] * st_ref[1:2, w])).astype(jnp.bfloat16)
        d1n[:, w] = nn_dot(pick[...], v).astype(jnp.bfloat16)
    for c in range(0, C, 256):
        re_[:, c : c + 256] = tn_dot(d1n[...], x_ref[:, c : c + 256]).astype(jnp.bfloat16)
    r_re.pair()
    out = []
    for n, c in enumerate(range(0, C, 256)):
        w = slice(c, c + 256)
        if n >= 2:
            out[n - 2].wait()
        gf[n % 2] = nn_dot(pick[...], dp3[:, w]) + nn_dot(d1n[...], wr[:, w])
        cp = pltpu.make_async_copy(gf.at[n % 2], gf_o.at[:, pl.ds(c, 256)], gs.at[n % 2])
        cp.start()
        out.append(cp)
        if n == 1:
            r_re.far()
        if n == 3:
            r_ex.back()
        if n == 5:
            r_di.tiles()
    r_re.tiles()
    r_di.back()
    r_re.back()
    out[-2].wait()
    out[-1].wait()
    for r in (r_pm, r_ex, r_di, r_re):
        r.done()


def bottleneck_back(*args):
    x, st, dpt, pm_in, h2 = args[0], args[2], args[7], args[9], args[16]
    N, C = x.shape
    Q, h2_, neck = args[18].shape
    h = h2_ // 2
    W = dpt.shape[1]
    PM = C + pm_in.shape[1]
    b16, f32 = jnp.bfloat16, jnp.float32
    S, V = jax.ShapeDtypeStruct, pltpu.VMEM
    blocks = [
        ((W // 8, PM), (W // 8, PM // 4)),
        ((neck, C // 8), (neck // 4, C // 8)),
        ((9, neck // 8, neck), (9, neck // 32, neck)),
        ((neck // 8, C), (neck // 32, C)),
    ]
    scratch = [
        V((W, PM), b16), V((neck, C), b16), V((9, neck, neck), b16), V((neck, C), b16), V((N, C), b16), V((N, C), b16),
        V((N, neck), f32), V((Q, 2 * h, neck), b16), V((N, neck), b16), V((Q, 2 * h, 128), b16), V((2, N, 256), f32),
        V((N, N), b16), DMA(()), DMA((2,)), DMA((2,)), DMA((2,)),
    ]
    for block, quarter in blocks:
        scratch += reduce_scratch(block, quarter)
    scratch += sum_sems(2, C) + sum_sems(2, neck) + sum_sems(2, neck)
    return pl.pallas_call(
        bottleneck_back_kernel,
        out_shape=[S((N, C), f32)] + [S(b, b16) for b, _ in blocks] + [S((2, C), f32), S((2, neck), f32), S((2, neck), f32)],
        in_specs=[VM] * 22 + [ANY],
        out_specs=[ANY] + [VM] * 7,
        scratch_shapes=scratch,
        compiler_params=pltpu.CompilerParams(collective_id=12, has_side_effects=True, vmem_limit_bytes=VLIM),
        name="bottleneck_back",
    )(*args)


def spaced_taps(src, key, kernels, acc, base, h, steps, sign, first_lane, dot, b):
    Q = key.shape[0]
    s = sign * steps[b]
    W = kernels.shape[1] if sign < 0 else src.shape[2]
    lanes = slice(first_lane, first_lane + W)
    for n, j in enumerate((0, -1, 1)):
        lo, hi = span(s * j, Q)
        here = key[lo:hi, pl.ds(base, h), :]
        got = None
        for i in (-1, 0, 1):
            at = pl.multiple_of(base + 16 * s * i, 16)
            ok = same_crop(here, key[lo + s * j : hi + s * j, pl.ds(at, h), :], W)
            v = jnp.where(ok, src[lo + s * j : hi + s * j, pl.ds(at, h), lanes], 0).reshape((hi - lo) * h, W)
            r = dot(v, kernels[9 * b + 3 * (i + 1) + j + 1])
            got = r if got is None else got + r
        if n == 0 and sign > 0:
            acc[...] = got
        else:
            acc[lo * h : hi * h] += got


def head_kernel(
    steps, yo, key, kern, y, wp, wm, wc, ins_ref, kb, lab, st_ref, gb, bb, gm, bm,
    lo_o, dp_o, dr_o, pm_o, pooled_o, dpool_o, size_o, sb_o, sm_o,
    acc, near, mine, far, ab, nb, lb, joined, nm, lm, merged, pn, ps, pr, ss, rs,
    *sems,
):
    sems = list(sems)
    f, d = greet(range(1, 8), range(1, 4))
    sum_b, sum_m, back_m, back_b = (Sum(sems[6 * n : 6 * n + 6], d, f) for n in range(4))
    Q, h = pn.shape[1], pn.shape[2]
    N = Q * h
    w = yo.shape[2]
    W = wp.shape[0]
    T = 8 * h
    c0 = f % 2
    me = f // 2
    f32, b16 = jnp.float32, jnp.bfloat16

    def step(n, _):
        k = 3 - n
        g = me ^ k
        for turn in range(2):
            dest = 2 * g + (1 - c0 if turn == 0 else c0)
            base = pl.multiple_of(PAD + h * dest, 16)
            if turn == 1:
                pltpu.make_async_remote_copy(
                    src_ref=pn.at[k], dst_ref=near.at[k], send_sem=ps.at[k], recv_sem=pr.at[k],
                    device_id=(d, f ^ 1), device_id_type=MESH,
                ).wait_recv()
            for b in range(3):
                lanes = slice(b * W, (b + 1) * W)
                spaced_taps(yo, key, kern, acc, base, h, steps, 1, 0, nt_dot, b)
                if turn == 0:
                    pn[k, :, :, lanes] = acc[...].astype(b16).reshape(Q, h, W)
                else:
                    val = acc[...] + near[k, :, :, lanes].astype(f32).reshape(N, W)
                    mine[k, :, :, lanes] = val.astype(b16).reshape(Q, h, W)
            if turn == 0:
                remote(pn.at[k], near.at[k], ps.at[k], pr.at[k], d, f ^ 1)
            else:

                @pl.when(k > 0)
                def _():
                    remote(mine.at[k], far.at[k], ss.at[k], rs.at[k], d, f ^ (2 * k))

        return 0

    lax.fori_loop(0, 4, step, 0)
    ab[:, :W] = nt_dot(y[...], wp[...])
    crop = (lax.broadcasted_iota(jnp.int32, (T, 128), 1) + 1).astype(f32)

    def crops(q, carry):
        total, size = carry
        one = (key[q, PAD : PAD + T, :].astype(f32) == crop).astype(f32).astype(b16)
        return total + tn_dot(one, yo[q, PAD : PAD + T, :]), size + tn_dot(one, jnp.ones((T, 128), b16))

    total, size = lax.fori_loop(0, Q, crops, (jnp.zeros((128, w), f32), jnp.zeros((128, 128), f32)))
    size = jnp.where(size > 0, size, 1.0)[:8]
    size_o[...] = size
    pooled = (total[:8] / size[:, :1]).astype(b16)
    pooled_o[...] = pooled
    part = nt_dot(pooled, kern[27])
    part = cat_rows([part[c : c + 1] for c in range(CROPS_TILE)])
    ins = wide(ins_ref[...], 2)
    for k in (3, 1, 2):
        pltpu.make_async_remote_copy(
            src_ref=mine.at[k], dst_ref=far.at[k], send_sem=ss.at[k], recv_sem=rs.at[k],
            device_id=(d, f ^ (2 * k)), device_id_type=MESH,
        ).wait()
    ones, squares = [], []
    for b in range(4):
        lanes = slice(b * W, (b + 1) * W)
        if b:
            src = slice((b - 1) * W, b * W)
            v = mine[0, :, :, src].astype(f32)
            for k in (1, 2, 3):
                v = v + far[k, :, :, src].astype(f32)
            ab[:, lanes] = v.reshape(N, W)
        s, t = column_sums(ab[:, lanes], ins_ref[...])
        ones.append(s)
        squares.append(t)
    sum_b.start([cat_rows(ones), cat_rows(squares), part])
    for k in range(4):
        pltpu.make_async_remote_copy(
            src_ref=pn.at[k], dst_ref=near.at[k], send_sem=ps.at[k], recv_sem=pr.at[k],
            device_id=(d, f ^ 1), device_id_type=MESH,
        ).wait_send()
    sum_b.turn()
    pool_act = sum_b.b2[d, 2:3, :]
    pool, pool_lean = bend(pool_act)
    pool = pool.astype(b16).astype(f32)
    here = wide(kb[...].astype(f32), W // 128)
    v = jnp.zeros((N, W), f32)
    for c in range(CROPS_TILE):
        v = jnp.where(here == c + 1.0, pool[:, c * W : (c + 1) * W], v)
    joined[:, 4 * W :] = v.astype(b16)
    tot = sum_b.result()
    count = st_ref[0:1, 0:1]
    mean = tot[0:1] / count
    inv_b = lax.rsqrt(tot[1:2] / count - mean * mean + eps)
    for b in range(4):
        lanes = slice(b * W, (b + 1) * W)
        n = (ab[:, lanes] - mean[:, lanes]) * inv_b[:, lanes]
        act, lean = bend(n * gb[:, lanes] + bb[:, lanes])
        joined[:, lanes] = act.astype(b16)
        nb[:, lanes] = n.astype(b16)
        lb[:, lanes] = lean.astype(b16)
    am = nt_dot(joined[...], wm[...])
    s, t = column_sums(am, ins_ref[...])
    sum_m.start([s, t])
    sum_m.turn()
    tot = sum_m.result()
    mean = tot[0:1] / count
    inv_m = lax.rsqrt(tot[1:2] / count - mean * mean + eps)
    n = (am - mean) * inv_m
    act, lean = bend(n * gm[...] + bm[...])
    merged[...] = act.astype(b16)
    nm[...] = n
    lm[...] = lean
    logits = nn_dot(merged[...], wc[...])
    lane = lax.broadcasted_iota(jnp.int32, (N, 128), 1)
    valid = lane < CLASSES
    top = jnp.max(jnp.where(valid, logits, -jnp.inf), axis=1, keepdims=True)
    ex = jnp.where(valid, jnp.exp(logits - top), 0.0)
    prob = ex / jnp.sum(ex, axis=1, keepdims=True)
    target = (lab[...] == lane.astype(f32)).astype(f32)
    dl = (ins_ref[...] * (prob - target) / count).astype(b16)
    e = nt_dot(dl, wc[...]) * lm[...]
    m = e * ins
    back_m.start([jnp.sum(m, axis=0, keepdims=True), jnp.sum(m * nm[...], axis=0, keepdims=True)])
    order = lax.broadcasted_iota(jnp.int32, (N, N), 1)
    rows = h // 4
    mm, r, q = order % 4, (order // 4) % rows, order // h
    hit = (r * (N // rows) + q * 4 + mm) == lax.broadcasted_iota(jnp.int32, (N, N), 0)
    lo_o[...] = nn_dot(hit.astype(f32).astype(b16), logits.astype(b16)).astype(b16)
    back_m.turn()
    J = joined.shape[1]
    pm_o[:, J : J + 128] = tn_dot(merged[...], dl).astype(b16)
    pm_o[:, J + 128 :] = jnp.zeros((W, pm_o.shape[1] - J - 128), b16)
    tot = back_m.result()
    sm_o[...] = tot
    dm = (ins * gm[...] * inv_m * (e - tot[0:1] / count - nm[...] * (tot[1:2] / count))).astype(b16)
    ones, crossed = [], []
    for b in range(4):
        lanes = slice(b * W, (b + 1) * W)
        v = nn_dot(dm, wm[:, lanes]) * lb[:, lanes].astype(f32)
        ab[:, lanes] = v
        v = v * ins
        ones.append(jnp.sum(v, axis=0, keepdims=True))
        crossed.append(jnp.sum(v * nb[:, lanes].astype(f32), axis=0, keepdims=True))
    v = nn_dot(dm, wm[:, 4 * W :])
    part = cat_rows(
        [jnp.sum(jnp.where(here == c + 1.0, v, 0.0), axis=0, keepdims=True) for c in range(CROPS_TILE)]
    )
    back_b.start([cat_rows(ones), cat_rows(crossed), part])
    pm_o[:, :J] = tn_dot(dm, joined[...]).astype(b16)
    back_b.turn()
    v = (back_b.b2[d, 2:3, :] * pool_lean).astype(b16)
    dpool_o[...] = jnp.zeros_like(dpool_o)
    for c in range(CROPS_TILE):
        dpool_o[c : c + 1, :] = v[:, c * W : (c + 1) * W]
    tot = back_b.result()
    sb_o[...] = tot[:2]
    for b in range(4):
        lanes = slice(b * W, (b + 1) * W)
        v = ab[:, lanes] - tot[0:1, lanes] / count - nb[:, lanes].astype(f32) * (tot[1:2, lanes] / count)
        v = (ins * v * (gb[:, lanes] * inv_b[:, lanes])).astype(b16)
        if b:
            dr_o[:, :, (b - 1) * W : b * W] = v.reshape(Q, h, W)
        else:
            dp_o[...] = v


def head(steps, width, *args):
    yo, key, kern, y, wp, wm = args[:6]
    N, C = y.shape
    Q = yo.shape[0]
    h = N // Q
    W = wp.shape[0]
    J = wm.shape[1]
    b16, f32 = jnp.bfloat16, jnp.float32
    S, V = jax.ShapeDtypeStruct, pltpu.VMEM
    return pl.pallas_call(
        functools.partial(head_kernel, steps),
        out_shape=[
            S((N, 128), b16), S((N, W), b16), S((Q, h, 3 * W), b16), S((W, width), b16), S((8, C // 8), b16),
            S((8, W), b16), S((8, 128), f32), S((2, 4 * W), f32), S((2, W), f32),
        ],
        in_specs=[VM] * 15,
        out_specs=[VM] * 9,
        scratch_shapes=[V((N, W), f32)]
        + [V((4, Q, h, 3 * W), b16)] * 3
        + [
            V((N, 4 * W), f32), V((N, 4 * W), b16), V((N, 4 * W), b16), V((N, J), b16), V((N, W), f32), V((N, W), f32),
            V((N, W), b16), V((4, Q, h, 3 * W), b16), DMA((4,)), DMA((4,)), DMA((4,)), DMA((4,)),
        ]
        + sum_sems(3, 4 * W) + sum_sems(2, W) + sum_sems(2, W) + sum_sems(3, 4 * W),
        compiler_params=pltpu.CompilerParams(collective_id=5, has_side_effects=True, vmem_limit_bytes=VLIM),
        name="head",
    )(*args)


def norm_coeffs(totals, squares, count):
    average = totals / count
    return average, lax.rsqrt(squares / count - average * average + eps)


def fast_body(
    features, crop_ids, labels, w_reduce, gain_reduce, bias_reduce, w_dilated, gain_dilated, bias_dilated,
    w_expand, gain_expand, bias_expand, w_point, gain_point, bias_point, w_rate, gain_rate, bias_rate,
    w_rate_double, gain_rate_double, bias_rate_double, w_rate_triple, gain_rate_triple, bias_rate_triple,
    w_pool, w_merge, gain_merge, bias_merge, w_classes,
):
    rows, cols, C = features.shape
    Q = cols // 4
    h = rows * 4
    N = rows * cols
    nf = lax.axis_size("fsdp")
    W = gain_point.shape[0]
    steps = (RATE // 4, 2 * RATE // 4, 3 * RATE // 4)
    place = lax.axis_index("fsdp")

    def perm(a):
        a = a.reshape((rows, Q, 4) + a.shape[2:])
        return jnp.swapaxes(a, 0, 1).reshape((N,) + a.shape[3:])

    def unperm(a):
        a = a.reshape((Q, rows, 4) + a.shape[1:])
        return jnp.swapaxes(a, 0, 1).reshape((rows, cols) + a.shape[3:])

    local_crop = perm(crop_ids) - lax.axis_index("dp") * CROPS_TILE
    in_crop = perm(crop_ids) >= 0
    inside = in_crop.astype(jnp.float32)[:, None]
    key_loc = jnp.where(in_crop, local_crop + 1, 0)
    kb = jnp.broadcast_to(key_loc.astype(jnp.bfloat16)[:, None], (N, 128))
    key_row = jnp.pad(key_loc.astype(jnp.float32).reshape(Q, h), ((0, 0), (0, 128 - h)))
    ins = jnp.broadcast_to(inside, (N, 128))
    rates = [jnp.swapaxes(w.reshape(9, C, -1), 1, 2) for w in (w_rate, w_rate_double, w_rate_triple)]
    vecs = [v[None, :] for v in (gain_reduce, bias_reduce, gain_dilated, bias_dilated, gain_expand, bias_expand)]
    (
        y_own, y, n_three, l_three, n_one, l_one, n_two, l_two, ext, h_two, key, kernel,
        wr, wd, full_expand, wp, wm, wc, count,
    ) = bottleneck(
        features.reshape(N, C), key_row, ins, vecs,
        [
            w_reduce.T, jnp.swapaxes(w_dilated.reshape(9, w_dilated.shape[2], -1), 1, 2), w_expand, w_point.T, w_merge.T,
            jnp.pad(w_classes, ((0, 0), (0, 128 - CLASSES))),
        ],
        rates + [w_pool.T[None]],
    )
    neck = gain_reduce.shape[0]
    stats = count
    count = count[0, 0]
    y = y.reshape(N, C)
    g_br = jnp.concatenate([gain_point, gain_rate, gain_rate_double, gain_rate_triple])[None]
    b_br = jnp.concatenate([bias_point, bias_rate, bias_rate_double, bias_rate_triple])[None]
    lab = jnp.broadcast_to(perm(labels).astype(jnp.float32)[:, None], (N, 128))
    J = wm.shape[1]
    width = J + 128 + -(C + J + 128) % 512
    logits, d_point, d_rates, rest, pooled, d_pool, sizes, st_br, st_m = head(
        steps, width, y_own, key, kernel, y, wp, wm, wc, ins, kb, lab, stats, g_br, b_br,
        gain_merge[None], bias_merge[None],
    )
    class_logits = logits[:, :CLASSES].reshape(rows, cols, CLASSES)
    gb_br, gg_br = st_br[0], st_br[1]
    gb_merge, gg_merge = st_m[0], st_m[1]
    d_y, grad_k = branches_back(d_rates, y_own, key, kernel, pooled, d_pool, sizes, steps)
    grad_k = grad_k.astype(jnp.float32)
    grad_features, pm, ex, di, re_, st3, st2, st1 = bottleneck_back(
        features.reshape(N, C), ins, stats, vecs[0], vecs[2], vecs[4], d_y.reshape(N, C), d_point, y, rest, wp,
        n_three, l_three, full_expand, n_two, l_two, h_two, wd, ext, n_one, l_one, wr, key,
    )
    pm = pm.astype(jnp.float32)
    grad_point, grad_merge, grad_classes = pm[:, :C].T, pm[:, C : C + 5 * W].T, pm[:, C + 5 * W : C + 5 * W + CLASSES]
    grad_features = grad_features.reshape(rows, cols, C)
    grad_reduce = re_.astype(jnp.float32).T
    grad_dilated = jnp.swapaxes(di.astype(jnp.float32), 1, 2).reshape(3, 3, neck, -1)
    grad_expand = ex.astype(jnp.float32)
    gg_expand, gb_expand, gg_dilated, gb_dilated, gg_reduce, gb_reduce = st3[1], st3[0], st2[1], st2[0], st1[1], st1[0]
    grad_pool = grad_k[27].T
    grad_k = jnp.swapaxes(grad_k[:27].reshape(3, 3, 3, -1, C), 3, 4)
    return (
        class_logits,
        grad_features,
        grad_reduce, gg_reduce, gb_reduce,
        grad_dilated, gg_dilated, gb_dilated,
        grad_expand, gg_expand, gb_expand,
        grad_point, gg_br[:W], gb_br[:W],
        grad_k[0], gg_br[W : 2 * W], gb_br[W : 2 * W],
        grad_k[1], gg_br[2 * W : 3 * W], gb_br[2 * W : 3 * W],
        grad_k[2], gg_br[3 * W :], gb_br[3 * W :],
        grad_pool,
        grad_merge, gg_merge, gb_merge,
        grad_classes,
    )


def passed_along(value, axis, by):
    count = lax.axis_size(axis)
    pairs = [(i, i + by) for i in range(count) if 0 <= i + by < count]
    return lax.ppermute(value, axis, pairs)


def padded(cells, sides, width):
    for axis, dim in sides:
        count = lax.axis_size(axis)
        ends = count - 1
        head = lax.slice_in_dim(cells, 0, width, axis=dim)
        tail = lax.slice_in_dim(cells, cells.shape[dim] - width, cells.shape[dim], axis=dim)
        cells = jnp.concatenate(
            [
                lax.ppermute(tail, axis, [(i, (i + 1) % count) for i in range(ends)]),
                cells,
                lax.ppermute(head, axis, [((i + 1) % count, i) for i in range(ends)]),
            ],
            axis=dim,
        )
    return cells


def flat_dot(first_op, second_op):
    return jnp.dot(first_op, second_op, preferred_element_type=jnp.float32)


def inner_dot(first_op, second_op):
    return lax.dot_general(
        first_op, second_op, (((0,), (0,)), ((), ())), preferred_element_type=jnp.float32
    )


def outer_dot(first_op, second_op):
    return lax.dot_general(
        first_op, second_op, (((1,), (1,)), ((), ())), preferred_element_type=jnp.float32
    )


def slope(values):
    gate_value = jax.nn.sigmoid(values)
    return gate_value * (1.0 + values * (1.0 - gate_value))


def widen_rows(values, extent, mover):
    row_count = values.shape[0]
    neighbours = -(-extent // row_count)
    above = [mover(values, distance) for distance in range(neighbours, 0, -1)]
    below = [mover(values, -distance) for distance in range(1, neighbours + 1)]
    stacked = jnp.concatenate(above + [values] + below, axis=0)
    start_row = neighbours * row_count - extent
    return stacked[start_row : start_row + row_count + 2 * extent]


def rim_slice(widened, spacing, margin, height):
    return widened[margin - spacing : margin + height + spacing]


def offset_table(broad_key_rows, crop_random_keys, spacing, margin):
    height, breadth = crop_random_keys.shape
    first_row = margin - spacing
    extended = jnp.pad(
        broad_key_rows[first_row : first_row + height + 2 * spacing], ((0, 0), (spacing, spacing))
    )
    tables = []
    for row_tap in range(3):
        for col_tap in range(3):
            nearby = extended[
                row_tap * spacing : row_tap * spacing + height,
                col_tap * spacing : col_tap * spacing + breadth,
            ]
            tables.append(
                ((nearby == crop_random_keys) & (crop_random_keys > 0))
                .astype(jnp.float32)
                .reshape(height * breadth, 1)
            )
    return tables


def spread_offsets(widened, kernel, tables, spacing, height, breadth):
    channels = widened.shape[2]
    extended = jnp.pad(widened, ((0, 0), (spacing, spacing), (0, 0)))
    summed = jnp.zeros((height * breadth, kernel.shape[3]), jnp.float32)
    for row_tap in range(3):
        for col_tap in range(3):
            nearby = extended[
                row_tap * spacing : row_tap * spacing + height,
                col_tap * spacing : col_tap * spacing + breadth,
            ]
            summed = summed + tables[3 * row_tap + col_tap] * flat_dot(
                nearby.reshape(height * breadth, channels), kernel[row_tap, col_tap]
            )
    return summed


def collect_taps(widened, kernel, tables, spacing, height, breadth):
    channels = widened.shape[2]
    extended = jnp.pad(widened, ((0, 0), (spacing, spacing), (0, 0)))
    summed = jnp.zeros((height * breadth, kernel.shape[2]), jnp.float32)
    for row_tap in range(3):
        for col_tap in range(3):
            back_row = 2 - row_tap
            back_col = 2 - col_tap
            nearby = extended[
                back_row * spacing : back_row * spacing + height,
                back_col * spacing : back_col * spacing + breadth,
            ]
            summed = summed + tables[3 * back_row + back_col] * outer_dot(
                nearby.reshape(height * breadth, channels), kernel[row_tap, col_tap]
            )
    return summed


def kernel_offsets(widened, grads_low, tables, spacing, height, breadth):
    channels = widened.shape[2]
    extended = jnp.pad(widened, ((0, 0), (spacing, spacing), (0, 0)))
    pieces = []
    for row_tap in range(3):
        for col_tap in range(3):
            nearby = extended[
                row_tap * spacing : row_tap * spacing + height,
                col_tap * spacing : col_tap * spacing + breadth,
            ]
            masked = (tables[3 * row_tap + col_tap] * grads_low).astype(jnp.bfloat16)
            pieces.append(inner_dot(nearby.reshape(height * breadth, channels), masked))
    return pieces


def statistics(partial_value):
    return lax.psum(partial_value, ("dp", "fsdp"))


def norm_apply(values, totals, squares, pixel_count, factor, offset):
    average = totals / pixel_count
    inverse = lax.rsqrt(squares / pixel_count - average * average + eps)
    normed = (values - average) * inverse
    return (normed * factor + offset, normed, inverse)


def norm_forward(values, inside, pixel_count, factor, offset):
    totals, squares = statistics(
        (jnp.sum(values * inside, axis=0), jnp.sum(values * values * inside, axis=0))
    )
    return norm_apply(values, totals, squares, pixel_count, factor, offset)


def norm_backward(upstream, normed, inverse, factor, inside, pixel_count):
    totals, crossed = lax.psum(
        (jnp.sum(upstream * inside, axis=0), jnp.sum(upstream * normed * inside, axis=0)),
        ("dp", "fsdp"),
    )
    passed = (
        inside
        * factor
        * inverse
        * (upstream - totals / pixel_count - normed * crossed / pixel_count)
    )
    return (passed, crossed, totals)


def body(
    features,
    crop_ids,
    labels,
    w_reduce,
    gain_reduce,
    bias_reduce,
    w_dilated,
    gain_dilated,
    bias_dilated,
    w_expand,
    gain_expand,
    bias_expand,
    w_point,
    gain_point,
    bias_point,
    w_rate,
    gain_rate,
    bias_rate,
    w_rate_double,
    gain_rate_double,
    bias_rate_double,
    w_rate_triple,
    gain_rate_triple,
    bias_rate_triple,
    w_pool,
    w_merge,
    gain_merge,
    bias_merge,
    w_classes,
):
    local_rows, local_columns, channels = features.shape
    pixel_values = local_rows * local_columns
    inputs_flat = features.reshape(pixel_values, channels)
    crop_random_keys = crop_ids + 1
    outer_extent = 3 * RATE
    spacings = (RATE, 2 * RATE, 3 * RATE)
    broad_key_rows = widen_rows(
        crop_random_keys,
        outer_extent,
        lambda piece, distance: passed_along(piece, "fsdp", distance),
    )
    inside = (crop_random_keys > 0).astype(jnp.float32).reshape(pixel_values, 1)
    inner_neck = offset_table(broad_key_rows, crop_random_keys, DILATION_SPAN, outer_extent)
    near_rates = [
        offset_table(broad_key_rows, crop_random_keys, spacing, outer_extent)
        for spacing in spacings
    ]
    (
        full_reduce,
        complete_dilated,
        full_expand,
        full_point,
        full_rate,
        full_double,
        full_triple,
        full_pool,
        full_merge,
        full_classes,
    ) = (
        lax.all_gather(w_reduce, "fsdp", axis=1, tiled=True),
        lax.all_gather(w_dilated, "fsdp", axis=3, tiled=True),
        lax.all_gather(w_expand, "fsdp", axis=1, tiled=True),
        lax.all_gather(w_point, "fsdp", axis=1, tiled=True),
        lax.all_gather(w_rate, "fsdp", axis=3, tiled=True),
        lax.all_gather(w_rate_double, "fsdp", axis=3, tiled=True),
        lax.all_gather(w_rate_triple, "fsdp", axis=3, tiled=True),
        lax.all_gather(w_pool, "fsdp", axis=1, tiled=True),
        lax.all_gather(w_merge, "fsdp", axis=1, tiled=True),
        lax.all_gather(w_classes, "fsdp", axis=0, tiled=True),
    )
    rate_kernels = (full_rate, full_double, full_triple)
    rate_gains = (gain_rate, gain_rate_double, gain_rate_triple)
    rate_biases = (bias_rate, bias_rate_double, bias_rate_triple)
    act_one = flat_dot(inputs_flat, full_reduce)
    totals, squares, pixel_count = statistics(
        (
            jnp.sum(act_one * inside, axis=0),
            jnp.sum(act_one * act_one * inside, axis=0),
            jnp.sum(inside),
        )
    )
    pre_one, normed_one, inverse_one = norm_apply(
        act_one, totals, squares, pixel_count, gain_reduce, bias_reduce
    )
    first_hidden = jax.nn.silu(pre_one).astype(jnp.bfloat16)
    first_broad = padded(
        first_hidden.reshape(local_rows, local_columns, -1), (("fsdp", 0),), DILATION_SPAN
    )
    second_activation = spread_offsets(
        first_broad, complete_dilated, inner_neck, DILATION_SPAN, local_rows, local_columns
    )
    pre_two, normed_two, inverse_two = norm_forward(
        second_activation, inside, pixel_count, gain_dilated, bias_dilated
    )
    hidden_two = jax.nn.silu(pre_two).astype(jnp.bfloat16)
    act_three = flat_dot(hidden_two, full_expand)
    pre_three, normed_three, inverse_three = norm_forward(
        act_three, inside, pixel_count, gain_expand, bias_expand
    )
    pre_three = pre_three + inputs_flat
    block_out = jax.nn.silu(pre_three).astype(jnp.bfloat16)
    wide_block = widen_rows(
        block_out.reshape(local_rows, local_columns, channels),
        outer_extent,
        lambda piece, distance: passed_along(piece, "fsdp", distance),
    )
    point_act = flat_dot(block_out, full_point)
    pre_point, normed_point, inverse_point = norm_forward(
        point_act, inside, pixel_count, gain_point, bias_point
    )
    branch_point = jax.nn.silu(pre_point).astype(jnp.bfloat16)
    rate_states = []
    rate_branches = []
    for kernel, factor, offset, spacing, tables in zip(
        rate_kernels, rate_gains, rate_biases, spacings, near_rates
    ):
        rate_act = spread_offsets(
            rim_slice(wide_block, spacing, outer_extent, local_rows),
            kernel,
            tables,
            spacing,
            local_rows,
            local_columns,
        )
        pre_rate, normed_rate, inverse_rate = norm_forward(
            rate_act, inside, pixel_count, factor, offset
        )
        rate_states.append((pre_rate, normed_rate, inverse_rate))
        rate_branches.append(jax.nn.silu(pre_rate).astype(jnp.bfloat16))
    crop_flat = crop_ids.reshape(pixel_values)
    crop_total = CROPS_TILE
    first_crop = lax.axis_index("dp") * crop_total
    owner_group = lax.axis_size("fsdp")
    owner_place = lax.axis_index("fsdp")
    local_crop = crop_flat - first_crop
    member = local_crop[:, None] == jnp.arange(crop_total)[None, :]
    member_low = member.astype(jnp.bfloat16)
    crop_sums = inner_dot(member_low, block_out)
    crop_sizes = jnp.sum(member.astype(jnp.float32), axis=0)
    crop_sums, crop_sizes = lax.psum((crop_sums, crop_sizes), "fsdp")
    pooled = (crop_sums / crop_sizes[:, None]).astype(jnp.bfloat16)
    pool_act = flat_dot(pooled, full_pool)
    pool_low = jax.nn.silu(pool_act).astype(jnp.bfloat16)
    branch_pool = flat_dot(member_low, pool_low).astype(jnp.bfloat16)
    joined = jnp.concatenate([branch_point] + rate_branches + [branch_pool], axis=1)
    merge_act = flat_dot(joined, full_merge)
    pre_merge, normed_merge, inverse_merge = norm_forward(
        merge_act, inside, pixel_count, gain_merge, bias_merge
    )
    merged = jax.nn.silu(pre_merge).astype(jnp.bfloat16)
    logits_full = flat_dot(merged, full_classes)
    class_logits = logits_full.astype(jnp.bfloat16).reshape(local_rows, local_columns, -1)
    (
        full_reduce,
        complete_dilated,
        full_expand,
        full_point,
        full_rate,
        full_double,
        full_triple,
        full_pool,
        full_merge,
        full_classes,
    ) = (
        lax.all_gather(w_reduce, "fsdp", axis=1, tiled=True),
        lax.all_gather(w_dilated, "fsdp", axis=3, tiled=True),
        lax.all_gather(w_expand, "fsdp", axis=1, tiled=True),
        lax.all_gather(w_point, "fsdp", axis=1, tiled=True),
        lax.all_gather(w_rate, "fsdp", axis=3, tiled=True),
        lax.all_gather(w_rate_double, "fsdp", axis=3, tiled=True),
        lax.all_gather(w_rate_triple, "fsdp", axis=3, tiled=True),
        lax.all_gather(w_pool, "fsdp", axis=1, tiled=True),
        lax.all_gather(w_merge, "fsdp", axis=1, tiled=True),
        lax.all_gather(w_classes, "fsdp", axis=0, tiled=True),
    )
    rate_kernels = (full_rate, full_double, full_triple)
    highest = jnp.max(logits_full, axis=1, keepdims=True)
    shifted = jnp.exp(logits_full - highest)
    probability = shifted / jnp.sum(shifted, axis=1, keepdims=True)
    targets = (labels.reshape(pixel_values, 1) == jnp.arange(CLASSES)[None, :]).astype(jnp.float32)
    grad_logits = (inside * (probability - targets) / pixel_count).astype(jnp.bfloat16)
    grad_classes = inner_dot(merged, grad_logits)
    grad_merged = outer_dot(grad_logits, full_classes)
    passed, grad_gain_merge, grad_bias_merge = norm_backward(
        grad_merged * slope(pre_merge), normed_merge, inverse_merge, gain_merge, inside, pixel_count
    )
    grad_merge_act = passed.astype(jnp.bfloat16)
    grad_merge = inner_dot(joined, grad_merge_act)
    grad_joined = outer_dot(grad_merge_act, full_merge)
    branch_width = full_merge.shape[1]
    passed, grad_gain_point, grad_bias_point = norm_backward(
        grad_joined[:, :branch_width] * slope(pre_point),
        normed_point,
        inverse_point,
        gain_point,
        inside,
        pixel_count,
    )
    grad_point_act = passed.astype(jnp.bfloat16)
    grad_point = inner_dot(block_out, grad_point_act)
    grad_block = outer_dot(grad_point_act, full_point)
    rate_grads = []
    rate_weight_grads = []
    rate_gain_grads = []
    rate_bias_grads = []
    for branch in range(3):
        column = (1 + branch) * branch_width
        pre_rate, normed_rate, inverse_rate = rate_states[branch]
        passed, gain_grad, bias_grad = norm_backward(
            grad_joined[:, column : column + branch_width] * slope(pre_rate),
            normed_rate,
            inverse_rate,
            rate_gains[branch],
            inside,
            pixel_count,
        )
        grad_rate_act = passed.astype(jnp.bfloat16)
        pieces = kernel_offsets(
            rim_slice(wide_block, spacings[branch], outer_extent, local_rows),
            grad_rate_act,
            near_rates[branch],
            spacings[branch],
            local_rows,
            local_columns,
        )
        rate_weight_grads.append(jnp.stack(pieces).reshape(3, 3, channels, branch_width))
        rate_grads.append(grad_rate_act)
        rate_gain_grads.append(gain_grad)
        rate_bias_grads.append(bias_grad)
    rate_grads_low = jnp.concatenate(rate_grads, axis=1).reshape(local_rows, local_columns, -1)
    wide_grad_rate = widen_rows(
        rate_grads_low, outer_extent, lambda piece, distance: passed_along(piece, "fsdp", distance)
    )
    for branch in range(3):
        grad_slab = wide_grad_rate[:, :, branch * branch_width : (branch + 1) * branch_width]
        grad_block = grad_block + collect_taps(
            rim_slice(grad_slab, spacings[branch], outer_extent, local_rows),
            rate_kernels[branch],
            near_rates[branch],
            spacings[branch],
            local_rows,
            local_columns,
        )
    crop_grad = lax.dot_general(
        member.astype(jnp.float32),
        grad_joined[:, 4 * branch_width :],
        (((0,), (0,)), ((), ())),
        precision=lax.Precision.HIGHEST,
        preferred_element_type=jnp.float32,
    )
    crop_grad = lax.psum(crop_grad, "fsdp")
    grad_pool_act = (crop_grad * slope(pool_act)).astype(jnp.bfloat16)
    owned_crops = (jnp.arange(crop_total) % owner_group == owner_place).astype(jnp.float32)[:, None]
    grad_pool = inner_dot(pooled, (grad_pool_act * owned_crops).astype(jnp.bfloat16))
    grad_pooled = outer_dot(grad_pool_act, full_pool) / crop_sizes[:, None]
    grad_block = grad_block + inside * jnp.take(
        grad_pooled, jnp.clip(local_crop, 0, crop_total - 1), axis=0
    )
    grad_pre_three = grad_block * slope(pre_three)
    passed, grad_gain_expand, grad_bias_expand = norm_backward(
        grad_pre_three, normed_three, inverse_three, gain_expand, inside, pixel_count
    )
    grad_three = passed.astype(jnp.bfloat16)
    grad_expand = inner_dot(hidden_two, grad_three)
    grad_hidden_two = outer_dot(grad_three, full_expand)
    passed, grad_gain_dilated, grad_bias_dilated = norm_backward(
        grad_hidden_two * slope(pre_two), normed_two, inverse_two, gain_dilated, inside, pixel_count
    )
    second_gradient = passed.astype(jnp.bfloat16)
    dilated_fragments = kernel_offsets(
        first_broad, second_gradient, inner_neck, DILATION_SPAN, local_rows, local_columns
    )
    grad_dilated = jnp.stack(dilated_fragments).reshape(
        3, 3, second_gradient.shape[1], second_gradient.shape[1]
    )
    broad_neck_gradient = padded(
        second_gradient.reshape(local_rows, local_columns, -1), (("fsdp", 0),), DILATION_SPAN
    )
    grad_hidden_one = collect_taps(
        broad_neck_gradient, complete_dilated, inner_neck, DILATION_SPAN, local_rows, local_columns
    )
    passed, grad_gain_reduce, grad_bias_reduce = norm_backward(
        grad_hidden_one * slope(pre_one), normed_one, inverse_one, gain_reduce, inside, pixel_count
    )
    grad_one = passed.astype(jnp.bfloat16)
    grad_reduce = inner_dot(inputs_flat, grad_one)
    grad_features = (grad_pre_three + outer_dot(grad_one, full_reduce)).reshape(
        local_rows, local_columns, channels
    )
    shards = (
        lax.psum_scatter(grad_reduce, "fsdp", scatter_dimension=1, tiled=True),
        lax.psum_scatter(grad_dilated, "fsdp", scatter_dimension=3, tiled=True),
        lax.psum_scatter(grad_expand, "fsdp", scatter_dimension=1, tiled=True),
        lax.psum_scatter(grad_point, "fsdp", scatter_dimension=1, tiled=True),
        lax.psum_scatter(rate_weight_grads[0], "fsdp", scatter_dimension=3, tiled=True),
        lax.psum_scatter(rate_weight_grads[1], "fsdp", scatter_dimension=3, tiled=True),
        lax.psum_scatter(rate_weight_grads[2], "fsdp", scatter_dimension=3, tiled=True),
        lax.psum_scatter(grad_pool, "fsdp", scatter_dimension=1, tiled=True),
        lax.psum_scatter(grad_merge, "fsdp", scatter_dimension=1, tiled=True),
        lax.psum_scatter(grad_classes, "fsdp", scatter_dimension=0, tiled=True),
    )
    shards = (
        lax.psum(shards[0].astype(jnp.bfloat16), "dp").astype(jnp.float32),
        lax.psum(shards[1].astype(jnp.bfloat16), "dp").astype(jnp.float32),
        lax.psum(shards[2].astype(jnp.bfloat16), "dp").astype(jnp.float32),
        lax.psum(shards[3].astype(jnp.bfloat16), "dp").astype(jnp.float32),
        lax.psum(shards[4].astype(jnp.bfloat16), "dp").astype(jnp.float32),
        lax.psum(shards[5].astype(jnp.bfloat16), "dp").astype(jnp.float32),
        lax.psum(shards[6].astype(jnp.bfloat16), "dp").astype(jnp.float32),
        lax.psum(shards[7].astype(jnp.bfloat16), "dp").astype(jnp.float32),
        lax.psum(shards[8].astype(jnp.bfloat16), "dp").astype(jnp.float32),
        lax.psum(shards[9].astype(jnp.bfloat16), "dp").astype(jnp.float32),
    )
    return (
        class_logits,
        grad_features,
        shards[0],
        grad_gain_reduce,
        grad_bias_reduce,
        shards[1],
        grad_gain_dilated,
        grad_bias_dilated,
        shards[2],
        grad_gain_expand,
        grad_bias_expand,
        shards[3],
        grad_gain_point,
        grad_bias_point,
        shards[4],
        rate_gain_grads[0],
        rate_bias_grads[0],
        shards[5],
        rate_gain_grads[1],
        rate_bias_grads[1],
        shards[6],
        rate_gain_grads[2],
        rate_bias_grads[2],
        shards[7],
        shards[8],
        grad_gain_merge,
        grad_bias_merge,
        shards[9],
    )


def solution(mesh):
    tiled = mesh.shape["fsdp"] == 8 and mesh.shape["dp"] == 4

    return jax.shard_map(
        fast_body if tiled else body,
        mesh=mesh,
        in_specs=(
            P(("dp", "fsdp"), None, None),
            P(("dp", "fsdp"), None),
            P(("dp", "fsdp"), None),
            P(None, "fsdp"),
            P(),
            P(),
            P(None, None, None, "fsdp"),
            P(),
            P(),
            P(None, "fsdp"),
            P(),
            P(),
            P(None, "fsdp"),
            P(),
            P(),
            P(None, None, None, "fsdp"),
            P(),
            P(),
            P(None, None, None, "fsdp"),
            P(),
            P(),
            P(None, None, None, "fsdp"),
            P(),
            P(),
            P(None, "fsdp"),
            P(None, "fsdp"),
            P(),
            P(),
            P("fsdp", None),
        ),
        out_specs=(
            P(("dp", "fsdp"), None, None),
            P(("dp", "fsdp"), None, None),
            P(None, "fsdp"),
            P(),
            P(),
            P(None, None, None, "fsdp"),
            P(),
            P(),
            P(None, "fsdp"),
            P(),
            P(),
            P(None, "fsdp"),
            P(),
            P(),
            P(None, None, None, "fsdp"),
            P(),
            P(),
            P(None, None, None, "fsdp"),
            P(),
            P(),
            P(None, None, None, "fsdp"),
            P(),
            P(),
            P(None, "fsdp"),
            P(None, "fsdp"),
            P(),
            P(),
            P("fsdp", None),
        ),
        check_vma=False,
    )
```

```python
import functools
import jax
import jax.numpy as jnp
from jax import lax
from jax.experimental import pallas as pl
from jax.experimental.pallas import tpu as pltpu
from jax.sharding import PartitionSpec as P


CLASSES = 19
CROPS_TILE = 4
DILATION_SPAN = 4
RATE = 12

eps = 1e-05

MESH = pl.DeviceIdType.MESH
ANY = pl.BlockSpec(memory_space=pl.ANY)
VM = pl.BlockSpec(memory_space=pltpu.VMEM)
DMA = pltpu.SemaphoreType.DMA
PAD = 144
VLIM = 60 * 2**20


def greet(fs, ds):
    f = lax.axis_index("fsdp")
    d = lax.axis_index("dp")
    bar = pltpu.get_barrier_semaphore()
    for k in fs:
        pl.semaphore_signal(bar, inc=1, device_id=(d, f ^ k), device_id_type=MESH)
    for k in ds:
        pl.semaphore_signal(bar, inc=1, device_id=(d ^ k, f), device_id_type=MESH)
    pl.semaphore_wait(bar, len(fs) + len(ds))
    return f, d


def remote(src, dst, ss, rs, d, f):
    c = pltpu.make_async_remote_copy(
        src_ref=src, dst_ref=dst, send_sem=ss, recv_sem=rs, device_id=(d, f), device_id_type=MESH
    )
    c.start()
    return c


def sum_kernel(x_ref, o_ref, b1, b2, s1, r1, s2, r2):
    f, d = greet(range(1, 8), range(1, 4))
    b1[f] = x_ref[...]
    cps = [remote(x_ref, b1.at[f], s1.at[k], r1.at[k], d, f ^ k) for k in range(1, 8)]
    for c in cps:
        c.wait()
    tot = b1[0]
    for k in range(1, 8):
        tot = tot + b1[k]
    b2[d] = tot
    cps = [remote(b2.at[d], b2.at[d], s2.at[k], r2.at[k], d ^ k, f) for k in range(1, 4)]
    for c in cps:
        c.wait()
    tot = b2[0]
    for k in range(1, 4):
        tot = tot + b2[k]
    o_ref[...] = tot


def total_sum(rows, cid):
    x = jnp.stack(rows)
    R, C = x.shape
    return pl.pallas_call(
        sum_kernel,
        out_shape=jax.ShapeDtypeStruct((R, C), jnp.float32),
        in_specs=[VM],
        out_specs=VM,
        scratch_shapes=[
            pltpu.VMEM((8, R, C), jnp.float32),
            pltpu.VMEM((4, R, C), jnp.float32),
            DMA((8,)),
            DMA((8,)),
            DMA((4,)),
            DMA((4,)),
        ],
        compiler_params=pltpu.CompilerParams(collective_id=cid, has_side_effects=True),
        name=f"total_sum_{cid}",
    )(x)


def spread_kernel(x_ref, o_ref, ss, rs, ls):
    f, d = greet(range(1, 8), ())
    w = o_ref.shape[2]
    h = x_ref.shape[1]
    dst = o_ref.at[:, pl.ds(pl.multiple_of(PAD + h * f, 16), h), :]

    def part(g):
        return x_ref.at[:, :, pl.ds(pl.multiple_of(g * w, 128), w)]

    cps = [remote(part(f ^ k), dst, ss.at[k], rs.at[k], d, f ^ k) for k in (6, 7, 2, 3, 4, 5, 1)]
    own = pltpu.make_async_copy(part(f), dst, ls)
    own.start()
    for c in cps:
        c.wait()
    own.wait()


def spread_channels(x, cid):
    q, h, C = x.shape
    return pl.pallas_call(
        spread_kernel,
        out_shape=jax.ShapeDtypeStruct((q, 8 * h + 2 * PAD, C // 8), x.dtype),
        in_specs=[VM],
        out_specs=ANY,
        scratch_shapes=[DMA((8,)), DMA((8,)), DMA(())],
        compiler_params=pltpu.CompilerParams(collective_id=cid, has_side_effects=True, vmem_limit_bytes=VLIM),
        name=f"spread_{cid}",
    )(x)


def collect_kernel(x_ref, o_ref, ss, rs, ls):
    f, d = greet(range(1, 8), ())
    w = x_ref.shape[2]
    h = o_ref.shape[1]
    dst = o_ref.at[:, :, pl.ds(pl.multiple_of(f * w, 128), w)]

    def part(g):
        return x_ref.at[:, pl.ds(pl.multiple_of(h * g, 16), h), :]

    cps = [remote(part(f ^ k), dst, ss.at[k], rs.at[k], d, f ^ k) for k in (6, 7, 2, 3, 4, 5, 1)]
    own = pltpu.make_async_copy(part(f), dst, ls)
    own.start()
    for c in cps:
        c.wait()
    own.wait()


def collect_channels(x, cid):
    q, t, w = x.shape
    return pl.pallas_call(
        collect_kernel,
        out_shape=jax.ShapeDtypeStruct((q, t // 8, 8 * w), x.dtype),
        in_specs=[VM],
        out_specs=ANY,
        scratch_shapes=[DMA((8,)), DMA((8,)), DMA(())],
        compiler_params=pltpu.CompilerParams(collective_id=cid, has_side_effects=True, vmem_limit_bytes=VLIM),
        name=f"collect_{cid}",
    )(x)


def gather_kernel(x_ref, o_ref, ss, rs, ps, pr, ls):
    f, d = greet((1, 2, 4, 6), ())
    h = x_ref.shape[1]

    def slot(g):
        return o_ref.at[:, pl.ds(pl.multiple_of(PAD + h * g, 16), h), :]

    cps = [remote(x_ref, slot(f), ss.at[k], rs.at[k], d, f ^ (2 * k)) for k in (3, 1, 2)]
    own = pltpu.make_async_copy(x_ref, slot(f), ls)
    own.start()
    pair = [remote(x_ref, slot(f), ps.at[0], pr.at[0], d, f ^ 1)]
    for k, c in zip((3, 1, 2), cps):
        c.wait_recv()
        got = slot(f ^ (2 * k))
        pair.append(remote(got, got, ps.at[k], pr.at[k], d, f ^ 1))
    for c in cps:
        c.wait_send()
    for c in pair:
        c.wait()
    own.wait()


def gather_rows(x, cid):
    q, h, C = x.shape
    return pl.pallas_call(
        gather_kernel,
        out_shape=jax.ShapeDtypeStruct((q, 8 * h + 2 * PAD, C), x.dtype),
        in_specs=[VM],
        out_specs=ANY,
        scratch_shapes=[DMA((4,)), DMA((4,)), DMA((4,)), DMA((4,)), DMA(())],
        compiler_params=pltpu.CompilerParams(collective_id=cid, has_side_effects=True, vmem_limit_bytes=VLIM),
        name=f"gather_{cid}",
    )(x)


def scatter_kernel(x_ref, o_ref, near, mine, far, ps, pr, ss, rs):
    f, d = greet((1, 2, 4, 6), ())
    c0 = f & 1
    pair = [
        remote(x_ref.at[2 * k + 1 - c0], near.at[k], ps.at[k], pr.at[k], d, f ^ 1) for k in range(4)
    ]
    me = lax.shift_right_logical(f, 1)
    cps = []
    for c in pair:
        c.wait()
    for k in (3, 1, 2, 0):
        g = me ^ k
        val = x_ref[2 * g + c0].astype(jnp.float32) + near[g].astype(jnp.float32)
        if k:
            mine[k] = val.astype(mine.dtype)
            cps.append(remote(mine.at[k], far.at[k], ss.at[k], rs.at[k], d, f ^ (2 * k)))
        else:
            o_ref[...] = val
    for c in cps:
        c.wait()
    o_ref[...] += far[1].astype(jnp.float32) + far[2].astype(jnp.float32) + far[3].astype(jnp.float32)


def scatter_sum(x, cid):
    n, R, C = x.shape
    return pl.pallas_call(
        scatter_kernel,
        out_shape=jax.ShapeDtypeStruct((R, C), jnp.float32),
        in_specs=[VM],
        out_specs=VM,
        scratch_shapes=[
            pltpu.VMEM((4, R, C), x.dtype),
            pltpu.VMEM((4, R, C), x.dtype),
            pltpu.VMEM((4, R, C), x.dtype),
            DMA((4,)),
            DMA((4,)),
            DMA((4,)),
            DMA((4,)),
        ],
        compiler_params=pltpu.CompilerParams(collective_id=cid, has_side_effects=True, vmem_limit_bytes=VLIM),
        name=f"scatter_{cid}",
    )(x)


def nt_dot(a, b):
    return lax.dot_general(a, b, (((1,), (1,)), ((), ())), preferred_element_type=jnp.float32)


def nn_dot(a, b):
    return lax.dot_general(a, b, (((1,), (0,)), ((), ())), preferred_element_type=jnp.float32)


def tn_dot(a, b):
    return lax.dot_general(a, b, (((0,), (0,)), ((), ())), preferred_element_type=jnp.float32)


def span(shift, count):
    return max(0, -shift), min(count, count - shift)


def conv_forward_kernel(steps, y_ref, key_ref, k_ref, o_ref, acc):
    Q = y_ref.shape[0]
    h = o_ref.shape[2]
    w = y_ref.shape[2]
    out = k_ref.shape[1]
    dest = pl.program_id(0)
    base = PAD + h * dest
    T = 8 * h
    for b, s in enumerate(steps):
        acc[...] = jnp.zeros_like(acc)
        for i in (-1, 0, 1):
            first = h * dest + 16 * s * i

            @pl.when((first + h > 0) & (first < T))
            def _():
                at = pl.multiple_of(base + 16 * s * i, 16)
                for j in (-1, 0, 1):
                    lo, hi = span(s * j, Q)
                    here = key_ref[lo:hi, pl.ds(pl.multiple_of(base, 16), h), :]
                    there = key_ref[lo + s * j : hi + s * j, pl.ds(at, h), :]
                    ok = (here == there) & (here > 0)
                    ok = jnp.concatenate([ok] * (w // 128), axis=2)
                    x = jnp.where(ok, y_ref[lo + s * j : hi + s * j, pl.ds(at, h), :], 0)
                    x = x.reshape((hi - lo) * h, w)
                    acc[lo * h : hi * h] += nt_dot(x, k_ref[9 * b + 3 * (i + 1) + j + 1])

        o_ref[0, :, :, b * out : (b + 1) * out] = acc[...].reshape(Q, h, out).astype(o_ref.dtype)


def conv_forward(y, key, k, steps):
    Q, TT, w = y.shape
    h = (TT - 2 * PAD) // 8
    out = k.shape[1]
    return pl.pallas_call(
        functools.partial(conv_forward_kernel, steps),
        out_shape=jax.ShapeDtypeStruct((8, Q, h, 3 * out), jnp.bfloat16),
        grid=(8,),
        in_specs=[VM, VM, VM],
        out_specs=pl.BlockSpec((1, Q, h, 3 * out), lambda i: (i, 0, 0, 0)),
        scratch_shapes=[pltpu.VMEM((Q * h, out), jnp.float32)],
        compiler_params=pltpu.CompilerParams(vmem_limit_bytes=VLIM),
        name="conv_forward",
    )(y, key, k)


def conv_data_kernel(steps, g_ref, key_ref, k_ref, o_ref, acc):
    Q = g_ref.shape[0]
    h = o_ref.shape[1]
    w = o_ref.shape[2]
    out = k_ref.shape[1]
    dest = pl.program_id(0)
    base = PAD + h * dest
    T = 8 * h
    acc[...] = jnp.zeros_like(acc)
    for b, s in enumerate(steps):
        for i in (-1, 0, 1):
            first = h * dest - 16 * s * i

            @pl.when((first + h > 0) & (first < T))
            def _():
                at = pl.multiple_of(base - 16 * s * i, 16)
                for j in (-1, 0, 1):
                    lo, hi = span(-s * j, Q)
                    here = key_ref[lo:hi, pl.ds(pl.multiple_of(base, 16), h), :]
                    there = key_ref[lo - s * j : hi - s * j, pl.ds(at, h), :]
                    ok = (here == there) & (here > 0)
                    ok = jnp.concatenate([ok] * (out // 128), axis=2)
                    x = jnp.where(
                        ok, g_ref[lo - s * j : hi - s * j, pl.ds(at, h), b * out : (b + 1) * out], 0
                    )
                    x = x.reshape((hi - lo) * h, out)
                    acc[lo * h : hi * h] += nn_dot(x, k_ref[9 * b + 3 * (i + 1) + j + 1])

    o_ref[...] = acc[...].reshape(Q, h, w).astype(o_ref.dtype)


def conv_data(g, key, k, steps):
    Q, TT, _ = g.shape
    h = (TT - 2 * PAD) // 8
    w = k.shape[2]
    return pl.pallas_call(
        functools.partial(conv_data_kernel, steps),
        out_shape=jax.ShapeDtypeStruct((Q, 8 * h, w), jnp.bfloat16),
        grid=(8,),
        in_specs=[VM, VM, VM],
        out_specs=pl.BlockSpec((Q, h, w), lambda i: (0, i, 0)),
        scratch_shapes=[pltpu.VMEM((Q * h, w), jnp.float32)],
        compiler_params=pltpu.CompilerParams(vmem_limit_bytes=VLIM),
        name="conv_data",
    )(g, key, k)


def conv_weight_kernel(steps, y_ref, key_ref, g_ref, o_ref, x_ref):
    Q = y_ref.shape[0]
    w = y_ref.shape[2]
    out = o_ref.shape[1]
    TT = y_ref.shape[1]
    T = TT - 2 * PAD
    b = pl.program_id(0)
    for n, s in enumerate(steps):

        @pl.when(b == n)
        def _():
            for i in (-1, 0, 1):
                r0, r1 = span(16 * s * i, T)
                r0, r1 = r0 // 128 * 128, -(-r1 // 128) * 128
                for j in (-1, 0, 1):
                    lo, hi = span(s * j, Q)
                    L = r1 - r0

                    def one(q, _):
                        here = key_ref[q, PAD + r0 : PAD + r1, :]
                        a = PAD + r0 + 16 * s * i
                        there = key_ref[q + s * j, a : a + L, :]
                        ok = (here == there) & (here > 0)
                        ok = jnp.concatenate([ok] * (w // 128), axis=1)
                        x = jnp.where(ok, y_ref[q + s * j, a : a + L, :], 0)
                        x_ref[pl.ds(pl.multiple_of((q - lo) * L, 128), L), :] = x
                        return 0

                    lax.fori_loop(lo, hi, one, 0)
                    d = g_ref[lo:hi, PAD + r0 : PAD + r1, n * out : (n + 1) * out]
                    d = d.reshape((hi - lo) * L, out)
                    o_ref[3 * (i + 1) + j + 1] = tn_dot(d, x_ref[: (hi - lo) * L, :]).astype(o_ref.dtype)


def conv_weight(y, key, g, steps, out):
    Q, TT, w = y.shape
    T = TT - 2 * PAD
    return pl.pallas_call(
        functools.partial(conv_weight_kernel, steps),
        out_shape=jax.ShapeDtypeStruct((27, out, w), jnp.bfloat16),
        grid=(3,),
        in_specs=[VM, VM, VM],
        out_specs=pl.BlockSpec((9, out, w), lambda i: (i, 0, 0)),
        scratch_shapes=[pltpu.VMEM((Q * T, w), jnp.bfloat16)],
        compiler_params=pltpu.CompilerParams(vmem_limit_bytes=VLIM),
        name="conv_weight",
    )(y, key, g)


class Gather:
    def __init__(self, src, slot, sems, d, f):
        self.src, self.slot, self.sems, self.d, self.f = src, slot, sems, d, f

    def start(self):
        far_s, far_r, near_s, near_r, local = self.sems
        d, f = self.d, self.f
        mine = self.slot(f)
        self.far = {k: remote(self.src, mine, far_s.at[k], far_r.at[k], d, f ^ (2 * k)) for k in (3, 1, 2)}
        self.near = [remote(self.src, mine, near_s.at[0], near_r.at[0], d, f ^ 1)]
        self.own = pltpu.make_async_copy(self.src, mine, local)
        self.own.start()

    def forward(self):
        far_s, far_r, near_s, near_r, local = self.sems
        for k in (1, 2, 3):
            self.far[k].wait_recv()
            got = self.slot(self.f ^ (2 * k))
            self.near.append(remote(got, got, near_s.at[k], near_r.at[k], self.d, self.f ^ 1))

    def arrive(self):
        self.own.wait()
        for c in self.near:
            c.wait_recv()

    def finish(self):
        for c in list(self.far.values()) + self.near:
            c.wait_send()


class HalfGather:
    def __init__(self, src, slot, half, sems, d, f):
        self.src, self.slot, self.half, self.sems, self.d, self.f = src, slot, half, sems, d, f

    def start(self):
        far_s, far_r, near_s, near_r, side_s, side_r, local = self.sems
        d, f = self.d, self.f
        mine = self.slot(f)
        a = self.half(d % 2)
        self.far = {
            k: remote(self.src.at[a], mine.at[a], far_s.at[k], far_r.at[k], d, f ^ (2 * k)) for k in (3, 1, 2)
        }
        self.near = [remote(self.src, mine, near_s.at[0], near_r.at[0], d, f ^ 1)]
        self.own = pltpu.make_async_copy(self.src, mine, local)
        self.own.start()

    def forward(self):
        far_s, far_r, near_s, near_r, side_s, side_r, local = self.sems
        d, f = self.d, self.f
        a = self.half(d % 2)
        self.side = {}
        for k in (1, 2, 3):
            self.far[k].wait_recv()
            got = self.slot(f ^ (2 * k)).at[a]
            self.side[k] = remote(got, got, side_s.at[k], side_r.at[k], d ^ 1, f)
            self.near.append(remote(got, got, near_s.at[k], near_r.at[k], d, f ^ 1))

    def arrive(self):
        far_s, far_r, near_s, near_r, side_s, side_r, local = self.sems
        d, f = self.d, self.f
        b = self.half(1 - d % 2)
        for k in (1, 2, 3):
            self.side[k].wait_recv()
            got = self.slot(f ^ (2 * k)).at[b]
            self.near.append(remote(got, got, near_s.at[k + 3], near_r.at[k + 3], d, f ^ 1))
        self.own.wait()
        for c in self.near:
            c.wait_recv()

    def finish(self):
        for c in list(self.far.values()) + self.near + list(self.side.values()):
            c.wait_send()


def half_sems():
    return [DMA((4,)), DMA((4,)), DMA((7,)), DMA((7,)), DMA((4,)), DMA((4,)), DMA(())]


def gather_sems():
    return [DMA((4,)), DMA((4,)), DMA((4,)), DMA((4,)), DMA(())]


def sum_sems(R, C):
    return [
        pltpu.VMEM((8, R, C), jnp.float32),
        pltpu.VMEM((4, R, C), jnp.float32),
        DMA((8,)),
        DMA((8,)),
        DMA((4,)),
        DMA((4,)),
    ]


def sum_all(rows, bufs, d, f):
    b1, b2, s1, r1, s2, r2 = bufs
    for n, row in enumerate(rows):
        b1[f, n : n + 1, :] = row
    cps = [remote(b1.at[f], b1.at[f], s1.at[k], r1.at[k], d, f ^ k) for k in (6, 2, 4, 7, 3, 5, 1)]
    for c in cps:
        c.wait()
    tot = b1[0]
    for k in range(1, 8):
        tot = tot + b1[k]
    b2[d] = tot
    cps = [remote(b2.at[d], b2.at[d], s2.at[k], r2.at[k], d ^ k, f) for k in (3, 2, 1)]
    for c in cps:
        c.wait()
    tot = b2[0]
    for k in range(1, 4):
        tot = tot + b2[k]
    return tot


def column_sums(a, ins):
    m = a * jnp.concatenate([ins] * (a.shape[1] // 128), axis=1)
    return jnp.sum(m, axis=0, keepdims=True), jnp.sum(m * a, axis=0, keepdims=True)


def bend(p):
    g = 1.0 / (1.0 + jnp.exp(-p))
    return p * g, g * (1.0 + p * (1.0 - g))


def same_crop(here, there, width):
    ok = (here == there) & (here > 0)
    return jnp.concatenate([ok] * (width // 128), axis=ok.ndim - 1)


def cat_rows(parts):
    return jnp.concatenate(parts, axis=1)


def bottleneck_kernel(
    x_ref, kb_ref, ins_ref, gr, br, gd, bd, ge, be,
    wr_s, wd_s, we_s, wp_s, wm_s, wc_s, k_s0, k_s1, k_s2, kp_s,
    yo_o, y_o, n3_o, l3_o, n1_o, l1_o, n2_o, l2_o, ext_o, h2_o, key_o, k_o, wr_o, wd_o, we_o, wp_o, wm_o, wc_o, cnt_o,
    xp, a1, a2, a3, ext, h2, y, n3, l3, n1, l1, n2, l2, key, wr, wd, we,
    *sems,
):
    sems = list(sems)

    def take(n):
        got = sems[:n]
        del sems[:n]
        return got

    f, d = greet(range(1, 8), range(1, 4))
    N, C = x_ref.shape
    Q, h = ext.shape[0], ext.shape[1] // 2
    e = h // 2
    rows = h // 4
    neck = a1.shape[1]
    T = 8 * h

    def rows_of(ref, n):
        return lambda g: ref.at[pl.ds(pl.multiple_of(n * g, n), n)]

    nr, nd_, ne, np_ = wr_s.shape[0], wd_s.shape[1], we_s.shape[1], wp_s.shape[0]
    def half(n, lead=()):
        return lambda a: lead + (pl.ds(pl.multiple_of(n * a, n), n),)

    g_wr = Gather(wr_s, rows_of(wr, nr), take(5), d, f)
    g_wd = [
        HalfGather(
            wd_s.at[pl.ds(3 * i, 3)],
            lambda g, i=i: wd.at[pl.ds(3 * i, 3), pl.ds(pl.multiple_of(nd_ * g, 16), nd_), :],
            half(nd_ // 2, (slice(None),)), take(7), d, f,
        )
        for i in range(3)
    ]
    g_we = HalfGather(
        we_s, lambda g: we.at[:, pl.ds(pl.multiple_of(ne * g, 128), ne)], half(we_s.shape[0] // 2), take(7), d, f
    )
    g_wp = Gather(wp_s, rows_of(wp_o, np_), take(5), d, f)
    g_wm = Gather(wm_s, rows_of(wm_o, np_), take(5), d, f)
    g_wc = Gather(wc_s, rows_of(wc_o, np_), take(5), d, f)
    ks, kr, kl, zs, zk, hs, hr, ys, yr, yl, os_, qs, qr, kc = take(14)
    sum1, sum2, sum3 = (Sum(take(6), d, f) for _ in range(3))

    key_sent = [
        remote(kb_ref, kc.at[f], qs.at[k], qr.at[k], d, f ^ k) for k in (6, 7, 2, 3, 4, 5, 1)
    ]
    kc[f] = kb_ref[...]
    g_wr.start()
    g_wd[0].start()
    order = lax.broadcasted_iota(jnp.int32, (N, N), 0)
    m, r, q = order % 4, (order // 4) % rows, order // h
    pick = (r * (N // rows) + q * 4 + m) == lax.broadcasted_iota(jnp.int32, (N, N), 1)
    pick = pick.astype(jnp.float32).astype(jnp.bfloat16)
    for c in range(0, C, 256):
        xp[:, c : c + 256] = nn_dot(pick, x_ref[:, c : c + 256]).astype(jnp.bfloat16)
    key[:, :PAD, :] = jnp.zeros((Q, PAD, 128), jnp.bfloat16)
    key[:, PAD + T :, :] = jnp.zeros((Q, PAD, 128), jnp.bfloat16)
    g_wr.forward()
    g_wd[1].start()
    g_wd[2].start()
    g_wr.arrive()
    g_wd[0].forward()
    sums, squares = [], []
    for c in range(0, neck, 256):
        a = nt_dot(xp[...], wr[c : c + 256, :])
        a1[:, c : c + 256] = a
        s, t = column_sums(a, ins_ref[...])
        sums.append(s)
        squares.append(t)
    inside = jnp.sum(ins_ref[...], axis=0, keepdims=True)
    sum1.start([cat_rows(sums), cat_rows(squares), cat_rows([inside] * (neck // 128))])
    g_we.start()
    g_wd[1].forward()
    g_wd[2].forward()
    kparts = (k_s0, k_s1, k_s2, kp_s)

    def kslot(b, g, lo, n):
        o = kparts[b].shape[1]
        return k_o.at[pl.ds(9 * b, kparts[b].shape[0]), pl.ds(pl.multiple_of(o * g + lo, 16), n), :]

    kcp, kfar = [], {}
    pieces = [(b, k) for b in range(3) for k in (6, 7, 2, 3, 4, 5)]

    def out(*ns):
        for b, k in [pieces[n] for n in ns]:
            src = kparts[b]
            o = src.shape[1] // 2
            lo = pl.multiple_of(o * (d % 2), 16)
            to = pl.ds(pl.multiple_of((f ^ k) * 256, 128), 256)
            kfar[b, k] = remote(
                src.at[:, pl.ds(lo, o), to], kslot(b, f, lo, o), ks.at[b, k], kr.at[b, k], d, f ^ k
            )

    def aside(*ns):
        for b, k in [pieces[n] for n in ns]:
            o = kparts[b].shape[1] // 2
            lo = pl.multiple_of(o * (d % 2), 16)
            kfar[b, k].wait_recv()
            got = kslot(b, f ^ k, lo, o)
            kcp.append(remote(got, got, zs.at[b, k], zk.at[b, k], d ^ 1, f))

    for b, src in enumerate(kparts):
        o = src.shape[1]
        for k in (6, 7, 2, 3, 4, 5, 1) if b == 3 else (1,):
            to = pl.ds(pl.multiple_of((f ^ k) * 256, 128), 256)
            kcp.append(remote(src.at[:, :, to], kslot(b, f, 0, o), ks.at[b, k], kr.at[b, k], d, f ^ k))
        own = pl.ds(pl.multiple_of(f * 256, 128), 256)
        c = pltpu.make_async_copy(src.at[:, :, own], kslot(b, f, 0, o), kl.at[b])
        c.start()
        kcp.append(c)
    sum1.turn()
    out(0, 1)
    st = sum1.result()
    out(2, 3)
    g_we.forward()
    count = st[2:3, :]
    cnt_o[...] = jnp.zeros_like(cnt_o)
    cnt_o[0:1, :neck] = count
    mean = st[0:1] / count
    inv = lax.rsqrt(st[1:2] / count - mean * mean + eps)
    cnt_o[1:2, :neck] = inv
    for c in range(0, neck, 256):
        w = slice(c, c + 256)
        n = (a1[:, w] - mean[:, w]) * inv[:, w]
        act, lean = bend(n * gr[:, w] + br[:, w])
        ext[:, e : e + h, w] = act.astype(jnp.bfloat16).reshape(Q, h, 256)
        n1[:, w] = n.astype(jnp.bfloat16)
        l1[:, w] = lean.astype(jnp.bfloat16)
    up = remote(ext.at[:, pl.ds(e, e)], ext.at[:, pl.ds(e + h, e)], hs.at[0], hr.at[0], d, lax.rem(f + 7, 8))
    down = remote(ext.at[:, pl.ds(h, e)], ext.at[:, pl.ds(0, e)], hs.at[1], hr.at[1], d, lax.rem(f + 1, 8))
    for c in key_sent:
        c.wait()
    for g in range(8):
        turned = kc[g].T
        for q in range(Q):
            key[q, PAD + h * g : PAD + h * g + h, :] = jnp.broadcast_to(turned[:h, q : q + 1], (h, 128)).astype(jnp.bfloat16)
    outs = [(n1, n1_o), (l1, l1_o), (key, key_o), (wr, wr_o)]
    base = pl.multiple_of(PAD + h * f, 16)
    up.wait()
    down.wait()
    outs.append((ext, ext_o))
    outs.append((wd, wd_o))
    a2[...] = jnp.zeros_like(a2)
    for i in range(3):
        g_wd[i].arrive()
        for j in (1, 0, 2):
            lo, hi = span(j - 1, Q)
            ok = same_crop(
                key[lo:hi, pl.ds(base, h), :],
                key[lo + j - 1 : hi + j - 1, pl.ds(pl.multiple_of(base + e * (i - 1), 16), h), :],
                neck,
            )
            v = jnp.where(ok, ext[lo + j - 1 : hi + j - 1, e * i : e * i + h, :], 0).reshape((hi - lo) * h, neck)
            for c in range(0, neck, 256):
                a2[lo * h : hi * h, c : c + 256] += nt_dot(v, wd[3 * i + j, c : c + 256, :])
            if (3 * i + j) % 2 == 0 and i < 2 + (j == 0):
                out(4 + (3 * i + j) // 2)
    sums, squares = [], []
    for c in range(0, neck, 256):
        s, t = column_sums(a2[:, c : c + 256], ins_ref[...])
        sums.append(s)
        squares.append(t)
    sum2.start([cat_rows(sums), cat_rows(squares)])
    aside(0, 1, 2, 3)
    sum2.turn()
    out(8, 9)
    st = sum2.result()
    out(10)
    mean = st[0:1] / count
    inv = lax.rsqrt(st[1:2] / count - mean * mean + eps)
    cnt_o[2:3, :neck] = inv
    for c in range(0, neck, 256):
        w = slice(c, c + 256)
        n = (a2[:, w] - mean[:, w]) * inv[:, w]
        act, lean = bend(n * gd[:, w] + bd[:, w])
        h2[:, w] = act.astype(jnp.bfloat16)
        n2[:, w] = n.astype(jnp.bfloat16)
        l2[:, w] = lean.astype(jnp.bfloat16)
    outs += [(n2, n2_o), (l2, l2_o), (h2, h2_o)]
    g_we.arrive()
    outs.append((we, we_o))
    sums, squares = [], []
    for c in range(0, C, 256):
        n = c // 256
        if n % 2 == 0:
            out(11 + n // 2)
        else:
            aside(4 + n // 2)
        a = nn_dot(h2[...], we[:, c : c + 256])
        a3[:, c : c + 256] = a
        s, t = column_sums(a, ins_ref[...])
        sums.append(s)
        squares.append(t)
    sum3.start([cat_rows(sums), cat_rows(squares)])
    aside(8, 9)
    sum3.turn()
    out(15, 16, 17)
    for g in (g_wp, g_wm, g_wc):
        g.start()
    st = sum3.result()
    total = count[:, :1]
    mean3 = st[0:1] / total
    inv3 = lax.rsqrt(st[1:2] / total - mean3 * mean3 + eps)
    coef = sum3.b1
    coef[0, 0:1, :] = mean3
    coef[0, 1:2, :] = inv3
    cnt_o[3:4, :] = inv3
    sent = []
    dst = yo_o.at[:, pl.ds(base, h), :]
    for m, k in enumerate((6, 7, 2, 3, 4, 5, 1, 0)):
        aside(10 + m)
        g = f ^ k
        w = pl.ds(pl.multiple_of(g * 256, 256), 256)
        n = (a3[:, w] - coef[0, 0:1, w]) * coef[0, 1:2, w]
        act, lean = bend(n * ge[:, w] + be[:, w] + xp[:, w].astype(jnp.float32))
        y[:, :, w] = act.astype(jnp.bfloat16).reshape(Q, h, 256)
        n3[:, w] = n.astype(jnp.bfloat16)
        l3[:, w] = lean.astype(jnp.bfloat16)
        part = y.at[:, :, w]
        if k:
            sent.append(remote(part, dst, ys.at[k], yr.at[k], d, g))
        else:
            own = pltpu.make_async_copy(part, dst, yl)
            own.start()
            sent.append(own)
    outs += [(y, y_o), (n3, n3_o), (l3, l3_o)]
    saved = []
    for n, (src, to) in enumerate(outs):
        c = pltpu.make_async_copy(src, to, os_.at[n])
        c.start()
        saved.append(c)
    for g in (g_wp, g_wm, g_wc):
        g.forward()
    for g in (g_wp, g_wm, g_wc):
        g.arrive()
    for g in [g_wr, g_we, g_wp, g_wm, g_wc] + g_wd:
        g.finish()
    for c in kfar.values():
        c.wait_send()
    for c in kcp + sent + saved:
        c.wait()


def bottleneck(x, kb, ins, vecs, shards, kparts):
    N, C = x.shape
    Q = kb.shape[0]
    h = N // Q
    wr, wd, we, wp, wm, wc = shards
    neck = we.shape[0]
    W = 8 * wp.shape[0]
    b16, f32 = jnp.bfloat16, jnp.float32
    S = jax.ShapeDtypeStruct
    TT = 8 * h + 2 * PAD
    outs = [
        S((Q, TT, C // 8), b16), S((Q, h, C), b16), S((N, C), b16), S((N, C), b16),
        S((N, neck), b16), S((N, neck), b16), S((N, neck), b16), S((N, neck), b16),
        S((Q, 2 * h, neck), b16), S((N, neck), b16), S((Q, TT, 128), b16), S((28, W, C // 8), b16),
        S((neck, C), b16), S((9, neck, neck), b16), S((neck, C), b16), S((W, C), b16), S((W, wm.shape[1]), b16),
        S((W, 128), b16), S((8, C), f32),
    ]
    V = pltpu.VMEM
    scratch = [
        V((N, C), b16), V((N, neck), f32), V((N, neck), f32), V((N, C), f32), V((Q, 2 * h, neck), b16), V((N, neck), b16),
        V((Q, h, C), b16), V((N, C), b16), V((N, C), b16),
        V((N, neck), b16), V((N, neck), b16), V((N, neck), b16), V((N, neck), b16), V((Q, TT, 128), b16),
        V((neck, C), b16), V((9, neck, neck), b16), V((neck, C), b16),
    ]
    scratch += gather_sems() + half_sems() * 4 + gather_sems() * 3
    scratch += [DMA((4, 8)), DMA((4, 8)), DMA((4,)), DMA((4, 8)), DMA((4, 8)), DMA((2,)), DMA((2,)), DMA((8,)), DMA((8,)), DMA(()), DMA((16,))]
    scratch += [DMA((8,)), DMA((8,)), V((8, Q, 128), f32)]
    scratch += sum_sems(3, neck) + sum_sems(2, neck) + sum_sems(2, C)
    return pl.pallas_call(
        bottleneck_kernel,
        out_shape=outs,
        in_specs=[VM] * 9 + [ANY] * 10,
        out_specs=[ANY] * 18 + [VM],
        scratch_shapes=scratch,
        compiler_params=pltpu.CompilerParams(collective_id=1, has_side_effects=True, vmem_limit_bytes=VLIM),
        name="bottleneck",
    )(x, kb, ins, *vecs, *shards, *kparts)


def branches_back_kernel(
    steps, d_ref, y_ref, key_ref, k_ref, pooled_ref, dr_ref, size_ref, dy_o, gk_o,
    g, gt, gk, fin, in1, in2, dyo, acc, gp, *sems,
):
    sems = list(sems)
    f, d = greet(range(1, 8), range(1, 4))
    Q, h, w = y_ref.shape[0], d_ref.shape[1], y_ref.shape[2]
    W = k_ref.shape[1]
    T = 8 * h
    o = W // 8
    taps = gk.shape[0] // 2
    gathers = [
        Gather(
            d_ref.at[:, :, pl.ds(b * W, W)],
            lambda n, b=b: g.at[:, pl.ds(pl.multiple_of(PAD + h * n, 16), h), pl.ds(b * W, W)],
            sems[5 * b : 5 * b + 5], d, f,
        )
        for b in range(3)
    ]
    ws, wr, wl, ds_, dr_, dl, s1, r1, s2, r2, s3, r3 = sems[15:]
    for c in gathers:
        c.start()
    outer = d % 3 == 0

    def two(ref, t):
        return ref.at[pl.ds(2 * t, 2)]

    def to_inner(t):
        return pltpu.make_async_remote_copy(
            src_ref=two(gk, t), dst_ref=two(in1, t), send_sem=s1.at[t], recv_sem=r1.at[t],
            device_id=(d ^ 1, f), device_id_type=MESH,
        )

    def across(t):
        return pltpu.make_async_remote_copy(
            src_ref=two(gk, t), dst_ref=two(in2, t), send_sem=s2.at[t], recv_sem=r2.at[t],
            device_id=(d ^ 3, f), device_id_type=MESH,
        )

    def to_outer(t):
        return pltpu.make_async_remote_copy(
            src_ref=two(fin, t), dst_ref=two(fin, t), send_sem=s3.at[t], recv_sem=r3.at[t],
            device_id=(d ^ 1, f), device_id_type=MESH,
        )

    def hand(t):
        @pl.when(outer)
        def _():
            to_inner(t).start()

    def first(t):
        @pl.when(jnp.logical_not(outer))
        def _():
            to_inner(t).wait_recv()
            for n in (2 * t, 2 * t + 1):
                gk[n] = (gk[n].astype(jnp.float32) + in1[n].astype(jnp.float32)).astype(gk.dtype)
            across(t).start()

    def second(t):
        @pl.when(jnp.logical_not(outer))
        def _():
            across(t).wait_recv()
            for n in (2 * t, 2 * t + 1):
                fin[n] = (gk[n].astype(jnp.float32) + in2[n].astype(jnp.float32)).astype(fin.dtype)
            to_outer(t).start()

        @pl.when(outer)
        def _():
            to_outer(t).wait_recv()

    gk[27] = tn_dot(dr_ref[...], pooled_ref[...]).astype(gk.dtype)
    gp[...] = nn_dot(dr_ref[...], k_ref[27]) / size_ref[:, :1]
    for b, s in enumerate(steps):
        gathers[b].forward()
        gathers[b].arrive()

        def turn(q, _):
            gt[b * W : (b + 1) * W, pl.ds(pl.multiple_of(q * T, 256), T)] = g[q, PAD : PAD + T, b * W : (b + 1) * W].T
            return 0

        lax.fori_loop(0, Q, turn, 0)
        for i in (-1, 0, 1):
            for j in (-1, 0, 1):
                lo, hi = span(s * j, Q)
                a = PAD + 16 * s * i

                got = None
                for q in range(lo, hi):
                    ok = same_crop(key_ref[q, PAD : PAD + T, :], key_ref[q + s * j, a : a + T, :], w)
                    v = jnp.where(ok, y_ref[q + s * j, a : a + T, :], 0)
                    r = nn_dot(gt[b * W : (b + 1) * W, q * T : (q + 1) * T], v)
                    got = r if got is None else got + r
                t = 9 * b + 3 * (i + 1) + j + 1
                gk[t] = got.astype(gk.dtype)
                if t % 2:
                    hand(t // 2)
                if b == 2 and t % 2:
                    first((t - 18) // 2)
    hand(13)
    cps = []
    ready = 4

    dst = dy_o.at[:, :, pl.ds(pl.multiple_of(w * f, 128), w)]

    def rows_of(k):
        return pl.ds(pl.multiple_of(h * (f ^ k), 16), h)

    def dest_step(m, _):
        k = 7 - m
        dest = f ^ k
        base = pl.multiple_of(PAD + h * dest, 16)
        here = key_ref[:, pl.ds(base, h), :].astype(jnp.float32).reshape(Q * h, 128)
        here = jnp.concatenate([here] * (w // 128), axis=1)
        @pl.when(m % 2 == 1)
        def _():
            first(ready + m // 2)
            second(m // 2)

        total = jnp.zeros((Q * h, w), jnp.float32)
        for c in range(CROPS_TILE):
            total = jnp.where(here == c + 1.0, gp[c : c + 1, :], total)
        acc[...] = total
        for b in range(3):
            spaced_taps(g, key_ref, k_ref, acc, base, h, steps, -1, b * W, nn_dot, b)
        rows = rows_of(k)
        dyo[:, rows, :] = acc[...].reshape(Q, h, w).astype(dyo.dtype)
        src = dyo.at[:, rows, :]

        @pl.when(k > 0)
        def _():
            remote(src, dst, ds_.at[k], dr_.at[k], d, dest)

        @pl.when(k == 0)
        def _():
            pltpu.make_async_copy(src, dst, dl).start()

        return 0

    lax.fori_loop(0, 8, dest_step, 0)

    def first_when(t):
        @pl.when(t < taps)
        def _():
            first(t)

    groups = (4, 5, 3, 2)
    at = 0
    for n, size in enumerate(groups):
        stop = at + size
        lax.fori_loop(max(at, 4), stop, lambda t, _: (first_when(t + ready), second(t), 0)[-1], 0)
        for k in (6, 7, 2, 3, 4, 5, 1, 0):
            src = fin.at[pl.ds(2 * at, 2 * size), pl.ds(pl.multiple_of(o * (f ^ k), 16), o), :]
            to = gk_o.at[pl.ds(2 * at, 2 * size), :, pl.ds(pl.multiple_of(w * f, 128), w)]
            if k:
                cps.append(remote(src, to, ws.at[n, k], wr.at[n, k], d, f ^ k))
            else:
                c = pltpu.make_async_copy(src, to, wl.at[n])
                c.start()
                cps.append(c)
        at = stop
    for k in range(1, 8):
        c = pltpu.make_async_remote_copy(
            src_ref=dyo.at[:, rows_of(k), :], dst_ref=dst, send_sem=ds_.at[k], recv_sem=dr_.at[k],
            device_id=(d, f ^ k), device_id_type=MESH,
        )
        c.wait()
    pltpu.make_async_copy(dyo.at[:, rows_of(0), :], dst, dl).wait()
    for c in gathers:
        c.finish()
    for c in cps:
        c.wait()

    def sent(t, _):
        @pl.when(outer)
        def _():
            to_inner(t).wait_send()

        @pl.when(jnp.logical_not(outer))
        def _():
            across(t).wait_send()
            to_outer(t).wait_send()

        return 0

    lax.fori_loop(0, taps, sent, 0)


def branches_back(d, y, key, k, pooled, dr, sizes, steps):
    Q, h, W3 = d.shape
    TT, w = y.shape[1:]
    W = W3 // 3
    T = 8 * h
    b16, f32 = jnp.bfloat16, jnp.float32
    V = pltpu.VMEM
    return pl.pallas_call(
        functools.partial(branches_back_kernel, steps),
        out_shape=[jax.ShapeDtypeStruct((Q, h, 8 * w), b16), jax.ShapeDtypeStruct((28, W // 8, 8 * w), b16)],
        in_specs=[VM] * 7,
        out_specs=[ANY] * 2,
        scratch_shapes=[
            V((Q, TT, W3), b16), V((W3, Q * T), b16), V((28, W, w), b16), V((28, W, w), b16),
            V((28, W, w), b16), V((28, W, w), b16), V((Q, T, w), b16),
            V((Q * h, w), f32), V((8, w), f32),
        ]
        + gather_sems() * 3
        + [DMA((4, 8)), DMA((4, 8)), DMA((4,)), DMA((8,)), DMA((8,)), DMA(())]
        + [DMA((14,))] * 6,
        compiler_params=pltpu.CompilerParams(collective_id=10, has_side_effects=True, vmem_limit_bytes=VLIM),
        name="branches_back",
    )(d, y, key, k, pooled, dr, sizes)


class Sum:
    def __init__(self, bufs, d, f):
        self.b1, self.b2, self.s1, self.r1, self.s2, self.r2 = bufs
        self.d, self.f = d, f

    def start(self, rows):
        b1, d, f = self.b1, self.d, self.f
        for n, row in enumerate(rows):
            b1[f, n : n + 1, :] = row
        self.cps = [remote(b1.at[f], b1.at[f], self.s1.at[k], self.r1.at[k], d, f ^ k) for k in (6, 2, 4, 7, 3, 5, 1)]

    def turn(self):
        b1, b2, d, f = self.b1, self.b2, self.d, self.f
        for c in self.cps:
            c.wait()
        tot = b1[0]
        for k in range(1, 8):
            tot = tot + b1[k]
        b2[d] = tot
        self.cps = [remote(b2.at[d], b2.at[d], self.s2.at[k], self.r2.at[k], d ^ k, f) for k in (3, 2, 1)]

    def result(self):
        for c in self.cps:
            c.wait()
        tot = self.b2[0]
        for k in range(1, 4):
            tot = tot + self.b2[k]
        return tot


class Reduce:
    def __init__(self, full, part, near, far, tot, zin, zo, out, sems, d, f):
        self.full, self.part, self.near, self.fars, self.tot, self.out = full, part, near, far, tot, out
        self.zin, self.zo, self.d, self.f = zin, zo, d, f
        self.sems = sems
        self.c0 = f % 2
        self.me = f // 2

    def pair(self):
        ps, pr = self.sems[:2]
        self.cps = [
            remote(self.full.at[self.part(2 * g + 1 - self.c0)], self.near.at[g], ps.at[g], pr.at[g], self.d, self.f ^ 1)
            for g in range(4)
        ]

    def far(self):
        ss, rs = self.sems[2:4]
        for c in self.cps:
            c.wait()
        self.cps = []
        for k in (3, 1, 2, 0):
            g = self.me ^ k
            val = self.full[self.part(2 * g + self.c0)].astype(jnp.float32) + self.near[g].astype(jnp.float32)
            self.near[g] = val.astype(self.near.dtype)
            if k:
                self.cps.append(
                    remote(self.near.at[g], self.fars.at[k], ss.at[k], rs.at[k], self.d, self.f ^ (2 * k))
                )

    def to_inner(self):
        ss, rs = self.sems[4:6]
        return pltpu.make_async_remote_copy(
            src_ref=self.tot, dst_ref=self.zin, send_sem=ss.at[0], recv_sem=rs.at[0],
            device_id=(self.d ^ 1, self.f), device_id_type=MESH,
        )

    def across(self):
        ss, rs = self.sems[4:6]
        return pltpu.make_async_remote_copy(
            src_ref=self.tot, dst_ref=self.zo, send_sem=ss.at[1], recv_sem=rs.at[1],
            device_id=(self.d ^ 3, self.f), device_id_type=MESH,
        )

    def to_outer(self):
        ss, rs = self.sems[4:6]
        return pltpu.make_async_remote_copy(
            src_ref=self.out, dst_ref=self.out, send_sem=ss.at[2], recv_sem=rs.at[2],
            device_id=(self.d ^ 1, self.f), device_id_type=MESH,
        )

    def tiles(self):
        for c in self.cps:
            c.wait()
        val = self.near[self.me].astype(jnp.float32)
        for k in (1, 2, 3):
            val = val + self.fars[k].astype(jnp.float32)
        self.tot[...] = val.astype(self.tot.dtype)

        @pl.when(self.d % 3 == 0)
        def _():
            self.to_inner().start()

    def middle(self):
        @pl.when(self.d % 3 > 0)
        def _():
            self.to_inner().wait_recv()
            val = self.tot[...].astype(jnp.float32) + self.zin[...].astype(jnp.float32)
            self.tot[...] = val.astype(self.tot.dtype)
            self.across().start()

    def last(self):
        @pl.when(self.d % 3 > 0)
        def _():
            self.across().wait_recv()
            val = self.tot[...].astype(jnp.float32) + self.zo[...].astype(jnp.float32)
            self.out[...] = val.astype(self.out.dtype)
            self.to_outer().start()

    def done(self):
        @pl.when(self.d % 3 == 0)
        def _():
            self.to_inner().wait_send()
            self.to_outer().wait_recv()

        @pl.when(self.d % 3 > 0)
        def _():
            self.across().wait_send()
            self.to_outer().wait_send()


def reduce_scratch(block):
    V, b16 = pltpu.VMEM, jnp.bfloat16
    return [V((4,) + block, b16), V((4,) + block, b16), V(block, b16), V(block, b16), V(block, b16)] + [DMA((4,))] * 6


def wide(row, n):
    return jnp.concatenate([row] * n, axis=1)


def bottleneck_back_kernel(
    x_ref, ins_ref, st_ref, gr, gd, ge, dy, dpt, y_ref, pm_in, wp, n3, l3, we, n2, l2, h2, wd, ext, n1, l1, wr, key_any,
    gf_o, pm_o, ex_o, di_o, re_o, s3_o, s2_o, s1_o,
    pm, ex, di, re_, dp3, d3, acc, ext2, d1n, key, gf, pick, ksem, hs, hr, gs,
    *sems,
):
    sems = list(sems)

    def take(n):
        got = sems[:n]
        del sems[:n]
        return got

    f, d = greet(range(1, 8), range(1, 4))
    N, C = x_ref.shape
    Q, h = ext2.shape[0], ext2.shape[1] // 2
    e = h // 2
    rows = h // 4
    neck = acc.shape[1]
    nb = neck // 8
    nw = pm.shape[0] // 8
    W = dpt.shape[1]

    def ds(i, n):
        return pl.ds(pl.multiple_of(n * i, n), n)

    def reducer(full, part, out):
        near, far, tot, zin, zo = take(5)
        return Reduce(full, part, near, far, tot, zin, zo, out, take(6), d, f)

    r_pm = reducer(pm, lambda g: (ds(g, nw),), pm_o)
    r_ex = reducer(ex, lambda g: (slice(None), ds(g, C // 8)), ex_o)
    r_di = [
        reducer(di.at[pl.ds(3 * i, 3)], lambda g: (slice(None), ds(g, nb)), di_o.at[pl.ds(3 * i, 3)]) for i in range(3)
    ]
    r_re = reducer(re_, lambda g: (ds(g, nb),), re_o)
    sum3, sum2, sum1 = (Sum(take(6), d, f) for _ in range(3))

    kcp = pltpu.make_async_copy(key_any.at[:, pl.ds(pl.multiple_of(PAD - e + h * f, 16), 2 * h), :], key, ksem)
    kcp.start()
    count = st_ref[0:1, 0:1]
    for c in range(0, C, 256):
        pm[:, c : c + 256] = tn_dot(dpt[...], y_ref[:, c : c + 256]).astype(jnp.bfloat16)
    pm[:, C:] = pm_in[...]
    r_pm.pair()
    ones, crossed = [], []
    ins = wide(ins_ref[...], 2)
    for c in range(0, C, 256):
        w = slice(c, c + 256)
        v = dy[:, w].astype(jnp.float32) + nn_dot(dpt[...], wp[:, w])
        v = v * l3[:, w].astype(jnp.float32)
        dp3[:, w] = v.astype(jnp.bfloat16)
        v = v * ins
        ones.append(jnp.sum(v, axis=0, keepdims=True))
        crossed.append(jnp.sum(v * n3[:, w].astype(jnp.float32), axis=0, keepdims=True))
    sum3.start([cat_rows(ones), cat_rows(crossed)])
    order = lax.broadcasted_iota(jnp.int32, (N, N), 1)
    m, r, q = order % 4, (order // 4) % rows, order // h
    hit = (r * (N // rows) + q * 4 + m) == lax.broadcasted_iota(jnp.int32, (N, N), 0)
    pick[...] = hit.astype(jnp.float32).astype(jnp.bfloat16)
    sum3.turn()
    r_pm.far()
    tot = sum3.result()
    s3_o[...] = tot
    for c in range(0, C, 256):
        w = slice(c, c + 256)
        v = dp3[:, w].astype(jnp.float32) - tot[0:1, w] / count - n3[:, w].astype(jnp.float32) * (tot[1:2, w] / count)
        d3[:, w] = (ins * v * (ge[:, w] * st_ref[3:4, w])).astype(jnp.bfloat16)
    ones, crossed = [], []
    for c in range(0, neck, 256):
        w = slice(c, c + 256)
        v = nt_dot(d3[...], we[w, :]) * l2[:, w].astype(jnp.float32)
        acc[:, w] = v
        v = v * ins
        ones.append(jnp.sum(v, axis=0, keepdims=True))
        crossed.append(jnp.sum(v * n2[:, w].astype(jnp.float32), axis=0, keepdims=True))
    sum2.start([cat_rows(ones), cat_rows(crossed)])
    for c in range(0, C, 256):
        ex[:, c : c + 256] = tn_dot(h2[...], d3[:, c : c + 256]).astype(jnp.bfloat16)
    sum2.turn()
    r_ex.pair()
    tot = sum2.result()
    s2_o[...] = tot
    for c in range(0, neck, 256):
        w = slice(c, c + 256)
        v = acc[:, w] - tot[0:1, w] / count - n2[:, w].astype(jnp.float32) * (tot[1:2, w] / count)
        v = ins * v * (gd[:, w] * st_ref[2:3, w])
        ext2[:, e : e + h, w] = v.astype(jnp.bfloat16).reshape(Q, h, 256)
    up = remote(ext2.at[:, pl.ds(e, e)], ext2.at[:, pl.ds(e + h, e)], hs.at[0], hr.at[0], d, lax.rem(f + 7, 8))
    down = remote(ext2.at[:, pl.ds(h, e)], ext2.at[:, pl.ds(0, e)], hs.at[1], hr.at[1], d, lax.rem(f + 1, 8))
    kcp.wait()
    r_pm.tiles()
    r_ex.far()
    for i in range(3):
        for j in range(3):
            lo, hi = span(j - 1, Q)
            ok = same_crop(
                key[lo:hi, e : e + h, :], key[lo + j - 1 : hi + j - 1, e * i : e * i + h, :], neck
            )
            v = jnp.where(ok, ext[lo + j - 1 : hi + j - 1, e * i : e * i + h, :], 0).reshape((hi - lo) * h, neck)
            g = ext2[lo:hi, e : e + h, :].reshape((hi - lo) * h, neck)
            di[3 * i + j] = tn_dot(g, v).astype(jnp.bfloat16)
        r_di[i].pair()
    up.wait()
    r_pm.middle()
    down.wait()
    acc[...] = jnp.zeros_like(acc)
    for i in range(3):
        for j in (1, 0, 2):
            lo, hi = span(1 - j, Q)
            ok = same_crop(
                key[lo:hi, e : e + h, :], key[lo + 1 - j : hi + 1 - j, e * (2 - i) : e * (2 - i) + h, :], neck
            )
            v = jnp.where(ok, ext2[lo + 1 - j : hi + 1 - j, e * (2 - i) : e * (2 - i) + h, :], 0)
            v = v.reshape((hi - lo) * h, neck)
            for c in range(0, neck, 256):
                acc[lo * h : hi * h, c : c + 256] += nn_dot(v, wd[3 * i + j, :, c : c + 256])
    ones, crossed = [], []
    for c in range(0, neck, 256):
        w = slice(c, c + 256)
        v = acc[:, w] * l1[:, w].astype(jnp.float32)
        acc[:, w] = v
        v = v * ins
        ones.append(jnp.sum(v, axis=0, keepdims=True))
        crossed.append(jnp.sum(v * n1[:, w].astype(jnp.float32), axis=0, keepdims=True))
    sum1.start([cat_rows(ones), cat_rows(crossed)])
    for r in r_di:
        r.far()
    sum1.turn()
    r_pm.last()
    r_ex.tiles()
    tot = sum1.result()
    s1_o[...] = tot
    for c in range(0, neck, 256):
        w = slice(c, c + 256)
        v = acc[:, w] - tot[0:1, w] / count - n1[:, w].astype(jnp.float32) * (tot[1:2, w] / count)
        v = (ins * v * (gr[:, w] * st_ref[1:2, w])).astype(jnp.bfloat16)
        d1n[:, w] = nn_dot(pick[...], v).astype(jnp.bfloat16)
    for c in range(0, C, 256):
        re_[:, c : c + 256] = tn_dot(d1n[...], x_ref[:, c : c + 256]).astype(jnp.bfloat16)
    r_re.pair()
    r_di[0].tiles()
    r_re.far()
    r_ex.middle()
    out = []
    for n, c in enumerate(range(0, C, 256)):
        w = slice(c, c + 256)
        if n >= 2:
            out[n - 2].wait()
        gf[n % 2] = nn_dot(pick[...], dp3[:, w]) + nn_dot(d1n[...], wr[:, w])
        cp = pltpu.make_async_copy(gf.at[n % 2], gf_o.at[:, pl.ds(c, 256)], gs.at[n % 2])
        cp.start()
        out.append(cp)
        if n == 1:
            r_di[0].middle()
            r_ex.last()
        if n == 3:
            r_di[1].tiles()
            r_di[0].last()
        if n == 5:
            r_di[1].middle()
        if n == 7:
            r_di[2].tiles()
            r_di[1].last()
    r_di[2].middle()
    r_re.tiles()
    r_di[2].last()
    r_re.middle()
    r_re.last()
    out[-2].wait()
    out[-1].wait()
    for r in [r_pm, r_ex, r_re] + r_di:
        r.done()


def bottleneck_back(*args):
    x, st, dpt, pm_in, h2 = args[0], args[2], args[7], args[9], args[16]
    N, C = x.shape
    Q, h2_, neck = args[18].shape
    h = h2_ // 2
    W = dpt.shape[1]
    PM = C + pm_in.shape[1]
    b16, f32 = jnp.bfloat16, jnp.float32
    S, V = jax.ShapeDtypeStruct, pltpu.VMEM
    blocks = [(W // 8, PM), (neck, C // 8), (9, neck // 8, neck), (neck // 8, C)]
    scratch = [
        V((W, PM), b16), V((neck, C), b16), V((9, neck, neck), b16), V((neck, C), b16), V((N, C), b16), V((N, C), b16),
        V((N, neck), f32), V((Q, 2 * h, neck), b16), V((N, neck), b16), V((Q, 2 * h, 128), b16), V((2, N, 256), f32),
        V((N, N), b16), DMA(()), DMA((2,)), DMA((2,)), DMA((2,)),
    ]
    for n in (0, 1, 2, 2, 2, 3):
        scratch += reduce_scratch((3,) + blocks[2][1:] if n == 2 else blocks[n])
    scratch += sum_sems(2, C) + sum_sems(2, neck) + sum_sems(2, neck)
    return pl.pallas_call(
        bottleneck_back_kernel,
        out_shape=[S((N, C), f32)] + [S(b, b16) for b in blocks] + [S((2, C), f32), S((2, neck), f32), S((2, neck), f32)],
        in_specs=[VM] * 22 + [ANY],
        out_specs=[ANY] + [VM] * 7,
        scratch_shapes=scratch,
        compiler_params=pltpu.CompilerParams(collective_id=12, has_side_effects=True, vmem_limit_bytes=VLIM),
        name="bottleneck_back",
    )(*args)


def spaced_taps(src, key, kernels, acc, base, h, steps, sign, first_lane, dot, b):
    Q = key.shape[0]
    s = sign * steps[b]
    W = kernels.shape[1] if sign < 0 else src.shape[2]
    lanes = slice(first_lane, first_lane + W)
    for n, j in enumerate((0, -1, 1)):
        lo, hi = span(s * j, Q)
        here = key[lo:hi, pl.ds(base, h), :]
        got = None
        for i in (-1, 0, 1):
            at = pl.multiple_of(base + 16 * s * i, 16)
            ok = same_crop(here, key[lo + s * j : hi + s * j, pl.ds(at, h), :], W)
            v = jnp.where(ok, src[lo + s * j : hi + s * j, pl.ds(at, h), lanes], 0).reshape((hi - lo) * h, W)
            r = dot(v, kernels[9 * b + 3 * (i + 1) + j + 1])
            got = r if got is None else got + r
        if n == 0 and sign > 0:
            acc[...] = got
        else:
            acc[lo * h : hi * h] += got


def head_kernel(
    steps, yo, key, kern, y, wp, wm, wc, ins_ref, kb, lab, st_ref, gb, bb, gm, bm,
    lo_o, dp_o, dr_o, pm_o, pooled_o, dpool_o, size_o, sb_o, sm_o,
    acc, near, mine, far, ab, nb, lb, joined, nm, lm, merged, pn, ps, pr, ss, rs,
    *sems,
):
    sems = list(sems)
    f, d = greet(range(1, 8), range(1, 4))
    sum_b, sum_m, back_m, back_b = (Sum(sems[6 * n : 6 * n + 6], d, f) for n in range(4))
    Q, h = pn.shape[1], pn.shape[2]
    N = Q * h
    w = yo.shape[2]
    W = wp.shape[0]
    T = 8 * h
    c0 = f % 2
    me = f // 2
    f32, b16 = jnp.float32, jnp.bfloat16

    def step(n, _):
        k = 3 - n
        g = me ^ k
        for turn in range(2):
            dest = 2 * g + (1 - c0 if turn == 0 else c0)
            base = pl.multiple_of(PAD + h * dest, 16)
            if turn == 1:
                pltpu.make_async_remote_copy(
                    src_ref=pn.at[k], dst_ref=near.at[k], send_sem=ps.at[k], recv_sem=pr.at[k],
                    device_id=(d, f ^ 1), device_id_type=MESH,
                ).wait_recv()
            for b in range(3):
                lanes = slice(b * W, (b + 1) * W)
                spaced_taps(yo, key, kern, acc, base, h, steps, 1, 0, nt_dot, b)
                if turn == 0:
                    pn[k, :, :, lanes] = acc[...].astype(b16).reshape(Q, h, W)
                else:
                    val = acc[...] + near[k, :, :, lanes].astype(f32).reshape(N, W)
                    mine[k, :, :, lanes] = val.astype(b16).reshape(Q, h, W)
            if turn == 0:
                remote(pn.at[k], near.at[k], ps.at[k], pr.at[k], d, f ^ 1)
            else:

                @pl.when(k > 0)
                def _():
                    remote(mine.at[k], far.at[k], ss.at[k], rs.at[k], d, f ^ (2 * k))

        return 0

    lax.fori_loop(0, 4, step, 0)
    ab[:, :W] = nt_dot(y[...], wp[...])
    crop = (lax.broadcasted_iota(jnp.int32, (T, 128), 1) + 1).astype(f32)

    def crops(q, carry):
        total, size = carry
        one = (key[q, PAD : PAD + T, :].astype(f32) == crop).astype(f32).astype(b16)
        return total + tn_dot(one, yo[q, PAD : PAD + T, :]), size + tn_dot(one, jnp.ones((T, 128), b16))

    total, size = lax.fori_loop(0, Q, crops, (jnp.zeros((128, w), f32), jnp.zeros((128, 128), f32)))
    size = jnp.where(size > 0, size, 1.0)[:8]
    size_o[...] = size
    pooled = (total[:8] / size[:, :1]).astype(b16)
    pooled_o[...] = pooled
    part = nt_dot(pooled, kern[27])
    part = cat_rows([part[c : c + 1] for c in range(CROPS_TILE)])
    ins = wide(ins_ref[...], 2)
    for k in (3, 1, 2):
        pltpu.make_async_remote_copy(
            src_ref=mine.at[k], dst_ref=far.at[k], send_sem=ss.at[k], recv_sem=rs.at[k],
            device_id=(d, f ^ (2 * k)), device_id_type=MESH,
        ).wait()
    ones, squares = [], []
    for b in range(4):
        lanes = slice(b * W, (b + 1) * W)
        if b:
            src = slice((b - 1) * W, b * W)
            v = mine[0, :, :, src].astype(f32)
            for k in (1, 2, 3):
                v = v + far[k, :, :, src].astype(f32)
            ab[:, lanes] = v.reshape(N, W)
        s, t = column_sums(ab[:, lanes], ins_ref[...])
        ones.append(s)
        squares.append(t)
    sum_b.start([cat_rows(ones), cat_rows(squares), part])
    for k in range(4):
        pltpu.make_async_remote_copy(
            src_ref=pn.at[k], dst_ref=near.at[k], send_sem=ps.at[k], recv_sem=pr.at[k],
            device_id=(d, f ^ 1), device_id_type=MESH,
        ).wait_send()
    sum_b.turn()
    pool_act = sum_b.b2[d, 2:3, :]
    pool, pool_lean = bend(pool_act)
    pool = pool.astype(b16).astype(f32)
    here = wide(kb[...].astype(f32), W // 128)
    v = jnp.zeros((N, W), f32)
    for c in range(CROPS_TILE):
        v = jnp.where(here == c + 1.0, pool[:, c * W : (c + 1) * W], v)
    joined[:, 4 * W :] = v.astype(b16)
    tot = sum_b.result()
    count = st_ref[0:1, 0:1]
    mean = tot[0:1] / count
    inv_b = lax.rsqrt(tot[1:2] / count - mean * mean + eps)
    for b in range(4):
        lanes = slice(b * W, (b + 1) * W)
        n = (ab[:, lanes] - mean[:, lanes]) * inv_b[:, lanes]
        act, lean = bend(n * gb[:, lanes] + bb[:, lanes])
        joined[:, lanes] = act.astype(b16)
        nb[:, lanes] = n.astype(b16)
        lb[:, lanes] = lean.astype(b16)
    am = nt_dot(joined[...], wm[...])
    s, t = column_sums(am, ins_ref[...])
    sum_m.start([s, t])
    sum_m.turn()
    tot = sum_m.result()
    mean = tot[0:1] / count
    inv_m = lax.rsqrt(tot[1:2] / count - mean * mean + eps)
    n = (am - mean) * inv_m
    act, lean = bend(n * gm[...] + bm[...])
    merged[...] = act.astype(b16)
    nm[...] = n
    lm[...] = lean
    logits = nn_dot(merged[...], wc[...])
    lane = lax.broadcasted_iota(jnp.int32, (N, 128), 1)
    valid = lane < CLASSES
    top = jnp.max(jnp.where(valid, logits, -jnp.inf), axis=1, keepdims=True)
    ex = jnp.where(valid, jnp.exp(logits - top), 0.0)
    prob = ex / jnp.sum(ex, axis=1, keepdims=True)
    target = (lab[...] == lane.astype(f32)).astype(f32)
    dl = (ins_ref[...] * (prob - target) / count).astype(b16)
    e = nt_dot(dl, wc[...]) * lm[...]
    m = e * ins
    back_m.start([jnp.sum(m, axis=0, keepdims=True), jnp.sum(m * nm[...], axis=0, keepdims=True)])
    order = lax.broadcasted_iota(jnp.int32, (N, N), 1)
    rows = h // 4
    mm, r, q = order % 4, (order // 4) % rows, order // h
    hit = (r * (N // rows) + q * 4 + mm) == lax.broadcasted_iota(jnp.int32, (N, N), 0)
    lo_o[...] = nn_dot(hit.astype(f32).astype(b16), logits.astype(b16)).astype(b16)
    back_m.turn()
    J = joined.shape[1]
    pm_o[:, J : J + 128] = tn_dot(merged[...], dl).astype(b16)
    pm_o[:, J + 128 :] = jnp.zeros((W, pm_o.shape[1] - J - 128), b16)
    tot = back_m.result()
    sm_o[...] = tot
    dm = (ins * gm[...] * inv_m * (e - tot[0:1] / count - nm[...] * (tot[1:2] / count))).astype(b16)
    ones, crossed = [], []
    for b in range(4):
        lanes = slice(b * W, (b + 1) * W)
        v = nn_dot(dm, wm[:, lanes]) * lb[:, lanes].astype(f32)
        ab[:, lanes] = v
        v = v * ins
        ones.append(jnp.sum(v, axis=0, keepdims=True))
        crossed.append(jnp.sum(v * nb[:, lanes].astype(f32), axis=0, keepdims=True))
    v = nn_dot(dm, wm[:, 4 * W :])
    part = cat_rows(
        [jnp.sum(jnp.where(here == c + 1.0, v, 0.0), axis=0, keepdims=True) for c in range(CROPS_TILE)]
    )
    back_b.start([cat_rows(ones), cat_rows(crossed), part])
    pm_o[:, :J] = tn_dot(dm, joined[...]).astype(b16)
    back_b.turn()
    v = (back_b.b2[d, 2:3, :] * pool_lean).astype(b16)
    dpool_o[...] = jnp.zeros_like(dpool_o)
    for c in range(CROPS_TILE):
        dpool_o[c : c + 1, :] = v[:, c * W : (c + 1) * W]
    tot = back_b.result()
    sb_o[...] = tot[:2]
    for b in range(4):
        lanes = slice(b * W, (b + 1) * W)
        v = ab[:, lanes] - tot[0:1, lanes] / count - nb[:, lanes].astype(f32) * (tot[1:2, lanes] / count)
        v = (ins * v * (gb[:, lanes] * inv_b[:, lanes])).astype(b16)
        if b:
            dr_o[:, :, (b - 1) * W : b * W] = v.reshape(Q, h, W)
        else:
            dp_o[...] = v


def head(steps, width, *args):
    yo, key, kern, y, wp, wm = args[:6]
    N, C = y.shape
    Q = yo.shape[0]
    h = N // Q
    W = wp.shape[0]
    J = wm.shape[1]
    b16, f32 = jnp.bfloat16, jnp.float32
    S, V = jax.ShapeDtypeStruct, pltpu.VMEM
    return pl.pallas_call(
        functools.partial(head_kernel, steps),
        out_shape=[
            S((N, 128), b16), S((N, W), b16), S((Q, h, 3 * W), b16), S((W, width), b16), S((8, C // 8), b16),
            S((8, W), b16), S((8, 128), f32), S((2, 4 * W), f32), S((2, W), f32),
        ],
        in_specs=[VM] * 15,
        out_specs=[VM] * 9,
        scratch_shapes=[V((N, W), f32)]
        + [V((4, Q, h, 3 * W), b16)] * 3
        + [
            V((N, 4 * W), f32), V((N, 4 * W), b16), V((N, 4 * W), b16), V((N, J), b16), V((N, W), f32), V((N, W), f32),
            V((N, W), b16), V((4, Q, h, 3 * W), b16), DMA((4,)), DMA((4,)), DMA((4,)), DMA((4,)),
        ]
        + sum_sems(3, 4 * W) + sum_sems(2, W) + sum_sems(2, W) + sum_sems(3, 4 * W),
        compiler_params=pltpu.CompilerParams(collective_id=5, has_side_effects=True, vmem_limit_bytes=VLIM),
        name="head",
    )(*args)


def widen_kernel(gk, pm, ex, di, re_, k0, k1, k2, pool, point, merge, dilated, expand, reduce_):
    for b, o in enumerate((k0, k1, k2)):

        def tap(t, _):
            o[t] = gk[9 * b + t].astype(jnp.float32)
            return 0

        lax.fori_loop(0, 9, tap, 0)
    pool[...] = gk[27].astype(jnp.float32)
    C = point.shape[1]
    point[...] = pm[:, :C].astype(jnp.float32)
    merge[...] = pm[:, C : C + merge.shape[1]].astype(jnp.float32)

    def rows(t, _):
        dilated[t] = di[t].astype(jnp.float32)
        return 0

    lax.fori_loop(0, 9, rows, 0)
    expand[...] = ex[...].astype(jnp.float32)
    reduce_[...] = re_[...].astype(jnp.float32)


def widen(gk, pm, ex, di, re_, J):
    _, o, C = gk.shape
    shapes = [(9, o, C)] * 3 + [(o, C), (o, C), (o, J), di.shape, ex.shape, re_.shape]
    return pl.pallas_call(
        widen_kernel,
        out_shape=[jax.ShapeDtypeStruct(v, jnp.float32) for v in shapes],
        in_specs=[VM] * 5,
        out_specs=[VM] * 9,
        compiler_params=pltpu.CompilerParams(vmem_limit_bytes=VLIM),
        name="widen",
    )(gk, pm, ex, di, re_)


def norm_coeffs(totals, squares, count):
    average = totals / count
    return average, lax.rsqrt(squares / count - average * average + eps)


def fast_body(
    features, crop_ids, labels, w_reduce, gain_reduce, bias_reduce, w_dilated, gain_dilated, bias_dilated,
    w_expand, gain_expand, bias_expand, w_point, gain_point, bias_point, w_rate, gain_rate, bias_rate,
    w_rate_double, gain_rate_double, bias_rate_double, w_rate_triple, gain_rate_triple, bias_rate_triple,
    w_pool, w_merge, gain_merge, bias_merge, w_classes,
):
    rows, cols, C = features.shape
    Q = cols // 4
    h = rows * 4
    N = rows * cols
    nf = lax.axis_size("fsdp")
    W = gain_point.shape[0]
    steps = (RATE // 4, 2 * RATE // 4, 3 * RATE // 4)
    place = lax.axis_index("fsdp")

    def perm(a):
        a = a.reshape((rows, Q, 4) + a.shape[2:])
        return jnp.swapaxes(a, 0, 1).reshape((N,) + a.shape[3:])

    def unperm(a):
        a = a.reshape((Q, rows, 4) + a.shape[1:])
        return jnp.swapaxes(a, 0, 1).reshape((rows, cols) + a.shape[3:])

    local_crop = perm(crop_ids) - lax.axis_index("dp") * CROPS_TILE
    in_crop = perm(crop_ids) >= 0
    inside = in_crop.astype(jnp.float32)[:, None]
    key_loc = jnp.where(in_crop, local_crop + 1, 0)
    kb = jnp.broadcast_to(key_loc.astype(jnp.bfloat16)[:, None], (N, 128))
    key_row = jnp.pad(key_loc.astype(jnp.float32).reshape(Q, h), ((0, 0), (0, 128 - h)))
    ins = jnp.broadcast_to(inside, (N, 128))
    rates = [jnp.swapaxes(w.reshape(9, C, -1), 1, 2) for w in (w_rate, w_rate_double, w_rate_triple)]
    vecs = [v[None, :] for v in (gain_reduce, bias_reduce, gain_dilated, bias_dilated, gain_expand, bias_expand)]
    (
        y_own, y, n_three, l_three, n_one, l_one, n_two, l_two, ext, h_two, key, kernel,
        wr, wd, full_expand, wp, wm, wc, count,
    ) = bottleneck(
        features.reshape(N, C), key_row, ins, vecs,
        [
            w_reduce.T, jnp.swapaxes(w_dilated.reshape(9, w_dilated.shape[2], -1), 1, 2), w_expand, w_point.T, w_merge.T,
            jnp.pad(w_classes, ((0, 0), (0, 128 - CLASSES))),
        ],
        rates + [w_pool.T[None]],
    )
    neck = gain_reduce.shape[0]
    stats = count
    count = count[0, 0]
    y = y.reshape(N, C)
    g_br = jnp.concatenate([gain_point, gain_rate, gain_rate_double, gain_rate_triple])[None]
    b_br = jnp.concatenate([bias_point, bias_rate, bias_rate_double, bias_rate_triple])[None]
    lab = jnp.broadcast_to(perm(labels).astype(jnp.float32)[:, None], (N, 128))
    J = wm.shape[1]
    width = J + 128 + -(C + J + 128) % 512
    logits, d_point, d_rates, rest, pooled, d_pool, sizes, st_br, st_m = head(
        steps, width, y_own, key, kernel, y, wp, wm, wc, ins, kb, lab, stats, g_br, b_br,
        gain_merge[None], bias_merge[None],
    )
    class_logits = logits[:, :CLASSES].reshape(rows, cols, CLASSES)
    gb_br, gg_br = st_br[0], st_br[1]
    gb_merge, gg_merge = st_m[0], st_m[1]
    d_y, grad_k = branches_back(d_rates, y_own, key, kernel, pooled, d_pool, sizes, steps)
    grad_features, pm, ex, di, re_, st3, st2, st1 = bottleneck_back(
        features.reshape(N, C), ins, stats, vecs[0], vecs[2], vecs[4], d_y.reshape(N, C), d_point, y, rest, wp,
        n_three, l_three, full_expand, n_two, l_two, h_two, wd, ext, n_one, l_one, wr, key,
    )
    grad_classes = pm[:, C + J : C + J + CLASSES].astype(jnp.float32)
    *grad_k, grad_pool, grad_point, grad_merge, grad_dilated, grad_expand, grad_reduce = widen(grad_k, pm, ex, di, re_, J)
    grad_k = [jnp.swapaxes(v.reshape(3, 3, -1, C), 2, 3) for v in grad_k]
    grad_pool, grad_point, grad_merge, grad_reduce = grad_pool.T, grad_point.T, grad_merge.T, grad_reduce.T
    grad_dilated = jnp.swapaxes(grad_dilated, 1, 2).reshape(3, 3, neck, -1)
    grad_features = grad_features.reshape(rows, cols, C)
    gg_expand, gb_expand, gg_dilated, gb_dilated, gg_reduce, gb_reduce = st3[1], st3[0], st2[1], st2[0], st1[1], st1[0]
    return (
        class_logits,
        grad_features,
        grad_reduce, gg_reduce, gb_reduce,
        grad_dilated, gg_dilated, gb_dilated,
        grad_expand, gg_expand, gb_expand,
        grad_point, gg_br[:W], gb_br[:W],
        grad_k[0], gg_br[W : 2 * W], gb_br[W : 2 * W],
        grad_k[1], gg_br[2 * W : 3 * W], gb_br[2 * W : 3 * W],
        grad_k[2], gg_br[3 * W :], gb_br[3 * W :],
        grad_pool,
        grad_merge, gg_merge, gb_merge,
        grad_classes,
    )


def passed_along(value, axis, by):
    count = lax.axis_size(axis)
    pairs = [(i, i + by) for i in range(count) if 0 <= i + by < count]
    return lax.ppermute(value, axis, pairs)


def padded(cells, sides, width):
    for axis, dim in sides:
        count = lax.axis_size(axis)
        ends = count - 1
        head = lax.slice_in_dim(cells, 0, width, axis=dim)
        tail = lax.slice_in_dim(cells, cells.shape[dim] - width, cells.shape[dim], axis=dim)
        cells = jnp.concatenate(
            [
                lax.ppermute(tail, axis, [(i, (i + 1) % count) for i in range(ends)]),
                cells,
                lax.ppermute(head, axis, [((i + 1) % count, i) for i in range(ends)]),
            ],
            axis=dim,
        )
    return cells


def flat_dot(first_op, second_op):
    return jnp.dot(first_op, second_op, preferred_element_type=jnp.float32)


def inner_dot(first_op, second_op):
    return lax.dot_general(
        first_op, second_op, (((0,), (0,)), ((), ())), preferred_element_type=jnp.float32
    )


def outer_dot(first_op, second_op):
    return lax.dot_general(
        first_op, second_op, (((1,), (1,)), ((), ())), preferred_element_type=jnp.float32
    )


def slope(values):
    gate_value = jax.nn.sigmoid(values)
    return gate_value * (1.0 + values * (1.0 - gate_value))


def widen_rows(values, extent, mover):
    row_count = values.shape[0]
    neighbours = -(-extent // row_count)
    above = [mover(values, distance) for distance in range(neighbours, 0, -1)]
    below = [mover(values, -distance) for distance in range(1, neighbours + 1)]
    stacked = jnp.concatenate(above + [values] + below, axis=0)
    start_row = neighbours * row_count - extent
    return stacked[start_row : start_row + row_count + 2 * extent]


def rim_slice(widened, spacing, margin, height):
    return widened[margin - spacing : margin + height + spacing]


def offset_table(broad_key_rows, crop_random_keys, spacing, margin):
    height, breadth = crop_random_keys.shape
    first_row = margin - spacing
    extended = jnp.pad(
        broad_key_rows[first_row : first_row + height + 2 * spacing], ((0, 0), (spacing, spacing))
    )
    tables = []
    for row_tap in range(3):
        for col_tap in range(3):
            nearby = extended[
                row_tap * spacing : row_tap * spacing + height,
                col_tap * spacing : col_tap * spacing + breadth,
            ]
            tables.append(
                ((nearby == crop_random_keys) & (crop_random_keys > 0))
                .astype(jnp.float32)
                .reshape(height * breadth, 1)
            )
    return tables


def spread_offsets(widened, kernel, tables, spacing, height, breadth):
    channels = widened.shape[2]
    extended = jnp.pad(widened, ((0, 0), (spacing, spacing), (0, 0)))
    summed = jnp.zeros((height * breadth, kernel.shape[3]), jnp.float32)
    for row_tap in range(3):
        for col_tap in range(3):
            nearby = extended[
                row_tap * spacing : row_tap * spacing + height,
                col_tap * spacing : col_tap * spacing + breadth,
            ]
            summed = summed + tables[3 * row_tap + col_tap] * flat_dot(
                nearby.reshape(height * breadth, channels), kernel[row_tap, col_tap]
            )
    return summed


def collect_taps(widened, kernel, tables, spacing, height, breadth):
    channels = widened.shape[2]
    extended = jnp.pad(widened, ((0, 0), (spacing, spacing), (0, 0)))
    summed = jnp.zeros((height * breadth, kernel.shape[2]), jnp.float32)
    for row_tap in range(3):
        for col_tap in range(3):
            back_row = 2 - row_tap
            back_col = 2 - col_tap
            nearby = extended[
                back_row * spacing : back_row * spacing + height,
                back_col * spacing : back_col * spacing + breadth,
            ]
            summed = summed + tables[3 * back_row + back_col] * outer_dot(
                nearby.reshape(height * breadth, channels), kernel[row_tap, col_tap]
            )
    return summed


def kernel_offsets(widened, grads_low, tables, spacing, height, breadth):
    channels = widened.shape[2]
    extended = jnp.pad(widened, ((0, 0), (spacing, spacing), (0, 0)))
    pieces = []
    for row_tap in range(3):
        for col_tap in range(3):
            nearby = extended[
                row_tap * spacing : row_tap * spacing + height,
                col_tap * spacing : col_tap * spacing + breadth,
            ]
            masked = (tables[3 * row_tap + col_tap] * grads_low).astype(jnp.bfloat16)
            pieces.append(inner_dot(nearby.reshape(height * breadth, channels), masked))
    return pieces


def statistics(partial_value):
    return lax.psum(partial_value, ("dp", "fsdp"))


def norm_apply(values, totals, squares, pixel_count, factor, offset):
    average = totals / pixel_count
    inverse = lax.rsqrt(squares / pixel_count - average * average + eps)
    normed = (values - average) * inverse
    return (normed * factor + offset, normed, inverse)


def norm_forward(values, inside, pixel_count, factor, offset):
    totals, squares = statistics(
        (jnp.sum(values * inside, axis=0), jnp.sum(values * values * inside, axis=0))
    )
    return norm_apply(values, totals, squares, pixel_count, factor, offset)


def norm_backward(upstream, normed, inverse, factor, inside, pixel_count):
    totals, crossed = lax.psum(
        (jnp.sum(upstream * inside, axis=0), jnp.sum(upstream * normed * inside, axis=0)),
        ("dp", "fsdp"),
    )
    passed = (
        inside
        * factor
        * inverse
        * (upstream - totals / pixel_count - normed * crossed / pixel_count)
    )
    return (passed, crossed, totals)


def body(
    features,
    crop_ids,
    labels,
    w_reduce,
    gain_reduce,
    bias_reduce,
    w_dilated,
    gain_dilated,
    bias_dilated,
    w_expand,
    gain_expand,
    bias_expand,
    w_point,
    gain_point,
    bias_point,
    w_rate,
    gain_rate,
    bias_rate,
    w_rate_double,
    gain_rate_double,
    bias_rate_double,
    w_rate_triple,
    gain_rate_triple,
    bias_rate_triple,
    w_pool,
    w_merge,
    gain_merge,
    bias_merge,
    w_classes,
):
    local_rows, local_columns, channels = features.shape
    pixel_values = local_rows * local_columns
    inputs_flat = features.reshape(pixel_values, channels)
    crop_random_keys = crop_ids + 1
    outer_extent = 3 * RATE
    spacings = (RATE, 2 * RATE, 3 * RATE)
    broad_key_rows = widen_rows(
        crop_random_keys,
        outer_extent,
        lambda piece, distance: passed_along(piece, "fsdp", distance),
    )
    inside = (crop_random_keys > 0).astype(jnp.float32).reshape(pixel_values, 1)
    inner_neck = offset_table(broad_key_rows, crop_random_keys, DILATION_SPAN, outer_extent)
    near_rates = [
        offset_table(broad_key_rows, crop_random_keys, spacing, outer_extent)
        for spacing in spacings
    ]
    (
        full_reduce,
        complete_dilated,
        full_expand,
        full_point,
        full_rate,
        full_double,
        full_triple,
        full_pool,
        full_merge,
        full_classes,
    ) = (
        lax.all_gather(w_reduce, "fsdp", axis=1, tiled=True),
        lax.all_gather(w_dilated, "fsdp", axis=3, tiled=True),
        lax.all_gather(w_expand, "fsdp", axis=1, tiled=True),
        lax.all_gather(w_point, "fsdp", axis=1, tiled=True),
        lax.all_gather(w_rate, "fsdp", axis=3, tiled=True),
        lax.all_gather(w_rate_double, "fsdp", axis=3, tiled=True),
        lax.all_gather(w_rate_triple, "fsdp", axis=3, tiled=True),
        lax.all_gather(w_pool, "fsdp", axis=1, tiled=True),
        lax.all_gather(w_merge, "fsdp", axis=1, tiled=True),
        lax.all_gather(w_classes, "fsdp", axis=0, tiled=True),
    )
    rate_kernels = (full_rate, full_double, full_triple)
    rate_gains = (gain_rate, gain_rate_double, gain_rate_triple)
    rate_biases = (bias_rate, bias_rate_double, bias_rate_triple)
    act_one = flat_dot(inputs_flat, full_reduce)
    totals, squares, pixel_count = statistics(
        (
            jnp.sum(act_one * inside, axis=0),
            jnp.sum(act_one * act_one * inside, axis=0),
            jnp.sum(inside),
        )
    )
    pre_one, normed_one, inverse_one = norm_apply(
        act_one, totals, squares, pixel_count, gain_reduce, bias_reduce
    )
    first_hidden = jax.nn.silu(pre_one).astype(jnp.bfloat16)
    first_broad = padded(
        first_hidden.reshape(local_rows, local_columns, -1), (("fsdp", 0),), DILATION_SPAN
    )
    second_activation = spread_offsets(
        first_broad, complete_dilated, inner_neck, DILATION_SPAN, local_rows, local_columns
    )
    pre_two, normed_two, inverse_two = norm_forward(
        second_activation, inside, pixel_count, gain_dilated, bias_dilated
    )
    hidden_two = jax.nn.silu(pre_two).astype(jnp.bfloat16)
    act_three = flat_dot(hidden_two, full_expand)
    pre_three, normed_three, inverse_three = norm_forward(
        act_three, inside, pixel_count, gain_expand, bias_expand
    )
    pre_three = pre_three + inputs_flat
    block_out = jax.nn.silu(pre_three).astype(jnp.bfloat16)
    wide_block = widen_rows(
        block_out.reshape(local_rows, local_columns, channels),
        outer_extent,
        lambda piece, distance: passed_along(piece, "fsdp", distance),
    )
    point_act = flat_dot(block_out, full_point)
    pre_point, normed_point, inverse_point = norm_forward(
        point_act, inside, pixel_count, gain_point, bias_point
    )
    branch_point = jax.nn.silu(pre_point).astype(jnp.bfloat16)
    rate_states = []
    rate_branches = []
    for kernel, factor, offset, spacing, tables in zip(
        rate_kernels, rate_gains, rate_biases, spacings, near_rates
    ):
        rate_act = spread_offsets(
            rim_slice(wide_block, spacing, outer_extent, local_rows),
            kernel,
            tables,
            spacing,
            local_rows,
            local_columns,
        )
        pre_rate, normed_rate, inverse_rate = norm_forward(
            rate_act, inside, pixel_count, factor, offset
        )
        rate_states.append((pre_rate, normed_rate, inverse_rate))
        rate_branches.append(jax.nn.silu(pre_rate).astype(jnp.bfloat16))
    crop_flat = crop_ids.reshape(pixel_values)
    crop_total = CROPS_TILE
    first_crop = lax.axis_index("dp") * crop_total
    owner_group = lax.axis_size("fsdp")
    owner_place = lax.axis_index("fsdp")
    local_crop = crop_flat - first_crop
    member = local_crop[:, None] == jnp.arange(crop_total)[None, :]
    member_low = member.astype(jnp.bfloat16)
    crop_sums = inner_dot(member_low, block_out)
    crop_sizes = jnp.sum(member.astype(jnp.float32), axis=0)
    crop_sums, crop_sizes = lax.psum((crop_sums, crop_sizes), "fsdp")
    pooled = (crop_sums / crop_sizes[:, None]).astype(jnp.bfloat16)
    pool_act = flat_dot(pooled, full_pool)
    pool_low = jax.nn.silu(pool_act).astype(jnp.bfloat16)
    branch_pool = flat_dot(member_low, pool_low).astype(jnp.bfloat16)
    joined = jnp.concatenate([branch_point] + rate_branches + [branch_pool], axis=1)
    merge_act = flat_dot(joined, full_merge)
    pre_merge, normed_merge, inverse_merge = norm_forward(
        merge_act, inside, pixel_count, gain_merge, bias_merge
    )
    merged = jax.nn.silu(pre_merge).astype(jnp.bfloat16)
    logits_full = flat_dot(merged, full_classes)
    class_logits = logits_full.astype(jnp.bfloat16).reshape(local_rows, local_columns, -1)
    (
        full_reduce,
        complete_dilated,
        full_expand,
        full_point,
        full_rate,
        full_double,
        full_triple,
        full_pool,
        full_merge,
        full_classes,
    ) = (
        lax.all_gather(w_reduce, "fsdp", axis=1, tiled=True),
        lax.all_gather(w_dilated, "fsdp", axis=3, tiled=True),
        lax.all_gather(w_expand, "fsdp", axis=1, tiled=True),
        lax.all_gather(w_point, "fsdp", axis=1, tiled=True),
        lax.all_gather(w_rate, "fsdp", axis=3, tiled=True),
        lax.all_gather(w_rate_double, "fsdp", axis=3, tiled=True),
        lax.all_gather(w_rate_triple, "fsdp", axis=3, tiled=True),
        lax.all_gather(w_pool, "fsdp", axis=1, tiled=True),
        lax.all_gather(w_merge, "fsdp", axis=1, tiled=True),
        lax.all_gather(w_classes, "fsdp", axis=0, tiled=True),
    )
    rate_kernels = (full_rate, full_double, full_triple)
    highest = jnp.max(logits_full, axis=1, keepdims=True)
    shifted = jnp.exp(logits_full - highest)
    probability = shifted / jnp.sum(shifted, axis=1, keepdims=True)
    targets = (labels.reshape(pixel_values, 1) == jnp.arange(CLASSES)[None, :]).astype(jnp.float32)
    grad_logits = (inside * (probability - targets) / pixel_count).astype(jnp.bfloat16)
    grad_classes = inner_dot(merged, grad_logits)
    grad_merged = outer_dot(grad_logits, full_classes)
    passed, grad_gain_merge, grad_bias_merge = norm_backward(
        grad_merged * slope(pre_merge), normed_merge, inverse_merge, gain_merge, inside, pixel_count
    )
    grad_merge_act = passed.astype(jnp.bfloat16)
    grad_merge = inner_dot(joined, grad_merge_act)
    grad_joined = outer_dot(grad_merge_act, full_merge)
    branch_width = full_merge.shape[1]
    passed, grad_gain_point, grad_bias_point = norm_backward(
        grad_joined[:, :branch_width] * slope(pre_point),
        normed_point,
        inverse_point,
        gain_point,
        inside,
        pixel_count,
    )
    grad_point_act = passed.astype(jnp.bfloat16)
    grad_point = inner_dot(block_out, grad_point_act)
    grad_block = outer_dot(grad_point_act, full_point)
    rate_grads = []
    rate_weight_grads = []
    rate_gain_grads = []
    rate_bias_grads = []
    for branch in range(3):
        column = (1 + branch) * branch_width
        pre_rate, normed_rate, inverse_rate = rate_states[branch]
        passed, gain_grad, bias_grad = norm_backward(
            grad_joined[:, column : column + branch_width] * slope(pre_rate),
            normed_rate,
            inverse_rate,
            rate_gains[branch],
            inside,
            pixel_count,
        )
        grad_rate_act = passed.astype(jnp.bfloat16)
        pieces = kernel_offsets(
            rim_slice(wide_block, spacings[branch], outer_extent, local_rows),
            grad_rate_act,
            near_rates[branch],
            spacings[branch],
            local_rows,
            local_columns,
        )
        rate_weight_grads.append(jnp.stack(pieces).reshape(3, 3, channels, branch_width))
        rate_grads.append(grad_rate_act)
        rate_gain_grads.append(gain_grad)
        rate_bias_grads.append(bias_grad)
    rate_grads_low = jnp.concatenate(rate_grads, axis=1).reshape(local_rows, local_columns, -1)
    wide_grad_rate = widen_rows(
        rate_grads_low, outer_extent, lambda piece, distance: passed_along(piece, "fsdp", distance)
    )
    for branch in range(3):
        grad_slab = wide_grad_rate[:, :, branch * branch_width : (branch + 1) * branch_width]
        grad_block = grad_block + collect_taps(
            rim_slice(grad_slab, spacings[branch], outer_extent, local_rows),
            rate_kernels[branch],
            near_rates[branch],
            spacings[branch],
            local_rows,
            local_columns,
        )
    crop_grad = lax.dot_general(
        member.astype(jnp.float32),
        grad_joined[:, 4 * branch_width :],
        (((0,), (0,)), ((), ())),
        precision=lax.Precision.HIGHEST,
        preferred_element_type=jnp.float32,
    )
    crop_grad = lax.psum(crop_grad, "fsdp")
    grad_pool_act = (crop_grad * slope(pool_act)).astype(jnp.bfloat16)
    owned_crops = (jnp.arange(crop_total) % owner_group == owner_place).astype(jnp.float32)[:, None]
    grad_pool = inner_dot(pooled, (grad_pool_act * owned_crops).astype(jnp.bfloat16))
    grad_pooled = outer_dot(grad_pool_act, full_pool) / crop_sizes[:, None]
    grad_block = grad_block + inside * jnp.take(
        grad_pooled, jnp.clip(local_crop, 0, crop_total - 1), axis=0
    )
    grad_pre_three = grad_block * slope(pre_three)
    passed, grad_gain_expand, grad_bias_expand = norm_backward(
        grad_pre_three, normed_three, inverse_three, gain_expand, inside, pixel_count
    )
    grad_three = passed.astype(jnp.bfloat16)
    grad_expand = inner_dot(hidden_two, grad_three)
    grad_hidden_two = outer_dot(grad_three, full_expand)
    passed, grad_gain_dilated, grad_bias_dilated = norm_backward(
        grad_hidden_two * slope(pre_two), normed_two, inverse_two, gain_dilated, inside, pixel_count
    )
    second_gradient = passed.astype(jnp.bfloat16)
    dilated_fragments = kernel_offsets(
        first_broad, second_gradient, inner_neck, DILATION_SPAN, local_rows, local_columns
    )
    grad_dilated = jnp.stack(dilated_fragments).reshape(
        3, 3, second_gradient.shape[1], second_gradient.shape[1]
    )
    broad_neck_gradient = padded(
        second_gradient.reshape(local_rows, local_columns, -1), (("fsdp", 0),), DILATION_SPAN
    )
    grad_hidden_one = collect_taps(
        broad_neck_gradient, complete_dilated, inner_neck, DILATION_SPAN, local_rows, local_columns
    )
    passed, grad_gain_reduce, grad_bias_reduce = norm_backward(
        grad_hidden_one * slope(pre_one), normed_one, inverse_one, gain_reduce, inside, pixel_count
    )
    grad_one = passed.astype(jnp.bfloat16)
    grad_reduce = inner_dot(inputs_flat, grad_one)
    grad_features = (grad_pre_three + outer_dot(grad_one, full_reduce)).reshape(
        local_rows, local_columns, channels
    )
    shards = (
        lax.psum_scatter(grad_reduce, "fsdp", scatter_dimension=1, tiled=True),
        lax.psum_scatter(grad_dilated, "fsdp", scatter_dimension=3, tiled=True),
        lax.psum_scatter(grad_expand, "fsdp", scatter_dimension=1, tiled=True),
        lax.psum_scatter(grad_point, "fsdp", scatter_dimension=1, tiled=True),
        lax.psum_scatter(rate_weight_grads[0], "fsdp", scatter_dimension=3, tiled=True),
        lax.psum_scatter(rate_weight_grads[1], "fsdp", scatter_dimension=3, tiled=True),
        lax.psum_scatter(rate_weight_grads[2], "fsdp", scatter_dimension=3, tiled=True),
        lax.psum_scatter(grad_pool, "fsdp", scatter_dimension=1, tiled=True),
        lax.psum_scatter(grad_merge, "fsdp", scatter_dimension=1, tiled=True),
        lax.psum_scatter(grad_classes, "fsdp", scatter_dimension=0, tiled=True),
    )
    shards = (
        lax.psum(shards[0].astype(jnp.bfloat16), "dp").astype(jnp.float32),
        lax.psum(shards[1].astype(jnp.bfloat16), "dp").astype(jnp.float32),
        lax.psum(shards[2].astype(jnp.bfloat16), "dp").astype(jnp.float32),
        lax.psum(shards[3].astype(jnp.bfloat16), "dp").astype(jnp.float32),
        lax.psum(shards[4].astype(jnp.bfloat16), "dp").astype(jnp.float32),
        lax.psum(shards[5].astype(jnp.bfloat16), "dp").astype(jnp.float32),
        lax.psum(shards[6].astype(jnp.bfloat16), "dp").astype(jnp.float32),
        lax.psum(shards[7].astype(jnp.bfloat16), "dp").astype(jnp.float32),
        lax.psum(shards[8].astype(jnp.bfloat16), "dp").astype(jnp.float32),
        lax.psum(shards[9].astype(jnp.bfloat16), "dp").astype(jnp.float32),
    )
    return (
        class_logits,
        grad_features,
        shards[0],
        grad_gain_reduce,
        grad_bias_reduce,
        shards[1],
        grad_gain_dilated,
        grad_bias_dilated,
        shards[2],
        grad_gain_expand,
        grad_bias_expand,
        shards[3],
        grad_gain_point,
        grad_bias_point,
        shards[4],
        rate_gain_grads[0],
        rate_bias_grads[0],
        shards[5],
        rate_gain_grads[1],
        rate_bias_grads[1],
        shards[6],
        rate_gain_grads[2],
        rate_bias_grads[2],
        shards[7],
        shards[8],
        grad_gain_merge,
        grad_bias_merge,
        shards[9],
    )


def solution(mesh):
    tiled = mesh.shape["fsdp"] == 8 and mesh.shape["dp"] == 4

    return jax.shard_map(
        fast_body if tiled else body,
        mesh=mesh,
        in_specs=(
            P(("dp", "fsdp"), None, None),
            P(("dp", "fsdp"), None),
            P(("dp", "fsdp"), None),
            P(None, "fsdp"),
            P(),
            P(),
            P(None, None, None, "fsdp"),
            P(),
            P(),
            P(None, "fsdp"),
            P(),
            P(),
            P(None, "fsdp"),
            P(),
            P(),
            P(None, None, None, "fsdp"),
            P(),
            P(),
            P(None, None, None, "fsdp"),
            P(),
            P(),
            P(None, None, None, "fsdp"),
            P(),
            P(),
            P(None, "fsdp"),
            P(None, "fsdp"),
            P(),
            P(),
            P("fsdp", None),
        ),
        out_specs=(
            P(("dp", "fsdp"), None, None),
            P(("dp", "fsdp"), None, None),
            P(None, "fsdp"),
            P(),
            P(),
            P(None, None, None, "fsdp"),
            P(),
            P(),
            P(None, "fsdp"),
            P(),
            P(),
            P(None, "fsdp"),
            P(),
            P(),
            P(None, None, None, "fsdp"),
            P(),
            P(),
            P(None, None, None, "fsdp"),
            P(),
            P(),
            P(None, None, None, "fsdp"),
            P(),
            P(),
            P(None, "fsdp"),
            P(None, "fsdp"),
            P(),
            P(),
            P("fsdp", None),
        ),
        check_vma=False,
    )
```

```python
import functools
import jax
import jax.numpy as jnp
from jax import lax
from jax.experimental import pallas as pl
from jax.experimental.pallas import tpu as pltpu
from jax.sharding import PartitionSpec as P


CLASSES = 19
CROPS_TILE = 4
DILATION_SPAN = 4
RATE = 12

eps = 1e-05

MESH = pl.DeviceIdType.MESH
ANY = pl.BlockSpec(memory_space=pl.ANY)
VM = pl.BlockSpec(memory_space=pltpu.VMEM)
DMA = pltpu.SemaphoreType.DMA
PAD = 144
VLIM = 60 * 2**20


def greet(fs, ds):
    f = lax.axis_index("fsdp")
    d = lax.axis_index("dp")
    bar = pltpu.get_barrier_semaphore()
    for k in fs:
        pl.semaphore_signal(bar, inc=1, device_id=(d, f ^ k), device_id_type=MESH)
    for k in ds:
        pl.semaphore_signal(bar, inc=1, device_id=(d ^ k, f), device_id_type=MESH)
    pl.semaphore_wait(bar, len(fs) + len(ds))
    return f, d


def remote(src, dst, ss, rs, d, f):
    c = pltpu.make_async_remote_copy(
        src_ref=src, dst_ref=dst, send_sem=ss, recv_sem=rs, device_id=(d, f), device_id_type=MESH
    )
    c.start()
    return c


def sum_kernel(x_ref, o_ref, b1, b2, s1, r1, s2, r2):
    f, d = greet(range(1, 8), range(1, 4))
    b1[f] = x_ref[...]
    cps = [remote(x_ref, b1.at[f], s1.at[k], r1.at[k], d, f ^ k) for k in range(1, 8)]
    for c in cps:
        c.wait()
    tot = b1[0]
    for k in range(1, 8):
        tot = tot + b1[k]
    b2[d] = tot
    cps = [remote(b2.at[d], b2.at[d], s2.at[k], r2.at[k], d ^ k, f) for k in range(1, 4)]
    for c in cps:
        c.wait()
    tot = b2[0]
    for k in range(1, 4):
        tot = tot + b2[k]
    o_ref[...] = tot


def total_sum(rows, cid):
    x = jnp.stack(rows)
    R, C = x.shape
    return pl.pallas_call(
        sum_kernel,
        out_shape=jax.ShapeDtypeStruct((R, C), jnp.float32),
        in_specs=[VM],
        out_specs=VM,
        scratch_shapes=[
            pltpu.VMEM((8, R, C), jnp.float32),
            pltpu.VMEM((4, R, C), jnp.float32),
            DMA((8,)),
            DMA((8,)),
            DMA((4,)),
            DMA((4,)),
        ],
        compiler_params=pltpu.CompilerParams(collective_id=cid, has_side_effects=True),
        name=f"total_sum_{cid}",
    )(x)


def spread_kernel(x_ref, o_ref, ss, rs, ls):
    f, d = greet(range(1, 8), ())
    w = o_ref.shape[2]
    h = x_ref.shape[1]
    dst = o_ref.at[:, pl.ds(pl.multiple_of(PAD + h * f, 16), h), :]

    def part(g):
        return x_ref.at[:, :, pl.ds(pl.multiple_of(g * w, 128), w)]

    cps = [remote(part(f ^ k), dst, ss.at[k], rs.at[k], d, f ^ k) for k in (6, 7, 2, 3, 4, 5, 1)]
    own = pltpu.make_async_copy(part(f), dst, ls)
    own.start()
    for c in cps:
        c.wait()
    own.wait()


def spread_channels(x, cid):
    q, h, C = x.shape
    return pl.pallas_call(
        spread_kernel,
        out_shape=jax.ShapeDtypeStruct((q, 8 * h + 2 * PAD, C // 8), x.dtype),
        in_specs=[VM],
        out_specs=ANY,
        scratch_shapes=[DMA((8,)), DMA((8,)), DMA(())],
        compiler_params=pltpu.CompilerParams(collective_id=cid, has_side_effects=True, vmem_limit_bytes=VLIM),
        name=f"spread_{cid}",
    )(x)


def collect_kernel(x_ref, o_ref, ss, rs, ls):
    f, d = greet(range(1, 8), ())
    w = x_ref.shape[2]
    h = o_ref.shape[1]
    dst = o_ref.at[:, :, pl.ds(pl.multiple_of(f * w, 128), w)]

    def part(g):
        return x_ref.at[:, pl.ds(pl.multiple_of(h * g, 16), h), :]

    cps = [remote(part(f ^ k), dst, ss.at[k], rs.at[k], d, f ^ k) for k in (6, 7, 2, 3, 4, 5, 1)]
    own = pltpu.make_async_copy(part(f), dst, ls)
    own.start()
    for c in cps:
        c.wait()
    own.wait()


def collect_channels(x, cid):
    q, t, w = x.shape
    return pl.pallas_call(
        collect_kernel,
        out_shape=jax.ShapeDtypeStruct((q, t // 8, 8 * w), x.dtype),
        in_specs=[VM],
        out_specs=ANY,
        scratch_shapes=[DMA((8,)), DMA((8,)), DMA(())],
        compiler_params=pltpu.CompilerParams(collective_id=cid, has_side_effects=True, vmem_limit_bytes=VLIM),
        name=f"collect_{cid}",
    )(x)


def gather_kernel(x_ref, o_ref, ss, rs, ps, pr, ls):
    f, d = greet((1, 2, 4, 6), ())
    h = x_ref.shape[1]

    def slot(g):
        return o_ref.at[:, pl.ds(pl.multiple_of(PAD + h * g, 16), h), :]

    cps = [remote(x_ref, slot(f), ss.at[k], rs.at[k], d, f ^ (2 * k)) for k in (3, 1, 2)]
    own = pltpu.make_async_copy(x_ref, slot(f), ls)
    own.start()
    pair = [remote(x_ref, slot(f), ps.at[0], pr.at[0], d, f ^ 1)]
    for k, c in zip((3, 1, 2), cps):
        c.wait_recv()
        got = slot(f ^ (2 * k))
        pair.append(remote(got, got, ps.at[k], pr.at[k], d, f ^ 1))
    for c in cps:
        c.wait_send()
    for c in pair:
        c.wait()
    own.wait()


def gather_rows(x, cid):
    q, h, C = x.shape
    return pl.pallas_call(
        gather_kernel,
        out_shape=jax.ShapeDtypeStruct((q, 8 * h + 2 * PAD, C), x.dtype),
        in_specs=[VM],
        out_specs=ANY,
        scratch_shapes=[DMA((4,)), DMA((4,)), DMA((4,)), DMA((4,)), DMA(())],
        compiler_params=pltpu.CompilerParams(collective_id=cid, has_side_effects=True, vmem_limit_bytes=VLIM),
        name=f"gather_{cid}",
    )(x)


def scatter_kernel(x_ref, o_ref, near, mine, far, ps, pr, ss, rs):
    f, d = greet((1, 2, 4, 6), ())
    c0 = f & 1
    pair = [
        remote(x_ref.at[2 * k + 1 - c0], near.at[k], ps.at[k], pr.at[k], d, f ^ 1) for k in range(4)
    ]
    me = lax.shift_right_logical(f, 1)
    cps = []
    for c in pair:
        c.wait()
    for k in (3, 1, 2, 0):
        g = me ^ k
        val = x_ref[2 * g + c0].astype(jnp.float32) + near[g].astype(jnp.float32)
        if k:
            mine[k] = val.astype(mine.dtype)
            cps.append(remote(mine.at[k], far.at[k], ss.at[k], rs.at[k], d, f ^ (2 * k)))
        else:
            o_ref[...] = val
    for c in cps:
        c.wait()
    o_ref[...] += far[1].astype(jnp.float32) + far[2].astype(jnp.float32) + far[3].astype(jnp.float32)


def scatter_sum(x, cid):
    n, R, C = x.shape
    return pl.pallas_call(
        scatter_kernel,
        out_shape=jax.ShapeDtypeStruct((R, C), jnp.float32),
        in_specs=[VM],
        out_specs=VM,
        scratch_shapes=[
            pltpu.VMEM((4, R, C), x.dtype),
            pltpu.VMEM((4, R, C), x.dtype),
            pltpu.VMEM((4, R, C), x.dtype),
            DMA((4,)),
            DMA((4,)),
            DMA((4,)),
            DMA((4,)),
        ],
        compiler_params=pltpu.CompilerParams(collective_id=cid, has_side_effects=True, vmem_limit_bytes=VLIM),
        name=f"scatter_{cid}",
    )(x)


def nt_dot(a, b):
    return lax.dot_general(a, b, (((1,), (1,)), ((), ())), preferred_element_type=jnp.float32)


def nn_dot(a, b):
    return lax.dot_general(a, b, (((1,), (0,)), ((), ())), preferred_element_type=jnp.float32)


def tn_dot(a, b):
    return lax.dot_general(a, b, (((0,), (0,)), ((), ())), preferred_element_type=jnp.float32)


def span(shift, count):
    return max(0, -shift), min(count, count - shift)


def conv_forward_kernel(steps, y_ref, key_ref, k_ref, o_ref, acc):
    Q = y_ref.shape[0]
    h = o_ref.shape[2]
    w = y_ref.shape[2]
    out = k_ref.shape[1]
    dest = pl.program_id(0)
    base = PAD + h * dest
    T = 8 * h
    for b, s in enumerate(steps):
        acc[...] = jnp.zeros_like(acc)
        for i in (-1, 0, 1):
            first = h * dest + 16 * s * i

            @pl.when((first + h > 0) & (first < T))
            def _():
                at = pl.multiple_of(base + 16 * s * i, 16)
                for j in (-1, 0, 1):
                    lo, hi = span(s * j, Q)
                    here = key_ref[lo:hi, pl.ds(pl.multiple_of(base, 16), h), :]
                    there = key_ref[lo + s * j : hi + s * j, pl.ds(at, h), :]
                    ok = (here == there) & (here > 0)
                    ok = jnp.concatenate([ok] * (w // 128), axis=2)
                    x = jnp.where(ok, y_ref[lo + s * j : hi + s * j, pl.ds(at, h), :], 0)
                    x = x.reshape((hi - lo) * h, w)
                    acc[lo * h : hi * h] += nt_dot(x, k_ref[9 * b + 3 * (i + 1) + j + 1])

        o_ref[0, :, :, b * out : (b + 1) * out] = acc[...].reshape(Q, h, out).astype(o_ref.dtype)


def conv_forward(y, key, k, steps):
    Q, TT, w = y.shape
    h = (TT - 2 * PAD) // 8
    out = k.shape[1]
    return pl.pallas_call(
        functools.partial(conv_forward_kernel, steps),
        out_shape=jax.ShapeDtypeStruct((8, Q, h, 3 * out), jnp.bfloat16),
        grid=(8,),
        in_specs=[VM, VM, VM],
        out_specs=pl.BlockSpec((1, Q, h, 3 * out), lambda i: (i, 0, 0, 0)),
        scratch_shapes=[pltpu.VMEM((Q * h, out), jnp.float32)],
        compiler_params=pltpu.CompilerParams(vmem_limit_bytes=VLIM),
        name="conv_forward",
    )(y, key, k)


def conv_data_kernel(steps, g_ref, key_ref, k_ref, o_ref, acc):
    Q = g_ref.shape[0]
    h = o_ref.shape[1]
    w = o_ref.shape[2]
    out = k_ref.shape[1]
    dest = pl.program_id(0)
    base = PAD + h * dest
    T = 8 * h
    acc[...] = jnp.zeros_like(acc)
    for b, s in enumerate(steps):
        for i in (-1, 0, 1):
            first = h * dest - 16 * s * i

            @pl.when((first + h > 0) & (first < T))
            def _():
                at = pl.multiple_of(base - 16 * s * i, 16)
                for j in (-1, 0, 1):
                    lo, hi = span(-s * j, Q)
                    here = key_ref[lo:hi, pl.ds(pl.multiple_of(base, 16), h), :]
                    there = key_ref[lo - s * j : hi - s * j, pl.ds(at, h), :]
                    ok = (here == there) & (here > 0)
                    ok = jnp.concatenate([ok] * (out // 128), axis=2)
                    x = jnp.where(
                        ok, g_ref[lo - s * j : hi - s * j, pl.ds(at, h), b * out : (b + 1) * out], 0
                    )
                    x = x.reshape((hi - lo) * h, out)
                    acc[lo * h : hi * h] += nn_dot(x, k_ref[9 * b + 3 * (i + 1) + j + 1])

    o_ref[...] = acc[...].reshape(Q, h, w).astype(o_ref.dtype)


def conv_data(g, key, k, steps):
    Q, TT, _ = g.shape
    h = (TT - 2 * PAD) // 8
    w = k.shape[2]
    return pl.pallas_call(
        functools.partial(conv_data_kernel, steps),
        out_shape=jax.ShapeDtypeStruct((Q, 8 * h, w), jnp.bfloat16),
        grid=(8,),
        in_specs=[VM, VM, VM],
        out_specs=pl.BlockSpec((Q, h, w), lambda i: (0, i, 0)),
        scratch_shapes=[pltpu.VMEM((Q * h, w), jnp.float32)],
        compiler_params=pltpu.CompilerParams(vmem_limit_bytes=VLIM),
        name="conv_data",
    )(g, key, k)


def conv_weight_kernel(steps, y_ref, key_ref, g_ref, o_ref, x_ref):
    Q = y_ref.shape[0]
    w = y_ref.shape[2]
    out = o_ref.shape[1]
    TT = y_ref.shape[1]
    T = TT - 2 * PAD
    b = pl.program_id(0)
    for n, s in enumerate(steps):

        @pl.when(b == n)
        def _():
            for i in (-1, 0, 1):
                r0, r1 = span(16 * s * i, T)
                r0, r1 = r0 // 128 * 128, -(-r1 // 128) * 128
                for j in (-1, 0, 1):
                    lo, hi = span(s * j, Q)
                    L = r1 - r0

                    def one(q, _):
                        here = key_ref[q, PAD + r0 : PAD + r1, :]
                        a = PAD + r0 + 16 * s * i
                        there = key_ref[q + s * j, a : a + L, :]
                        ok = (here == there) & (here > 0)
                        ok = jnp.concatenate([ok] * (w // 128), axis=1)
                        x = jnp.where(ok, y_ref[q + s * j, a : a + L, :], 0)
                        x_ref[pl.ds(pl.multiple_of((q - lo) * L, 128), L), :] = x
                        return 0

                    lax.fori_loop(lo, hi, one, 0)
                    d = g_ref[lo:hi, PAD + r0 : PAD + r1, n * out : (n + 1) * out]
                    d = d.reshape((hi - lo) * L, out)
                    o_ref[3 * (i + 1) + j + 1] = tn_dot(d, x_ref[: (hi - lo) * L, :]).astype(o_ref.dtype)


def conv_weight(y, key, g, steps, out):
    Q, TT, w = y.shape
    T = TT - 2 * PAD
    return pl.pallas_call(
        functools.partial(conv_weight_kernel, steps),
        out_shape=jax.ShapeDtypeStruct((27, out, w), jnp.bfloat16),
        grid=(3,),
        in_specs=[VM, VM, VM],
        out_specs=pl.BlockSpec((9, out, w), lambda i: (i, 0, 0)),
        scratch_shapes=[pltpu.VMEM((Q * T, w), jnp.bfloat16)],
        compiler_params=pltpu.CompilerParams(vmem_limit_bytes=VLIM),
        name="conv_weight",
    )(y, key, g)


class Gather:
    def __init__(self, src, slot, sems, d, f):
        self.src, self.slot, self.sems, self.d, self.f = src, slot, sems, d, f

    def start(self):
        far_s, far_r, near_s, near_r, local = self.sems
        d, f = self.d, self.f
        mine = self.slot(f)
        self.far = {k: remote(self.src, mine, far_s.at[k], far_r.at[k], d, f ^ (2 * k)) for k in (3, 1, 2)}
        self.near = [remote(self.src, mine, near_s.at[0], near_r.at[0], d, f ^ 1)]
        self.own = pltpu.make_async_copy(self.src, mine, local)
        self.own.start()

    def forward(self):
        far_s, far_r, near_s, near_r, local = self.sems
        for k in (1, 2, 3):
            self.far[k].wait_recv()
            got = self.slot(self.f ^ (2 * k))
            self.near.append(remote(got, got, near_s.at[k], near_r.at[k], self.d, self.f ^ 1))

    def arrive(self):
        self.own.wait()
        for c in self.near:
            c.wait_recv()

    def finish(self):
        for c in list(self.far.values()) + self.near:
            c.wait_send()


class HalfGather:
    def __init__(self, src, slot, half, sems, d, f):
        self.src, self.slot, self.half, self.sems, self.d, self.f = src, slot, half, sems, d, f

    def start(self):
        far_s, far_r, near_s, near_r, side_s, side_r, local = self.sems
        d, f = self.d, self.f
        mine = self.slot(f)
        a = self.half(d % 2)
        self.far = {
            k: remote(self.src.at[a], mine.at[a], far_s.at[k], far_r.at[k], d, f ^ (2 * k)) for k in (3, 1, 2)
        }
        self.near = [remote(self.src, mine, near_s.at[0], near_r.at[0], d, f ^ 1)]
        self.own = pltpu.make_async_copy(self.src, mine, local)
        self.own.start()

    def forward(self):
        far_s, far_r, near_s, near_r, side_s, side_r, local = self.sems
        d, f = self.d, self.f
        a = self.half(d % 2)
        self.side = {}
        for k in (1, 2, 3):
            self.far[k].wait_recv()
            got = self.slot(f ^ (2 * k)).at[a]
            self.side[k] = remote(got, got, side_s.at[k], side_r.at[k], d ^ 1, f)
            self.near.append(remote(got, got, near_s.at[k], near_r.at[k], d, f ^ 1))

    def arrive(self):
        far_s, far_r, near_s, near_r, side_s, side_r, local = self.sems
        d, f = self.d, self.f
        b = self.half(1 - d % 2)
        for k in (1, 2, 3):
            self.side[k].wait_recv()
            got = self.slot(f ^ (2 * k)).at[b]
            self.near.append(remote(got, got, near_s.at[k + 3], near_r.at[k + 3], d, f ^ 1))
        self.own.wait()
        for c in self.near:
            c.wait_recv()

    def finish(self):
        for c in list(self.far.values()) + self.near + list(self.side.values()):
            c.wait_send()


def half_sems():
    return [DMA((4,)), DMA((4,)), DMA((7,)), DMA((7,)), DMA((4,)), DMA((4,)), DMA(())]


def gather_sems():
    return [DMA((4,)), DMA((4,)), DMA((4,)), DMA((4,)), DMA(())]


def sum_sems(R, C):
    return [
        pltpu.VMEM((8, R, C), jnp.float32),
        pltpu.VMEM((4, R, C), jnp.float32),
        DMA((8,)),
        DMA((8,)),
        DMA((4,)),
        DMA((4,)),
    ]


def sum_all(rows, bufs, d, f):
    b1, b2, s1, r1, s2, r2 = bufs
    for n, row in enumerate(rows):
        b1[f, n : n + 1, :] = row
    cps = [remote(b1.at[f], b1.at[f], s1.at[k], r1.at[k], d, f ^ k) for k in (6, 2, 4, 7, 3, 5, 1)]
    for c in cps:
        c.wait()
    tot = b1[0]
    for k in range(1, 8):
        tot = tot + b1[k]
    b2[d] = tot
    cps = [remote(b2.at[d], b2.at[d], s2.at[k], r2.at[k], d ^ k, f) for k in (3, 2, 1)]
    for c in cps:
        c.wait()
    tot = b2[0]
    for k in range(1, 4):
        tot = tot + b2[k]
    return tot


def column_sums(a, ins):
    m = a * jnp.concatenate([ins] * (a.shape[1] // 128), axis=1)
    return jnp.sum(m, axis=0, keepdims=True), jnp.sum(m * a, axis=0, keepdims=True)


def bend(p):
    g = 1.0 / (1.0 + jnp.exp(-p))
    return p * g, g * (1.0 + p * (1.0 - g))


def same_crop(here, there, width):
    ok = (here == there) & (here > 0)
    return jnp.concatenate([ok] * (width // 128), axis=ok.ndim - 1)


def cat_rows(parts):
    return jnp.concatenate(parts, axis=1)


def bottleneck_kernel(
    x_ref, kb_ref, ins_ref, gr, br, gd, bd, ge, be,
    wr_s, wd_s, we_s, wp_s, wm_s, wc_s, k_s0, k_s1, k_s2, kp_s,
    yo_o, y_o, n3_o, l3_o, n1_o, l1_o, n2_o, l2_o, ext_o, h2_o, key_o, k_o, wr_o, wd_o, we_o, wp_o, wm_o, wc_o, cnt_o,
    xp, a1, a2, a3, ext, h2, y, n3, l3, n1, l1, n2, l2, key, wr, wd, we,
    *sems,
):
    sems = list(sems)

    def take(n):
        got = sems[:n]
        del sems[:n]
        return got

    f, d = greet(range(1, 8), range(1, 4))
    N, C = x_ref.shape
    Q, h = ext.shape[0], ext.shape[1] // 2
    e = h // 2
    rows = h // 4
    neck = a1.shape[1]
    T = 8 * h

    def rows_of(ref, n):
        return lambda g: ref.at[pl.ds(pl.multiple_of(n * g, n), n)]

    nr, nd_, ne, np_ = wr_s.shape[0], wd_s.shape[1], we_s.shape[1], wp_s.shape[0]
    def half(n, lead=()):
        return lambda a: lead + (pl.ds(pl.multiple_of(n * a, n), n),)

    g_wr = Gather(wr_s, rows_of(wr, nr), take(5), d, f)
    g_wd = [
        HalfGather(
            wd_s.at[pl.ds(3 * i, 3)],
            lambda g, i=i: wd.at[pl.ds(3 * i, 3), pl.ds(pl.multiple_of(nd_ * g, 16), nd_), :],
            half(nd_ // 2, (slice(None),)), take(7), d, f,
        )
        for i in range(3)
    ]
    g_we = HalfGather(
        we_s, lambda g: we.at[:, pl.ds(pl.multiple_of(ne * g, 128), ne)], half(we_s.shape[0] // 2), take(7), d, f
    )
    g_wp = Gather(wp_s, rows_of(wp_o, np_), take(5), d, f)
    g_wm = Gather(wm_s, rows_of(wm_o, np_), take(5), d, f)
    g_wc = Gather(wc_s, rows_of(wc_o, np_), take(5), d, f)
    ks, kr, kl, zs, zk, hs, hr, ys, yr, yl, os_, qs, qr, kc = take(14)
    sum1, sum2, sum3 = (Sum(take(6), d, f) for _ in range(3))

    key_sent = [
        remote(kb_ref, kc.at[f], qs.at[k], qr.at[k], d, f ^ k) for k in (6, 7, 2, 3, 4, 5, 1)
    ]
    kc[f] = kb_ref[...]
    g_wr.start()
    g_wd[0].start()
    order = lax.broadcasted_iota(jnp.int32, (N, N), 0)
    m, r, q = order % 4, (order // 4) % rows, order // h
    pick = (r * (N // rows) + q * 4 + m) == lax.broadcasted_iota(jnp.int32, (N, N), 1)
    pick = pick.astype(jnp.float32).astype(jnp.bfloat16)
    for c in range(0, C, 256):
        xp[:, c : c + 256] = nn_dot(pick, x_ref[:, c : c + 256]).astype(jnp.bfloat16)
    key[:, :PAD, :] = jnp.zeros((Q, PAD, 128), jnp.bfloat16)
    key[:, PAD + T :, :] = jnp.zeros((Q, PAD, 128), jnp.bfloat16)
    g_wr.forward()
    g_wd[1].start()
    g_wd[2].start()
    g_wr.arrive()
    g_wd[0].forward()
    sums, squares = [], []
    for c in range(0, neck, 256):
        a = nt_dot(xp[...], wr[c : c + 256, :])
        a1[:, c : c + 256] = a
        s, t = column_sums(a, ins_ref[...])
        sums.append(s)
        squares.append(t)
    inside = jnp.sum(ins_ref[...], axis=0, keepdims=True)
    sum1.start([cat_rows(sums), cat_rows(squares), cat_rows([inside] * (neck // 128))])
    g_we.start()
    g_wd[1].forward()
    g_wd[2].forward()
    kparts = (k_s0, k_s1, k_s2, kp_s)

    def kslot(b, g, lo, n):
        o = kparts[b].shape[1]
        return k_o.at[pl.ds(9 * b, kparts[b].shape[0]), pl.ds(pl.multiple_of(o * g + lo, 16), n), :]

    kcp, kfar = [], {}
    pieces = [(b, k) for b in range(3) for k in (6, 7, 2, 3, 4, 5)]

    def out(*ns):
        for b, k in [pieces[n] for n in ns]:
            src = kparts[b]
            o = src.shape[1] // 2
            lo = pl.multiple_of(o * (d % 2), 16)
            to = pl.ds(pl.multiple_of((f ^ k) * 256, 128), 256)
            kfar[b, k] = remote(
                src.at[:, pl.ds(lo, o), to], kslot(b, f, lo, o), ks.at[b, k], kr.at[b, k], d, f ^ k
            )

    def aside(*ns):
        for b, k in [pieces[n] for n in ns]:
            o = kparts[b].shape[1] // 2
            lo = pl.multiple_of(o * (d % 2), 16)
            kfar[b, k].wait_recv()
            got = kslot(b, f ^ k, lo, o)
            kcp.append(remote(got, got, zs.at[b, k], zk.at[b, k], d ^ 1, f))

    for b, src in enumerate(kparts):
        o = src.shape[1]
        for k in (6, 7, 2, 3, 4, 5, 1) if b == 3 else (1,):
            to = pl.ds(pl.multiple_of((f ^ k) * 256, 128), 256)
            kcp.append(remote(src.at[:, :, to], kslot(b, f, 0, o), ks.at[b, k], kr.at[b, k], d, f ^ k))
        own = pl.ds(pl.multiple_of(f * 256, 128), 256)
        c = pltpu.make_async_copy(src.at[:, :, own], kslot(b, f, 0, o), kl.at[b])
        c.start()
        kcp.append(c)
    sum1.turn()
    out(0, 1)
    st = sum1.result()
    out(2, 3)
    g_we.forward()
    count = st[2:3, :]
    cnt_o[...] = jnp.zeros_like(cnt_o)
    cnt_o[0:1, :neck] = count
    mean = st[0:1] / count
    inv = lax.rsqrt(st[1:2] / count - mean * mean + eps)
    cnt_o[1:2, :neck] = inv
    for c in range(0, neck, 256):
        w = slice(c, c + 256)
        n = (a1[:, w] - mean[:, w]) * inv[:, w]
        act, lean = bend(n * gr[:, w] + br[:, w])
        ext[:, e : e + h, w] = act.astype(jnp.bfloat16).reshape(Q, h, 256)
        n1[:, w] = n.astype(jnp.bfloat16)
        l1[:, w] = lean.astype(jnp.bfloat16)
    up = remote(ext.at[:, pl.ds(e, e)], ext.at[:, pl.ds(e + h, e)], hs.at[0], hr.at[0], d, lax.rem(f + 7, 8))
    down = remote(ext.at[:, pl.ds(h, e)], ext.at[:, pl.ds(0, e)], hs.at[1], hr.at[1], d, lax.rem(f + 1, 8))
    for c in key_sent:
        c.wait()
    for g in range(8):
        turned = kc[g].T
        for q in range(Q):
            key[q, PAD + h * g : PAD + h * g + h, :] = jnp.broadcast_to(turned[:h, q : q + 1], (h, 128)).astype(jnp.bfloat16)
    outs = [(n1, n1_o), (l1, l1_o), (key, key_o), (wr, wr_o)]
    base = pl.multiple_of(PAD + h * f, 16)
    up.wait()
    down.wait()
    outs.append((ext, ext_o))
    outs.append((wd, wd_o))
    a2[...] = jnp.zeros_like(a2)
    for i in range(3):
        g_wd[i].arrive()
        for j in (1, 0, 2):
            lo, hi = span(j - 1, Q)
            ok = same_crop(
                key[lo:hi, pl.ds(base, h), :],
                key[lo + j - 1 : hi + j - 1, pl.ds(pl.multiple_of(base + e * (i - 1), 16), h), :],
                neck,
            )
            v = jnp.where(ok, ext[lo + j - 1 : hi + j - 1, e * i : e * i + h, :], 0).reshape((hi - lo) * h, neck)
            for c in range(0, neck, 256):
                a2[lo * h : hi * h, c : c + 256] += nt_dot(v, wd[3 * i + j, c : c + 256, :])
            if (3 * i + j) % 2 == 0 and i < 2 + (j == 0):
                out(4 + (3 * i + j) // 2)
    sums, squares = [], []
    for c in range(0, neck, 256):
        s, t = column_sums(a2[:, c : c + 256], ins_ref[...])
        sums.append(s)
        squares.append(t)
    sum2.start([cat_rows(sums), cat_rows(squares)])
    aside(0, 1, 2, 3)
    sum2.turn()
    out(8, 9)
    st = sum2.result()
    out(10)
    mean = st[0:1] / count
    inv = lax.rsqrt(st[1:2] / count - mean * mean + eps)
    cnt_o[2:3, :neck] = inv
    for c in range(0, neck, 256):
        w = slice(c, c + 256)
        n = (a2[:, w] - mean[:, w]) * inv[:, w]
        act, lean = bend(n * gd[:, w] + bd[:, w])
        h2[:, w] = act.astype(jnp.bfloat16)
        n2[:, w] = n.astype(jnp.bfloat16)
        l2[:, w] = lean.astype(jnp.bfloat16)
    outs += [(n2, n2_o), (l2, l2_o), (h2, h2_o)]
    g_we.arrive()
    outs.append((we, we_o))
    sums, squares = [], []
    for c in range(0, C, 256):
        n = c // 256
        if n % 2 == 0:
            out(11 + n // 2)
        else:
            aside(4 + n // 2)
        a = nn_dot(h2[...], we[:, c : c + 256])
        a3[:, c : c + 256] = a
        s, t = column_sums(a, ins_ref[...])
        sums.append(s)
        squares.append(t)
    sum3.start([cat_rows(sums), cat_rows(squares)])
    aside(8, 9)
    sum3.turn()
    out(15, 16, 17)
    for g in (g_wp, g_wm, g_wc):
        g.start()
    st = sum3.result()
    total = count[:, :1]
    mean3 = st[0:1] / total
    inv3 = lax.rsqrt(st[1:2] / total - mean3 * mean3 + eps)
    coef = sum3.b1
    coef[0, 0:1, :] = mean3
    coef[0, 1:2, :] = inv3
    cnt_o[3:4, :] = inv3
    sent = []
    dst = yo_o.at[:, pl.ds(base, h), :]
    for m, k in enumerate((6, 7, 2, 3, 4, 5, 1, 0)):
        aside(10 + m)
        g = f ^ k
        w = pl.ds(pl.multiple_of(g * 256, 256), 256)
        n = (a3[:, w] - coef[0, 0:1, w]) * coef[0, 1:2, w]
        act, lean = bend(n * ge[:, w] + be[:, w] + xp[:, w].astype(jnp.float32))
        y[:, :, w] = act.astype(jnp.bfloat16).reshape(Q, h, 256)
        n3[:, w] = n.astype(jnp.bfloat16)
        l3[:, w] = lean.astype(jnp.bfloat16)
        part = y.at[:, :, w]
        if k:
            sent.append(remote(part, dst, ys.at[k], yr.at[k], d, g))
        else:
            own = pltpu.make_async_copy(part, dst, yl)
            own.start()
            sent.append(own)
    outs += [(y, y_o), (n3, n3_o), (l3, l3_o)]
    saved = []
    for n, (src, to) in enumerate(outs):
        c = pltpu.make_async_copy(src, to, os_.at[n])
        c.start()
        saved.append(c)
    for g in (g_wp, g_wm, g_wc):
        g.forward()
    for g in (g_wp, g_wm, g_wc):
        g.arrive()
    for g in [g_wr, g_we, g_wp, g_wm, g_wc] + g_wd:
        g.finish()
    for c in kfar.values():
        c.wait_send()
    for c in kcp + sent + saved:
        c.wait()


def bottleneck(x, kb, ins, vecs, shards, kparts):
    N, C = x.shape
    Q = kb.shape[0]
    h = N // Q
    wr, wd, we, wp, wm, wc = shards
    neck = we.shape[0]
    W = 8 * wp.shape[0]
    b16, f32 = jnp.bfloat16, jnp.float32
    S = jax.ShapeDtypeStruct
    TT = 8 * h + 2 * PAD
    outs = [
        S((Q, TT, C // 8), b16), S((Q, h, C), b16), S((N, C), b16), S((N, C), b16),
        S((N, neck), b16), S((N, neck), b16), S((N, neck), b16), S((N, neck), b16),
        S((Q, 2 * h, neck), b16), S((N, neck), b16), S((Q, TT, 128), b16), S((28, W, C // 8), b16),
        S((neck, C), b16), S((9, neck, neck), b16), S((neck, C), b16), S((W, C), b16), S((W, wm.shape[1]), b16),
        S((W, 128), b16), S((8, C), f32),
    ]
    V = pltpu.VMEM
    scratch = [
        V((N, C), b16), V((N, neck), f32), V((N, neck), f32), V((N, C), f32), V((Q, 2 * h, neck), b16), V((N, neck), b16),
        V((Q, h, C), b16), V((N, C), b16), V((N, C), b16),
        V((N, neck), b16), V((N, neck), b16), V((N, neck), b16), V((N, neck), b16), V((Q, TT, 128), b16),
        V((neck, C), b16), V((9, neck, neck), b16), V((neck, C), b16),
    ]
    scratch += gather_sems() + half_sems() * 4 + gather_sems() * 3
    scratch += [DMA((4, 8)), DMA((4, 8)), DMA((4,)), DMA((4, 8)), DMA((4, 8)), DMA((2,)), DMA((2,)), DMA((8,)), DMA((8,)), DMA(()), DMA((16,))]
    scratch += [DMA((8,)), DMA((8,)), V((8, Q, 128), f32)]
    scratch += sum_sems(3, neck) + sum_sems(2, neck) + sum_sems(2, C)
    return pl.pallas_call(
        bottleneck_kernel,
        out_shape=outs,
        in_specs=[VM] * 9 + [ANY] * 10,
        out_specs=[ANY] * 18 + [VM],
        scratch_shapes=scratch,
        compiler_params=pltpu.CompilerParams(collective_id=1, has_side_effects=True, vmem_limit_bytes=VLIM),
        name="bottleneck",
    )(x, kb, ins, *vecs, *shards, *kparts)


def branches_back_kernel(
    steps, d_ref, y_ref, key_ref, k_ref, pooled_ref, dr_ref, size_ref, dy_o, gk_o, tail_o,
    g, gt, gk, fin, in1, in2, dyo, acc, gp, *sems,
):
    sems = list(sems)
    f, d = greet(range(1, 8), range(1, 4))
    Q, h, w = y_ref.shape[0], d_ref.shape[1], y_ref.shape[2]
    W = k_ref.shape[1]
    T = 8 * h
    o = W // 8
    taps = gk.shape[0] // 2
    gathers = [
        Gather(
            d_ref.at[:, :, pl.ds(b * W, W)],
            lambda n, b=b: g.at[:, pl.ds(pl.multiple_of(PAD + h * n, 16), h), pl.ds(b * W, W)],
            sems[5 * b : 5 * b + 5], d, f,
        )
        for b in range(3)
    ]
    ws, wr, wl, ds_, dr_, dl, s1, r1, s2, r2, s3, r3 = sems[15:]
    for c in gathers:
        c.start()
    outer = d % 3 == 0

    def two(ref, t):
        return ref.at[pl.ds(2 * t, 2)]

    def to_inner(t):
        return pltpu.make_async_remote_copy(
            src_ref=two(gk, t), dst_ref=two(in1, t), send_sem=s1.at[t], recv_sem=r1.at[t],
            device_id=(d ^ 1, f), device_id_type=MESH,
        )

    def across(t):
        return pltpu.make_async_remote_copy(
            src_ref=two(gk, t), dst_ref=two(in2, t), send_sem=s2.at[t], recv_sem=r2.at[t],
            device_id=(d ^ 3, f), device_id_type=MESH,
        )

    def to_outer(t):
        return pltpu.make_async_remote_copy(
            src_ref=two(fin, t), dst_ref=two(fin, t), send_sem=s3.at[t], recv_sem=r3.at[t],
            device_id=(d ^ 1, f), device_id_type=MESH,
        )

    def hand(t):
        @pl.when(outer)
        def _():
            to_inner(t).start()

    def first(t):
        @pl.when(jnp.logical_not(outer))
        def _():
            to_inner(t).wait_recv()
            for n in (2 * t, 2 * t + 1):
                gk[n] = (gk[n].astype(jnp.float32) + in1[n].astype(jnp.float32)).astype(gk.dtype)
            across(t).start()

    def second(t):
        @pl.when(jnp.logical_not(outer))
        def _():
            across(t).wait_recv()
            for n in (2 * t, 2 * t + 1):
                fin[n] = (gk[n].astype(jnp.float32) + in2[n].astype(jnp.float32)).astype(fin.dtype)
            to_outer(t).start()

        @pl.when(outer)
        def _():
            to_outer(t).wait_recv()

    tail_o[9] = tn_dot(dr_ref[...], pooled_ref[...]).astype(gk.dtype)
    gp[...] = nn_dot(dr_ref[...], k_ref[27]) / size_ref[:, :1]
    for b, s in enumerate(steps):
        gathers[b].forward()
        gathers[b].arrive()

        def turn(q, _):
            gt[b * W : (b + 1) * W, pl.ds(pl.multiple_of(q * T, 256), T)] = g[q, PAD : PAD + T, b * W : (b + 1) * W].T
            return 0

        lax.fori_loop(0, Q, turn, 0)
        for i in (-1, 0, 1):
            for j in (-1, 0, 1):
                lo, hi = span(s * j, Q)
                a = PAD + 16 * s * i

                got = None
                for q in range(lo, hi):
                    ok = same_crop(key_ref[q, PAD : PAD + T, :], key_ref[q + s * j, a : a + T, :], w)
                    v = jnp.where(ok, y_ref[q + s * j, a : a + T, :], 0)
                    r = nn_dot(gt[b * W : (b + 1) * W, q * T : (q + 1) * T], v)
                    got = r if got is None else got + r
                t = 9 * b + 3 * (i + 1) + j + 1
                if b < 2:
                    gk[t] = got.astype(gk.dtype)
                    if t % 2:
                        hand(t // 2)
                else:
                    tail_o[t - 18] = got.astype(gk.dtype)
                    if t % 2:
                        first((t - 18) // 2)
    cps = []
    ready = 4

    dst = dy_o.at[:, :, pl.ds(pl.multiple_of(w * f, 128), w)]

    def rows_of(k):
        return pl.ds(pl.multiple_of(h * (f ^ k), 16), h)

    def dest_step(m, _):
        k = 7 - m
        dest = f ^ k
        base = pl.multiple_of(PAD + h * dest, 16)
        here = key_ref[:, pl.ds(base, h), :].astype(jnp.float32).reshape(Q * h, 128)
        here = jnp.concatenate([here] * (w // 128), axis=1)
        @pl.when(m % 2 == 1)
        def _():
            first(ready + m // 2)
            second(m // 2)

        total = jnp.zeros((Q * h, w), jnp.float32)
        for c in range(CROPS_TILE):
            total = jnp.where(here == c + 1.0, gp[c : c + 1, :], total)
        acc[...] = total
        for b in range(3):
            spaced_taps(g, key_ref, k_ref, acc, base, h, steps, -1, b * W, nn_dot, b)
        rows = rows_of(k)
        dyo[:, rows, :] = acc[...].reshape(Q, h, w).astype(dyo.dtype)
        src = dyo.at[:, rows, :]

        @pl.when(k > 0)
        def _():
            remote(src, dst, ds_.at[k], dr_.at[k], d, dest)

        @pl.when(k == 0)
        def _():
            pltpu.make_async_copy(src, dst, dl).start()

        return 0

    lax.fori_loop(0, 8, dest_step, 0)

    def first_when(t):
        @pl.when(t < taps)
        def _():
            first(t)

    groups = (4, 3, 2)
    at = 0
    for n, size in enumerate(groups):
        stop = at + size
        lax.fori_loop(max(at, 4), stop, lambda t, _: (first_when(t + ready), second(t), 0)[-1], 0)
        for k in (6, 7, 2, 3, 4, 5, 1, 0):
            src = fin.at[pl.ds(2 * at, 2 * size), pl.ds(pl.multiple_of(o * (f ^ k), 16), o), :]
            to = gk_o.at[pl.ds(2 * at, 2 * size), :, pl.ds(pl.multiple_of(w * f, 128), w)]
            if k:
                cps.append(remote(src, to, ws.at[n, k], wr.at[n, k], d, f ^ k))
            else:
                c = pltpu.make_async_copy(src, to, wl.at[n])
                c.start()
                cps.append(c)
        at = stop
    for k in range(1, 8):
        c = pltpu.make_async_remote_copy(
            src_ref=dyo.at[:, rows_of(k), :], dst_ref=dst, send_sem=ds_.at[k], recv_sem=dr_.at[k],
            device_id=(d, f ^ k), device_id_type=MESH,
        )
        c.wait()
    pltpu.make_async_copy(dyo.at[:, rows_of(0), :], dst, dl).wait()
    for c in gathers:
        c.finish()
    for c in cps:
        c.wait()

    def sent(t, _):
        @pl.when(outer)
        def _():
            to_inner(t).wait_send()

        @pl.when(jnp.logical_not(outer))
        def _():
            across(t).wait_send()
            to_outer(t).wait_send()

        return 0

    lax.fori_loop(0, taps, sent, 0)


def branches_back(d, y, key, k, pooled, dr, sizes, steps):
    Q, h, W3 = d.shape
    TT, w = y.shape[1:]
    W = W3 // 3
    T = 8 * h
    b16, f32 = jnp.bfloat16, jnp.float32
    V = pltpu.VMEM
    return pl.pallas_call(
        functools.partial(branches_back_kernel, steps),
        out_shape=[jax.ShapeDtypeStruct((Q, h, 8 * w), b16), jax.ShapeDtypeStruct((18, W // 8, 8 * w), b16),
            jax.ShapeDtypeStruct((10, W, w), b16),
        ],
        in_specs=[VM] * 7,
        out_specs=[ANY] * 2 + [VM],
        scratch_shapes=[
            V((Q, TT, W3), b16), V((W3, Q * T), b16), V((18, W, w), b16), V((18, W, w), b16),
            V((18, W, w), b16), V((18, W, w), b16), V((Q, T, w), b16),
            V((Q * h, w), f32), V((8, w), f32),
        ]
        + gather_sems() * 3
        + [DMA((4, 8)), DMA((4, 8)), DMA((4,)), DMA((8,)), DMA((8,)), DMA(())]
        + [DMA((9,))] * 6,
        compiler_params=pltpu.CompilerParams(collective_id=10, has_side_effects=True, vmem_limit_bytes=VLIM),
        name="branches_back",
    )(d, y, key, k, pooled, dr, sizes)


class Sum:
    def __init__(self, bufs, d, f):
        self.b1, self.b2, self.s1, self.r1, self.s2, self.r2 = bufs
        self.d, self.f = d, f

    def start(self, rows):
        b1, d, f = self.b1, self.d, self.f
        for n, row in enumerate(rows):
            b1[f, n : n + 1, :] = row
        self.cps = [remote(b1.at[f], b1.at[f], self.s1.at[k], self.r1.at[k], d, f ^ k) for k in (6, 2, 4, 7, 3, 5, 1)]

    def turn(self):
        b1, b2, d, f = self.b1, self.b2, self.d, self.f
        for c in self.cps:
            c.wait()
        tot = b1[0]
        for k in range(1, 8):
            tot = tot + b1[k]
        b2[d] = tot
        self.cps = [remote(b2.at[d], b2.at[d], self.s2.at[k], self.r2.at[k], d ^ k, f) for k in (3, 2, 1)]

    def result(self):
        for c in self.cps:
            c.wait()
        tot = self.b2[0]
        for k in range(1, 4):
            tot = tot + self.b2[k]
        return tot


class Reduce:
    def __init__(self, full, part, half, near, far, corner, tot, zin, zo, out, sems, d, f):
        self.half, self.corner = half, corner
        self.full, self.part, self.near, self.fars, self.tot, self.out = full, part, near, far, tot, out
        self.zin, self.zo, self.d, self.f = zin, zo, d, f
        self.sems = sems
        self.c0 = f % 2
        self.me = f // 2

    def pair(self):
        ps, pr = self.sems[:2]
        self.cps = [
            remote(self.full.at[self.part(2 * g + 1 - self.c0)], self.near.at[g], ps.at[g], pr.at[g], self.d, self.f ^ 1)
            for g in range(4)
        ]

    def far(self):
        ss, rs = self.sems[2:4]
        for c in self.cps:
            c.wait()
        self.cps = []
        for k in (3, 1, 2, 0):
            g = self.me ^ k
            val = self.full[self.part(2 * g + self.c0)].astype(jnp.float32) + self.near[g].astype(jnp.float32)
            self.near[g] = val.astype(self.near.dtype)
            if k == 3:
                for a in (0, 1):
                    self.cps.append(
                        remote(
                            self.near.at[(g,) + self.half(a)], self.corner.at[self.half(a)], ss.at[a], rs.at[a],
                            self.d, self.f ^ (2 + 2 * a),
                        )
                    )

    def beside(self):
        ss, rs = self.sems[2:4]
        for c in self.cps:
            c.wait()
        self.cps = []
        for k in (1, 2):
            g = self.me ^ k
            a = self.half(2 - k)
            val = self.near[(g,) + a].astype(jnp.float32) + self.corner[a].astype(jnp.float32)
            self.near[(g,) + a] = val.astype(self.near.dtype)
            self.cps.append(
                remote(
                    self.near.at[g], self.fars.at[k - 1], ss.at[k + 1], rs.at[k + 1], self.d, self.f ^ (2 * k)
                )
            )

    def to_inner(self):
        ss, rs = self.sems[4:6]
        return pltpu.make_async_remote_copy(
            src_ref=self.tot, dst_ref=self.zin, send_sem=ss.at[0], recv_sem=rs.at[0],
            device_id=(self.d ^ 1, self.f), device_id_type=MESH,
        )

    def across(self):
        ss, rs = self.sems[4:6]
        return pltpu.make_async_remote_copy(
            src_ref=self.tot, dst_ref=self.zo, send_sem=ss.at[1], recv_sem=rs.at[1],
            device_id=(self.d ^ 3, self.f), device_id_type=MESH,
        )

    def to_outer(self):
        ss, rs = self.sems[4:6]
        return pltpu.make_async_remote_copy(
            src_ref=self.out, dst_ref=self.out, send_sem=ss.at[2], recv_sem=rs.at[2],
            device_id=(self.d ^ 1, self.f), device_id_type=MESH,
        )

    def tiles(self):
        for c in self.cps:
            c.wait()
        val = self.near[self.me].astype(jnp.float32)
        for k in (1, 2):
            val = val + self.fars[k - 1].astype(jnp.float32)
        self.tot[...] = val.astype(self.tot.dtype)

        @pl.when(self.d % 3 == 0)
        def _():
            self.to_inner().start()

    def middle(self):
        @pl.when(self.d % 3 > 0)
        def _():
            self.to_inner().wait_recv()
            val = self.tot[...].astype(jnp.float32) + self.zin[...].astype(jnp.float32)
            self.tot[...] = val.astype(self.tot.dtype)
            self.across().start()

    def last(self):
        @pl.when(self.d % 3 > 0)
        def _():
            self.across().wait_recv()
            val = self.tot[...].astype(jnp.float32) + self.zo[...].astype(jnp.float32)
            self.out[...] = val.astype(self.out.dtype)
            self.to_outer().start()

    def done(self):
        @pl.when(self.d % 3 == 0)
        def _():
            self.to_inner().wait_send()
            self.to_outer().wait_recv()

        @pl.when(self.d % 3 > 0)
        def _():
            self.across().wait_send()
            self.to_outer().wait_send()


def reduce_scratch(block):
    V, b16 = pltpu.VMEM, jnp.bfloat16
    return [V((4,) + block, b16), V((2,) + block, b16), V(block, b16), V(block, b16), V(block, b16), V(block, b16)] + [DMA((4,))] * 6


def wide(row, n):
    return jnp.concatenate([row] * n, axis=1)


def bottleneck_back_kernel(
    x_ref, ins_ref, st_ref, gr, gd, ge, dy, dpt, y_ref, pm_in, wp, n3, l3, we, n2, l2, h2, wd, ext, n1, l1, wr, key_any, tail,
    gf_o, pm_o, ex_o, di_o, re_o, s3_o, s2_o, s1_o, tk_o,
    pm, ex, di, dp3, d3, acc, ext2, d1n, key, gf, pick, in1, in2, ksem, hs, hr, gs, s1, r1, s2, r2, s3, r3, ws, wrs, wl,
    *sems,
):
    sems = list(sems)

    def take(n):
        got = sems[:n]
        del sems[:n]
        return got

    f, d = greet(range(1, 8), range(1, 4))
    N, C = x_ref.shape
    Q, h = ext2.shape[0], ext2.shape[1] // 2
    e = h // 2
    rows = h // 4
    neck = acc.shape[1]
    nb = neck // 8
    nw = pm.shape[0] // 8
    W = dpt.shape[1]

    def ds(i, n):
        return pl.ds(pl.multiple_of(n * i, n), n)

    def reducer(full, part, half, out):
        near, far, corner, tot, zin, zo = take(6)
        return Reduce(full, part, half, near, far, corner, tot, zin, zo, out, take(6), d, f)

    def half_rows(n):
        return lambda a: (pl.ds(a * n, n),)

    r_pm = reducer(pm, lambda g: (ds(g, nw),), half_rows(nw // 2), pm_o)
    r_ex = reducer(ex, lambda g: (slice(None), ds(g, C // 8)), half_rows(neck // 2), ex_o)
    r_di = [
        reducer(
            di.at[pl.ds(3 * i, 3)], lambda g: (slice(None), ds(g, nb)),
            lambda a: (slice(None), pl.ds(a * (nb // 2), nb // 2)), di_o.at[pl.ds(3 * i, 3)],
        )
        for i in range(3)
    ]
    re_ = ex
    r_re = reducer(re_, lambda g: (ds(g, nb),), half_rows(nb // 2), re_o)
    sum3, sum2, sum1 = (Sum(take(6), d, f) for _ in range(3))

    outer = d % 3 == 0
    o = in1.shape[1] // 8
    lanes = in1.shape[2]
    kout = []

    def move(src, dst, ss, rs, t, other):
        two = pl.ds(2 * t, 2)
        return pltpu.make_async_remote_copy(
            src_ref=src.at[two], dst_ref=dst.at[two], send_sem=ss.at[t], recv_sem=rs.at[t],
            device_id=(d ^ other, f), device_id_type=MESH,
        )

    def to_inner(t):
        return move(tail, in1, s1, r1, t, 1)

    def across(t):
        return move(in1, in2, s2, r2, t, 3)

    def to_outer(t):
        return move(in1, in1, s3, r3, t, 1)

    def hand(t):
        @pl.when(outer)
        def _():
            to_inner(t).start()

    def first(t):
        @pl.when(jnp.logical_not(outer))
        def _():
            to_inner(t).wait_recv()
            for n in (2 * t, 2 * t + 1):
                in1[n] = (in1[n].astype(jnp.float32) + tail[n].astype(jnp.float32)).astype(in1.dtype)
            across(t).start()

    def second(t):
        @pl.when(jnp.logical_not(outer))
        def _():
            across(t).wait()
            for n in (2 * t, 2 * t + 1):
                in1[n] = (in1[n].astype(jnp.float32) + in2[n].astype(jnp.float32)).astype(in1.dtype)
            to_outer(t).start()

    def keep(n, at, size):
        for t in range(at, at + size):

            @pl.when(outer)
            def _():
                to_outer(t).wait_recv()

        for k in (6, 7, 2, 3, 4, 5, 1, 0):
            src = in1.at[pl.ds(2 * at, 2 * size), pl.ds(pl.multiple_of(o * (f ^ k), 16), o), :]
            to = tk_o.at[pl.ds(2 * at, 2 * size), :, pl.ds(pl.multiple_of(lanes * f, 128), lanes)]
            if k:
                kout.append(remote(src, to, ws.at[n, k], wrs.at[n, k], d, f ^ k))
            else:
                c = pltpu.make_async_copy(src, to, wl.at[n])
                c.start()
                kout.append(c)

    hand(0)
    hand(1)
    kcp = pltpu.make_async_copy(key_any.at[:, pl.ds(pl.multiple_of(PAD - e + h * f, 16), 2 * h), :], key, ksem)
    kcp.start()
    count = st_ref[0:1, 0:1]
    for c in range(0, C, 256):
        pm[:, c : c + 256] = tn_dot(dpt[...], y_ref[:, c : c + 256]).astype(jnp.bfloat16)
    pm[:, C:] = pm_in[...]
    r_pm.pair()
    ones, crossed = [], []
    ins = wide(ins_ref[...], 2)
    for c in range(0, C, 256):
        w = slice(c, c + 256)
        if c == C // 2:
            first(0)
        v = dy[:, w].astype(jnp.float32) + nn_dot(dpt[...], wp[:, w])
        v = v * l3[:, w].astype(jnp.float32)
        dp3[:, w] = v.astype(jnp.bfloat16)
        v = v * ins
        ones.append(jnp.sum(v, axis=0, keepdims=True))
        crossed.append(jnp.sum(v * n3[:, w].astype(jnp.float32), axis=0, keepdims=True))
    sum3.start([cat_rows(ones), cat_rows(crossed)])
    order = lax.broadcasted_iota(jnp.int32, (N, N), 1)
    m, r, q = order % 4, (order // 4) % rows, order // h
    hit = (r * (N // rows) + q * 4 + m) == lax.broadcasted_iota(jnp.int32, (N, N), 0)
    pick[...] = hit.astype(jnp.float32).astype(jnp.bfloat16)
    sum3.turn()
    r_pm.far()
    tot = sum3.result()
    s3_o[...] = tot
    second(0)
    first(1)
    hand(2)
    for c in range(0, C, 256):
        w = slice(c, c + 256)
        v = dp3[:, w].astype(jnp.float32) - tot[0:1, w] / count - n3[:, w].astype(jnp.float32) * (tot[1:2, w] / count)
        d3[:, w] = (ins * v * (ge[:, w] * st_ref[3:4, w])).astype(jnp.bfloat16)
    ones, crossed = [], []
    for c in range(0, neck, 256):
        w = slice(c, c + 256)
        v = nt_dot(d3[...], we[w, :]) * l2[:, w].astype(jnp.float32)
        acc[:, w] = v
        v = v * ins
        ones.append(jnp.sum(v, axis=0, keepdims=True))
        crossed.append(jnp.sum(v * n2[:, w].astype(jnp.float32), axis=0, keepdims=True))
    sum2.start([cat_rows(ones), cat_rows(crossed)])
    for c in range(0, C, 256):
        ex[:, c : c + 256] = tn_dot(h2[...], d3[:, c : c + 256]).astype(jnp.bfloat16)
    sum2.turn()
    r_ex.pair()
    tot = sum2.result()
    s2_o[...] = tot
    for c in range(0, neck, 256):
        w = slice(c, c + 256)
        v = acc[:, w] - tot[0:1, w] / count - n2[:, w].astype(jnp.float32) * (tot[1:2, w] / count)
        v = ins * v * (gd[:, w] * st_ref[2:3, w])
        ext2[:, e : e + h, w] = v.astype(jnp.bfloat16).reshape(Q, h, 256)
    up = remote(ext2.at[:, pl.ds(e, e)], ext2.at[:, pl.ds(e + h, e)], hs.at[0], hr.at[0], d, lax.rem(f + 7, 8))
    down = remote(ext2.at[:, pl.ds(h, e)], ext2.at[:, pl.ds(0, e)], hs.at[1], hr.at[1], d, lax.rem(f + 1, 8))
    second(1)
    hand(3)
    kcp.wait()
    r_pm.beside()
    r_ex.far()
    first(2)
    for i in range(3):
        for j in range(3):
            lo, hi = span(j - 1, Q)
            ok = same_crop(
                key[lo:hi, e : e + h, :], key[lo + j - 1 : hi + j - 1, e * i : e * i + h, :], neck
            )
            v = jnp.where(ok, ext[lo + j - 1 : hi + j - 1, e * i : e * i + h, :], 0).reshape((hi - lo) * h, neck)
            g = ext2[lo:hi, e : e + h, :].reshape((hi - lo) * h, neck)
            di[3 * i + j] = tn_dot(g, v).astype(jnp.bfloat16)
        r_di[i].pair()
        if i == 0:
            hand(4)
            first(3)
            second(2)
        if i == 1:
            r_ex.beside()
    up.wait()
    down.wait()
    r_pm.tiles()
    acc[...] = jnp.zeros_like(acc)
    for i in range(3):
        if i == 1:
            first(4)
            second(3)
        for j in (1, 0, 2):
            lo, hi = span(1 - j, Q)
            ok = same_crop(
                key[lo:hi, e : e + h, :], key[lo + 1 - j : hi + 1 - j, e * (2 - i) : e * (2 - i) + h, :], neck
            )
            v = jnp.where(ok, ext2[lo + 1 - j : hi + 1 - j, e * (2 - i) : e * (2 - i) + h, :], 0)
            v = v.reshape((hi - lo) * h, neck)
            for c in range(0, neck, 256):
                acc[lo * h : hi * h, c : c + 256] += nn_dot(v, wd[3 * i + j, :, c : c + 256])
    ones, crossed = [], []
    for c in range(0, neck, 256):
        w = slice(c, c + 256)
        v = acc[:, w] * l1[:, w].astype(jnp.float32)
        acc[:, w] = v
        v = v * ins
        ones.append(jnp.sum(v, axis=0, keepdims=True))
        crossed.append(jnp.sum(v * n1[:, w].astype(jnp.float32), axis=0, keepdims=True))
    sum1.start([cat_rows(ones), cat_rows(crossed)])
    for r in r_di:
        r.far()
    r_pm.middle()
    sum1.turn()
    r_ex.tiles()
    second(4)
    r_pm.last()
    for r in r_di:
        r.beside()
    tot = sum1.result()
    s1_o[...] = tot
    for c in range(0, neck, 256):
        w = slice(c, c + 256)
        v = acc[:, w] - tot[0:1, w] / count - n1[:, w].astype(jnp.float32) * (tot[1:2, w] / count)
        v = (ins * v * (gr[:, w] * st_ref[1:2, w])).astype(jnp.bfloat16)
        d1n[:, w] = nn_dot(pick[...], v).astype(jnp.bfloat16)
    for c in range(0, C, 256):
        re_[:, c : c + 256] = tn_dot(d1n[...], x_ref[:, c : c + 256]).astype(jnp.bfloat16)
    r_re.pair()
    r_di[0].tiles()
    r_re.far()
    r_ex.middle()
    out = []
    for n, c in enumerate(range(0, C, 256)):
        w = slice(c, c + 256)
        if n >= 2:
            out[n - 2].wait()
        gf[n % 2] = nn_dot(pick[...], dp3[:, w]) + nn_dot(d1n[...], wr[:, w])
        cp = pltpu.make_async_copy(gf.at[n % 2], gf_o.at[:, pl.ds(c, 256)], gs.at[n % 2])
        cp.start()
        out.append(cp)
        if n == 0:
            r_re.beside()
        if n == 1:
            r_di[0].middle()
            r_ex.last()
        if n == 3:
            r_di[1].tiles()
            r_di[0].last()
        if n == 5:
            r_di[1].middle()
        if n == 7:
            r_di[2].tiles()
            r_di[1].last()
    keep(0, 0, 3)
    keep(1, 3, 2)
    r_di[2].middle()
    r_re.tiles()
    r_di[2].last()
    r_re.middle()
    r_re.last()
    out[-2].wait()
    out[-1].wait()
    for t in range(5):

        @pl.when(outer)
        def _():
            to_inner(t).wait_send()

        @pl.when(jnp.logical_not(outer))
        def _():
            to_outer(t).wait_send()

    for c in kout:
        c.wait()
    for r in [r_pm, r_ex, r_re] + r_di:
        r.done()


def bottleneck_back(*args):
    x, st, dpt, pm_in, h2 = args[0], args[2], args[7], args[9], args[16]
    N, C = x.shape
    Q, h2_, neck = args[18].shape
    h = h2_ // 2
    tail = args[23]
    W = dpt.shape[1]
    PM = C + pm_in.shape[1]
    b16, f32 = jnp.bfloat16, jnp.float32
    S, V = jax.ShapeDtypeStruct, pltpu.VMEM
    blocks = [(W // 8, PM), (neck, C // 8), (9, neck // 8, neck), (neck // 8, C)]
    scratch = [
        V((W, PM), b16), V((neck, C), b16), V((9, neck, neck), b16), V((N, C), b16), V((N, C), b16),
        V((N, neck), f32), V((Q, 2 * h, neck), b16), V((N, neck), b16), V((Q, 2 * h, 128), b16), V((2, N, 256), f32),
        V((N, N), b16), V(tail.shape, b16), V(tail.shape, b16),
        DMA(()), DMA((2,)), DMA((2,)), DMA((2,)),
    ]
    scratch += [DMA((5,))] * 6 + [DMA((2, 8)), DMA((2, 8)), DMA((2,))]
    for n in (0, 1, 2, 2, 2, 3):
        scratch += reduce_scratch((3,) + blocks[2][1:] if n == 2 else blocks[n])
    scratch += sum_sems(2, C) + sum_sems(2, neck) + sum_sems(2, neck)
    return pl.pallas_call(
        bottleneck_back_kernel,
        out_shape=[S((N, C), f32)] + [S(b, b16) for b in blocks] + [S((2, C), f32), S((2, neck), f32), S((2, neck), f32)]
        + [S((10, W // 8, C), b16)],
        in_specs=[VM] * 22 + [ANY, VM],
        out_specs=[ANY] + [VM] * 7 + [ANY],
        scratch_shapes=scratch,
        compiler_params=pltpu.CompilerParams(collective_id=12, has_side_effects=True, vmem_limit_bytes=VLIM),
        name="bottleneck_back",
    )(*args)


def spaced_taps(src, key, kernels, acc, base, h, steps, sign, first_lane, dot, b):
    Q = key.shape[0]
    s = sign * steps[b]
    W = kernels.shape[1] if sign < 0 else src.shape[2]
    lanes = slice(first_lane, first_lane + W)
    for n, j in enumerate((0, -1, 1)):
        lo, hi = span(s * j, Q)
        here = key[lo:hi, pl.ds(base, h), :]
        got = None
        for i in (-1, 0, 1):
            at = pl.multiple_of(base + 16 * s * i, 16)
            ok = same_crop(here, key[lo + s * j : hi + s * j, pl.ds(at, h), :], W)
            v = jnp.where(ok, src[lo + s * j : hi + s * j, pl.ds(at, h), lanes], 0).reshape((hi - lo) * h, W)
            r = dot(v, kernels[9 * b + 3 * (i + 1) + j + 1])
            got = r if got is None else got + r
        if n == 0 and sign > 0:
            acc[...] = got
        else:
            acc[lo * h : hi * h] += got


def head_kernel(
    steps, yo, key, kern, y, wp, wm, wc, ins_ref, kb, lab, st_ref, gb, bb, gm, bm,
    lo_o, dp_o, dr_o, pm_o, pooled_o, dpool_o, size_o, sb_o, sm_o,
    acc, near, mine, far, corner, ab, nb, lb, joined, nm, lm, merged, pn, ps, pr, ss, rs,
    *sems,
):
    sems = list(sems)
    f, d = greet(range(1, 8), range(1, 4))
    sum_b, sum_m, back_m, back_b = (Sum(sems[6 * n : 6 * n + 6], d, f) for n in range(4))
    Q, h = pn.shape[1], pn.shape[2]
    N = Q * h
    w = yo.shape[2]
    W = wp.shape[0]
    T = 8 * h
    c0 = f % 2
    me = f // 2
    f32, b16 = jnp.float32, jnp.bfloat16

    def step(n, _):
        k = 3 - n
        g = me ^ k
        for turn in range(2):
            dest = 2 * g + (1 - c0 if turn == 0 else c0)
            base = pl.multiple_of(PAD + h * dest, 16)
            if turn == 1:
                pltpu.make_async_remote_copy(
                    src_ref=pn.at[k], dst_ref=near.at[k], send_sem=ps.at[k], recv_sem=pr.at[k],
                    device_id=(d, f ^ 1), device_id_type=MESH,
                ).wait_recv()
            for b in range(3):
                lanes = slice(b * W, (b + 1) * W)
                spaced_taps(yo, key, kern, acc, base, h, steps, 1, 0, nt_dot, b)
                if turn == 0:
                    pn[k, :, :, lanes] = acc[...].astype(b16).reshape(Q, h, W)
                else:
                    val = acc[...] + near[k, :, :, lanes].astype(f32).reshape(N, W)
                    mine[k, :, :, lanes] = val.astype(b16).reshape(Q, h, W)
            if turn == 0:
                remote(pn.at[k], near.at[k], ps.at[k], pr.at[k], d, f ^ 1)
            else:

                @pl.when(k == 3)
                def _():
                    for a in (0, 1):
                        by_way(a).start()

        return 0

    def by_way(a):
        two = pl.ds(a * (Q // 2), Q // 2)
        return pltpu.make_async_remote_copy(
            src_ref=mine.at[3, two], dst_ref=corner.at[two], send_sem=ss.at[a], recv_sem=rs.at[a],
            device_id=(d, f ^ (2 + 2 * a)), device_id_type=MESH,
        )

    lax.fori_loop(0, 3, step, 0)
    for a in (0, 1):
        by_way(a).wait()
    out = []
    for k in (1, 2):
        two = slice((2 - k) * (Q // 2), (3 - k) * (Q // 2))
        for b in range(3):
            lanes = slice(b * W, (b + 1) * W)
            val = mine[k, two, :, lanes].astype(f32) + corner[two, :, lanes].astype(f32)
            mine[k, two, :, lanes] = val.astype(b16)
        out.append(remote(mine.at[k], far.at[k - 1], ss.at[k + 1], rs.at[k + 1], d, f ^ (2 * k)))
    lax.fori_loop(3, 4, step, 0)
    ab[:, :W] = nt_dot(y[...], wp[...])
    crop = (lax.broadcasted_iota(jnp.int32, (T, 128), 1) + 1).astype(f32)

    def crops(q, carry):
        total, size = carry
        one = (key[q, PAD : PAD + T, :].astype(f32) == crop).astype(f32).astype(b16)
        return total + tn_dot(one, yo[q, PAD : PAD + T, :]), size + tn_dot(one, jnp.ones((T, 128), b16))

    total, size = lax.fori_loop(0, Q, crops, (jnp.zeros((128, w), f32), jnp.zeros((128, 128), f32)))
    size = jnp.where(size > 0, size, 1.0)[:8]
    size_o[...] = size
    pooled = (total[:8] / size[:, :1]).astype(b16)
    pooled_o[...] = pooled
    part = nt_dot(pooled, kern[27])
    part = cat_rows([part[c : c + 1] for c in range(CROPS_TILE)])
    ins = wide(ins_ref[...], 2)
    for c in out:
        c.wait()
    ones, squares = [], []
    for b in range(4):
        lanes = slice(b * W, (b + 1) * W)
        if b:
            src = slice((b - 1) * W, b * W)
            v = mine[0, :, :, src].astype(f32)
            for k in (1, 2):
                v = v + far[k - 1, :, :, src].astype(f32)
            ab[:, lanes] = v.reshape(N, W)
        s, t = column_sums(ab[:, lanes], ins_ref[...])
        ones.append(s)
        squares.append(t)
    sum_b.start([cat_rows(ones), cat_rows(squares), part])
    for k in range(4):
        pltpu.make_async_remote_copy(
            src_ref=pn.at[k], dst_ref=near.at[k], send_sem=ps.at[k], recv_sem=pr.at[k],
            device_id=(d, f ^ 1), device_id_type=MESH,
        ).wait_send()
    sum_b.turn()
    pool_act = sum_b.b2[d, 2:3, :]
    pool, pool_lean = bend(pool_act)
    pool = pool.astype(b16).astype(f32)
    here = wide(kb[...].astype(f32), W // 128)
    v = jnp.zeros((N, W), f32)
    for c in range(CROPS_TILE):
        v = jnp.where(here == c + 1.0, pool[:, c * W : (c + 1) * W], v)
    joined[:, 4 * W :] = v.astype(b16)
    tot = sum_b.result()
    count = st_ref[0:1, 0:1]
    mean = tot[0:1] / count
    inv_b = lax.rsqrt(tot[1:2] / count - mean * mean + eps)
    for b in range(4):
        lanes = slice(b * W, (b + 1) * W)
        n = (ab[:, lanes] - mean[:, lanes]) * inv_b[:, lanes]
        act, lean = bend(n * gb[:, lanes] + bb[:, lanes])
        joined[:, lanes] = act.astype(b16)
        nb[:, lanes] = n.astype(b16)
        lb[:, lanes] = lean.astype(b16)
    am = nt_dot(joined[...], wm[...])
    s, t = column_sums(am, ins_ref[...])
    sum_m.start([s, t])
    sum_m.turn()
    tot = sum_m.result()
    mean = tot[0:1] / count
    inv_m = lax.rsqrt(tot[1:2] / count - mean * mean + eps)
    n = (am - mean) * inv_m
    act, lean = bend(n * gm[...] + bm[...])
    merged[...] = act.astype(b16)
    nm[...] = n
    lm[...] = lean
    logits = nn_dot(merged[...], wc[...])
    lane = lax.broadcasted_iota(jnp.int32, (N, 128), 1)
    valid = lane < CLASSES
    top = jnp.max(jnp.where(valid, logits, -jnp.inf), axis=1, keepdims=True)
    ex = jnp.where(valid, jnp.exp(logits - top), 0.0)
    prob = ex / jnp.sum(ex, axis=1, keepdims=True)
    target = (lab[...] == lane.astype(f32)).astype(f32)
    dl = (ins_ref[...] * (prob - target) / count).astype(b16)
    e = nt_dot(dl, wc[...]) * lm[...]
    m = e * ins
    back_m.start([jnp.sum(m, axis=0, keepdims=True), jnp.sum(m * nm[...], axis=0, keepdims=True)])
    order = lax.broadcasted_iota(jnp.int32, (N, N), 1)
    rows = h // 4
    mm, r, q = order % 4, (order // 4) % rows, order // h
    hit = (r * (N // rows) + q * 4 + mm) == lax.broadcasted_iota(jnp.int32, (N, N), 0)
    lo_o[...] = nn_dot(hit.astype(f32).astype(b16), logits.astype(b16)).astype(b16)
    back_m.turn()
    J = joined.shape[1]
    pm_o[:, J : J + 128] = tn_dot(merged[...], dl).astype(b16)
    pm_o[:, J + 128 :] = jnp.zeros((W, pm_o.shape[1] - J - 128), b16)
    tot = back_m.result()
    sm_o[...] = tot
    dm = (ins * gm[...] * inv_m * (e - tot[0:1] / count - nm[...] * (tot[1:2] / count))).astype(b16)
    ones, crossed = [], []
    for b in range(4):
        lanes = slice(b * W, (b + 1) * W)
        v = nn_dot(dm, wm[:, lanes]) * lb[:, lanes].astype(f32)
        ab[:, lanes] = v
        v = v * ins
        ones.append(jnp.sum(v, axis=0, keepdims=True))
        crossed.append(jnp.sum(v * nb[:, lanes].astype(f32), axis=0, keepdims=True))
    v = nn_dot(dm, wm[:, 4 * W :])
    part = cat_rows(
        [jnp.sum(jnp.where(here == c + 1.0, v, 0.0), axis=0, keepdims=True) for c in range(CROPS_TILE)]
    )
    back_b.start([cat_rows(ones), cat_rows(crossed), part])
    pm_o[:, :J] = tn_dot(dm, joined[...]).astype(b16)
    back_b.turn()
    v = (back_b.b2[d, 2:3, :] * pool_lean).astype(b16)
    dpool_o[...] = jnp.zeros_like(dpool_o)
    for c in range(CROPS_TILE):
        dpool_o[c : c + 1, :] = v[:, c * W : (c + 1) * W]
    tot = back_b.result()
    sb_o[...] = tot[:2]
    for b in range(4):
        lanes = slice(b * W, (b + 1) * W)
        v = ab[:, lanes] - tot[0:1, lanes] / count - nb[:, lanes].astype(f32) * (tot[1:2, lanes] / count)
        v = (ins * v * (gb[:, lanes] * inv_b[:, lanes])).astype(b16)
        if b:
            dr_o[:, :, (b - 1) * W : b * W] = v.reshape(Q, h, W)
        else:
            dp_o[...] = v


def head(steps, width, *args):
    yo, key, kern, y, wp, wm = args[:6]
    N, C = y.shape
    Q = yo.shape[0]
    h = N // Q
    W = wp.shape[0]
    J = wm.shape[1]
    b16, f32 = jnp.bfloat16, jnp.float32
    S, V = jax.ShapeDtypeStruct, pltpu.VMEM
    return pl.pallas_call(
        functools.partial(head_kernel, steps),
        out_shape=[
            S((N, 128), b16), S((N, W), b16), S((Q, h, 3 * W), b16), S((W, width), b16), S((8, C // 8), b16),
            S((8, W), b16), S((8, 128), f32), S((2, 4 * W), f32), S((2, W), f32),
        ],
        in_specs=[VM] * 15,
        out_specs=[VM] * 9,
        scratch_shapes=[V((N, W), f32)]
        + [V((4, Q, h, 3 * W), b16)] * 2 + [V((2, Q, h, 3 * W), b16), V((Q, h, 3 * W), b16)]
        + [
            V((N, 4 * W), f32), V((N, 4 * W), b16), V((N, 4 * W), b16), V((N, J), b16), V((N, W), f32), V((N, W), f32),
            V((N, W), b16), V((4, Q, h, 3 * W), b16), DMA((4,)), DMA((4,)), DMA((4,)), DMA((4,)),
        ]
        + sum_sems(3, 4 * W) + sum_sems(2, W) + sum_sems(2, W) + sum_sems(3, 4 * W),
        compiler_params=pltpu.CompilerParams(collective_id=5, has_side_effects=True, vmem_limit_bytes=VLIM),
        name="head",
    )(*args)


def widen_kernel(gk, tk, pm, ex, di, re_, k0, k1, k2, pool, point, merge, dilated, expand, reduce_):
    for b, o in enumerate((k0, k1, k2)):

        def tap(t, _):
            o[t] = (tk[t] if b == 2 else gk[9 * b + t]).astype(jnp.float32)
            return 0

        lax.fori_loop(0, 9, tap, 0)
    pool[...] = tk[9].astype(jnp.float32)
    C = point.shape[1]
    point[...] = pm[:, :C].astype(jnp.float32)
    merge[...] = pm[:, C : C + merge.shape[1]].astype(jnp.float32)

    def rows(t, _):
        dilated[t] = di[t].astype(jnp.float32)
        return 0

    lax.fori_loop(0, 9, rows, 0)
    expand[...] = ex[...].astype(jnp.float32)
    reduce_[...] = re_[...].astype(jnp.float32)


def widen(gk, tk, pm, ex, di, re_, J):
    _, o, C = gk.shape
    shapes = [(9, o, C)] * 3 + [(o, C), (o, C), (o, J), di.shape, ex.shape, re_.shape]
    return pl.pallas_call(
        widen_kernel,
        out_shape=[jax.ShapeDtypeStruct(v, jnp.float32) for v in shapes],
        in_specs=[VM] * 6,
        out_specs=[VM] * 9,
        compiler_params=pltpu.CompilerParams(vmem_limit_bytes=VLIM),
        name="widen",
    )(gk, tk, pm, ex, di, re_)


def norm_coeffs(totals, squares, count):
    average = totals / count
    return average, lax.rsqrt(squares / count - average * average + eps)


def fast_body(
    features, crop_ids, labels, w_reduce, gain_reduce, bias_reduce, w_dilated, gain_dilated, bias_dilated,
    w_expand, gain_expand, bias_expand, w_point, gain_point, bias_point, w_rate, gain_rate, bias_rate,
    w_rate_double, gain_rate_double, bias_rate_double, w_rate_triple, gain_rate_triple, bias_rate_triple,
    w_pool, w_merge, gain_merge, bias_merge, w_classes,
):
    rows, cols, C = features.shape
    Q = cols // 4
    h = rows * 4
    N = rows * cols
    nf = lax.axis_size("fsdp")
    W = gain_point.shape[0]
    steps = (RATE // 4, 2 * RATE // 4, 3 * RATE // 4)
    place = lax.axis_index("fsdp")

    def perm(a):
        a = a.reshape((rows, Q, 4) + a.shape[2:])
        return jnp.swapaxes(a, 0, 1).reshape((N,) + a.shape[3:])

    def unperm(a):
        a = a.reshape((Q, rows, 4) + a.shape[1:])
        return jnp.swapaxes(a, 0, 1).reshape((rows, cols) + a.shape[3:])

    local_crop = perm(crop_ids) - lax.axis_index("dp") * CROPS_TILE
    in_crop = perm(crop_ids) >= 0
    inside = in_crop.astype(jnp.float32)[:, None]
    key_loc = jnp.where(in_crop, local_crop + 1, 0)
    kb = jnp.broadcast_to(key_loc.astype(jnp.bfloat16)[:, None], (N, 128))
    key_row = jnp.pad(key_loc.astype(jnp.float32).reshape(Q, h), ((0, 0), (0, 128 - h)))
    ins = jnp.broadcast_to(inside, (N, 128))
    rates = [jnp.swapaxes(w.reshape(9, C, -1), 1, 2) for w in (w_rate, w_rate_double, w_rate_triple)]
    vecs = [v[None, :] for v in (gain_reduce, bias_reduce, gain_dilated, bias_dilated, gain_expand, bias_expand)]
    (
        y_own, y, n_three, l_three, n_one, l_one, n_two, l_two, ext, h_two, key, kernel,
        wr, wd, full_expand, wp, wm, wc, count,
    ) = bottleneck(
        features.reshape(N, C), key_row, ins, vecs,
        [
            w_reduce.T, jnp.swapaxes(w_dilated.reshape(9, w_dilated.shape[2], -1), 1, 2), w_expand, w_point.T, w_merge.T,
            jnp.pad(w_classes, ((0, 0), (0, 128 - CLASSES))),
        ],
        rates + [w_pool.T[None]],
    )
    neck = gain_reduce.shape[0]
    stats = count
    count = count[0, 0]
    y = y.reshape(N, C)
    g_br = jnp.concatenate([gain_point, gain_rate, gain_rate_double, gain_rate_triple])[None]
    b_br = jnp.concatenate([bias_point, bias_rate, bias_rate_double, bias_rate_triple])[None]
    lab = jnp.broadcast_to(perm(labels).astype(jnp.float32)[:, None], (N, 128))
    J = wm.shape[1]
    width = J + 128 + -(C + J + 128) % 512
    logits, d_point, d_rates, rest, pooled, d_pool, sizes, st_br, st_m = head(
        steps, width, y_own, key, kernel, y, wp, wm, wc, ins, kb, lab, stats, g_br, b_br,
        gain_merge[None], bias_merge[None],
    )
    class_logits = logits[:, :CLASSES].reshape(rows, cols, CLASSES)
    gb_br, gg_br = st_br[0], st_br[1]
    gb_merge, gg_merge = st_m[0], st_m[1]
    d_y, grad_k, tail = branches_back(d_rates, y_own, key, kernel, pooled, d_pool, sizes, steps)
    grad_features, pm, ex, di, re_, st3, st2, st1, tail = bottleneck_back(
        features.reshape(N, C), ins, stats, vecs[0], vecs[2], vecs[4], d_y.reshape(N, C), d_point, y, rest, wp,
        n_three, l_three, full_expand, n_two, l_two, h_two, wd, ext, n_one, l_one, wr, key, tail,
    )
    grad_classes = pm[:, C + J : C + J + CLASSES].astype(jnp.float32)
    *grad_k, grad_pool, grad_point, grad_merge, grad_dilated, grad_expand, grad_reduce = widen(grad_k, tail, pm, ex, di, re_, J)
    grad_k = [jnp.swapaxes(v.reshape(3, 3, -1, C), 2, 3) for v in grad_k]
    grad_pool, grad_point, grad_merge, grad_reduce = grad_pool.T, grad_point.T, grad_merge.T, grad_reduce.T
    grad_dilated = jnp.swapaxes(grad_dilated, 1, 2).reshape(3, 3, neck, -1)
    grad_features = grad_features.reshape(rows, cols, C)
    gg_expand, gb_expand, gg_dilated, gb_dilated, gg_reduce, gb_reduce = st3[1], st3[0], st2[1], st2[0], st1[1], st1[0]
    return (
        class_logits,
        grad_features,
        grad_reduce, gg_reduce, gb_reduce,
        grad_dilated, gg_dilated, gb_dilated,
        grad_expand, gg_expand, gb_expand,
        grad_point, gg_br[:W], gb_br[:W],
        grad_k[0], gg_br[W : 2 * W], gb_br[W : 2 * W],
        grad_k[1], gg_br[2 * W : 3 * W], gb_br[2 * W : 3 * W],
        grad_k[2], gg_br[3 * W :], gb_br[3 * W :],
        grad_pool,
        grad_merge, gg_merge, gb_merge,
        grad_classes,
    )


def passed_along(value, axis, by):
    count = lax.axis_size(axis)
    pairs = [(i, i + by) for i in range(count) if 0 <= i + by < count]
    return lax.ppermute(value, axis, pairs)


def padded(cells, sides, width):
    for axis, dim in sides:
        count = lax.axis_size(axis)
        ends = count - 1
        head = lax.slice_in_dim(cells, 0, width, axis=dim)
        tail = lax.slice_in_dim(cells, cells.shape[dim] - width, cells.shape[dim], axis=dim)
        cells = jnp.concatenate(
            [
                lax.ppermute(tail, axis, [(i, (i + 1) % count) for i in range(ends)]),
                cells,
                lax.ppermute(head, axis, [((i + 1) % count, i) for i in range(ends)]),
            ],
            axis=dim,
        )
    return cells


def flat_dot(first_op, second_op):
    return jnp.dot(first_op, second_op, preferred_element_type=jnp.float32)


def inner_dot(first_op, second_op):
    return lax.dot_general(
        first_op, second_op, (((0,), (0,)), ((), ())), preferred_element_type=jnp.float32
    )


def outer_dot(first_op, second_op):
    return lax.dot_general(
        first_op, second_op, (((1,), (1,)), ((), ())), preferred_element_type=jnp.float32
    )


def slope(values):
    gate_value = jax.nn.sigmoid(values)
    return gate_value * (1.0 + values * (1.0 - gate_value))


def widen_rows(values, extent, mover):
    row_count = values.shape[0]
    neighbours = -(-extent // row_count)
    above = [mover(values, distance) for distance in range(neighbours, 0, -1)]
    below = [mover(values, -distance) for distance in range(1, neighbours + 1)]
    stacked = jnp.concatenate(above + [values] + below, axis=0)
    start_row = neighbours * row_count - extent
    return stacked[start_row : start_row + row_count + 2 * extent]


def rim_slice(widened, spacing, margin, height):
    return widened[margin - spacing : margin + height + spacing]


def offset_table(broad_key_rows, crop_random_keys, spacing, margin):
    height, breadth = crop_random_keys.shape
    first_row = margin - spacing
    extended = jnp.pad(
        broad_key_rows[first_row : first_row + height + 2 * spacing], ((0, 0), (spacing, spacing))
    )
    tables = []
    for row_tap in range(3):
        for col_tap in range(3):
            nearby = extended[
                row_tap * spacing : row_tap * spacing + height,
                col_tap * spacing : col_tap * spacing + breadth,
            ]
            tables.append(
                ((nearby == crop_random_keys) & (crop_random_keys > 0))
                .astype(jnp.float32)
                .reshape(height * breadth, 1)
            )
    return tables


def spread_offsets(widened, kernel, tables, spacing, height, breadth):
    channels = widened.shape[2]
    extended = jnp.pad(widened, ((0, 0), (spacing, spacing), (0, 0)))
    summed = jnp.zeros((height * breadth, kernel.shape[3]), jnp.float32)
    for row_tap in range(3):
        for col_tap in range(3):
            nearby = extended[
                row_tap * spacing : row_tap * spacing + height,
                col_tap * spacing : col_tap * spacing + breadth,
            ]
            summed = summed + tables[3 * row_tap + col_tap] * flat_dot(
                nearby.reshape(height * breadth, channels), kernel[row_tap, col_tap]
            )
    return summed


def collect_taps(widened, kernel, tables, spacing, height, breadth):
    channels = widened.shape[2]
    extended = jnp.pad(widened, ((0, 0), (spacing, spacing), (0, 0)))
    summed = jnp.zeros((height * breadth, kernel.shape[2]), jnp.float32)
    for row_tap in range(3):
        for col_tap in range(3):
            back_row = 2 - row_tap
            back_col = 2 - col_tap
            nearby = extended[
                back_row * spacing : back_row * spacing + height,
                back_col * spacing : back_col * spacing + breadth,
            ]
            summed = summed + tables[3 * back_row + back_col] * outer_dot(
                nearby.reshape(height * breadth, channels), kernel[row_tap, col_tap]
            )
    return summed


def kernel_offsets(widened, grads_low, tables, spacing, height, breadth):
    channels = widened.shape[2]
    extended = jnp.pad(widened, ((0, 0), (spacing, spacing), (0, 0)))
    pieces = []
    for row_tap in range(3):
        for col_tap in range(3):
            nearby = extended[
                row_tap * spacing : row_tap * spacing + height,
                col_tap * spacing : col_tap * spacing + breadth,
            ]
            masked = (tables[3 * row_tap + col_tap] * grads_low).astype(jnp.bfloat16)
            pieces.append(inner_dot(nearby.reshape(height * breadth, channels), masked))
    return pieces


def statistics(partial_value):
    return lax.psum(partial_value, ("dp", "fsdp"))


def norm_apply(values, totals, squares, pixel_count, factor, offset):
    average = totals / pixel_count
    inverse = lax.rsqrt(squares / pixel_count - average * average + eps)
    normed = (values - average) * inverse
    return (normed * factor + offset, normed, inverse)


def norm_forward(values, inside, pixel_count, factor, offset):
    totals, squares = statistics(
        (jnp.sum(values * inside, axis=0), jnp.sum(values * values * inside, axis=0))
    )
    return norm_apply(values, totals, squares, pixel_count, factor, offset)


def norm_backward(upstream, normed, inverse, factor, inside, pixel_count):
    totals, crossed = lax.psum(
        (jnp.sum(upstream * inside, axis=0), jnp.sum(upstream * normed * inside, axis=0)),
        ("dp", "fsdp"),
    )
    passed = (
        inside
        * factor
        * inverse
        * (upstream - totals / pixel_count - normed * crossed / pixel_count)
    )
    return (passed, crossed, totals)


def body(
    features,
    crop_ids,
    labels,
    w_reduce,
    gain_reduce,
    bias_reduce,
    w_dilated,
    gain_dilated,
    bias_dilated,
    w_expand,
    gain_expand,
    bias_expand,
    w_point,
    gain_point,
    bias_point,
    w_rate,
    gain_rate,
    bias_rate,
    w_rate_double,
    gain_rate_double,
    bias_rate_double,
    w_rate_triple,
    gain_rate_triple,
    bias_rate_triple,
    w_pool,
    w_merge,
    gain_merge,
    bias_merge,
    w_classes,
):
    local_rows, local_columns, channels = features.shape
    pixel_values = local_rows * local_columns
    inputs_flat = features.reshape(pixel_values, channels)
    crop_random_keys = crop_ids + 1
    outer_extent = 3 * RATE
    spacings = (RATE, 2 * RATE, 3 * RATE)
    broad_key_rows = widen_rows(
        crop_random_keys,
        outer_extent,
        lambda piece, distance: passed_along(piece, "fsdp", distance),
    )
    inside = (crop_random_keys > 0).astype(jnp.float32).reshape(pixel_values, 1)
    inner_neck = offset_table(broad_key_rows, crop_random_keys, DILATION_SPAN, outer_extent)
    near_rates = [
        offset_table(broad_key_rows, crop_random_keys, spacing, outer_extent)
        for spacing in spacings
    ]
    (
        full_reduce,
        complete_dilated,
        full_expand,
        full_point,
        full_rate,
        full_double,
        full_triple,
        full_pool,
        full_merge,
        full_classes,
    ) = (
        lax.all_gather(w_reduce, "fsdp", axis=1, tiled=True),
        lax.all_gather(w_dilated, "fsdp", axis=3, tiled=True),
        lax.all_gather(w_expand, "fsdp", axis=1, tiled=True),
        lax.all_gather(w_point, "fsdp", axis=1, tiled=True),
        lax.all_gather(w_rate, "fsdp", axis=3, tiled=True),
        lax.all_gather(w_rate_double, "fsdp", axis=3, tiled=True),
        lax.all_gather(w_rate_triple, "fsdp", axis=3, tiled=True),
        lax.all_gather(w_pool, "fsdp", axis=1, tiled=True),
        lax.all_gather(w_merge, "fsdp", axis=1, tiled=True),
        lax.all_gather(w_classes, "fsdp", axis=0, tiled=True),
    )
    rate_kernels = (full_rate, full_double, full_triple)
    rate_gains = (gain_rate, gain_rate_double, gain_rate_triple)
    rate_biases = (bias_rate, bias_rate_double, bias_rate_triple)
    act_one = flat_dot(inputs_flat, full_reduce)
    totals, squares, pixel_count = statistics(
        (
            jnp.sum(act_one * inside, axis=0),
            jnp.sum(act_one * act_one * inside, axis=0),
            jnp.sum(inside),
        )
    )
    pre_one, normed_one, inverse_one = norm_apply(
        act_one, totals, squares, pixel_count, gain_reduce, bias_reduce
    )
    first_hidden = jax.nn.silu(pre_one).astype(jnp.bfloat16)
    first_broad = padded(
        first_hidden.reshape(local_rows, local_columns, -1), (("fsdp", 0),), DILATION_SPAN
    )
    second_activation = spread_offsets(
        first_broad, complete_dilated, inner_neck, DILATION_SPAN, local_rows, local_columns
    )
    pre_two, normed_two, inverse_two = norm_forward(
        second_activation, inside, pixel_count, gain_dilated, bias_dilated
    )
    hidden_two = jax.nn.silu(pre_two).astype(jnp.bfloat16)
    act_three = flat_dot(hidden_two, full_expand)
    pre_three, normed_three, inverse_three = norm_forward(
        act_three, inside, pixel_count, gain_expand, bias_expand
    )
    pre_three = pre_three + inputs_flat
    block_out = jax.nn.silu(pre_three).astype(jnp.bfloat16)
    wide_block = widen_rows(
        block_out.reshape(local_rows, local_columns, channels),
        outer_extent,
        lambda piece, distance: passed_along(piece, "fsdp", distance),
    )
    point_act = flat_dot(block_out, full_point)
    pre_point, normed_point, inverse_point = norm_forward(
        point_act, inside, pixel_count, gain_point, bias_point
    )
    branch_point = jax.nn.silu(pre_point).astype(jnp.bfloat16)
    rate_states = []
    rate_branches = []
    for kernel, factor, offset, spacing, tables in zip(
        rate_kernels, rate_gains, rate_biases, spacings, near_rates
    ):
        rate_act = spread_offsets(
            rim_slice(wide_block, spacing, outer_extent, local_rows),
            kernel,
            tables,
            spacing,
            local_rows,
            local_columns,
        )
        pre_rate, normed_rate, inverse_rate = norm_forward(
            rate_act, inside, pixel_count, factor, offset
        )
        rate_states.append((pre_rate, normed_rate, inverse_rate))
        rate_branches.append(jax.nn.silu(pre_rate).astype(jnp.bfloat16))
    crop_flat = crop_ids.reshape(pixel_values)
    crop_total = CROPS_TILE
    first_crop = lax.axis_index("dp") * crop_total
    owner_group = lax.axis_size("fsdp")
    owner_place = lax.axis_index("fsdp")
    local_crop = crop_flat - first_crop
    member = local_crop[:, None] == jnp.arange(crop_total)[None, :]
    member_low = member.astype(jnp.bfloat16)
    crop_sums = inner_dot(member_low, block_out)
    crop_sizes = jnp.sum(member.astype(jnp.float32), axis=0)
    crop_sums, crop_sizes = lax.psum((crop_sums, crop_sizes), "fsdp")
    pooled = (crop_sums / crop_sizes[:, None]).astype(jnp.bfloat16)
    pool_act = flat_dot(pooled, full_pool)
    pool_low = jax.nn.silu(pool_act).astype(jnp.bfloat16)
    branch_pool = flat_dot(member_low, pool_low).astype(jnp.bfloat16)
    joined = jnp.concatenate([branch_point] + rate_branches + [branch_pool], axis=1)
    merge_act = flat_dot(joined, full_merge)
    pre_merge, normed_merge, inverse_merge = norm_forward(
        merge_act, inside, pixel_count, gain_merge, bias_merge
    )
    merged = jax.nn.silu(pre_merge).astype(jnp.bfloat16)
    logits_full = flat_dot(merged, full_classes)
    class_logits = logits_full.astype(jnp.bfloat16).reshape(local_rows, local_columns, -1)
    (
        full_reduce,
        complete_dilated,
        full_expand,
        full_point,
        full_rate,
        full_double,
        full_triple,
        full_pool,
        full_merge,
        full_classes,
    ) = (
        lax.all_gather(w_reduce, "fsdp", axis=1, tiled=True),
        lax.all_gather(w_dilated, "fsdp", axis=3, tiled=True),
        lax.all_gather(w_expand, "fsdp", axis=1, tiled=True),
        lax.all_gather(w_point, "fsdp", axis=1, tiled=True),
        lax.all_gather(w_rate, "fsdp", axis=3, tiled=True),
        lax.all_gather(w_rate_double, "fsdp", axis=3, tiled=True),
        lax.all_gather(w_rate_triple, "fsdp", axis=3, tiled=True),
        lax.all_gather(w_pool, "fsdp", axis=1, tiled=True),
        lax.all_gather(w_merge, "fsdp", axis=1, tiled=True),
        lax.all_gather(w_classes, "fsdp", axis=0, tiled=True),
    )
    rate_kernels = (full_rate, full_double, full_triple)
    highest = jnp.max(logits_full, axis=1, keepdims=True)
    shifted = jnp.exp(logits_full - highest)
    probability = shifted / jnp.sum(shifted, axis=1, keepdims=True)
    targets = (labels.reshape(pixel_values, 1) == jnp.arange(CLASSES)[None, :]).astype(jnp.float32)
    grad_logits = (inside * (probability - targets) / pixel_count).astype(jnp.bfloat16)
    grad_classes = inner_dot(merged, grad_logits)
    grad_merged = outer_dot(grad_logits, full_classes)
    passed, grad_gain_merge, grad_bias_merge = norm_backward(
        grad_merged * slope(pre_merge), normed_merge, inverse_merge, gain_merge, inside, pixel_count
    )
    grad_merge_act = passed.astype(jnp.bfloat16)
    grad_merge = inner_dot(joined, grad_merge_act)
    grad_joined = outer_dot(grad_merge_act, full_merge)
    branch_width = full_merge.shape[1]
    passed, grad_gain_point, grad_bias_point = norm_backward(
        grad_joined[:, :branch_width] * slope(pre_point),
        normed_point,
        inverse_point,
        gain_point,
        inside,
        pixel_count,
    )
    grad_point_act = passed.astype(jnp.bfloat16)
    grad_point = inner_dot(block_out, grad_point_act)
    grad_block = outer_dot(grad_point_act, full_point)
    rate_grads = []
    rate_weight_grads = []
    rate_gain_grads = []
    rate_bias_grads = []
    for branch in range(3):
        column = (1 + branch) * branch_width
        pre_rate, normed_rate, inverse_rate = rate_states[branch]
        passed, gain_grad, bias_grad = norm_backward(
            grad_joined[:, column : column + branch_width] * slope(pre_rate),
            normed_rate,
            inverse_rate,
            rate_gains[branch],
            inside,
            pixel_count,
        )
        grad_rate_act = passed.astype(jnp.bfloat16)
        pieces = kernel_offsets(
            rim_slice(wide_block, spacings[branch], outer_extent, local_rows),
            grad_rate_act,
            near_rates[branch],
            spacings[branch],
            local_rows,
            local_columns,
        )
        rate_weight_grads.append(jnp.stack(pieces).reshape(3, 3, channels, branch_width))
        rate_grads.append(grad_rate_act)
        rate_gain_grads.append(gain_grad)
        rate_bias_grads.append(bias_grad)
    rate_grads_low = jnp.concatenate(rate_grads, axis=1).reshape(local_rows, local_columns, -1)
    wide_grad_rate = widen_rows(
        rate_grads_low, outer_extent, lambda piece, distance: passed_along(piece, "fsdp", distance)
    )
    for branch in range(3):
        grad_slab = wide_grad_rate[:, :, branch * branch_width : (branch + 1) * branch_width]
        grad_block = grad_block + collect_taps(
            rim_slice(grad_slab, spacings[branch], outer_extent, local_rows),
            rate_kernels[branch],
            near_rates[branch],
            spacings[branch],
            local_rows,
            local_columns,
        )
    crop_grad = lax.dot_general(
        member.astype(jnp.float32),
        grad_joined[:, 4 * branch_width :],
        (((0,), (0,)), ((), ())),
        precision=lax.Precision.HIGHEST,
        preferred_element_type=jnp.float32,
    )
    crop_grad = lax.psum(crop_grad, "fsdp")
    grad_pool_act = (crop_grad * slope(pool_act)).astype(jnp.bfloat16)
    owned_crops = (jnp.arange(crop_total) % owner_group == owner_place).astype(jnp.float32)[:, None]
    grad_pool = inner_dot(pooled, (grad_pool_act * owned_crops).astype(jnp.bfloat16))
    grad_pooled = outer_dot(grad_pool_act, full_pool) / crop_sizes[:, None]
    grad_block = grad_block + inside * jnp.take(
        grad_pooled, jnp.clip(local_crop, 0, crop_total - 1), axis=0
    )
    grad_pre_three = grad_block * slope(pre_three)
    passed, grad_gain_expand, grad_bias_expand = norm_backward(
        grad_pre_three, normed_three, inverse_three, gain_expand, inside, pixel_count
    )
    grad_three = passed.astype(jnp.bfloat16)
    grad_expand = inner_dot(hidden_two, grad_three)
    grad_hidden_two = outer_dot(grad_three, full_expand)
    passed, grad_gain_dilated, grad_bias_dilated = norm_backward(
        grad_hidden_two * slope(pre_two), normed_two, inverse_two, gain_dilated, inside, pixel_count
    )
    second_gradient = passed.astype(jnp.bfloat16)
    dilated_fragments = kernel_offsets(
        first_broad, second_gradient, inner_neck, DILATION_SPAN, local_rows, local_columns
    )
    grad_dilated = jnp.stack(dilated_fragments).reshape(
        3, 3, second_gradient.shape[1], second_gradient.shape[1]
    )
    broad_neck_gradient = padded(
        second_gradient.reshape(local_rows, local_columns, -1), (("fsdp", 0),), DILATION_SPAN
    )
    grad_hidden_one = collect_taps(
        broad_neck_gradient, complete_dilated, inner_neck, DILATION_SPAN, local_rows, local_columns
    )
    passed, grad_gain_reduce, grad_bias_reduce = norm_backward(
        grad_hidden_one * slope(pre_one), normed_one, inverse_one, gain_reduce, inside, pixel_count
    )
    grad_one = passed.astype(jnp.bfloat16)
    grad_reduce = inner_dot(inputs_flat, grad_one)
    grad_features = (grad_pre_three + outer_dot(grad_one, full_reduce)).reshape(
        local_rows, local_columns, channels
    )
    shards = (
        lax.psum_scatter(grad_reduce, "fsdp", scatter_dimension=1, tiled=True),
        lax.psum_scatter(grad_dilated, "fsdp", scatter_dimension=3, tiled=True),
        lax.psum_scatter(grad_expand, "fsdp", scatter_dimension=1, tiled=True),
        lax.psum_scatter(grad_point, "fsdp", scatter_dimension=1, tiled=True),
        lax.psum_scatter(rate_weight_grads[0], "fsdp", scatter_dimension=3, tiled=True),
        lax.psum_scatter(rate_weight_grads[1], "fsdp", scatter_dimension=3, tiled=True),
        lax.psum_scatter(rate_weight_grads[2], "fsdp", scatter_dimension=3, tiled=True),
        lax.psum_scatter(grad_pool, "fsdp", scatter_dimension=1, tiled=True),
        lax.psum_scatter(grad_merge, "fsdp", scatter_dimension=1, tiled=True),
        lax.psum_scatter(grad_classes, "fsdp", scatter_dimension=0, tiled=True),
    )
    shards = (
        lax.psum(shards[0].astype(jnp.bfloat16), "dp").astype(jnp.float32),
        lax.psum(shards[1].astype(jnp.bfloat16), "dp").astype(jnp.float32),
        lax.psum(shards[2].astype(jnp.bfloat16), "dp").astype(jnp.float32),
        lax.psum(shards[3].astype(jnp.bfloat16), "dp").astype(jnp.float32),
        lax.psum(shards[4].astype(jnp.bfloat16), "dp").astype(jnp.float32),
        lax.psum(shards[5].astype(jnp.bfloat16), "dp").astype(jnp.float32),
        lax.psum(shards[6].astype(jnp.bfloat16), "dp").astype(jnp.float32),
        lax.psum(shards[7].astype(jnp.bfloat16), "dp").astype(jnp.float32),
        lax.psum(shards[8].astype(jnp.bfloat16), "dp").astype(jnp.float32),
        lax.psum(shards[9].astype(jnp.bfloat16), "dp").astype(jnp.float32),
    )
    return (
        class_logits,
        grad_features,
        shards[0],
        grad_gain_reduce,
        grad_bias_reduce,
        shards[1],
        grad_gain_dilated,
        grad_bias_dilated,
        shards[2],
        grad_gain_expand,
        grad_bias_expand,
        shards[3],
        grad_gain_point,
        grad_bias_point,
        shards[4],
        rate_gain_grads[0],
        rate_bias_grads[0],
        shards[5],
        rate_gain_grads[1],
        rate_bias_grads[1],
        shards[6],
        rate_gain_grads[2],
        rate_bias_grads[2],
        shards[7],
        shards[8],
        grad_gain_merge,
        grad_bias_merge,
        shards[9],
    )


def solution(mesh):
    tiled = mesh.shape["fsdp"] == 8 and mesh.shape["dp"] == 4

    return jax.shard_map(
        fast_body if tiled else body,
        mesh=mesh,
        in_specs=(
            P(("dp", "fsdp"), None, None),
            P(("dp", "fsdp"), None),
            P(("dp", "fsdp"), None),
            P(None, "fsdp"),
            P(),
            P(),
            P(None, None, None, "fsdp"),
            P(),
            P(),
            P(None, "fsdp"),
            P(),
            P(),
            P(None, "fsdp"),
            P(),
            P(),
            P(None, None, None, "fsdp"),
            P(),
            P(),
            P(None, None, None, "fsdp"),
            P(),
            P(),
            P(None, None, None, "fsdp"),
            P(),
            P(),
            P(None, "fsdp"),
            P(None, "fsdp"),
            P(),
            P(),
            P("fsdp", None),
        ),
        out_specs=(
            P(("dp", "fsdp"), None, None),
            P(("dp", "fsdp"), None, None),
            P(None, "fsdp"),
            P(),
            P(),
            P(None, None, None, "fsdp"),
            P(),
            P(),
            P(None, "fsdp"),
            P(),
            P(),
            P(None, "fsdp"),
            P(),
            P(),
            P(None, None, None, "fsdp"),
            P(),
            P(),
            P(None, None, None, "fsdp"),
            P(),
            P(),
            P(None, None, None, "fsdp"),
            P(),
            P(),
            P(None, "fsdp"),
            P(None, "fsdp"),
            P(),
            P(),
            P("fsdp", None),
        ),
        check_vma=False,
    )
```

```python
import functools
import jax
import jax.numpy as jnp
from jax import lax
from jax.experimental import pallas as pl
from jax.experimental.pallas import tpu as pltpu
from jax.sharding import PartitionSpec as P


CLASSES = 19
CROPS_TILE = 4
DILATION_SPAN = 4
RATE = 12

eps = 1e-05

MESH = pl.DeviceIdType.MESH
ANY = pl.BlockSpec(memory_space=pl.ANY)
VM = pl.BlockSpec(memory_space=pltpu.VMEM)
DMA = pltpu.SemaphoreType.DMA
PAD = 144
VLIM = 60 * 2**20


def greet(fs, ds):
    f = lax.axis_index("fsdp")
    d = lax.axis_index("dp")
    bar = pltpu.get_barrier_semaphore()
    for k in fs:
        pl.semaphore_signal(bar, inc=1, device_id=(d, f ^ k), device_id_type=MESH)
    for k in ds:
        pl.semaphore_signal(bar, inc=1, device_id=(d ^ k, f), device_id_type=MESH)
    pl.semaphore_wait(bar, len(fs) + len(ds))
    return f, d


def remote(src, dst, ss, rs, d, f):
    c = pltpu.make_async_remote_copy(
        src_ref=src, dst_ref=dst, send_sem=ss, recv_sem=rs, device_id=(d, f), device_id_type=MESH
    )
    c.start()
    return c


def sum_kernel(x_ref, o_ref, b1, b2, s1, r1, s2, r2):
    f, d = greet(range(1, 8), range(1, 4))
    b1[f] = x_ref[...]
    cps = [remote(x_ref, b1.at[f], s1.at[k], r1.at[k], d, f ^ k) for k in range(1, 8)]
    for c in cps:
        c.wait()
    tot = b1[0]
    for k in range(1, 8):
        tot = tot + b1[k]
    b2[d] = tot
    cps = [remote(b2.at[d], b2.at[d], s2.at[k], r2.at[k], d ^ k, f) for k in range(1, 4)]
    for c in cps:
        c.wait()
    tot = b2[0]
    for k in range(1, 4):
        tot = tot + b2[k]
    o_ref[...] = tot


def total_sum(rows, cid):
    x = jnp.stack(rows)
    R, C = x.shape
    return pl.pallas_call(
        sum_kernel,
        out_shape=jax.ShapeDtypeStruct((R, C), jnp.float32),
        in_specs=[VM],
        out_specs=VM,
        scratch_shapes=[
            pltpu.VMEM((8, R, C), jnp.float32),
            pltpu.VMEM((4, R, C), jnp.float32),
            DMA((8,)),
            DMA((8,)),
            DMA((4,)),
            DMA((4,)),
        ],
        compiler_params=pltpu.CompilerParams(collective_id=cid, has_side_effects=True),
        name=f"total_sum_{cid}",
    )(x)


def spread_kernel(x_ref, o_ref, ss, rs, ls):
    f, d = greet(range(1, 8), ())
    w = o_ref.shape[2]
    h = x_ref.shape[1]
    dst = o_ref.at[:, pl.ds(pl.multiple_of(PAD + h * f, 16), h), :]

    def part(g):
        return x_ref.at[:, :, pl.ds(pl.multiple_of(g * w, 128), w)]

    cps = [remote(part(f ^ k), dst, ss.at[k], rs.at[k], d, f ^ k) for k in (6, 7, 2, 3, 4, 5, 1)]
    own = pltpu.make_async_copy(part(f), dst, ls)
    own.start()
    for c in cps:
        c.wait()
    own.wait()


def spread_channels(x, cid):
    q, h, C = x.shape
    return pl.pallas_call(
        spread_kernel,
        out_shape=jax.ShapeDtypeStruct((q, 8 * h + 2 * PAD, C // 8), x.dtype),
        in_specs=[VM],
        out_specs=ANY,
        scratch_shapes=[DMA((8,)), DMA((8,)), DMA(())],
        compiler_params=pltpu.CompilerParams(collective_id=cid, has_side_effects=True, vmem_limit_bytes=VLIM),
        name=f"spread_{cid}",
    )(x)


def collect_kernel(x_ref, o_ref, ss, rs, ls):
    f, d = greet(range(1, 8), ())
    w = x_ref.shape[2]
    h = o_ref.shape[1]
    dst = o_ref.at[:, :, pl.ds(pl.multiple_of(f * w, 128), w)]

    def part(g):
        return x_ref.at[:, pl.ds(pl.multiple_of(h * g, 16), h), :]

    cps = [remote(part(f ^ k), dst, ss.at[k], rs.at[k], d, f ^ k) for k in (6, 7, 2, 3, 4, 5, 1)]
    own = pltpu.make_async_copy(part(f), dst, ls)
    own.start()
    for c in cps:
        c.wait()
    own.wait()


def collect_channels(x, cid):
    q, t, w = x.shape
    return pl.pallas_call(
        collect_kernel,
        out_shape=jax.ShapeDtypeStruct((q, t // 8, 8 * w), x.dtype),
        in_specs=[VM],
        out_specs=ANY,
        scratch_shapes=[DMA((8,)), DMA((8,)), DMA(())],
        compiler_params=pltpu.CompilerParams(collective_id=cid, has_side_effects=True, vmem_limit_bytes=VLIM),
        name=f"collect_{cid}",
    )(x)


def gather_kernel(x_ref, o_ref, ss, rs, ps, pr, ls):
    f, d = greet((1, 2, 4, 6), ())
    h = x_ref.shape[1]

    def slot(g):
        return o_ref.at[:, pl.ds(pl.multiple_of(PAD + h * g, 16), h), :]

    cps = [remote(x_ref, slot(f), ss.at[k], rs.at[k], d, f ^ (2 * k)) for k in (3, 1, 2)]
    own = pltpu.make_async_copy(x_ref, slot(f), ls)
    own.start()
    pair = [remote(x_ref, slot(f), ps.at[0], pr.at[0], d, f ^ 1)]
    for k, c in zip((3, 1, 2), cps):
        c.wait_recv()
        got = slot(f ^ (2 * k))
        pair.append(remote(got, got, ps.at[k], pr.at[k], d, f ^ 1))
    for c in cps:
        c.wait_send()
    for c in pair:
        c.wait()
    own.wait()


def gather_rows(x, cid):
    q, h, C = x.shape
    return pl.pallas_call(
        gather_kernel,
        out_shape=jax.ShapeDtypeStruct((q, 8 * h + 2 * PAD, C), x.dtype),
        in_specs=[VM],
        out_specs=ANY,
        scratch_shapes=[DMA((4,)), DMA((4,)), DMA((4,)), DMA((4,)), DMA(())],
        compiler_params=pltpu.CompilerParams(collective_id=cid, has_side_effects=True, vmem_limit_bytes=VLIM),
        name=f"gather_{cid}",
    )(x)


def scatter_kernel(x_ref, o_ref, near, mine, far, ps, pr, ss, rs):
    f, d = greet((1, 2, 4, 6), ())
    c0 = f & 1
    pair = [
        remote(x_ref.at[2 * k + 1 - c0], near.at[k], ps.at[k], pr.at[k], d, f ^ 1) for k in range(4)
    ]
    me = lax.shift_right_logical(f, 1)
    cps = []
    for c in pair:
        c.wait()
    for k in (3, 1, 2, 0):
        g = me ^ k
        val = x_ref[2 * g + c0].astype(jnp.float32) + near[g].astype(jnp.float32)
        if k:
            mine[k] = val.astype(mine.dtype)
            cps.append(remote(mine.at[k], far.at[k], ss.at[k], rs.at[k], d, f ^ (2 * k)))
        else:
            o_ref[...] = val
    for c in cps:
        c.wait()
    o_ref[...] += far[1].astype(jnp.float32) + far[2].astype(jnp.float32) + far[3].astype(jnp.float32)


def scatter_sum(x, cid):
    n, R, C = x.shape
    return pl.pallas_call(
        scatter_kernel,
        out_shape=jax.ShapeDtypeStruct((R, C), jnp.float32),
        in_specs=[VM],
        out_specs=VM,
        scratch_shapes=[
            pltpu.VMEM((4, R, C), x.dtype),
            pltpu.VMEM((4, R, C), x.dtype),
            pltpu.VMEM((4, R, C), x.dtype),
            DMA((4,)),
            DMA((4,)),
            DMA((4,)),
            DMA((4,)),
        ],
        compiler_params=pltpu.CompilerParams(collective_id=cid, has_side_effects=True, vmem_limit_bytes=VLIM),
        name=f"scatter_{cid}",
    )(x)


def nt_dot(a, b):
    return lax.dot_general(a, b, (((1,), (1,)), ((), ())), preferred_element_type=jnp.float32)


def nn_dot(a, b):
    return lax.dot_general(a, b, (((1,), (0,)), ((), ())), preferred_element_type=jnp.float32)


def tn_dot(a, b):
    return lax.dot_general(a, b, (((0,), (0,)), ((), ())), preferred_element_type=jnp.float32)


def span(shift, count):
    return max(0, -shift), min(count, count - shift)


def conv_forward_kernel(steps, y_ref, key_ref, k_ref, o_ref, acc):
    Q = y_ref.shape[0]
    h = o_ref.shape[2]
    w = y_ref.shape[2]
    out = k_ref.shape[1]
    dest = pl.program_id(0)
    base = PAD + h * dest
    T = 8 * h
    for b, s in enumerate(steps):
        acc[...] = jnp.zeros_like(acc)
        for i in (-1, 0, 1):
            first = h * dest + 16 * s * i

            @pl.when((first + h > 0) & (first < T))
            def _():
                at = pl.multiple_of(base + 16 * s * i, 16)
                for j in (-1, 0, 1):
                    lo, hi = span(s * j, Q)
                    here = key_ref[lo:hi, pl.ds(pl.multiple_of(base, 16), h), :]
                    there = key_ref[lo + s * j : hi + s * j, pl.ds(at, h), :]
                    ok = (here == there) & (here > 0)
                    ok = jnp.concatenate([ok] * (w // 128), axis=2)
                    x = jnp.where(ok, y_ref[lo + s * j : hi + s * j, pl.ds(at, h), :], 0)
                    x = x.reshape((hi - lo) * h, w)
                    acc[lo * h : hi * h] += nt_dot(x, k_ref[9 * b + 3 * (i + 1) + j + 1])

        o_ref[0, :, :, b * out : (b + 1) * out] = acc[...].reshape(Q, h, out).astype(o_ref.dtype)


def conv_forward(y, key, k, steps):
    Q, TT, w = y.shape
    h = (TT - 2 * PAD) // 8
    out = k.shape[1]
    return pl.pallas_call(
        functools.partial(conv_forward_kernel, steps),
        out_shape=jax.ShapeDtypeStruct((8, Q, h, 3 * out), jnp.bfloat16),
        grid=(8,),
        in_specs=[VM, VM, VM],
        out_specs=pl.BlockSpec((1, Q, h, 3 * out), lambda i: (i, 0, 0, 0)),
        scratch_shapes=[pltpu.VMEM((Q * h, out), jnp.float32)],
        compiler_params=pltpu.CompilerParams(vmem_limit_bytes=VLIM),
        name="conv_forward",
    )(y, key, k)


def conv_data_kernel(steps, g_ref, key_ref, k_ref, o_ref, acc):
    Q = g_ref.shape[0]
    h = o_ref.shape[1]
    w = o_ref.shape[2]
    out = k_ref.shape[1]
    dest = pl.program_id(0)
    base = PAD + h * dest
    T = 8 * h
    acc[...] = jnp.zeros_like(acc)
    for b, s in enumerate(steps):
        for i in (-1, 0, 1):
            first = h * dest - 16 * s * i

            @pl.when((first + h > 0) & (first < T))
            def _():
                at = pl.multiple_of(base - 16 * s * i, 16)
                for j in (-1, 0, 1):
                    lo, hi = span(-s * j, Q)
                    here = key_ref[lo:hi, pl.ds(pl.multiple_of(base, 16), h), :]
                    there = key_ref[lo - s * j : hi - s * j, pl.ds(at, h), :]
                    ok = (here == there) & (here > 0)
                    ok = jnp.concatenate([ok] * (out // 128), axis=2)
                    x = jnp.where(
                        ok, g_ref[lo - s * j : hi - s * j, pl.ds(at, h), b * out : (b + 1) * out], 0
                    )
                    x = x.reshape((hi - lo) * h, out)
                    acc[lo * h : hi * h] += nn_dot(x, k_ref[9 * b + 3 * (i + 1) + j + 1])

    o_ref[...] = acc[...].reshape(Q, h, w).astype(o_ref.dtype)


def conv_data(g, key, k, steps):
    Q, TT, _ = g.shape
    h = (TT - 2 * PAD) // 8
    w = k.shape[2]
    return pl.pallas_call(
        functools.partial(conv_data_kernel, steps),
        out_shape=jax.ShapeDtypeStruct((Q, 8 * h, w), jnp.bfloat16),
        grid=(8,),
        in_specs=[VM, VM, VM],
        out_specs=pl.BlockSpec((Q, h, w), lambda i: (0, i, 0)),
        scratch_shapes=[pltpu.VMEM((Q * h, w), jnp.float32)],
        compiler_params=pltpu.CompilerParams(vmem_limit_bytes=VLIM),
        name="conv_data",
    )(g, key, k)


def conv_weight_kernel(steps, y_ref, key_ref, g_ref, o_ref, x_ref):
    Q = y_ref.shape[0]
    w = y_ref.shape[2]
    out = o_ref.shape[1]
    TT = y_ref.shape[1]
    T = TT - 2 * PAD
    b = pl.program_id(0)
    for n, s in enumerate(steps):

        @pl.when(b == n)
        def _():
            for i in (-1, 0, 1):
                r0, r1 = span(16 * s * i, T)
                r0, r1 = r0 // 128 * 128, -(-r1 // 128) * 128
                for j in (-1, 0, 1):
                    lo, hi = span(s * j, Q)
                    L = r1 - r0

                    def one(q, _):
                        here = key_ref[q, PAD + r0 : PAD + r1, :]
                        a = PAD + r0 + 16 * s * i
                        there = key_ref[q + s * j, a : a + L, :]
                        ok = (here == there) & (here > 0)
                        ok = jnp.concatenate([ok] * (w // 128), axis=1)
                        x = jnp.where(ok, y_ref[q + s * j, a : a + L, :], 0)
                        x_ref[pl.ds(pl.multiple_of((q - lo) * L, 128), L), :] = x
                        return 0

                    lax.fori_loop(lo, hi, one, 0)
                    d = g_ref[lo:hi, PAD + r0 : PAD + r1, n * out : (n + 1) * out]
                    d = d.reshape((hi - lo) * L, out)
                    o_ref[3 * (i + 1) + j + 1] = tn_dot(d, x_ref[: (hi - lo) * L, :]).astype(o_ref.dtype)


def conv_weight(y, key, g, steps, out):
    Q, TT, w = y.shape
    T = TT - 2 * PAD
    return pl.pallas_call(
        functools.partial(conv_weight_kernel, steps),
        out_shape=jax.ShapeDtypeStruct((27, out, w), jnp.bfloat16),
        grid=(3,),
        in_specs=[VM, VM, VM],
        out_specs=pl.BlockSpec((9, out, w), lambda i: (i, 0, 0)),
        scratch_shapes=[pltpu.VMEM((Q * T, w), jnp.bfloat16)],
        compiler_params=pltpu.CompilerParams(vmem_limit_bytes=VLIM),
        name="conv_weight",
    )(y, key, g)


class Load:
    def __init__(self, sems, **pairs):
        self.cps = {}
        for n, (name, (src, dst)) in enumerate(pairs.items()):
            self.cps[name] = pltpu.make_async_copy(src, dst, sems.at[n])
            self.cps[name].start()

    def need(self, *names):
        for name in names:
            self.cps.pop(name).wait()


class Gather:
    def __init__(self, src, slot, sems, d, f):
        self.src, self.slot, self.sems, self.d, self.f = src, slot, sems, d, f

    def start(self):
        far_s, far_r, near_s, near_r, local = self.sems
        d, f = self.d, self.f
        mine = self.slot(f)
        self.far = {k: remote(self.src, mine, far_s.at[k], far_r.at[k], d, f ^ (2 * k)) for k in (3, 1, 2)}
        self.near = [remote(self.src, mine, near_s.at[0], near_r.at[0], d, f ^ 1)]
        self.own = pltpu.make_async_copy(self.src, mine, local)
        self.own.start()

    def forward(self):
        far_s, far_r, near_s, near_r, local = self.sems
        for k in (1, 2, 3):
            self.far[k].wait_recv()
            got = self.slot(self.f ^ (2 * k))
            self.near.append(remote(got, got, near_s.at[k], near_r.at[k], self.d, self.f ^ 1))

    def arrive(self):
        self.own.wait()
        for c in self.near:
            c.wait_recv()

    def finish(self):
        for c in list(self.far.values()) + self.near:
            c.wait_send()


class HalfGather:
    def __init__(self, src, slot, half, sems, d, f):
        self.src, self.slot, self.half, self.sems, self.d, self.f = src, slot, half, sems, d, f

    def start(self):
        far_s, far_r, near_s, near_r, side_s, side_r, local = self.sems
        d, f = self.d, self.f
        mine = self.slot(f)
        a = self.half(d % 2)
        self.far = {
            k: remote(self.src.at[a], mine.at[a], far_s.at[k], far_r.at[k], d, f ^ (2 * k)) for k in (3, 1, 2)
        }
        self.near = [remote(self.src, mine, near_s.at[0], near_r.at[0], d, f ^ 1)]
        self.own = pltpu.make_async_copy(self.src, mine, local)
        self.own.start()

    def forward(self):
        far_s, far_r, near_s, near_r, side_s, side_r, local = self.sems
        d, f = self.d, self.f
        a = self.half(d % 2)
        self.side = {}
        for k in (1, 2, 3):
            self.far[k].wait_recv()
            got = self.slot(f ^ (2 * k)).at[a]
            self.side[k] = remote(got, got, side_s.at[k], side_r.at[k], d ^ 1, f)
            self.near.append(remote(got, got, near_s.at[k], near_r.at[k], d, f ^ 1))

    def arrive(self):
        far_s, far_r, near_s, near_r, side_s, side_r, local = self.sems
        d, f = self.d, self.f
        b = self.half(1 - d % 2)
        for k in (1, 2, 3):
            self.side[k].wait_recv()
            got = self.slot(f ^ (2 * k)).at[b]
            self.near.append(remote(got, got, near_s.at[k + 3], near_r.at[k + 3], d, f ^ 1))
        self.own.wait()
        for c in self.near:
            c.wait_recv()

    def finish(self):
        for c in list(self.far.values()) + self.near + list(self.side.values()):
            c.wait_send()


def half_sems():
    return [DMA((4,)), DMA((4,)), DMA((7,)), DMA((7,)), DMA((4,)), DMA((4,)), DMA(())]


def gather_sems():
    return [DMA((4,)), DMA((4,)), DMA((4,)), DMA((4,)), DMA(())]


def sum_sems(R, C):
    return [
        pltpu.VMEM((8, R, C), jnp.float32),
        pltpu.VMEM((4, R, C), jnp.float32),
        DMA((8,)),
        DMA((8,)),
        DMA((4,)),
        DMA((4,)),
    ]


def sum_all(rows, bufs, d, f):
    b1, b2, s1, r1, s2, r2 = bufs
    for n, row in enumerate(rows):
        b1[f, n : n + 1, :] = row
    cps = [remote(b1.at[f], b1.at[f], s1.at[k], r1.at[k], d, f ^ k) for k in (6, 2, 4, 7, 3, 5, 1)]
    for c in cps:
        c.wait()
    tot = b1[0]
    for k in range(1, 8):
        tot = tot + b1[k]
    b2[d] = tot
    cps = [remote(b2.at[d], b2.at[d], s2.at[k], r2.at[k], d ^ k, f) for k in (3, 2, 1)]
    for c in cps:
        c.wait()
    tot = b2[0]
    for k in range(1, 4):
        tot = tot + b2[k]
    return tot


def column_sums(a, ins):
    m = a * jnp.concatenate([ins] * (a.shape[1] // 128), axis=1)
    return jnp.sum(m, axis=0, keepdims=True), jnp.sum(m * a, axis=0, keepdims=True)


def bend(p):
    g = 1.0 / (1.0 + jnp.exp(-p))
    return p * g, g * (1.0 + p * (1.0 - g))


def same_crop(here, there, width):
    ok = (here == there) & (here > 0)
    return jnp.concatenate([ok] * (width // 128), axis=ok.ndim - 1)


def cat_rows(parts):
    return jnp.concatenate(parts, axis=1)


def bottleneck_kernel(
    x_ref, kb_ref, ins_ref, gr, br, gd, bd, ge, be,
    wr_s, wd_s, we_s, wp_s, wm_s, wc_s, k_s0, k_s1, k_s2, kp_s,
    yo_o, y_o, n3_o, l3_o, n1_o, l1_o, n2_o, l2_o, ext_o, h2_o, key_o, k_o, wr_o, wd_o, we_o, wp_o, wm_o, wc_o, cnt_o,
    xp, a1, a2, a3, ext, h2, y, n3, l3, n1, l1, n2, l2, key, wr, wd, we,
    *sems,
):
    sems = list(sems)

    def take(n):
        got = sems[:n]
        del sems[:n]
        return got

    f, d = greet(range(1, 8), range(1, 4))
    N, C = x_ref.shape
    Q, h = ext.shape[0], ext.shape[1] // 2
    e = h // 2
    rows = h // 4
    neck = a1.shape[1]
    T = 8 * h

    def rows_of(ref, n):
        return lambda g: ref.at[pl.ds(pl.multiple_of(n * g, n), n)]

    nr, nd_, ne, np_ = wr_s.shape[0], wd_s.shape[1], we_s.shape[1], wp_s.shape[0]
    def half(n, lead=()):
        return lambda a: lead + (pl.ds(pl.multiple_of(n * a, n), n),)

    g_wr = Gather(wr_s, rows_of(wr, nr), take(5), d, f)
    g_wd = [
        HalfGather(
            wd_s.at[pl.ds(3 * i, 3)],
            lambda g, i=i: wd.at[pl.ds(3 * i, 3), pl.ds(pl.multiple_of(nd_ * g, 16), nd_), :],
            half(nd_ // 2, (slice(None),)), take(7), d, f,
        )
        for i in range(3)
    ]
    g_we = HalfGather(
        we_s, lambda g: we.at[:, pl.ds(pl.multiple_of(ne * g, 128), ne)], half(we_s.shape[0] // 2), take(7), d, f
    )
    g_wp = Gather(wp_s, rows_of(wp_o, np_), take(5), d, f)
    g_wm = Gather(wm_s, rows_of(wm_o, np_), take(5), d, f)
    g_wc = Gather(wc_s, rows_of(wc_o, np_), take(5), d, f)
    ks, kr, kl, zs, zk, hs, hr, ys, yr, yl, os_, qs, qr, kc = take(14)
    sum1, sum2, sum3 = (Sum(take(6), d, f) for _ in range(3))

    key_sent = [
        remote(kb_ref, kc.at[f], qs.at[k], qr.at[k], d, f ^ k) for k in (6, 7, 2, 3, 4, 5, 1)
    ]
    kc[f] = kb_ref[...]
    g_wr.start()
    g_wd[0].start()
    order = lax.broadcasted_iota(jnp.int32, (N, N), 0)
    m, r, q = order % 4, (order // 4) % rows, order // h
    pick = (r * (N // rows) + q * 4 + m) == lax.broadcasted_iota(jnp.int32, (N, N), 1)
    pick = pick.astype(jnp.float32).astype(jnp.bfloat16)
    for c in range(0, C, 256):
        xp[:, c : c + 256] = nn_dot(pick, x_ref[:, c : c + 256]).astype(jnp.bfloat16)
    key[:, :PAD, :] = jnp.zeros((Q, PAD, 128), jnp.bfloat16)
    key[:, PAD + T :, :] = jnp.zeros((Q, PAD, 128), jnp.bfloat16)
    g_wr.forward()
    g_wd[1].start()
    g_wd[2].start()
    g_wr.arrive()
    g_wd[0].forward()
    sums, squares = [], []
    for c in range(0, neck, 256):
        a = nt_dot(xp[...], wr[c : c + 256, :])
        a1[:, c : c + 256] = a
        s, t = column_sums(a, ins_ref[...])
        sums.append(s)
        squares.append(t)
    inside = jnp.sum(ins_ref[...], axis=0, keepdims=True)
    sum1.start([cat_rows(sums), cat_rows(squares), cat_rows([inside] * (neck // 128))])
    g_we.start()
    g_wd[1].forward()
    g_wd[2].forward()
    kparts = (k_s0, k_s1, k_s2, kp_s)

    def kslot(b, g, lo, n):
        o = kparts[b].shape[1]
        return k_o.at[pl.ds(9 * b, kparts[b].shape[0]), pl.ds(pl.multiple_of(o * g + lo, 16), n), :]

    kcp, kfar = [], {}
    pieces = [(b, k) for b in range(3) for k in (6, 7, 2, 3, 4, 5)]

    def out(*ns):
        for b, k in [pieces[n] for n in ns]:
            src = kparts[b]
            o = src.shape[1] // 2
            lo = pl.multiple_of(o * (d % 2), 16)
            to = pl.ds(pl.multiple_of((f ^ k) * 256, 128), 256)
            kfar[b, k] = remote(
                src.at[:, pl.ds(lo, o), to], kslot(b, f, lo, o), ks.at[b, k], kr.at[b, k], d, f ^ k
            )

    def aside(*ns):
        for b, k in [pieces[n] for n in ns]:
            o = kparts[b].shape[1] // 2
            lo = pl.multiple_of(o * (d % 2), 16)
            kfar[b, k].wait_recv()
            got = kslot(b, f ^ k, lo, o)
            kcp.append(remote(got, got, zs.at[b, k], zk.at[b, k], d ^ 1, f))

    for b, src in enumerate(kparts):
        o = src.shape[1]
        for k in (6, 7, 2, 3, 4, 5, 1) if b == 3 else (1,):
            to = pl.ds(pl.multiple_of((f ^ k) * 256, 128), 256)
            kcp.append(remote(src.at[:, :, to], kslot(b, f, 0, o), ks.at[b, k], kr.at[b, k], d, f ^ k))
        own = pl.ds(pl.multiple_of(f * 256, 128), 256)
        c = pltpu.make_async_copy(src.at[:, :, own], kslot(b, f, 0, o), kl.at[b])
        c.start()
        kcp.append(c)
    sum1.turn()
    out(0, 1)
    st = sum1.result()
    out(2, 3)
    g_we.forward()
    count = st[2:3, :]
    cnt_o[...] = jnp.zeros_like(cnt_o)
    cnt_o[0:1, :neck] = count
    mean = st[0:1] / count
    inv = lax.rsqrt(st[1:2] / count - mean * mean + eps)
    cnt_o[1:2, :neck] = inv
    for c in range(0, neck, 256):
        w = slice(c, c + 256)
        n = (a1[:, w] - mean[:, w]) * inv[:, w]
        act, lean = bend(n * gr[:, w] + br[:, w])
        ext[:, e : e + h, w] = act.astype(jnp.bfloat16).reshape(Q, h, 256)
        n1[:, w] = n.astype(jnp.bfloat16)
        l1[:, w] = lean.astype(jnp.bfloat16)
    up = remote(ext.at[:, pl.ds(e, e)], ext.at[:, pl.ds(e + h, e)], hs.at[0], hr.at[0], d, lax.rem(f + 7, 8))
    down = remote(ext.at[:, pl.ds(h, e)], ext.at[:, pl.ds(0, e)], hs.at[1], hr.at[1], d, lax.rem(f + 1, 8))
    for c in key_sent:
        c.wait()
    for g in range(8):
        turned = kc[g].T
        for q in range(Q):
            key[q, PAD + h * g : PAD + h * g + h, :] = jnp.broadcast_to(turned[:h, q : q + 1], (h, 128)).astype(jnp.bfloat16)
    outs = [(n1, n1_o), (l1, l1_o), (key, key_o), (wr, wr_o)]
    base = pl.multiple_of(PAD + h * f, 16)
    up.wait()
    down.wait()
    outs.append((ext, ext_o))
    outs.append((wd, wd_o))
    a2[...] = jnp.zeros_like(a2)
    for i in range(3):
        g_wd[i].arrive()
        for j in (1, 0, 2):
            lo, hi = span(j - 1, Q)
            ok = same_crop(
                key[lo:hi, pl.ds(base, h), :],
                key[lo + j - 1 : hi + j - 1, pl.ds(pl.multiple_of(base + e * (i - 1), 16), h), :],
                neck,
            )
            v = jnp.where(ok, ext[lo + j - 1 : hi + j - 1, e * i : e * i + h, :], 0).reshape((hi - lo) * h, neck)
            for c in range(0, neck, 256):
                a2[lo * h : hi * h, c : c + 256] += nt_dot(v, wd[3 * i + j, c : c + 256, :])
            if (3 * i + j) % 2 == 0 and i < 2 + (j == 0):
                out(4 + (3 * i + j) // 2)
    sums, squares = [], []
    for c in range(0, neck, 256):
        s, t = column_sums(a2[:, c : c + 256], ins_ref[...])
        sums.append(s)
        squares.append(t)
    sum2.start([cat_rows(sums), cat_rows(squares)])
    aside(0, 1, 2, 3)
    sum2.turn()
    out(8, 9)
    st = sum2.result()
    out(10)
    mean = st[0:1] / count
    inv = lax.rsqrt(st[1:2] / count - mean * mean + eps)
    cnt_o[2:3, :neck] = inv
    for c in range(0, neck, 256):
        w = slice(c, c + 256)
        n = (a2[:, w] - mean[:, w]) * inv[:, w]
        act, lean = bend(n * gd[:, w] + bd[:, w])
        h2[:, w] = act.astype(jnp.bfloat16)
        n2[:, w] = n.astype(jnp.bfloat16)
        l2[:, w] = lean.astype(jnp.bfloat16)
    outs += [(n2, n2_o), (l2, l2_o), (h2, h2_o)]
    g_we.arrive()
    outs.append((we, we_o))
    sums, squares = [], []
    for c in range(0, C, 256):
        n = c // 256
        if n % 2 == 0:
            out(11 + n // 2)
        else:
            aside(4 + n // 2)
        a = nn_dot(h2[...], we[:, c : c + 256])
        a3[:, c : c + 256] = a
        s, t = column_sums(a, ins_ref[...])
        sums.append(s)
        squares.append(t)
    sum3.start([cat_rows(sums), cat_rows(squares)])
    aside(8, 9)
    sum3.turn()
    out(15, 16, 17)
    for g in (g_wp, g_wm, g_wc):
        g.start()
    st = sum3.result()
    total = count[:, :1]
    mean3 = st[0:1] / total
    inv3 = lax.rsqrt(st[1:2] / total - mean3 * mean3 + eps)
    coef = sum3.b1
    coef[0, 0:1, :] = mean3
    coef[0, 1:2, :] = inv3
    cnt_o[3:4, :] = inv3
    sent = []
    dst = yo_o.at[:, pl.ds(base, h), :]
    for m, k in enumerate((6, 7, 2, 3, 4, 5, 1, 0)):
        aside(10 + m)
        g = f ^ k
        w = pl.ds(pl.multiple_of(g * 256, 256), 256)
        n = (a3[:, w] - coef[0, 0:1, w]) * coef[0, 1:2, w]
        act, lean = bend(n * ge[:, w] + be[:, w] + xp[:, w].astype(jnp.float32))
        y[:, :, w] = act.astype(jnp.bfloat16).reshape(Q, h, 256)
        n3[:, w] = n.astype(jnp.bfloat16)
        l3[:, w] = lean.astype(jnp.bfloat16)
        part = y.at[:, :, w]
        if k:
            sent.append(remote(part, dst, ys.at[k], yr.at[k], d, g))
        else:
            own = pltpu.make_async_copy(part, dst, yl)
            own.start()
            sent.append(own)
    outs += [(y, y_o), (n3, n3_o), (l3, l3_o)]
    saved = []
    for n, (src, to) in enumerate(outs):
        c = pltpu.make_async_copy(src, to, os_.at[n])
        c.start()
        saved.append(c)
    for g in (g_wp, g_wm, g_wc):
        g.forward()
    for g in (g_wp, g_wm, g_wc):
        g.arrive()
    for g in [g_wr, g_we, g_wp, g_wm, g_wc] + g_wd:
        g.finish()
    for c in kfar.values():
        c.wait_send()
    for c in kcp + sent + saved:
        c.wait()


def bottleneck(x, kb, ins, vecs, shards, kparts):
    N, C = x.shape
    Q = kb.shape[0]
    h = N // Q
    wr, wd, we, wp, wm, wc = shards
    neck = we.shape[0]
    W = 8 * wp.shape[0]
    b16, f32 = jnp.bfloat16, jnp.float32
    S = jax.ShapeDtypeStruct
    TT = 8 * h + 2 * PAD
    outs = [
        S((Q, TT, C // 8), b16), S((Q, h, C), b16), S((N, C), b16), S((N, C), b16),
        S((N, neck), b16), S((N, neck), b16), S((N, neck), b16), S((N, neck), b16),
        S((Q, 2 * h, neck), b16), S((N, neck), b16), S((Q, TT, 128), b16), S((28, W, C // 8), b16),
        S((neck, C), b16), S((9, neck, neck), b16), S((neck, C), b16), S((W, C), b16), S((W, wm.shape[1]), b16),
        S((W, 128), b16), S((8, C), f32),
    ]
    V = pltpu.VMEM
    scratch = [
        V((N, C), b16), V((N, neck), f32), V((N, neck), f32), V((N, C), f32), V((Q, 2 * h, neck), b16), V((N, neck), b16),
        V((Q, h, C), b16), V((N, C), b16), V((N, C), b16),
        V((N, neck), b16), V((N, neck), b16), V((N, neck), b16), V((N, neck), b16), V((Q, TT, 128), b16),
        V((neck, C), b16), V((9, neck, neck), b16), V((neck, C), b16),
    ]
    scratch += gather_sems() + half_sems() * 4 + gather_sems() * 3
    scratch += [DMA((4, 8)), DMA((4, 8)), DMA((4,)), DMA((4, 8)), DMA((4, 8)), DMA((2,)), DMA((2,)), DMA((8,)), DMA((8,)), DMA(()), DMA((16,))]
    scratch += [DMA((8,)), DMA((8,)), V((8, Q, 128), f32)]
    scratch += sum_sems(3, neck) + sum_sems(2, neck) + sum_sems(2, C)
    return pl.pallas_call(
        bottleneck_kernel,
        out_shape=outs,
        in_specs=[VM] * 9 + [ANY] * 10,
        out_specs=[ANY] * 18 + [VM],
        scratch_shapes=scratch,
        compiler_params=pltpu.CompilerParams(collective_id=1, has_side_effects=True, vmem_limit_bytes=VLIM),
        name="bottleneck",
    )(x, kb, ins, *vecs, *shards, *kparts)


def branches_back_kernel(
    steps, d_ref, y_any, key_any, k_any, pooled_ref, dr_ref, size_ref, dy_o, gk_o, tail_o,
    g, gt, gk, fin, in1, in2, dyo, acc, gp, y_ref, key_ref, k_ref, lsem, *sems,
):
    sems = list(sems)
    load = Load(lsem, key=(key_any, key_ref), y=(y_any, y_ref), k=(k_any, k_ref))
    f, d = greet(range(1, 8), range(1, 4))
    Q, h, w = y_ref.shape[0], d_ref.shape[1], y_ref.shape[2]
    W = k_ref.shape[1]
    T = 8 * h
    o = W // 8
    taps = gk.shape[0] // 2
    gathers = [
        Gather(
            d_ref.at[:, :, pl.ds(b * W, W)],
            lambda n, b=b: g.at[:, pl.ds(pl.multiple_of(PAD + h * n, 16), h), pl.ds(b * W, W)],
            sems[5 * b : 5 * b + 5], d, f,
        )
        for b in range(3)
    ]
    ws, wr, wl, ds_, dr_, dl, s1, r1, s2, r2, s3, r3 = sems[15:]
    for c in gathers:
        c.start()
    outer = d % 3 == 0

    def two(ref, t):
        return ref.at[pl.ds(2 * t, 2)]

    def to_inner(t):
        return pltpu.make_async_remote_copy(
            src_ref=two(gk, t), dst_ref=two(in1, t), send_sem=s1.at[t], recv_sem=r1.at[t],
            device_id=(d ^ 1, f), device_id_type=MESH,
        )

    def across(t):
        return pltpu.make_async_remote_copy(
            src_ref=two(gk, t), dst_ref=two(in2, t), send_sem=s2.at[t], recv_sem=r2.at[t],
            device_id=(d ^ 3, f), device_id_type=MESH,
        )

    def to_outer(t):
        return pltpu.make_async_remote_copy(
            src_ref=two(fin, t), dst_ref=two(fin, t), send_sem=s3.at[t], recv_sem=r3.at[t],
            device_id=(d ^ 1, f), device_id_type=MESH,
        )

    def hand(t):
        @pl.when(outer)
        def _():
            to_inner(t).start()

    def first(t):
        @pl.when(jnp.logical_not(outer))
        def _():
            to_inner(t).wait_recv()
            for n in (2 * t, 2 * t + 1):
                gk[n] = (gk[n].astype(jnp.float32) + in1[n].astype(jnp.float32)).astype(gk.dtype)
            across(t).start()

    def second(t):
        @pl.when(jnp.logical_not(outer))
        def _():
            across(t).wait_recv()
            for n in (2 * t, 2 * t + 1):
                fin[n] = (gk[n].astype(jnp.float32) + in2[n].astype(jnp.float32)).astype(fin.dtype)
            to_outer(t).start()

        @pl.when(outer)
        def _():
            to_outer(t).wait_recv()

    load.need("key", "y", "k")
    tail_o[9] = tn_dot(dr_ref[...], pooled_ref[...]).astype(gk.dtype)
    gp[...] = nn_dot(dr_ref[...], k_ref[27]) / size_ref[:, :1]
    for b, s in enumerate(steps):
        gathers[b].forward()
        gathers[b].arrive()

        def turn(q, _):
            gt[b * W : (b + 1) * W, pl.ds(pl.multiple_of(q * T, 256), T)] = g[q, PAD : PAD + T, b * W : (b + 1) * W].T
            return 0

        lax.fori_loop(0, Q, turn, 0)
        for i in (-1, 0, 1):
            for j in (-1, 0, 1):
                lo, hi = span(s * j, Q)
                a = PAD + 16 * s * i

                got = None
                for q in range(lo, hi):
                    ok = same_crop(key_ref[q, PAD : PAD + T, :], key_ref[q + s * j, a : a + T, :], w)
                    v = jnp.where(ok, y_ref[q + s * j, a : a + T, :], 0)
                    r = nn_dot(gt[b * W : (b + 1) * W, q * T : (q + 1) * T], v)
                    got = r if got is None else got + r
                t = 9 * b + 3 * (i + 1) + j + 1
                if b < 2:
                    gk[t] = got.astype(gk.dtype)
                    if t % 2:
                        hand(t // 2)
                else:
                    tail_o[t - 18] = got.astype(gk.dtype)
                    if t % 2:
                        first((t - 18) // 2)
    cps = []
    ready = 4

    dst = dy_o.at[:, :, pl.ds(pl.multiple_of(w * f, 128), w)]

    def rows_of(k):
        return pl.ds(pl.multiple_of(h * (f ^ k), 16), h)

    def dest_step(m, _):
        k = 7 - m
        dest = f ^ k
        base = pl.multiple_of(PAD + h * dest, 16)
        here = key_ref[:, pl.ds(base, h), :].astype(jnp.float32).reshape(Q * h, 128)
        here = jnp.concatenate([here] * (w // 128), axis=1)
        @pl.when(m % 2 == 1)
        def _():
            first(ready + m // 2)
            second(m // 2)

        total = jnp.zeros((Q * h, w), jnp.float32)
        for c in range(CROPS_TILE):
            total = jnp.where(here == c + 1.0, gp[c : c + 1, :], total)
        acc[...] = total
        for b in range(3):
            spaced_taps(g, key_ref, k_ref, acc, base, h, steps, -1, b * W, nn_dot, b)
        rows = rows_of(k)
        dyo[:, rows, :] = acc[...].reshape(Q, h, w).astype(dyo.dtype)
        src = dyo.at[:, rows, :]

        @pl.when(k > 0)
        def _():
            remote(src, dst, ds_.at[k], dr_.at[k], d, dest)

        @pl.when(k == 0)
        def _():
            pltpu.make_async_copy(src, dst, dl).start()

        return 0

    lax.fori_loop(0, 8, dest_step, 0)

    def first_when(t):
        @pl.when(t < taps)
        def _():
            first(t)

    groups = (4, 3, 2)
    at = 0
    for n, size in enumerate(groups):
        stop = at + size
        lax.fori_loop(max(at, 4), stop, lambda t, _: (first_when(t + ready), second(t), 0)[-1], 0)
        for k in (6, 7, 2, 3, 4, 5, 1, 0):
            src = fin.at[pl.ds(2 * at, 2 * size), pl.ds(pl.multiple_of(o * (f ^ k), 16), o), :]
            to = gk_o.at[pl.ds(2 * at, 2 * size), :, pl.ds(pl.multiple_of(w * f, 128), w)]
            if k:
                cps.append(remote(src, to, ws.at[n, k], wr.at[n, k], d, f ^ k))
            else:
                c = pltpu.make_async_copy(src, to, wl.at[n])
                c.start()
                cps.append(c)
        at = stop
    for k in range(1, 8):
        c = pltpu.make_async_remote_copy(
            src_ref=dyo.at[:, rows_of(k), :], dst_ref=dst, send_sem=ds_.at[k], recv_sem=dr_.at[k],
            device_id=(d, f ^ k), device_id_type=MESH,
        )
        c.wait()
    pltpu.make_async_copy(dyo.at[:, rows_of(0), :], dst, dl).wait()
    for c in gathers:
        c.finish()
    for c in cps:
        c.wait()

    def sent(t, _):
        @pl.when(outer)
        def _():
            to_inner(t).wait_send()

        @pl.when(jnp.logical_not(outer))
        def _():
            across(t).wait_send()
            to_outer(t).wait_send()

        return 0

    lax.fori_loop(0, taps, sent, 0)


def branches_back(d, y, key, k, pooled, dr, sizes, steps):
    Q, h, W3 = d.shape
    TT, w = y.shape[1:]
    W = W3 // 3
    T = 8 * h
    b16, f32 = jnp.bfloat16, jnp.float32
    V = pltpu.VMEM
    return pl.pallas_call(
        functools.partial(branches_back_kernel, steps),
        out_shape=[jax.ShapeDtypeStruct((Q, h, 8 * w), b16), jax.ShapeDtypeStruct((18, W // 8, 8 * w), b16),
            jax.ShapeDtypeStruct((10, W, w), b16),
        ],
        in_specs=[VM] + [ANY] * 3 + [VM] * 3,
        out_specs=[ANY] * 2 + [VM],
        scratch_shapes=[
            V((Q, TT, W3), b16), V((W3, Q * T), b16), V((18, W, w), b16), V((18, W, w), b16),
            V((18, W, w), b16), V((18, W, w), b16), V((Q, T, w), b16),
            V((Q * h, w), f32), V((8, w), f32), V(y.shape, b16), V(key.shape, b16), V(k.shape, b16), DMA((3,)),
        ]
        + gather_sems() * 3
        + [DMA((4, 8)), DMA((4, 8)), DMA((4,)), DMA((8,)), DMA((8,)), DMA(())]
        + [DMA((9,))] * 6,
        compiler_params=pltpu.CompilerParams(collective_id=10, has_side_effects=True, vmem_limit_bytes=VLIM),
        name="branches_back",
    )(d, y, key, k, pooled, dr, sizes)


class Sum:
    def __init__(self, bufs, d, f):
        self.b1, self.b2, self.s1, self.r1, self.s2, self.r2 = bufs
        self.d, self.f = d, f

    def start(self, rows):
        b1, d, f = self.b1, self.d, self.f
        for n, row in enumerate(rows):
            b1[f, n : n + 1, :] = row
        self.cps = [remote(b1.at[f], b1.at[f], self.s1.at[k], self.r1.at[k], d, f ^ k) for k in (6, 2, 4, 7, 3, 5, 1)]

    def turn(self):
        b1, b2, d, f = self.b1, self.b2, self.d, self.f
        for c in self.cps:
            c.wait()
        tot = b1[0]
        for k in range(1, 8):
            tot = tot + b1[k]
        b2[d] = tot
        self.cps = [remote(b2.at[d], b2.at[d], self.s2.at[k], self.r2.at[k], d ^ k, f) for k in (3, 2, 1)]

    def result(self):
        for c in self.cps:
            c.wait()
        tot = self.b2[0]
        for k in range(1, 4):
            tot = tot + self.b2[k]
        return tot


class Reduce:
    def __init__(self, full, part, half, near, far, corner, tot, zin, zo, out, sems, d, f):
        self.half, self.corner = half, corner
        self.full, self.part, self.near, self.fars, self.tot, self.out = full, part, near, far, tot, out
        self.zin, self.zo, self.d, self.f = zin, zo, d, f
        self.sems = sems
        self.c0 = f % 2
        self.me = f // 2

    def pair(self):
        ps, pr = self.sems[:2]
        self.cps = [
            remote(self.full.at[self.part(2 * g + 1 - self.c0)], self.near.at[g], ps.at[g], pr.at[g], self.d, self.f ^ 1)
            for g in range(4)
        ]

    def far(self):
        ss, rs = self.sems[2:4]
        for c in self.cps:
            c.wait()
        self.cps = []
        for k in (3, 1, 2, 0):
            g = self.me ^ k
            val = self.full[self.part(2 * g + self.c0)].astype(jnp.float32) + self.near[g].astype(jnp.float32)
            self.near[g] = val.astype(self.near.dtype)
            if k == 3:
                for a in (0, 1):
                    self.cps.append(
                        remote(
                            self.near.at[(g,) + self.half(a)], self.corner.at[self.half(a)], ss.at[a], rs.at[a],
                            self.d, self.f ^ (2 + 2 * a),
                        )
                    )

    def beside(self):
        ss, rs = self.sems[2:4]
        for c in self.cps:
            c.wait()
        self.cps = []
        for k in (1, 2):
            g = self.me ^ k
            a = self.half(2 - k)
            val = self.near[(g,) + a].astype(jnp.float32) + self.corner[a].astype(jnp.float32)
            self.near[(g,) + a] = val.astype(self.near.dtype)
            self.cps.append(
                remote(
                    self.near.at[g], self.fars.at[k - 1], ss.at[k + 1], rs.at[k + 1], self.d, self.f ^ (2 * k)
                )
            )

    def to_inner(self):
        ss, rs = self.sems[4:6]
        return pltpu.make_async_remote_copy(
            src_ref=self.tot, dst_ref=self.zin, send_sem=ss.at[0], recv_sem=rs.at[0],
            device_id=(self.d ^ 1, self.f), device_id_type=MESH,
        )

    def across(self):
        ss, rs = self.sems[4:6]
        return pltpu.make_async_remote_copy(
            src_ref=self.tot, dst_ref=self.zo, send_sem=ss.at[1], recv_sem=rs.at[1],
            device_id=(self.d ^ 3, self.f), device_id_type=MESH,
        )

    def to_outer(self):
        ss, rs = self.sems[4:6]
        return pltpu.make_async_remote_copy(
            src_ref=self.out, dst_ref=self.out, send_sem=ss.at[2], recv_sem=rs.at[2],
            device_id=(self.d ^ 1, self.f), device_id_type=MESH,
        )

    def tiles(self):
        for c in self.cps:
            c.wait()
        val = self.near[self.me].astype(jnp.float32)
        for k in (1, 2):
            val = val + self.fars[k - 1].astype(jnp.float32)
        self.tot[...] = val.astype(self.tot.dtype)

        @pl.when(self.d % 3 == 0)
        def _():
            self.to_inner().start()

    def middle(self):
        @pl.when(self.d % 3 > 0)
        def _():
            self.to_inner().wait_recv()
            val = self.tot[...].astype(jnp.float32) + self.zin[...].astype(jnp.float32)
            self.tot[...] = val.astype(self.tot.dtype)
            self.across().start()

    def last(self):
        @pl.when(self.d % 3 > 0)
        def _():
            self.across().wait_recv()
            val = self.tot[...].astype(jnp.float32) + self.zo[...].astype(jnp.float32)
            self.out[...] = val.astype(self.out.dtype)
            self.to_outer().start()

    def done(self):
        @pl.when(self.d % 3 == 0)
        def _():
            self.to_inner().wait_send()
            self.to_outer().wait_recv()

        @pl.when(self.d % 3 > 0)
        def _():
            self.across().wait_send()
            self.to_outer().wait_send()


def reduce_scratch(block):
    V, b16 = pltpu.VMEM, jnp.bfloat16
    return [V((4,) + block, b16), V((2,) + block, b16), V(block, b16), V(block, b16), V(block, b16), V(block, b16)] + [DMA((4,))] * 6


def wide(row, n):
    return jnp.concatenate([row] * n, axis=1)


def bottleneck_back_kernel(
    x_any, ins_ref, st_ref, gr, gd, ge, dy_any, dpt, y_any, pm_in, wp_any, n3_any, l3_any, we_any, n2_any, l2_any, h2_any,
    wd_any, ext_any, n1_any, l1_any, wr_any, key_any, tail_any,
    gf_o, pm_o, ex_o, di_o, re_o, s3_o, s2_o, s1_o, tk_o,
    pm, ex, di, dp3, acc, ext2, d1n, key, gf, pick, in1, in2,
    x_ref, dy, y_ref, wp, n3, l3, we, n2, l2, h2, wd, ext, n1, l1, wr, tail, lsem, ksem, hs, hr, gs, s1, r1, s2, r2, s3, r3, ws, wrs, wl,
    *sems,
):
    sems = list(sems)

    def take(n):
        got = sems[:n]
        del sems[:n]
        return got

    load = Load(
        lsem, tail=(tail_any, tail), y=(y_any, y_ref), wp=(wp_any, wp), dy=(dy_any, dy), l3=(l3_any, l3), n3=(n3_any, n3),
        we=(we_any, we), l2=(l2_any, l2), n2=(n2_any, n2), h2=(h2_any, h2), ext=(ext_any, ext), wd=(wd_any, wd),
        l1=(l1_any, l1), n1=(n1_any, n1), x=(x_any, x_ref), wr=(wr_any, wr),
    )
    f, d = greet(range(1, 8), range(1, 4))
    N, C = x_ref.shape
    Q, h = ext2.shape[0], ext2.shape[1] // 2
    e = h // 2
    rows = h // 4
    neck = acc.shape[1]
    nb = neck // 8
    nw = pm.shape[0] // 8
    W = dpt.shape[1]

    def ds(i, n):
        return pl.ds(pl.multiple_of(n * i, n), n)

    def reducer(full, part, half, out):
        near, far, corner, tot, zin, zo = take(6)
        return Reduce(full, part, half, near, far, corner, tot, zin, zo, out, take(6), d, f)

    def half_rows(n):
        return lambda a: (pl.ds(a * n, n),)

    r_pm = reducer(pm, lambda g: (ds(g, nw),), half_rows(nw // 2), pm_o)
    r_ex = reducer(ex, lambda g: (slice(None), ds(g, C // 8)), half_rows(neck // 2), ex_o)
    r_di = [
        reducer(
            di.at[pl.ds(3 * i, 3)], lambda g: (slice(None), ds(g, nb)),
            lambda a: (slice(None), pl.ds(a * (nb // 2), nb // 2)), di_o.at[pl.ds(3 * i, 3)],
        )
        for i in range(3)
    ]
    re_ = ex
    d3 = dy
    r_re = reducer(re_, lambda g: (ds(g, nb),), half_rows(nb // 2), re_o)
    sum3, sum2, sum1 = (Sum(take(6), d, f) for _ in range(3))

    outer = d % 3 == 0
    o = in1.shape[1] // 8
    lanes = in1.shape[2]
    kout = []

    def move(src, dst, ss, rs, t, other):
        two = pl.ds(2 * t, 2)
        return pltpu.make_async_remote_copy(
            src_ref=src.at[two], dst_ref=dst.at[two], send_sem=ss.at[t], recv_sem=rs.at[t],
            device_id=(d ^ other, f), device_id_type=MESH,
        )

    def to_inner(t):
        return move(tail, in1, s1, r1, t, 1)

    def across(t):
        return move(in1, in2, s2, r2, t, 3)

    def to_outer(t):
        return move(in1, in1, s3, r3, t, 1)

    def hand(t):
        @pl.when(outer)
        def _():
            to_inner(t).start()

    def first(t):
        @pl.when(jnp.logical_not(outer))
        def _():
            to_inner(t).wait_recv()
            for n in (2 * t, 2 * t + 1):
                in1[n] = (in1[n].astype(jnp.float32) + tail[n].astype(jnp.float32)).astype(in1.dtype)
            across(t).start()

    def second(t):
        @pl.when(jnp.logical_not(outer))
        def _():
            across(t).wait()
            for n in (2 * t, 2 * t + 1):
                in1[n] = (in1[n].astype(jnp.float32) + in2[n].astype(jnp.float32)).astype(in1.dtype)
            to_outer(t).start()

    def keep(n, at, size):
        for t in range(at, at + size):

            @pl.when(outer)
            def _():
                to_outer(t).wait_recv()

        for k in (6, 7, 2, 3, 4, 5, 1, 0):
            src = in1.at[pl.ds(2 * at, 2 * size), pl.ds(pl.multiple_of(o * (f ^ k), 16), o), :]
            to = tk_o.at[pl.ds(2 * at, 2 * size), :, pl.ds(pl.multiple_of(lanes * f, 128), lanes)]
            if k:
                kout.append(remote(src, to, ws.at[n, k], wrs.at[n, k], d, f ^ k))
            else:
                c = pltpu.make_async_copy(src, to, wl.at[n])
                c.start()
                kout.append(c)

    load.need("tail")
    hand(0)
    hand(1)
    kcp = pltpu.make_async_copy(key_any.at[:, pl.ds(pl.multiple_of(PAD - e + h * f, 16), 2 * h), :], key, ksem)
    kcp.start()
    count = st_ref[0:1, 0:1]
    load.need("y")
    for c in range(0, C, 256):
        pm[:, c : c + 256] = tn_dot(dpt[...], y_ref[:, c : c + 256]).astype(jnp.bfloat16)
    pm[:, C:] = pm_in[...]
    r_pm.pair()
    load.need("wp", "dy", "l3", "n3")
    ones, crossed = [], []
    ins = wide(ins_ref[...], 2)
    for c in range(0, C, 256):
        w = slice(c, c + 256)
        if c == C // 2:
            first(0)
        v = dy[:, w].astype(jnp.float32) + nn_dot(dpt[...], wp[:, w])
        v = v * l3[:, w].astype(jnp.float32)
        dp3[:, w] = v.astype(jnp.bfloat16)
        v = v * ins
        ones.append(jnp.sum(v, axis=0, keepdims=True))
        crossed.append(jnp.sum(v * n3[:, w].astype(jnp.float32), axis=0, keepdims=True))
    sum3.start([cat_rows(ones), cat_rows(crossed)])
    order = lax.broadcasted_iota(jnp.int32, (N, N), 1)
    m, r, q = order % 4, (order // 4) % rows, order // h
    hit = (r * (N // rows) + q * 4 + m) == lax.broadcasted_iota(jnp.int32, (N, N), 0)
    pick[...] = hit.astype(jnp.float32).astype(jnp.bfloat16)
    sum3.turn()
    r_pm.far()
    tot = sum3.result()
    s3_o[...] = tot
    second(0)
    first(1)
    hand(2)
    for c in range(0, C, 256):
        w = slice(c, c + 256)
        v = dp3[:, w].astype(jnp.float32) - tot[0:1, w] / count - n3[:, w].astype(jnp.float32) * (tot[1:2, w] / count)
        d3[:, w] = (ins * v * (ge[:, w] * st_ref[3:4, w])).astype(jnp.bfloat16)
    load.need("we", "l2", "n2")
    ones, crossed = [], []
    for c in range(0, neck, 256):
        w = slice(c, c + 256)
        v = nt_dot(d3[...], we[w, :]) * l2[:, w].astype(jnp.float32)
        acc[:, w] = v
        v = v * ins
        ones.append(jnp.sum(v, axis=0, keepdims=True))
        crossed.append(jnp.sum(v * n2[:, w].astype(jnp.float32), axis=0, keepdims=True))
    sum2.start([cat_rows(ones), cat_rows(crossed)])
    load.need("h2")
    for c in range(0, C, 256):
        ex[:, c : c + 256] = tn_dot(h2[...], d3[:, c : c + 256]).astype(jnp.bfloat16)
    sum2.turn()
    r_ex.pair()
    tot = sum2.result()
    s2_o[...] = tot
    for c in range(0, neck, 256):
        w = slice(c, c + 256)
        v = acc[:, w] - tot[0:1, w] / count - n2[:, w].astype(jnp.float32) * (tot[1:2, w] / count)
        v = ins * v * (gd[:, w] * st_ref[2:3, w])
        ext2[:, e : e + h, w] = v.astype(jnp.bfloat16).reshape(Q, h, 256)
    up = remote(ext2.at[:, pl.ds(e, e)], ext2.at[:, pl.ds(e + h, e)], hs.at[0], hr.at[0], d, lax.rem(f + 7, 8))
    down = remote(ext2.at[:, pl.ds(h, e)], ext2.at[:, pl.ds(0, e)], hs.at[1], hr.at[1], d, lax.rem(f + 1, 8))
    second(1)
    hand(3)
    kcp.wait()
    load.need("ext", "wd", "l1", "n1")
    r_pm.beside()
    r_ex.far()
    first(2)
    for i in range(3):
        for j in range(3):
            lo, hi = span(j - 1, Q)
            ok = same_crop(
                key[lo:hi, e : e + h, :], key[lo + j - 1 : hi + j - 1, e * i : e * i + h, :], neck
            )
            v = jnp.where(ok, ext[lo + j - 1 : hi + j - 1, e * i : e * i + h, :], 0).reshape((hi - lo) * h, neck)
            g = ext2[lo:hi, e : e + h, :].reshape((hi - lo) * h, neck)
            di[3 * i + j] = tn_dot(g, v).astype(jnp.bfloat16)
        r_di[i].pair()
        if i == 0:
            hand(4)
            first(3)
            second(2)
        if i == 1:
            r_ex.beside()
    up.wait()
    down.wait()
    r_pm.tiles()
    acc[...] = jnp.zeros_like(acc)
    for i in range(3):
        if i == 1:
            first(4)
            second(3)
        for j in (1, 0, 2):
            lo, hi = span(1 - j, Q)
            ok = same_crop(
                key[lo:hi, e : e + h, :], key[lo + 1 - j : hi + 1 - j, e * (2 - i) : e * (2 - i) + h, :], neck
            )
            v = jnp.where(ok, ext2[lo + 1 - j : hi + 1 - j, e * (2 - i) : e * (2 - i) + h, :], 0)
            v = v.reshape((hi - lo) * h, neck)
            for c in range(0, neck, 256):
                acc[lo * h : hi * h, c : c + 256] += nn_dot(v, wd[3 * i + j, :, c : c + 256])
    ones, crossed = [], []
    for c in range(0, neck, 256):
        w = slice(c, c + 256)
        v = acc[:, w] * l1[:, w].astype(jnp.float32)
        acc[:, w] = v
        v = v * ins
        ones.append(jnp.sum(v, axis=0, keepdims=True))
        crossed.append(jnp.sum(v * n1[:, w].astype(jnp.float32), axis=0, keepdims=True))
    sum1.start([cat_rows(ones), cat_rows(crossed)])
    for r in r_di:
        r.far()
    r_pm.middle()
    sum1.turn()
    r_ex.tiles()
    second(4)
    r_pm.last()
    for r in r_di:
        r.beside()
    tot = sum1.result()
    s1_o[...] = tot
    for c in range(0, neck, 256):
        w = slice(c, c + 256)
        v = acc[:, w] - tot[0:1, w] / count - n1[:, w].astype(jnp.float32) * (tot[1:2, w] / count)
        v = (ins * v * (gr[:, w] * st_ref[1:2, w])).astype(jnp.bfloat16)
        d1n[:, w] = nn_dot(pick[...], v).astype(jnp.bfloat16)
    load.need("x", "wr")
    for c in range(0, C, 256):
        re_[:, c : c + 256] = tn_dot(d1n[...], x_ref[:, c : c + 256]).astype(jnp.bfloat16)
    r_re.pair()
    r_di[0].tiles()
    r_re.far()
    r_ex.middle()
    out = []
    for n, c in enumerate(range(0, C, 256)):
        w = slice(c, c + 256)
        if n >= 2:
            out[n - 2].wait()
        gf[n % 2] = nn_dot(pick[...], dp3[:, w]) + nn_dot(d1n[...], wr[:, w])
        cp = pltpu.make_async_copy(gf.at[n % 2], gf_o.at[:, pl.ds(c, 256)], gs.at[n % 2])
        cp.start()
        out.append(cp)
        if n == 0:
            r_re.beside()
        if n == 1:
            r_di[0].middle()
            r_ex.last()
        if n == 3:
            r_di[1].tiles()
            r_di[0].last()
        if n == 5:
            r_di[1].middle()
        if n == 7:
            r_di[2].tiles()
            r_di[1].last()
    keep(0, 0, 3)
    keep(1, 3, 2)
    r_di[2].middle()
    r_re.tiles()
    r_di[2].last()
    r_re.middle()
    r_re.last()
    out[-2].wait()
    out[-1].wait()
    for t in range(5):

        @pl.when(outer)
        def _():
            to_inner(t).wait_send()

        @pl.when(jnp.logical_not(outer))
        def _():
            to_outer(t).wait_send()

    for c in kout:
        c.wait()
    for r in [r_pm, r_ex, r_re] + r_di:
        r.done()


def bottleneck_back(*args):
    x, st, dpt, pm_in, h2 = args[0], args[2], args[7], args[9], args[16]
    N, C = x.shape
    Q, h2_, neck = args[18].shape
    h = h2_ // 2
    tail = args[23]
    W = dpt.shape[1]
    PM = C + pm_in.shape[1]
    b16, f32 = jnp.bfloat16, jnp.float32
    S, V = jax.ShapeDtypeStruct, pltpu.VMEM
    blocks = [(W // 8, PM), (neck, C // 8), (9, neck // 8, neck), (neck // 8, C)]
    scratch = [
        V((W, PM), b16), V((neck, C), b16), V((9, neck, neck), b16), V((N, C), b16),
        V((N, neck), f32), V((Q, 2 * h, neck), b16), V((N, neck), b16), V((Q, 2 * h, 128), b16), V((2, N, 256), f32),
        V((N, N), b16), V(tail.shape, b16), V(tail.shape, b16),
    ]
    scratch += [V(args[n].shape, args[n].dtype) for n in (0, 6, 8, 10, 11, 12, 13, 14, 15, 16, 17, 18, 19, 20, 21, 23)]
    scratch += [
        DMA((16,)),
        DMA(()), DMA((2,)), DMA((2,)), DMA((2,)),
    ]
    scratch += [DMA((5,))] * 6 + [DMA((2, 8)), DMA((2, 8)), DMA((2,))]
    for n in (0, 1, 2, 2, 2, 3):
        scratch += reduce_scratch((3,) + blocks[2][1:] if n == 2 else blocks[n])
    scratch += sum_sems(2, C) + sum_sems(2, neck) + sum_sems(2, neck)
    return pl.pallas_call(
        bottleneck_back_kernel,
        out_shape=[S((N, C), f32)] + [S(b, b16) for b in blocks] + [S((2, C), f32), S((2, neck), f32), S((2, neck), f32)]
        + [S((10, W // 8, C), b16)],
        in_specs=[VM if n in (1, 2, 3, 4, 5, 7, 9) else ANY for n in range(24)],
        out_specs=[ANY] + [VM] * 7 + [ANY],
        scratch_shapes=scratch,
        compiler_params=pltpu.CompilerParams(collective_id=12, has_side_effects=True, vmem_limit_bytes=VLIM),
        name="bottleneck_back",
    )(*args)


def spaced_taps(src, key, kernels, acc, base, h, steps, sign, first_lane, dot, b):
    Q = key.shape[0]
    s = sign * steps[b]
    W = kernels.shape[1] if sign < 0 else src.shape[2]
    lanes = slice(first_lane, first_lane + W)
    for n, j in enumerate((0, -1, 1)):
        lo, hi = span(s * j, Q)
        here = key[lo:hi, pl.ds(base, h), :]
        got = None
        for i in (-1, 0, 1):
            at = pl.multiple_of(base + 16 * s * i, 16)
            ok = same_crop(here, key[lo + s * j : hi + s * j, pl.ds(at, h), :], W)
            v = jnp.where(ok, src[lo + s * j : hi + s * j, pl.ds(at, h), lanes], 0).reshape((hi - lo) * h, W)
            r = dot(v, kernels[9 * b + 3 * (i + 1) + j + 1])
            got = r if got is None else got + r
        if n == 0 and sign > 0:
            acc[...] = got
        else:
            acc[lo * h : hi * h] += got


def head_kernel(
    steps, yo, key, kern, y_any, wp_any, wm_any, wc, ins_ref, kb, lab, st_ref, gb, bb, gm, bm,
    lo_o, dp_o, dr_o, pm_o, pooled_o, dpool_o, size_o, sb_o, sm_o,
    acc, near, mine, far, corner, ab, nb, lb, joined, nm, lm, merged, pn, ps, pr, ss, rs, y, wp, wm, lsem,
    *sems,
):
    sems = list(sems)
    load = Load(lsem, y=(y_any, y), wp=(wp_any, wp), wm=(wm_any, wm))
    f, d = greet(range(1, 8), range(1, 4))
    sum_b, sum_m, back_m, back_b = (Sum(sems[6 * n : 6 * n + 6], d, f) for n in range(4))
    Q, h = pn.shape[1], pn.shape[2]
    N = Q * h
    w = yo.shape[2]
    W = wp.shape[0]
    T = 8 * h
    c0 = f % 2
    me = f // 2
    f32, b16 = jnp.float32, jnp.bfloat16

    def step(n, _):
        k = 3 - n
        g = me ^ k
        for turn in range(2):
            dest = 2 * g + (1 - c0 if turn == 0 else c0)
            base = pl.multiple_of(PAD + h * dest, 16)
            if turn == 1:
                pltpu.make_async_remote_copy(
                    src_ref=pn.at[k], dst_ref=near.at[k], send_sem=ps.at[k], recv_sem=pr.at[k],
                    device_id=(d, f ^ 1), device_id_type=MESH,
                ).wait_recv()
            for b in range(3):
                lanes = slice(b * W, (b + 1) * W)
                spaced_taps(yo, key, kern, acc, base, h, steps, 1, 0, nt_dot, b)
                if turn == 0:
                    pn[k, :, :, lanes] = acc[...].astype(b16).reshape(Q, h, W)
                else:
                    val = acc[...] + near[k, :, :, lanes].astype(f32).reshape(N, W)
                    mine[k, :, :, lanes] = val.astype(b16).reshape(Q, h, W)
            if turn == 0:
                remote(pn.at[k], near.at[k], ps.at[k], pr.at[k], d, f ^ 1)
            else:

                @pl.when(k == 3)
                def _():
                    for a in (0, 1):
                        by_way(a).start()

        return 0

    def by_way(a):
        two = pl.ds(a * (Q // 2), Q // 2)
        return pltpu.make_async_remote_copy(
            src_ref=mine.at[3, two], dst_ref=corner.at[two], send_sem=ss.at[a], recv_sem=rs.at[a],
            device_id=(d, f ^ (2 + 2 * a)), device_id_type=MESH,
        )

    lax.fori_loop(0, 3, step, 0)
    for a in (0, 1):
        by_way(a).wait()
    out = []
    for k in (1, 2):
        two = slice((2 - k) * (Q // 2), (3 - k) * (Q // 2))
        for b in range(3):
            lanes = slice(b * W, (b + 1) * W)
            val = mine[k, two, :, lanes].astype(f32) + corner[two, :, lanes].astype(f32)
            mine[k, two, :, lanes] = val.astype(b16)
        out.append(remote(mine.at[k], far.at[k - 1], ss.at[k + 1], rs.at[k + 1], d, f ^ (2 * k)))
    lax.fori_loop(3, 4, step, 0)
    load.need("y", "wp", "wm")
    ab[:, :W] = nt_dot(y[...], wp[...])
    crop = (lax.broadcasted_iota(jnp.int32, (T, 128), 1) + 1).astype(f32)

    def crops(q, carry):
        total, size = carry
        one = (key[q, PAD : PAD + T, :].astype(f32) == crop).astype(f32).astype(b16)
        return total + tn_dot(one, yo[q, PAD : PAD + T, :]), size + tn_dot(one, jnp.ones((T, 128), b16))

    total, size = lax.fori_loop(0, Q, crops, (jnp.zeros((128, w), f32), jnp.zeros((128, 128), f32)))
    size = jnp.where(size > 0, size, 1.0)[:8]
    size_o[...] = size
    pooled = (total[:8] / size[:, :1]).astype(b16)
    pooled_o[...] = pooled
    part = nt_dot(pooled, kern[27])
    part = cat_rows([part[c : c + 1] for c in range(CROPS_TILE)])
    ins = wide(ins_ref[...], 2)
    for c in out:
        c.wait()
    ones, squares = [], []
    for b in range(4):
        lanes = slice(b * W, (b + 1) * W)
        if b:
            src = slice((b - 1) * W, b * W)
            v = mine[0, :, :, src].astype(f32)
            for k in (1, 2):
                v = v + far[k - 1, :, :, src].astype(f32)
            ab[:, lanes] = v.reshape(N, W)
        s, t = column_sums(ab[:, lanes], ins_ref[...])
        ones.append(s)
        squares.append(t)
    sum_b.start([cat_rows(ones), cat_rows(squares), part])
    for k in range(4):
        pltpu.make_async_remote_copy(
            src_ref=pn.at[k], dst_ref=near.at[k], send_sem=ps.at[k], recv_sem=pr.at[k],
            device_id=(d, f ^ 1), device_id_type=MESH,
        ).wait_send()
    sum_b.turn()
    pool_act = sum_b.b2[d, 2:3, :]
    pool, pool_lean = bend(pool_act)
    pool = pool.astype(b16).astype(f32)
    here = wide(kb[...].astype(f32), W // 128)
    v = jnp.zeros((N, W), f32)
    for c in range(CROPS_TILE):
        v = jnp.where(here == c + 1.0, pool[:, c * W : (c + 1) * W], v)
    joined[:, 4 * W :] = v.astype(b16)
    tot = sum_b.result()
    count = st_ref[0:1, 0:1]
    mean = tot[0:1] / count
    inv_b = lax.rsqrt(tot[1:2] / count - mean * mean + eps)
    for b in range(4):
        lanes = slice(b * W, (b + 1) * W)
        n = (ab[:, lanes] - mean[:, lanes]) * inv_b[:, lanes]
        act, lean = bend(n * gb[:, lanes] + bb[:, lanes])
        joined[:, lanes] = act.astype(b16)
        nb[:, lanes] = n.astype(b16)
        lb[:, lanes] = lean.astype(b16)
    am = nt_dot(joined[...], wm[...])
    s, t = column_sums(am, ins_ref[...])
    sum_m.start([s, t])
    sum_m.turn()
    tot = sum_m.result()
    mean = tot[0:1] / count
    inv_m = lax.rsqrt(tot[1:2] / count - mean * mean + eps)
    n = (am - mean) * inv_m
    act, lean = bend(n * gm[...] + bm[...])
    merged[...] = act.astype(b16)
    nm[...] = n
    lm[...] = lean
    logits = nn_dot(merged[...], wc[...])
    lane = lax.broadcasted_iota(jnp.int32, (N, 128), 1)
    valid = lane < CLASSES
    top = jnp.max(jnp.where(valid, logits, -jnp.inf), axis=1, keepdims=True)
    ex = jnp.where(valid, jnp.exp(logits - top), 0.0)
    prob = ex / jnp.sum(ex, axis=1, keepdims=True)
    target = (lab[...] == lane.astype(f32)).astype(f32)
    dl = (ins_ref[...] * (prob - target) / count).astype(b16)
    e = nt_dot(dl, wc[...]) * lm[...]
    m = e * ins
    back_m.start([jnp.sum(m, axis=0, keepdims=True), jnp.sum(m * nm[...], axis=0, keepdims=True)])
    order = lax.broadcasted_iota(jnp.int32, (N, N), 1)
    rows = h // 4
    mm, r, q = order % 4, (order // 4) % rows, order // h
    hit = (r * (N // rows) + q * 4 + mm) == lax.broadcasted_iota(jnp.int32, (N, N), 0)
    lo_o[...] = nn_dot(hit.astype(f32).astype(b16), logits.astype(b16)).astype(b16)
    back_m.turn()
    J = joined.shape[1]
    pm_o[:, J : J + 128] = tn_dot(merged[...], dl).astype(b16)
    pm_o[:, J + 128 :] = jnp.zeros((W, pm_o.shape[1] - J - 128), b16)
    tot = back_m.result()
    sm_o[...] = tot
    dm = (ins * gm[...] * inv_m * (e - tot[0:1] / count - nm[...] * (tot[1:2] / count))).astype(b16)
    ones, crossed = [], []
    for b in range(4):
        lanes = slice(b * W, (b + 1) * W)
        v = nn_dot(dm, wm[:, lanes]) * lb[:, lanes].astype(f32)
        ab[:, lanes] = v
        v = v * ins
        ones.append(jnp.sum(v, axis=0, keepdims=True))
        crossed.append(jnp.sum(v * nb[:, lanes].astype(f32), axis=0, keepdims=True))
    v = nn_dot(dm, wm[:, 4 * W :])
    part = cat_rows(
        [jnp.sum(jnp.where(here == c + 1.0, v, 0.0), axis=0, keepdims=True) for c in range(CROPS_TILE)]
    )
    back_b.start([cat_rows(ones), cat_rows(crossed), part])
    pm_o[:, :J] = tn_dot(dm, joined[...]).astype(b16)
    back_b.turn()
    v = (back_b.b2[d, 2:3, :] * pool_lean).astype(b16)
    dpool_o[...] = jnp.zeros_like(dpool_o)
    for c in range(CROPS_TILE):
        dpool_o[c : c + 1, :] = v[:, c * W : (c + 1) * W]
    tot = back_b.result()
    sb_o[...] = tot[:2]
    for b in range(4):
        lanes = slice(b * W, (b + 1) * W)
        v = ab[:, lanes] - tot[0:1, lanes] / count - nb[:, lanes].astype(f32) * (tot[1:2, lanes] / count)
        v = (ins * v * (gb[:, lanes] * inv_b[:, lanes])).astype(b16)
        if b:
            dr_o[:, :, (b - 1) * W : b * W] = v.reshape(Q, h, W)
        else:
            dp_o[...] = v


def head(steps, width, *args):
    yo, key, kern, y, wp, wm = args[:6]
    N, C = y.shape
    Q = yo.shape[0]
    h = N // Q
    W = wp.shape[0]
    J = wm.shape[1]
    b16, f32 = jnp.bfloat16, jnp.float32
    S, V = jax.ShapeDtypeStruct, pltpu.VMEM
    return pl.pallas_call(
        functools.partial(head_kernel, steps),
        out_shape=[
            S((N, 128), b16), S((N, W), b16), S((Q, h, 3 * W), b16), S((W, width), b16), S((8, C // 8), b16),
            S((8, W), b16), S((8, 128), f32), S((2, 4 * W), f32), S((2, W), f32),
        ],
        in_specs=[VM] * 3 + [ANY] * 3 + [VM] * 9,
        out_specs=[VM] * 9,
        scratch_shapes=[V((N, W), f32)]
        + [V((4, Q, h, 3 * W), b16)] * 2 + [V((2, Q, h, 3 * W), b16), V((Q, h, 3 * W), b16)]
        + [
            V((N, 4 * W), f32), V((N, 4 * W), b16), V((N, 4 * W), b16), V((N, J), b16), V((N, W), f32), V((N, W), f32),
            V((N, W), b16), V((4, Q, h, 3 * W), b16), DMA((4,)), DMA((4,)), DMA((4,)), DMA((4,)),
            V(y.shape, b16), V(wp.shape, b16), V(wm.shape, b16), DMA((3,)),
        ]
        + sum_sems(3, 4 * W) + sum_sems(2, W) + sum_sems(2, W) + sum_sems(3, 4 * W),
        compiler_params=pltpu.CompilerParams(collective_id=5, has_side_effects=True, vmem_limit_bytes=VLIM),
        name="head",
    )(*args)


def widen_kernel(gk, tk, pm, ex, di, re_, k0, k1, k2, pool, point, merge, dilated, expand, reduce_):
    for b, o in enumerate((k0, k1, k2)):

        def tap(t, _):
            o[t] = (tk[t] if b == 2 else gk[9 * b + t]).astype(jnp.float32)
            return 0

        lax.fori_loop(0, 9, tap, 0)
    pool[...] = tk[9].astype(jnp.float32)
    C = point.shape[1]
    point[...] = pm[:, :C].astype(jnp.float32)
    merge[...] = pm[:, C : C + merge.shape[1]].astype(jnp.float32)

    def rows(t, _):
        dilated[t] = di[t].astype(jnp.float32)
        return 0

    lax.fori_loop(0, 9, rows, 0)
    expand[...] = ex[...].astype(jnp.float32)
    reduce_[...] = re_[...].astype(jnp.float32)


def widen(gk, tk, pm, ex, di, re_, J):
    _, o, C = gk.shape
    shapes = [(9, o, C)] * 3 + [(o, C), (o, C), (o, J), di.shape, ex.shape, re_.shape]
    return pl.pallas_call(
        widen_kernel,
        out_shape=[jax.ShapeDtypeStruct(v, jnp.float32) for v in shapes],
        in_specs=[VM] * 6,
        out_specs=[VM] * 9,
        compiler_params=pltpu.CompilerParams(vmem_limit_bytes=VLIM),
        name="widen",
    )(gk, tk, pm, ex, di, re_)


def norm_coeffs(totals, squares, count):
    average = totals / count
    return average, lax.rsqrt(squares / count - average * average + eps)


def fast_body(
    features, crop_ids, labels, w_reduce, gain_reduce, bias_reduce, w_dilated, gain_dilated, bias_dilated,
    w_expand, gain_expand, bias_expand, w_point, gain_point, bias_point, w_rate, gain_rate, bias_rate,
    w_rate_double, gain_rate_double, bias_rate_double, w_rate_triple, gain_rate_triple, bias_rate_triple,
    w_pool, w_merge, gain_merge, bias_merge, w_classes,
):
    rows, cols, C = features.shape
    Q = cols // 4
    h = rows * 4
    N = rows * cols
    nf = lax.axis_size("fsdp")
    W = gain_point.shape[0]
    steps = (RATE // 4, 2 * RATE // 4, 3 * RATE // 4)
    place = lax.axis_index("fsdp")

    def perm(a):
        a = a.reshape((rows, Q, 4) + a.shape[2:])
        return jnp.swapaxes(a, 0, 1).reshape((N,) + a.shape[3:])

    def unperm(a):
        a = a.reshape((Q, rows, 4) + a.shape[1:])
        return jnp.swapaxes(a, 0, 1).reshape((rows, cols) + a.shape[3:])

    local_crop = perm(crop_ids) - lax.axis_index("dp") * CROPS_TILE
    in_crop = perm(crop_ids) >= 0
    inside = in_crop.astype(jnp.float32)[:, None]
    key_loc = jnp.where(in_crop, local_crop + 1, 0)
    kb = jnp.broadcast_to(key_loc.astype(jnp.bfloat16)[:, None], (N, 128))
    key_row = jnp.pad(key_loc.astype(jnp.float32).reshape(Q, h), ((0, 0), (0, 128 - h)))
    ins = jnp.broadcast_to(inside, (N, 128))
    rates = [jnp.swapaxes(w.reshape(9, C, -1), 1, 2) for w in (w_rate, w_rate_double, w_rate_triple)]
    vecs = [v[None, :] for v in (gain_reduce, bias_reduce, gain_dilated, bias_dilated, gain_expand, bias_expand)]
    (
        y_own, y, n_three, l_three, n_one, l_one, n_two, l_two, ext, h_two, key, kernel,
        wr, wd, full_expand, wp, wm, wc, count,
    ) = bottleneck(
        features.reshape(N, C), key_row, ins, vecs,
        [
            w_reduce.T, jnp.swapaxes(w_dilated.reshape(9, w_dilated.shape[2], -1), 1, 2), w_expand, w_point.T, w_merge.T,
            jnp.pad(w_classes, ((0, 0), (0, 128 - CLASSES))),
        ],
        rates + [w_pool.T[None]],
    )
    neck = gain_reduce.shape[0]
    stats = count
    count = count[0, 0]
    y = y.reshape(N, C)
    g_br = jnp.concatenate([gain_point, gain_rate, gain_rate_double, gain_rate_triple])[None]
    b_br = jnp.concatenate([bias_point, bias_rate, bias_rate_double, bias_rate_triple])[None]
    lab = jnp.broadcast_to(perm(labels).astype(jnp.float32)[:, None], (N, 128))
    J = wm.shape[1]
    width = J + 128 + -(C + J + 128) % 512
    logits, d_point, d_rates, rest, pooled, d_pool, sizes, st_br, st_m = head(
        steps, width, y_own, key, kernel, y, wp, wm, wc, ins, kb, lab, stats, g_br, b_br,
        gain_merge[None], bias_merge[None],
    )
    class_logits = logits[:, :CLASSES].reshape(rows, cols, CLASSES)
    gb_br, gg_br = st_br[0], st_br[1]
    gb_merge, gg_merge = st_m[0], st_m[1]
    d_y, grad_k, tail = branches_back(d_rates, y_own, key, kernel, pooled, d_pool, sizes, steps)
    grad_features, pm, ex, di, re_, st3, st2, st1, tail = bottleneck_back(
        features.reshape(N, C), ins, stats, vecs[0], vecs[2], vecs[4], d_y.reshape(N, C), d_point, y, rest, wp,
        n_three, l_three, full_expand, n_two, l_two, h_two, wd, ext, n_one, l_one, wr, key, tail,
    )
    grad_classes = pm[:, C + J : C + J + CLASSES].astype(jnp.float32)
    *grad_k, grad_pool, grad_point, grad_merge, grad_dilated, grad_expand, grad_reduce = widen(grad_k, tail, pm, ex, di, re_, J)
    grad_k = [jnp.swapaxes(v.reshape(3, 3, -1, C), 2, 3) for v in grad_k]
    grad_pool, grad_point, grad_merge, grad_reduce = grad_pool.T, grad_point.T, grad_merge.T, grad_reduce.T
    grad_dilated = jnp.swapaxes(grad_dilated, 1, 2).reshape(3, 3, neck, -1)
    grad_features = grad_features.reshape(rows, cols, C)
    gg_expand, gb_expand, gg_dilated, gb_dilated, gg_reduce, gb_reduce = st3[1], st3[0], st2[1], st2[0], st1[1], st1[0]
    return (
        class_logits,
        grad_features,
        grad_reduce, gg_reduce, gb_reduce,
        grad_dilated, gg_dilated, gb_dilated,
        grad_expand, gg_expand, gb_expand,
        grad_point, gg_br[:W], gb_br[:W],
        grad_k[0], gg_br[W : 2 * W], gb_br[W : 2 * W],
        grad_k[1], gg_br[2 * W : 3 * W], gb_br[2 * W : 3 * W],
        grad_k[2], gg_br[3 * W :], gb_br[3 * W :],
        grad_pool,
        grad_merge, gg_merge, gb_merge,
        grad_classes,
    )


def passed_along(value, axis, by):
    count = lax.axis_size(axis)
    pairs = [(i, i + by) for i in range(count) if 0 <= i + by < count]
    return lax.ppermute(value, axis, pairs)


def padded(cells, sides, width):
    for axis, dim in sides:
        count = lax.axis_size(axis)
        ends = count - 1
        head = lax.slice_in_dim(cells, 0, width, axis=dim)
        tail = lax.slice_in_dim(cells, cells.shape[dim] - width, cells.shape[dim], axis=dim)
        cells = jnp.concatenate(
            [
                lax.ppermute(tail, axis, [(i, (i + 1) % count) for i in range(ends)]),
                cells,
                lax.ppermute(head, axis, [((i + 1) % count, i) for i in range(ends)]),
            ],
            axis=dim,
        )
    return cells


def flat_dot(first_op, second_op):
    return jnp.dot(first_op, second_op, preferred_element_type=jnp.float32)


def inner_dot(first_op, second_op):
    return lax.dot_general(
        first_op, second_op, (((0,), (0,)), ((), ())), preferred_element_type=jnp.float32
    )


def outer_dot(first_op, second_op):
    return lax.dot_general(
        first_op, second_op, (((1,), (1,)), ((), ())), preferred_element_type=jnp.float32
    )


def slope(values):
    gate_value = jax.nn.sigmoid(values)
    return gate_value * (1.0 + values * (1.0 - gate_value))


def widen_rows(values, extent, mover):
    row_count = values.shape[0]
    neighbours = -(-extent // row_count)
    above = [mover(values, distance) for distance in range(neighbours, 0, -1)]
    below = [mover(values, -distance) for distance in range(1, neighbours + 1)]
    stacked = jnp.concatenate(above + [values] + below, axis=0)
    start_row = neighbours * row_count - extent
    return stacked[start_row : start_row + row_count + 2 * extent]


def rim_slice(widened, spacing, margin, height):
    return widened[margin - spacing : margin + height + spacing]


def offset_table(broad_key_rows, crop_random_keys, spacing, margin):
    height, breadth = crop_random_keys.shape
    first_row = margin - spacing
    extended = jnp.pad(
        broad_key_rows[first_row : first_row + height + 2 * spacing], ((0, 0), (spacing, spacing))
    )
    tables = []
    for row_tap in range(3):
        for col_tap in range(3):
            nearby = extended[
                row_tap * spacing : row_tap * spacing + height,
                col_tap * spacing : col_tap * spacing + breadth,
            ]
            tables.append(
                ((nearby == crop_random_keys) & (crop_random_keys > 0))
                .astype(jnp.float32)
                .reshape(height * breadth, 1)
            )
    return tables


def spread_offsets(widened, kernel, tables, spacing, height, breadth):
    channels = widened.shape[2]
    extended = jnp.pad(widened, ((0, 0), (spacing, spacing), (0, 0)))
    summed = jnp.zeros((height * breadth, kernel.shape[3]), jnp.float32)
    for row_tap in range(3):
        for col_tap in range(3):
            nearby = extended[
                row_tap * spacing : row_tap * spacing + height,
                col_tap * spacing : col_tap * spacing + breadth,
            ]
            summed = summed + tables[3 * row_tap + col_tap] * flat_dot(
                nearby.reshape(height * breadth, channels), kernel[row_tap, col_tap]
            )
    return summed


def collect_taps(widened, kernel, tables, spacing, height, breadth):
    channels = widened.shape[2]
    extended = jnp.pad(widened, ((0, 0), (spacing, spacing), (0, 0)))
    summed = jnp.zeros((height * breadth, kernel.shape[2]), jnp.float32)
    for row_tap in range(3):
        for col_tap in range(3):
            back_row = 2 - row_tap
            back_col = 2 - col_tap
            nearby = extended[
                back_row * spacing : back_row * spacing + height,
                back_col * spacing : back_col * spacing + breadth,
            ]
            summed = summed + tables[3 * back_row + back_col] * outer_dot(
                nearby.reshape(height * breadth, channels), kernel[row_tap, col_tap]
            )
    return summed


def kernel_offsets(widened, grads_low, tables, spacing, height, breadth):
    channels = widened.shape[2]
    extended = jnp.pad(widened, ((0, 0), (spacing, spacing), (0, 0)))
    pieces = []
    for row_tap in range(3):
        for col_tap in range(3):
            nearby = extended[
                row_tap * spacing : row_tap * spacing + height,
                col_tap * spacing : col_tap * spacing + breadth,
            ]
            masked = (tables[3 * row_tap + col_tap] * grads_low).astype(jnp.bfloat16)
            pieces.append(inner_dot(nearby.reshape(height * breadth, channels), masked))
    return pieces


def statistics(partial_value):
    return lax.psum(partial_value, ("dp", "fsdp"))


def norm_apply(values, totals, squares, pixel_count, factor, offset):
    average = totals / pixel_count
    inverse = lax.rsqrt(squares / pixel_count - average * average + eps)
    normed = (values - average) * inverse
    return (normed * factor + offset, normed, inverse)


def norm_forward(values, inside, pixel_count, factor, offset):
    totals, squares = statistics(
        (jnp.sum(values * inside, axis=0), jnp.sum(values * values * inside, axis=0))
    )
    return norm_apply(values, totals, squares, pixel_count, factor, offset)


def norm_backward(upstream, normed, inverse, factor, inside, pixel_count):
    totals, crossed = lax.psum(
        (jnp.sum(upstream * inside, axis=0), jnp.sum(upstream * normed * inside, axis=0)),
        ("dp", "fsdp"),
    )
    passed = (
        inside
        * factor
        * inverse
        * (upstream - totals / pixel_count - normed * crossed / pixel_count)
    )
    return (passed, crossed, totals)


def body(
    features,
    crop_ids,
    labels,
    w_reduce,
    gain_reduce,
    bias_reduce,
    w_dilated,
    gain_dilated,
    bias_dilated,
    w_expand,
    gain_expand,
    bias_expand,
    w_point,
    gain_point,
    bias_point,
    w_rate,
    gain_rate,
    bias_rate,
    w_rate_double,
    gain_rate_double,
    bias_rate_double,
    w_rate_triple,
    gain_rate_triple,
    bias_rate_triple,
    w_pool,
    w_merge,
    gain_merge,
    bias_merge,
    w_classes,
):
    local_rows, local_columns, channels = features.shape
    pixel_values = local_rows * local_columns
    inputs_flat = features.reshape(pixel_values, channels)
    crop_random_keys = crop_ids + 1
    outer_extent = 3 * RATE
    spacings = (RATE, 2 * RATE, 3 * RATE)
    broad_key_rows = widen_rows(
        crop_random_keys,
        outer_extent,
        lambda piece, distance: passed_along(piece, "fsdp", distance),
    )
    inside = (crop_random_keys > 0).astype(jnp.float32).reshape(pixel_values, 1)
    inner_neck = offset_table(broad_key_rows, crop_random_keys, DILATION_SPAN, outer_extent)
    near_rates = [
        offset_table(broad_key_rows, crop_random_keys, spacing, outer_extent)
        for spacing in spacings
    ]
    (
        full_reduce,
        complete_dilated,
        full_expand,
        full_point,
        full_rate,
        full_double,
        full_triple,
        full_pool,
        full_merge,
        full_classes,
    ) = (
        lax.all_gather(w_reduce, "fsdp", axis=1, tiled=True),
        lax.all_gather(w_dilated, "fsdp", axis=3, tiled=True),
        lax.all_gather(w_expand, "fsdp", axis=1, tiled=True),
        lax.all_gather(w_point, "fsdp", axis=1, tiled=True),
        lax.all_gather(w_rate, "fsdp", axis=3, tiled=True),
        lax.all_gather(w_rate_double, "fsdp", axis=3, tiled=True),
        lax.all_gather(w_rate_triple, "fsdp", axis=3, tiled=True),
        lax.all_gather(w_pool, "fsdp", axis=1, tiled=True),
        lax.all_gather(w_merge, "fsdp", axis=1, tiled=True),
        lax.all_gather(w_classes, "fsdp", axis=0, tiled=True),
    )
    rate_kernels = (full_rate, full_double, full_triple)
    rate_gains = (gain_rate, gain_rate_double, gain_rate_triple)
    rate_biases = (bias_rate, bias_rate_double, bias_rate_triple)
    act_one = flat_dot(inputs_flat, full_reduce)
    totals, squares, pixel_count = statistics(
        (
            jnp.sum(act_one * inside, axis=0),
            jnp.sum(act_one * act_one * inside, axis=0),
            jnp.sum(inside),
        )
    )
    pre_one, normed_one, inverse_one = norm_apply(
        act_one, totals, squares, pixel_count, gain_reduce, bias_reduce
    )
    first_hidden = jax.nn.silu(pre_one).astype(jnp.bfloat16)
    first_broad = padded(
        first_hidden.reshape(local_rows, local_columns, -1), (("fsdp", 0),), DILATION_SPAN
    )
    second_activation = spread_offsets(
        first_broad, complete_dilated, inner_neck, DILATION_SPAN, local_rows, local_columns
    )
    pre_two, normed_two, inverse_two = norm_forward(
        second_activation, inside, pixel_count, gain_dilated, bias_dilated
    )
    hidden_two = jax.nn.silu(pre_two).astype(jnp.bfloat16)
    act_three = flat_dot(hidden_two, full_expand)
    pre_three, normed_three, inverse_three = norm_forward(
        act_three, inside, pixel_count, gain_expand, bias_expand
    )
    pre_three = pre_three + inputs_flat
    block_out = jax.nn.silu(pre_three).astype(jnp.bfloat16)
    wide_block = widen_rows(
        block_out.reshape(local_rows, local_columns, channels),
        outer_extent,
        lambda piece, distance: passed_along(piece, "fsdp", distance),
    )
    point_act = flat_dot(block_out, full_point)
    pre_point, normed_point, inverse_point = norm_forward(
        point_act, inside, pixel_count, gain_point, bias_point
    )
    branch_point = jax.nn.silu(pre_point).astype(jnp.bfloat16)
    rate_states = []
    rate_branches = []
    for kernel, factor, offset, spacing, tables in zip(
        rate_kernels, rate_gains, rate_biases, spacings, near_rates
    ):
        rate_act = spread_offsets(
            rim_slice(wide_block, spacing, outer_extent, local_rows),
            kernel,
            tables,
            spacing,
            local_rows,
            local_columns,
        )
        pre_rate, normed_rate, inverse_rate = norm_forward(
            rate_act, inside, pixel_count, factor, offset
        )
        rate_states.append((pre_rate, normed_rate, inverse_rate))
        rate_branches.append(jax.nn.silu(pre_rate).astype(jnp.bfloat16))
    crop_flat = crop_ids.reshape(pixel_values)
    crop_total = CROPS_TILE
    first_crop = lax.axis_index("dp") * crop_total
    owner_group = lax.axis_size("fsdp")
    owner_place = lax.axis_index("fsdp")
    local_crop = crop_flat - first_crop
    member = local_crop[:, None] == jnp.arange(crop_total)[None, :]
    member_low = member.astype(jnp.bfloat16)
    crop_sums = inner_dot(member_low, block_out)
    crop_sizes = jnp.sum(member.astype(jnp.float32), axis=0)
    crop_sums, crop_sizes = lax.psum((crop_sums, crop_sizes), "fsdp")
    pooled = (crop_sums / crop_sizes[:, None]).astype(jnp.bfloat16)
    pool_act = flat_dot(pooled, full_pool)
    pool_low = jax.nn.silu(pool_act).astype(jnp.bfloat16)
    branch_pool = flat_dot(member_low, pool_low).astype(jnp.bfloat16)
    joined = jnp.concatenate([branch_point] + rate_branches + [branch_pool], axis=1)
    merge_act = flat_dot(joined, full_merge)
    pre_merge, normed_merge, inverse_merge = norm_forward(
        merge_act, inside, pixel_count, gain_merge, bias_merge
    )
    merged = jax.nn.silu(pre_merge).astype(jnp.bfloat16)
    logits_full = flat_dot(merged, full_classes)
    class_logits = logits_full.astype(jnp.bfloat16).reshape(local_rows, local_columns, -1)
    (
        full_reduce,
        complete_dilated,
        full_expand,
        full_point,
        full_rate,
        full_double,
        full_triple,
        full_pool,
        full_merge,
        full_classes,
    ) = (
        lax.all_gather(w_reduce, "fsdp", axis=1, tiled=True),
        lax.all_gather(w_dilated, "fsdp", axis=3, tiled=True),
        lax.all_gather(w_expand, "fsdp", axis=1, tiled=True),
        lax.all_gather(w_point, "fsdp", axis=1, tiled=True),
        lax.all_gather(w_rate, "fsdp", axis=3, tiled=True),
        lax.all_gather(w_rate_double, "fsdp", axis=3, tiled=True),
        lax.all_gather(w_rate_triple, "fsdp", axis=3, tiled=True),
        lax.all_gather(w_pool, "fsdp", axis=1, tiled=True),
        lax.all_gather(w_merge, "fsdp", axis=1, tiled=True),
        lax.all_gather(w_classes, "fsdp", axis=0, tiled=True),
    )
    rate_kernels = (full_rate, full_double, full_triple)
    highest = jnp.max(logits_full, axis=1, keepdims=True)
    shifted = jnp.exp(logits_full - highest)
    probability = shifted / jnp.sum(shifted, axis=1, keepdims=True)
    targets = (labels.reshape(pixel_values, 1) == jnp.arange(CLASSES)[None, :]).astype(jnp.float32)
    grad_logits = (inside * (probability - targets) / pixel_count).astype(jnp.bfloat16)
    grad_classes = inner_dot(merged, grad_logits)
    grad_merged = outer_dot(grad_logits, full_classes)
    passed, grad_gain_merge, grad_bias_merge = norm_backward(
        grad_merged * slope(pre_merge), normed_merge, inverse_merge, gain_merge, inside, pixel_count
    )
    grad_merge_act = passed.astype(jnp.bfloat16)
    grad_merge = inner_dot(joined, grad_merge_act)
    grad_joined = outer_dot(grad_merge_act, full_merge)
    branch_width = full_merge.shape[1]
    passed, grad_gain_point, grad_bias_point = norm_backward(
        grad_joined[:, :branch_width] * slope(pre_point),
        normed_point,
        inverse_point,
        gain_point,
        inside,
        pixel_count,
    )
    grad_point_act = passed.astype(jnp.bfloat16)
    grad_point = inner_dot(block_out, grad_point_act)
    grad_block = outer_dot(grad_point_act, full_point)
    rate_grads = []
    rate_weight_grads = []
    rate_gain_grads = []
    rate_bias_grads = []
    for branch in range(3):
        column = (1 + branch) * branch_width
        pre_rate, normed_rate, inverse_rate = rate_states[branch]
        passed, gain_grad, bias_grad = norm_backward(
            grad_joined[:, column : column + branch_width] * slope(pre_rate),
            normed_rate,
            inverse_rate,
            rate_gains[branch],
            inside,
            pixel_count,
        )
        grad_rate_act = passed.astype(jnp.bfloat16)
        pieces = kernel_offsets(
            rim_slice(wide_block, spacings[branch], outer_extent, local_rows),
            grad_rate_act,
            near_rates[branch],
            spacings[branch],
            local_rows,
            local_columns,
        )
        rate_weight_grads.append(jnp.stack(pieces).reshape(3, 3, channels, branch_width))
        rate_grads.append(grad_rate_act)
        rate_gain_grads.append(gain_grad)
        rate_bias_grads.append(bias_grad)
    rate_grads_low = jnp.concatenate(rate_grads, axis=1).reshape(local_rows, local_columns, -1)
    wide_grad_rate = widen_rows(
        rate_grads_low, outer_extent, lambda piece, distance: passed_along(piece, "fsdp", distance)
    )
    for branch in range(3):
        grad_slab = wide_grad_rate[:, :, branch * branch_width : (branch + 1) * branch_width]
        grad_block = grad_block + collect_taps(
            rim_slice(grad_slab, spacings[branch], outer_extent, local_rows),
            rate_kernels[branch],
            near_rates[branch],
            spacings[branch],
            local_rows,
            local_columns,
        )
    crop_grad = lax.dot_general(
        member.astype(jnp.float32),
        grad_joined[:, 4 * branch_width :],
        (((0,), (0,)), ((), ())),
        precision=lax.Precision.HIGHEST,
        preferred_element_type=jnp.float32,
    )
    crop_grad = lax.psum(crop_grad, "fsdp")
    grad_pool_act = (crop_grad * slope(pool_act)).astype(jnp.bfloat16)
    owned_crops = (jnp.arange(crop_total) % owner_group == owner_place).astype(jnp.float32)[:, None]
    grad_pool = inner_dot(pooled, (grad_pool_act * owned_crops).astype(jnp.bfloat16))
    grad_pooled = outer_dot(grad_pool_act, full_pool) / crop_sizes[:, None]
    grad_block = grad_block + inside * jnp.take(
        grad_pooled, jnp.clip(local_crop, 0, crop_total - 1), axis=0
    )
    grad_pre_three = grad_block * slope(pre_three)
    passed, grad_gain_expand, grad_bias_expand = norm_backward(
        grad_pre_three, normed_three, inverse_three, gain_expand, inside, pixel_count
    )
    grad_three = passed.astype(jnp.bfloat16)
    grad_expand = inner_dot(hidden_two, grad_three)
    grad_hidden_two = outer_dot(grad_three, full_expand)
    passed, grad_gain_dilated, grad_bias_dilated = norm_backward(
        grad_hidden_two * slope(pre_two), normed_two, inverse_two, gain_dilated, inside, pixel_count
    )
    second_gradient = passed.astype(jnp.bfloat16)
    dilated_fragments = kernel_offsets(
        first_broad, second_gradient, inner_neck, DILATION_SPAN, local_rows, local_columns
    )
    grad_dilated = jnp.stack(dilated_fragments).reshape(
        3, 3, second_gradient.shape[1], second_gradient.shape[1]
    )
    broad_neck_gradient = padded(
        second_gradient.reshape(local_rows, local_columns, -1), (("fsdp", 0),), DILATION_SPAN
    )
    grad_hidden_one = collect_taps(
        broad_neck_gradient, complete_dilated, inner_neck, DILATION_SPAN, local_rows, local_columns
    )
    passed, grad_gain_reduce, grad_bias_reduce = norm_backward(
        grad_hidden_one * slope(pre_one), normed_one, inverse_one, gain_reduce, inside, pixel_count
    )
    grad_one = passed.astype(jnp.bfloat16)
    grad_reduce = inner_dot(inputs_flat, grad_one)
    grad_features = (grad_pre_three + outer_dot(grad_one, full_reduce)).reshape(
        local_rows, local_columns, channels
    )
    shards = (
        lax.psum_scatter(grad_reduce, "fsdp", scatter_dimension=1, tiled=True),
        lax.psum_scatter(grad_dilated, "fsdp", scatter_dimension=3, tiled=True),
        lax.psum_scatter(grad_expand, "fsdp", scatter_dimension=1, tiled=True),
        lax.psum_scatter(grad_point, "fsdp", scatter_dimension=1, tiled=True),
        lax.psum_scatter(rate_weight_grads[0], "fsdp", scatter_dimension=3, tiled=True),
        lax.psum_scatter(rate_weight_grads[1], "fsdp", scatter_dimension=3, tiled=True),
        lax.psum_scatter(rate_weight_grads[2], "fsdp", scatter_dimension=3, tiled=True),
        lax.psum_scatter(grad_pool, "fsdp", scatter_dimension=1, tiled=True),
        lax.psum_scatter(grad_merge, "fsdp", scatter_dimension=1, tiled=True),
        lax.psum_scatter(grad_classes, "fsdp", scatter_dimension=0, tiled=True),
    )
    shards = (
        lax.psum(shards[0].astype(jnp.bfloat16), "dp").astype(jnp.float32),
        lax.psum(shards[1].astype(jnp.bfloat16), "dp").astype(jnp.float32),
        lax.psum(shards[2].astype(jnp.bfloat16), "dp").astype(jnp.float32),
        lax.psum(shards[3].astype(jnp.bfloat16), "dp").astype(jnp.float32),
        lax.psum(shards[4].astype(jnp.bfloat16), "dp").astype(jnp.float32),
        lax.psum(shards[5].astype(jnp.bfloat16), "dp").astype(jnp.float32),
        lax.psum(shards[6].astype(jnp.bfloat16), "dp").astype(jnp.float32),
        lax.psum(shards[7].astype(jnp.bfloat16), "dp").astype(jnp.float32),
        lax.psum(shards[8].astype(jnp.bfloat16), "dp").astype(jnp.float32),
        lax.psum(shards[9].astype(jnp.bfloat16), "dp").astype(jnp.float32),
    )
    return (
        class_logits,
        grad_features,
        shards[0],
        grad_gain_reduce,
        grad_bias_reduce,
        shards[1],
        grad_gain_dilated,
        grad_bias_dilated,
        shards[2],
        grad_gain_expand,
        grad_bias_expand,
        shards[3],
        grad_gain_point,
        grad_bias_point,
        shards[4],
        rate_gain_grads[0],
        rate_bias_grads[0],
        shards[5],
        rate_gain_grads[1],
        rate_bias_grads[1],
        shards[6],
        rate_gain_grads[2],
        rate_bias_grads[2],
        shards[7],
        shards[8],
        grad_gain_merge,
        grad_bias_merge,
        shards[9],
    )


def solution(mesh):
    tiled = mesh.shape["fsdp"] == 8 and mesh.shape["dp"] == 4

    return jax.shard_map(
        fast_body if tiled else body,
        mesh=mesh,
        in_specs=(
            P(("dp", "fsdp"), None, None),
            P(("dp", "fsdp"), None),
            P(("dp", "fsdp"), None),
            P(None, "fsdp"),
            P(),
            P(),
            P(None, None, None, "fsdp"),
            P(),
            P(),
            P(None, "fsdp"),
            P(),
            P(),
            P(None, "fsdp"),
            P(),
            P(),
            P(None, None, None, "fsdp"),
            P(),
            P(),
            P(None, None, None, "fsdp"),
            P(),
            P(),
            P(None, None, None, "fsdp"),
            P(),
            P(),
            P(None, "fsdp"),
            P(None, "fsdp"),
            P(),
            P(),
            P("fsdp", None),
        ),
        out_specs=(
            P(("dp", "fsdp"), None, None),
            P(("dp", "fsdp"), None, None),
            P(None, "fsdp"),
            P(),
            P(),
            P(None, None, None, "fsdp"),
            P(),
            P(),
            P(None, "fsdp"),
            P(),
            P(),
            P(None, "fsdp"),
            P(),
            P(),
            P(None, None, None, "fsdp"),
            P(),
            P(),
            P(None, None, None, "fsdp"),
            P(),
            P(),
            P(None, None, None, "fsdp"),
            P(),
            P(),
            P(None, "fsdp"),
            P(None, "fsdp"),
            P(),
            P(),
            P("fsdp", None),
        ),
        check_vma=False,
    )
```

```python
import functools
import jax
import jax.numpy as jnp
from jax import lax
from jax.experimental import pallas as pl
from jax.experimental.pallas import tpu as pltpu
from jax.sharding import PartitionSpec as P


CLASSES = 19
CROPS_TILE = 4
DILATION_SPAN = 4
RATE = 12

eps = 1e-05

MESH = pl.DeviceIdType.MESH
ANY = pl.BlockSpec(memory_space=pl.ANY)
VM = pl.BlockSpec(memory_space=pltpu.VMEM)
DMA = pltpu.SemaphoreType.DMA
PAD = 144
VLIM = 60 * 2**20


def greet(fs, ds):
    f = lax.axis_index("fsdp")
    d = lax.axis_index("dp")
    bar = pltpu.get_barrier_semaphore()
    for k in fs:
        pl.semaphore_signal(bar, inc=1, device_id=(d, f ^ k), device_id_type=MESH)
    for k in ds:
        pl.semaphore_signal(bar, inc=1, device_id=(d ^ k, f), device_id_type=MESH)
    pl.semaphore_wait(bar, len(fs) + len(ds))
    return f, d


def remote(src, dst, ss, rs, d, f):
    c = pltpu.make_async_remote_copy(
        src_ref=src, dst_ref=dst, send_sem=ss, recv_sem=rs, device_id=(d, f), device_id_type=MESH
    )
    c.start()
    return c


def sum_kernel(x_ref, o_ref, b1, b2, s1, r1, s2, r2):
    f, d = greet(range(1, 8), range(1, 4))
    b1[f] = x_ref[...]
    cps = [remote(x_ref, b1.at[f], s1.at[k], r1.at[k], d, f ^ k) for k in range(1, 8)]
    for c in cps:
        c.wait()
    tot = b1[0]
    for k in range(1, 8):
        tot = tot + b1[k]
    b2[d] = tot
    cps = [remote(b2.at[d], b2.at[d], s2.at[k], r2.at[k], d ^ k, f) for k in range(1, 4)]
    for c in cps:
        c.wait()
    tot = b2[0]
    for k in range(1, 4):
        tot = tot + b2[k]
    o_ref[...] = tot


def total_sum(rows, cid):
    x = jnp.stack(rows)
    R, C = x.shape
    return pl.pallas_call(
        sum_kernel,
        out_shape=jax.ShapeDtypeStruct((R, C), jnp.float32),
        in_specs=[VM],
        out_specs=VM,
        scratch_shapes=[
            pltpu.VMEM((8, R, C), jnp.float32),
            pltpu.VMEM((4, R, C), jnp.float32),
            DMA((8,)),
            DMA((8,)),
            DMA((4,)),
            DMA((4,)),
        ],
        compiler_params=pltpu.CompilerParams(collective_id=cid, has_side_effects=True),
        name=f"total_sum_{cid}",
    )(x)


def spread_kernel(x_ref, o_ref, ss, rs, ls):
    f, d = greet(range(1, 8), ())
    w = o_ref.shape[2]
    h = x_ref.shape[1]
    dst = o_ref.at[:, pl.ds(pl.multiple_of(PAD + h * f, 16), h), :]

    def part(g):
        return x_ref.at[:, :, pl.ds(pl.multiple_of(g * w, 128), w)]

    cps = [remote(part(f ^ k), dst, ss.at[k], rs.at[k], d, f ^ k) for k in (6, 7, 2, 3, 4, 5, 1)]
    own = pltpu.make_async_copy(part(f), dst, ls)
    own.start()
    for c in cps:
        c.wait()
    own.wait()


def spread_channels(x, cid):
    q, h, C = x.shape
    return pl.pallas_call(
        spread_kernel,
        out_shape=jax.ShapeDtypeStruct((q, 8 * h + 2 * PAD, C // 8), x.dtype),
        in_specs=[VM],
        out_specs=ANY,
        scratch_shapes=[DMA((8,)), DMA((8,)), DMA(())],
        compiler_params=pltpu.CompilerParams(collective_id=cid, has_side_effects=True, vmem_limit_bytes=VLIM),
        name=f"spread_{cid}",
    )(x)


def collect_kernel(x_ref, o_ref, ss, rs, ls):
    f, d = greet(range(1, 8), ())
    w = x_ref.shape[2]
    h = o_ref.shape[1]
    dst = o_ref.at[:, :, pl.ds(pl.multiple_of(f * w, 128), w)]

    def part(g):
        return x_ref.at[:, pl.ds(pl.multiple_of(h * g, 16), h), :]

    cps = [remote(part(f ^ k), dst, ss.at[k], rs.at[k], d, f ^ k) for k in (6, 7, 2, 3, 4, 5, 1)]
    own = pltpu.make_async_copy(part(f), dst, ls)
    own.start()
    for c in cps:
        c.wait()
    own.wait()


def collect_channels(x, cid):
    q, t, w = x.shape
    return pl.pallas_call(
        collect_kernel,
        out_shape=jax.ShapeDtypeStruct((q, t // 8, 8 * w), x.dtype),
        in_specs=[VM],
        out_specs=ANY,
        scratch_shapes=[DMA((8,)), DMA((8,)), DMA(())],
        compiler_params=pltpu.CompilerParams(collective_id=cid, has_side_effects=True, vmem_limit_bytes=VLIM),
        name=f"collect_{cid}",
    )(x)


def gather_kernel(x_ref, o_ref, ss, rs, ps, pr, ls):
    f, d = greet((1, 2, 4, 6), ())
    h = x_ref.shape[1]

    def slot(g):
        return o_ref.at[:, pl.ds(pl.multiple_of(PAD + h * g, 16), h), :]

    cps = [remote(x_ref, slot(f), ss.at[k], rs.at[k], d, f ^ (2 * k)) for k in (3, 1, 2)]
    own = pltpu.make_async_copy(x_ref, slot(f), ls)
    own.start()
    pair = [remote(x_ref, slot(f), ps.at[0], pr.at[0], d, f ^ 1)]
    for k, c in zip((3, 1, 2), cps):
        c.wait_recv()
        got = slot(f ^ (2 * k))
        pair.append(remote(got, got, ps.at[k], pr.at[k], d, f ^ 1))
    for c in cps:
        c.wait_send()
    for c in pair:
        c.wait()
    own.wait()


def gather_rows(x, cid):
    q, h, C = x.shape
    return pl.pallas_call(
        gather_kernel,
        out_shape=jax.ShapeDtypeStruct((q, 8 * h + 2 * PAD, C), x.dtype),
        in_specs=[VM],
        out_specs=ANY,
        scratch_shapes=[DMA((4,)), DMA((4,)), DMA((4,)), DMA((4,)), DMA(())],
        compiler_params=pltpu.CompilerParams(collective_id=cid, has_side_effects=True, vmem_limit_bytes=VLIM),
        name=f"gather_{cid}",
    )(x)


def scatter_kernel(x_ref, o_ref, near, mine, far, ps, pr, ss, rs):
    f, d = greet((1, 2, 4, 6), ())
    c0 = f & 1
    pair = [
        remote(x_ref.at[2 * k + 1 - c0], near.at[k], ps.at[k], pr.at[k], d, f ^ 1) for k in range(4)
    ]
    me = lax.shift_right_logical(f, 1)
    cps = []
    for c in pair:
        c.wait()
    for k in (3, 1, 2, 0):
        g = me ^ k
        val = x_ref[2 * g + c0].astype(jnp.float32) + near[g].astype(jnp.float32)
        if k:
            mine[k] = val.astype(mine.dtype)
            cps.append(remote(mine.at[k], far.at[k], ss.at[k], rs.at[k], d, f ^ (2 * k)))
        else:
            o_ref[...] = val
    for c in cps:
        c.wait()
    o_ref[...] += far[1].astype(jnp.float32) + far[2].astype(jnp.float32) + far[3].astype(jnp.float32)


def scatter_sum(x, cid):
    n, R, C = x.shape
    return pl.pallas_call(
        scatter_kernel,
        out_shape=jax.ShapeDtypeStruct((R, C), jnp.float32),
        in_specs=[VM],
        out_specs=VM,
        scratch_shapes=[
            pltpu.VMEM((4, R, C), x.dtype),
            pltpu.VMEM((4, R, C), x.dtype),
            pltpu.VMEM((4, R, C), x.dtype),
            DMA((4,)),
            DMA((4,)),
            DMA((4,)),
            DMA((4,)),
        ],
        compiler_params=pltpu.CompilerParams(collective_id=cid, has_side_effects=True, vmem_limit_bytes=VLIM),
        name=f"scatter_{cid}",
    )(x)


def nt_dot(a, b):
    return lax.dot_general(a, b, (((1,), (1,)), ((), ())), preferred_element_type=jnp.float32)


def nn_dot(a, b):
    return lax.dot_general(a, b, (((1,), (0,)), ((), ())), preferred_element_type=jnp.float32)


def tn_dot(a, b):
    return lax.dot_general(a, b, (((0,), (0,)), ((), ())), preferred_element_type=jnp.float32)


def span(shift, count):
    return max(0, -shift), min(count, count - shift)


def conv_forward_kernel(steps, y_ref, key_ref, k_ref, o_ref, acc):
    Q = y_ref.shape[0]
    h = o_ref.shape[2]
    w = y_ref.shape[2]
    out = k_ref.shape[1]
    dest = pl.program_id(0)
    base = PAD + h * dest
    T = 8 * h
    for b, s in enumerate(steps):
        acc[...] = jnp.zeros_like(acc)
        for i in (-1, 0, 1):
            first = h * dest + 16 * s * i

            @pl.when((first + h > 0) & (first < T))
            def _():
                at = pl.multiple_of(base + 16 * s * i, 16)
                for j in (-1, 0, 1):
                    lo, hi = span(s * j, Q)
                    here = key_ref[lo:hi, pl.ds(pl.multiple_of(base, 16), h), :]
                    there = key_ref[lo + s * j : hi + s * j, pl.ds(at, h), :]
                    ok = (here == there) & (here > 0)
                    ok = jnp.concatenate([ok] * (w // 128), axis=2)
                    x = jnp.where(ok, y_ref[lo + s * j : hi + s * j, pl.ds(at, h), :], 0)
                    x = x.reshape((hi - lo) * h, w)
                    acc[lo * h : hi * h] += nt_dot(x, k_ref[9 * b + 3 * (i + 1) + j + 1])

        o_ref[0, :, :, b * out : (b + 1) * out] = acc[...].reshape(Q, h, out).astype(o_ref.dtype)


def conv_forward(y, key, k, steps):
    Q, TT, w = y.shape
    h = (TT - 2 * PAD) // 8
    out = k.shape[1]
    return pl.pallas_call(
        functools.partial(conv_forward_kernel, steps),
        out_shape=jax.ShapeDtypeStruct((8, Q, h, 3 * out), jnp.bfloat16),
        grid=(8,),
        in_specs=[VM, VM, VM],
        out_specs=pl.BlockSpec((1, Q, h, 3 * out), lambda i: (i, 0, 0, 0)),
        scratch_shapes=[pltpu.VMEM((Q * h, out), jnp.float32)],
        compiler_params=pltpu.CompilerParams(vmem_limit_bytes=VLIM),
        name="conv_forward",
    )(y, key, k)


def conv_data_kernel(steps, g_ref, key_ref, k_ref, o_ref, acc):
    Q = g_ref.shape[0]
    h = o_ref.shape[1]
    w = o_ref.shape[2]
    out = k_ref.shape[1]
    dest = pl.program_id(0)
    base = PAD + h * dest
    T = 8 * h
    acc[...] = jnp.zeros_like(acc)
    for b, s in enumerate(steps):
        for i in (-1, 0, 1):
            first = h * dest - 16 * s * i

            @pl.when((first + h > 0) & (first < T))
            def _():
                at = pl.multiple_of(base - 16 * s * i, 16)
                for j in (-1, 0, 1):
                    lo, hi = span(-s * j, Q)
                    here = key_ref[lo:hi, pl.ds(pl.multiple_of(base, 16), h), :]
                    there = key_ref[lo - s * j : hi - s * j, pl.ds(at, h), :]
                    ok = (here == there) & (here > 0)
                    ok = jnp.concatenate([ok] * (out // 128), axis=2)
                    x = jnp.where(
                        ok, g_ref[lo - s * j : hi - s * j, pl.ds(at, h), b * out : (b + 1) * out], 0
                    )
                    x = x.reshape((hi - lo) * h, out)
                    acc[lo * h : hi * h] += nn_dot(x, k_ref[9 * b + 3 * (i + 1) + j + 1])

    o_ref[...] = acc[...].reshape(Q, h, w).astype(o_ref.dtype)


def conv_data(g, key, k, steps):
    Q, TT, _ = g.shape
    h = (TT - 2 * PAD) // 8
    w = k.shape[2]
    return pl.pallas_call(
        functools.partial(conv_data_kernel, steps),
        out_shape=jax.ShapeDtypeStruct((Q, 8 * h, w), jnp.bfloat16),
        grid=(8,),
        in_specs=[VM, VM, VM],
        out_specs=pl.BlockSpec((Q, h, w), lambda i: (0, i, 0)),
        scratch_shapes=[pltpu.VMEM((Q * h, w), jnp.float32)],
        compiler_params=pltpu.CompilerParams(vmem_limit_bytes=VLIM),
        name="conv_data",
    )(g, key, k)


def conv_weight_kernel(steps, y_ref, key_ref, g_ref, o_ref, x_ref):
    Q = y_ref.shape[0]
    w = y_ref.shape[2]
    out = o_ref.shape[1]
    TT = y_ref.shape[1]
    T = TT - 2 * PAD
    b = pl.program_id(0)
    for n, s in enumerate(steps):

        @pl.when(b == n)
        def _():
            for i in (-1, 0, 1):
                r0, r1 = span(16 * s * i, T)
                r0, r1 = r0 // 128 * 128, -(-r1 // 128) * 128
                for j in (-1, 0, 1):
                    lo, hi = span(s * j, Q)
                    L = r1 - r0

                    def one(q, _):
                        here = key_ref[q, PAD + r0 : PAD + r1, :]
                        a = PAD + r0 + 16 * s * i
                        there = key_ref[q + s * j, a : a + L, :]
                        ok = (here == there) & (here > 0)
                        ok = jnp.concatenate([ok] * (w // 128), axis=1)
                        x = jnp.where(ok, y_ref[q + s * j, a : a + L, :], 0)
                        x_ref[pl.ds(pl.multiple_of((q - lo) * L, 128), L), :] = x
                        return 0

                    lax.fori_loop(lo, hi, one, 0)
                    d = g_ref[lo:hi, PAD + r0 : PAD + r1, n * out : (n + 1) * out]
                    d = d.reshape((hi - lo) * L, out)
                    o_ref[3 * (i + 1) + j + 1] = tn_dot(d, x_ref[: (hi - lo) * L, :]).astype(o_ref.dtype)


def conv_weight(y, key, g, steps, out):
    Q, TT, w = y.shape
    T = TT - 2 * PAD
    return pl.pallas_call(
        functools.partial(conv_weight_kernel, steps),
        out_shape=jax.ShapeDtypeStruct((27, out, w), jnp.bfloat16),
        grid=(3,),
        in_specs=[VM, VM, VM],
        out_specs=pl.BlockSpec((9, out, w), lambda i: (i, 0, 0)),
        scratch_shapes=[pltpu.VMEM((Q * T, w), jnp.bfloat16)],
        compiler_params=pltpu.CompilerParams(vmem_limit_bytes=VLIM),
        name="conv_weight",
    )(y, key, g)


class Load:
    def __init__(self, sems, **pairs):
        self.cps = {}
        for n, (name, (src, dst)) in enumerate(pairs.items()):
            self.cps[name] = pltpu.make_async_copy(src, dst, sems.at[n])
            self.cps[name].start()

    def need(self, *names):
        for name in names:
            self.cps.pop(name).wait()


class Gather:
    def __init__(self, src, slot, sems, d, f):
        self.src, self.slot, self.sems, self.d, self.f = src, slot, sems, d, f

    def start(self):
        far_s, far_r, near_s, near_r, local = self.sems
        d, f = self.d, self.f
        mine = self.slot(f)
        self.far = {k: remote(self.src, mine, far_s.at[k], far_r.at[k], d, f ^ (2 * k)) for k in (3, 1, 2)}
        self.near = [remote(self.src, mine, near_s.at[0], near_r.at[0], d, f ^ 1)]
        self.own = pltpu.make_async_copy(self.src, mine, local)
        self.own.start()

    def forward(self):
        far_s, far_r, near_s, near_r, local = self.sems
        for k in (1, 2, 3):
            self.far[k].wait_recv()
            got = self.slot(self.f ^ (2 * k))
            self.near.append(remote(got, got, near_s.at[k], near_r.at[k], self.d, self.f ^ 1))

    def arrive(self):
        self.own.wait()
        for c in self.near:
            c.wait_recv()

    def finish(self):
        for c in list(self.far.values()) + self.near:
            c.wait_send()


class HalfGather:
    def __init__(self, src, slot, half, sems, d, f):
        self.src, self.slot, self.half, self.sems, self.d, self.f = src, slot, half, sems, d, f

    def start(self):
        far_s, far_r, near_s, near_r, side_s, side_r, local = self.sems
        d, f = self.d, self.f
        mine = self.slot(f)
        a = self.half(d % 2)
        self.far = {
            k: remote(self.src.at[a], mine.at[a], far_s.at[k], far_r.at[k], d, f ^ (2 * k)) for k in (3, 1, 2)
        }
        self.near = [remote(self.src, mine, near_s.at[0], near_r.at[0], d, f ^ 1)]
        self.own = pltpu.make_async_copy(self.src, mine, local)
        self.own.start()

    def forward(self):
        far_s, far_r, near_s, near_r, side_s, side_r, local = self.sems
        d, f = self.d, self.f
        a = self.half(d % 2)
        self.side = {}
        for k in (1, 2, 3):
            self.far[k].wait_recv()
            got = self.slot(f ^ (2 * k)).at[a]
            self.side[k] = remote(got, got, side_s.at[k], side_r.at[k], d ^ 1, f)
            self.near.append(remote(got, got, near_s.at[k], near_r.at[k], d, f ^ 1))

    def arrive(self):
        far_s, far_r, near_s, near_r, side_s, side_r, local = self.sems
        d, f = self.d, self.f
        b = self.half(1 - d % 2)
        for k in (1, 2, 3):
            self.side[k].wait_recv()
            got = self.slot(f ^ (2 * k)).at[b]
            self.near.append(remote(got, got, near_s.at[k + 3], near_r.at[k + 3], d, f ^ 1))
        self.own.wait()
        for c in self.near:
            c.wait_recv()

    def finish(self):
        for c in list(self.far.values()) + self.near + list(self.side.values()):
            c.wait_send()


def half_sems():
    return [DMA((4,)), DMA((4,)), DMA((7,)), DMA((7,)), DMA((4,)), DMA((4,)), DMA(())]


def gather_sems():
    return [DMA((4,)), DMA((4,)), DMA((4,)), DMA((4,)), DMA(())]


def sum_sems(R, C):
    return [
        pltpu.VMEM((8, R, C), jnp.float32),
        pltpu.VMEM((4, R, C), jnp.float32),
        DMA((8,)),
        DMA((8,)),
        DMA((4,)),
        DMA((4,)),
    ]


def sum_all(rows, bufs, d, f):
    b1, b2, s1, r1, s2, r2 = bufs
    for n, row in enumerate(rows):
        b1[f, n : n + 1, :] = row
    cps = [remote(b1.at[f], b1.at[f], s1.at[k], r1.at[k], d, f ^ k) for k in (6, 2, 4, 7, 3, 5, 1)]
    for c in cps:
        c.wait()
    tot = b1[0]
    for k in range(1, 8):
        tot = tot + b1[k]
    b2[d] = tot
    cps = [remote(b2.at[d], b2.at[d], s2.at[k], r2.at[k], d ^ k, f) for k in (3, 2, 1)]
    for c in cps:
        c.wait()
    tot = b2[0]
    for k in range(1, 4):
        tot = tot + b2[k]
    return tot


def column_sums(a, ins):
    m = a * jnp.concatenate([ins] * (a.shape[1] // 128), axis=1)
    return jnp.sum(m, axis=0, keepdims=True), jnp.sum(m * a, axis=0, keepdims=True)


def bend(p):
    g = 1.0 / (1.0 + jnp.exp(-p))
    return p * g, g * (1.0 + p * (1.0 - g))


def same_crop(here, there, width):
    ok = (here == there) & (here > 0)
    return jnp.concatenate([ok] * (width // 128), axis=ok.ndim - 1)


def cat_rows(parts):
    return jnp.concatenate(parts, axis=1)


def bottleneck_kernel(
    x_any, kb_ref, ins_ref, gr, br, gd, bd, ge, be,
    wr_s, wd_s, we_s, wp_s, wm_s, wc_s, k_s0, k_s1, k_s2, kp_s,
    yo_o, y_o, n3_o, l3_o, n1_o, l1_o, n2_o, l2_o, ext_o, h2_o, key_o, k_o, wr_o, wd_o, we_o, wp_o, wm_o, wc_o, cnt_o,
    x_ref, lsem, xp, a1, a2, a3, ext, h2, y, n3, l3, n1, l1, n2, l2, key, wr, wd, we,
    *sems,
):
    sems = list(sems)

    def take(n):
        got = sems[:n]
        del sems[:n]
        return got

    load = Load(lsem, x=(x_any, x_ref))
    f, d = greet(range(1, 8), range(1, 4))
    N, C = x_ref.shape
    Q, h = ext.shape[0], ext.shape[1] // 2
    e = h // 2
    rows = h // 4
    neck = a1.shape[1]
    T = 8 * h

    def rows_of(ref, n):
        return lambda g: ref.at[pl.ds(pl.multiple_of(n * g, n), n)]

    nr, nd_, ne, np_ = wr_s.shape[0], wd_s.shape[1], we_s.shape[1], wp_s.shape[0]
    def half(n, lead=()):
        return lambda a: lead + (pl.ds(pl.multiple_of(n * a, n), n),)

    g_wr = Gather(wr_s, rows_of(wr, nr), take(5), d, f)
    g_wd = [
        HalfGather(
            wd_s.at[pl.ds(3 * i, 3)],
            lambda g, i=i: wd.at[pl.ds(3 * i, 3), pl.ds(pl.multiple_of(nd_ * g, 16), nd_), :],
            half(nd_ // 2, (slice(None),)), take(7), d, f,
        )
        for i in range(3)
    ]
    g_we = HalfGather(
        we_s, lambda g: we.at[:, pl.ds(pl.multiple_of(ne * g, 128), ne)], half(we_s.shape[0] // 2), take(7), d, f
    )
    g_wp = Gather(wp_s, rows_of(wp_o, np_), take(5), d, f)
    g_wm = Gather(wm_s, rows_of(wm_o, np_), take(5), d, f)
    g_wc = Gather(wc_s, rows_of(wc_o, np_), take(5), d, f)
    ks, kr, kl, zs, zk, hs, hr, ys, yr, yl, os_, qs, qr, kc = take(14)
    sum1, sum2, sum3 = (Sum(take(6), d, f) for _ in range(3))

    key_sent = [
        remote(kb_ref, kc.at[f], qs.at[k], qr.at[k], d, f ^ k) for k in (6, 7, 2, 3, 4, 5, 1)
    ]
    kc[f] = kb_ref[...]
    g_wr.start()
    g_wd[0].start()
    order = lax.broadcasted_iota(jnp.int32, (N, N), 0)
    m, r, q = order % 4, (order // 4) % rows, order // h
    pick = (r * (N // rows) + q * 4 + m) == lax.broadcasted_iota(jnp.int32, (N, N), 1)
    pick = pick.astype(jnp.float32).astype(jnp.bfloat16)
    load.need("x")
    for c in range(0, C, 256):
        xp[:, c : c + 256] = nn_dot(pick, x_ref[:, c : c + 256]).astype(jnp.bfloat16)
    key[:, :PAD, :] = jnp.zeros((Q, PAD, 128), jnp.bfloat16)
    key[:, PAD + T :, :] = jnp.zeros((Q, PAD, 128), jnp.bfloat16)
    g_wr.forward()
    g_wd[1].start()
    g_wd[2].start()
    g_wr.arrive()
    g_wd[0].forward()
    sums, squares = [], []
    for c in range(0, neck, 256):
        a = nt_dot(xp[...], wr[c : c + 256, :])
        a1[:, c : c + 256] = a
        s, t = column_sums(a, ins_ref[...])
        sums.append(s)
        squares.append(t)
    inside = jnp.sum(ins_ref[...], axis=0, keepdims=True)
    sum1.start([cat_rows(sums), cat_rows(squares), cat_rows([inside] * (neck // 128))])
    g_we.start()
    kparts = (k_s0, k_s1, k_s2, kp_s)

    def kslot(b, g, lo, n):
        o = kparts[b].shape[1]
        return k_o.at[pl.ds(9 * b, kparts[b].shape[0]), pl.ds(pl.multiple_of(o * g + lo, 16), n), :]

    kcp, kfar = [], {}
    pieces = [(b, k) for b in range(3) for k in (6, 7, 2, 3, 4, 5)]

    def out(*ns):
        for b, k in [pieces[n] for n in ns]:
            src = kparts[b]
            o = src.shape[1] // 2
            lo = pl.multiple_of(o * (d % 2), 16)
            to = pl.ds(pl.multiple_of((f ^ k) * 256, 128), 256)
            kfar[b, k] = remote(
                src.at[:, pl.ds(lo, o), to], kslot(b, f, lo, o), ks.at[b, k], kr.at[b, k], d, f ^ k
            )

    def aside(*ns):
        for b, k in [pieces[n] for n in ns]:
            o = kparts[b].shape[1] // 2
            lo = pl.multiple_of(o * (d % 2), 16)
            kfar[b, k].wait_recv()
            got = kslot(b, f ^ k, lo, o)
            kcp.append(remote(got, got, zs.at[b, k], zk.at[b, k], d ^ 1, f))

    for b, src in enumerate(kparts):
        o = src.shape[1]
        for k in (6, 7, 2, 3, 4, 5, 1) if b == 3 else (1,):
            to = pl.ds(pl.multiple_of((f ^ k) * 256, 128), 256)
            kcp.append(remote(src.at[:, :, to], kslot(b, f, 0, o), ks.at[b, k], kr.at[b, k], d, f ^ k))
        own = pl.ds(pl.multiple_of(f * 256, 128), 256)
        c = pltpu.make_async_copy(src.at[:, :, own], kslot(b, f, 0, o), kl.at[b])
        c.start()
        kcp.append(c)
    sum1.turn()
    g_wd[1].forward()
    g_wd[2].forward()
    out(0, 1)
    st = sum1.result()
    out(2, 3)
    g_we.forward()
    count = st[2:3, :]
    cnt_o[...] = jnp.zeros_like(cnt_o)
    cnt_o[0:1, :neck] = count
    mean = st[0:1] / count
    inv = lax.rsqrt(st[1:2] / count - mean * mean + eps)
    cnt_o[1:2, :neck] = inv
    for c in range(0, neck, 256):
        w = slice(c, c + 256)
        n = (a1[:, w] - mean[:, w]) * inv[:, w]
        act, lean = bend(n * gr[:, w] + br[:, w])
        ext[:, e : e + h, w] = act.astype(jnp.bfloat16).reshape(Q, h, 256)
        n1[:, w] = n.astype(jnp.bfloat16)
        l1[:, w] = lean.astype(jnp.bfloat16)
    up = remote(ext.at[:, pl.ds(e, e)], ext.at[:, pl.ds(e + h, e)], hs.at[0], hr.at[0], d, lax.rem(f + 7, 8))
    down = remote(ext.at[:, pl.ds(h, e)], ext.at[:, pl.ds(0, e)], hs.at[1], hr.at[1], d, lax.rem(f + 1, 8))
    for c in key_sent:
        c.wait()
    for g in range(8):
        turned = kc[g].T
        for q in range(Q):
            key[q, PAD + h * g : PAD + h * g + h, :] = jnp.broadcast_to(turned[:h, q : q + 1], (h, 128)).astype(jnp.bfloat16)
    outs = [(n1, n1_o), (l1, l1_o), (key, key_o), (wr, wr_o)]
    base = pl.multiple_of(PAD + h * f, 16)
    up.wait()
    down.wait()
    outs.append((ext, ext_o))
    outs.append((wd, wd_o))
    a2[...] = jnp.zeros_like(a2)
    for i in range(3):
        g_wd[i].arrive()
        for j in (1, 0, 2):
            lo, hi = span(j - 1, Q)
            ok = same_crop(
                key[lo:hi, pl.ds(base, h), :],
                key[lo + j - 1 : hi + j - 1, pl.ds(pl.multiple_of(base + e * (i - 1), 16), h), :],
                neck,
            )
            v = jnp.where(ok, ext[lo + j - 1 : hi + j - 1, e * i : e * i + h, :], 0).reshape((hi - lo) * h, neck)
            for c in range(0, neck, 256):
                a2[lo * h : hi * h, c : c + 256] += nt_dot(v, wd[3 * i + j, c : c + 256, :])
            if (3 * i + j) % 2 == 0 and i < 2 + (j == 0):
                out(4 + (3 * i + j) // 2)
    sums, squares = [], []
    for c in range(0, neck, 256):
        s, t = column_sums(a2[:, c : c + 256], ins_ref[...])
        sums.append(s)
        squares.append(t)
    sum2.start([cat_rows(sums), cat_rows(squares)])
    aside(0, 1, 2, 3)
    sum2.turn()
    out(8, 9)
    for g in (g_wp, g_wm, g_wc):
        g.start()
    st = sum2.result()
    out(10)
    mean = st[0:1] / count
    inv = lax.rsqrt(st[1:2] / count - mean * mean + eps)
    cnt_o[2:3, :neck] = inv
    for c in range(0, neck, 256):
        w = slice(c, c + 256)
        n = (a2[:, w] - mean[:, w]) * inv[:, w]
        act, lean = bend(n * gd[:, w] + bd[:, w])
        h2[:, w] = act.astype(jnp.bfloat16)
        n2[:, w] = n.astype(jnp.bfloat16)
        l2[:, w] = lean.astype(jnp.bfloat16)
    outs += [(n2, n2_o), (l2, l2_o), (h2, h2_o)]
    g_we.arrive()
    outs.append((we, we_o))
    sums, squares = [], []
    for c in range(0, C, 256):
        n = c // 256
        if n % 2 == 0:
            out(11 + n // 2)
        else:
            aside(4 + n // 2)
        a = nn_dot(h2[...], we[:, c : c + 256])
        a3[:, c : c + 256] = a
        s, t = column_sums(a, ins_ref[...])
        sums.append(s)
        squares.append(t)
    sum3.start([cat_rows(sums), cat_rows(squares)])
    aside(8, 9)
    out(15, 16, 17)
    sum3.turn()
    st = sum3.result()
    total = count[:, :1]
    mean3 = st[0:1] / total
    inv3 = lax.rsqrt(st[1:2] / total - mean3 * mean3 + eps)
    coef = sum3.b1
    coef[0, 0:1, :] = mean3
    coef[0, 1:2, :] = inv3
    cnt_o[3:4, :] = inv3
    sent = []
    dst = yo_o.at[:, pl.ds(base, h), :]
    for m, k in enumerate((6, 7, 2, 3, 4, 5, 1, 0)):
        aside(10 + m)
        g = f ^ k
        w = pl.ds(pl.multiple_of(g * 256, 256), 256)
        n = (a3[:, w] - coef[0, 0:1, w]) * coef[0, 1:2, w]
        act, lean = bend(n * ge[:, w] + be[:, w] + xp[:, w].astype(jnp.float32))
        y[:, :, w] = act.astype(jnp.bfloat16).reshape(Q, h, 256)
        n3[:, w] = n.astype(jnp.bfloat16)
        l3[:, w] = lean.astype(jnp.bfloat16)
        part = y.at[:, :, w]
        if k:
            sent.append(remote(part, dst, ys.at[k], yr.at[k], d, g))
        else:
            own = pltpu.make_async_copy(part, dst, yl)
            own.start()
            sent.append(own)
    outs += [(y, y_o), (n3, n3_o), (l3, l3_o)]
    saved = []
    for n, (src, to) in enumerate(outs):
        c = pltpu.make_async_copy(src, to, os_.at[n])
        c.start()
        saved.append(c)
    for g in (g_wp, g_wm, g_wc):
        g.forward()
    for g in (g_wp, g_wm, g_wc):
        g.arrive()
    for g in [g_wr, g_we, g_wp, g_wm, g_wc] + g_wd:
        g.finish()
    for c in kfar.values():
        c.wait_send()
    for c in kcp + sent + saved:
        c.wait()


def bottleneck(x, kb, ins, vecs, shards, kparts):
    N, C = x.shape
    Q = kb.shape[0]
    h = N // Q
    wr, wd, we, wp, wm, wc = shards
    neck = we.shape[0]
    W = 8 * wp.shape[0]
    b16, f32 = jnp.bfloat16, jnp.float32
    S = jax.ShapeDtypeStruct
    TT = 8 * h + 2 * PAD
    outs = [
        S((Q, TT, C // 8), b16), S((Q, h, C), b16), S((N, C), b16), S((N, C), b16),
        S((N, neck), b16), S((N, neck), b16), S((N, neck), b16), S((N, neck), b16),
        S((Q, 2 * h, neck), b16), S((N, neck), b16), S((Q, TT, 128), b16), S((28, W, C // 8), b16),
        S((neck, C), b16), S((9, neck, neck), b16), S((neck, C), b16), S((W, C), b16), S((W, wm.shape[1]), b16),
        S((W, 128), b16), S((8, C), f32),
    ]
    V = pltpu.VMEM
    scratch = [
        V((N, C), b16), DMA((1,)), V((N, C), b16), V((N, neck), f32), V((N, neck), f32), V((N, C), f32), V((Q, 2 * h, neck), b16), V((N, neck), b16),
        V((Q, h, C), b16), V((N, C), b16), V((N, C), b16),
        V((N, neck), b16), V((N, neck), b16), V((N, neck), b16), V((N, neck), b16), V((Q, TT, 128), b16),
        V((neck, C), b16), V((9, neck, neck), b16), V((neck, C), b16),
    ]
    scratch += gather_sems() + half_sems() * 4 + gather_sems() * 3
    scratch += [DMA((4, 8)), DMA((4, 8)), DMA((4,)), DMA((4, 8)), DMA((4, 8)), DMA((2,)), DMA((2,)), DMA((8,)), DMA((8,)), DMA(()), DMA((16,))]
    scratch += [DMA((8,)), DMA((8,)), V((8, Q, 128), f32)]
    scratch += sum_sems(3, neck) + sum_sems(2, neck) + sum_sems(2, C)
    return pl.pallas_call(
        bottleneck_kernel,
        out_shape=outs,
        in_specs=[ANY] + [VM] * 8 + [ANY] * 10,
        out_specs=[ANY] * 18 + [VM],
        scratch_shapes=scratch,
        compiler_params=pltpu.CompilerParams(collective_id=1, has_side_effects=True, vmem_limit_bytes=VLIM),
        name="bottleneck",
    )(x, kb, ins, *vecs, *shards, *kparts)


def branches_back_kernel(
    steps, d_ref, y_any, key_any, k_any, pooled_ref, dr_ref, size_ref, dy_o, gk_o, tail_o,
    g, gt, gk, fin, in1, in2, dyo, acc, gp, y_ref, key_ref, k_ref, lsem, *sems,
):
    sems = list(sems)
    load = Load(lsem, key=(key_any, key_ref), y=(y_any, y_ref), k=(k_any, k_ref))
    f, d = greet(range(1, 8), range(1, 4))
    Q, h, w = y_ref.shape[0], d_ref.shape[1], y_ref.shape[2]
    W = k_ref.shape[1]
    T = 8 * h
    o = W // 8
    taps = gk.shape[0] // 2
    gathers = [
        Gather(
            d_ref.at[:, :, pl.ds(b * W, W)],
            lambda n, b=b: g.at[:, pl.ds(pl.multiple_of(PAD + h * n, 16), h), pl.ds(b * W, W)],
            sems[5 * b : 5 * b + 5], d, f,
        )
        for b in range(3)
    ]
    ws, wr, wl, ds_, dr_, dl, s1, r1, s2, r2, s3, r3 = sems[15:]
    for c in gathers:
        c.start()
    outer = d % 3 == 0

    def two(ref, t):
        return ref.at[pl.ds(2 * t, 2)]

    def to_inner(t):
        return pltpu.make_async_remote_copy(
            src_ref=two(gk, t), dst_ref=two(in1, t), send_sem=s1.at[t], recv_sem=r1.at[t],
            device_id=(d ^ 1, f), device_id_type=MESH,
        )

    def across(t):
        return pltpu.make_async_remote_copy(
            src_ref=two(gk, t), dst_ref=two(in2, t), send_sem=s2.at[t], recv_sem=r2.at[t],
            device_id=(d ^ 3, f), device_id_type=MESH,
        )

    def to_outer(t):
        return pltpu.make_async_remote_copy(
            src_ref=two(fin, t), dst_ref=two(fin, t), send_sem=s3.at[t], recv_sem=r3.at[t],
            device_id=(d ^ 1, f), device_id_type=MESH,
        )

    def hand(t):
        @pl.when(outer)
        def _():
            to_inner(t).start()

    def first(t):
        @pl.when(jnp.logical_not(outer))
        def _():
            to_inner(t).wait_recv()
            for n in (2 * t, 2 * t + 1):
                gk[n] = (gk[n].astype(jnp.float32) + in1[n].astype(jnp.float32)).astype(gk.dtype)
            across(t).start()

    def second(t):
        @pl.when(jnp.logical_not(outer))
        def _():
            across(t).wait_recv()
            for n in (2 * t, 2 * t + 1):
                fin[n] = (gk[n].astype(jnp.float32) + in2[n].astype(jnp.float32)).astype(fin.dtype)
            to_outer(t).start()

        @pl.when(outer)
        def _():
            to_outer(t).wait_recv()

    load.need("key", "y", "k")
    tail_o[9] = tn_dot(dr_ref[...], pooled_ref[...]).astype(gk.dtype)
    gp[...] = nn_dot(dr_ref[...], k_ref[27]) / size_ref[:, :1]
    for b, s in enumerate(steps):
        gathers[b].forward()
        gathers[b].arrive()

        def turn(q, _):
            gt[b * W : (b + 1) * W, pl.ds(pl.multiple_of(q * T, 256), T)] = g[q, PAD : PAD + T, b * W : (b + 1) * W].T
            return 0

        lax.fori_loop(0, Q, turn, 0)
        for i in (-1, 0, 1):
            for j in (-1, 0, 1):
                lo, hi = span(s * j, Q)
                a = PAD + 16 * s * i

                got = None
                for q in range(lo, hi):
                    ok = same_crop(key_ref[q, PAD : PAD + T, :], key_ref[q + s * j, a : a + T, :], w)
                    v = jnp.where(ok, y_ref[q + s * j, a : a + T, :], 0)
                    r = nn_dot(gt[b * W : (b + 1) * W, q * T : (q + 1) * T], v)
                    got = r if got is None else got + r
                t = 9 * b + 3 * (i + 1) + j + 1
                if b < 2:
                    gk[t] = got.astype(gk.dtype)
                    if t % 2:
                        hand(t // 2)
                else:
                    tail_o[t - 18] = got.astype(gk.dtype)
                    if t % 2:
                        first((t - 18) // 2)
    cps = []
    ready = 4

    dst = dy_o.at[:, :, pl.ds(pl.multiple_of(w * f, 128), w)]

    def rows_of(k):
        return pl.ds(pl.multiple_of(h * (f ^ k), 16), h)

    def dest_step(m, _):
        k = 7 - m
        dest = f ^ k
        base = pl.multiple_of(PAD + h * dest, 16)
        here = key_ref[:, pl.ds(base, h), :].astype(jnp.float32).reshape(Q * h, 128)
        here = jnp.concatenate([here] * (w // 128), axis=1)
        @pl.when(m % 2 == 1)
        def _():
            first(ready + m // 2)
            second(m // 2)

        total = jnp.zeros((Q * h, w), jnp.float32)
        for c in range(CROPS_TILE):
            total = jnp.where(here == c + 1.0, gp[c : c + 1, :], total)
        acc[...] = total
        for b in range(3):
            spaced_taps(g, key_ref, k_ref, acc, base, h, steps, -1, b * W, nn_dot, b)
        rows = rows_of(k)
        dyo[:, rows, :] = acc[...].reshape(Q, h, w).astype(dyo.dtype)
        src = dyo.at[:, rows, :]

        @pl.when(k > 0)
        def _():
            remote(src, dst, ds_.at[k], dr_.at[k], d, dest)

        @pl.when(k == 0)
        def _():
            pltpu.make_async_copy(src, dst, dl).start()

        return 0

    lax.fori_loop(0, 8, dest_step, 0)

    def first_when(t):
        @pl.when(t < taps)
        def _():
            first(t)

    groups = (4, 3, 2)
    at = 0
    for n, size in enumerate(groups):
        stop = at + size
        lax.fori_loop(max(at, 4), stop, lambda t, _: (first_when(t + ready), second(t), 0)[-1], 0)
        for k in (6, 7, 2, 3, 4, 5, 1, 0):
            src = fin.at[pl.ds(2 * at, 2 * size), pl.ds(pl.multiple_of(o * (f ^ k), 16), o), :]
            to = gk_o.at[pl.ds(2 * at, 2 * size), :, pl.ds(pl.multiple_of(w * f, 128), w)]
            if k:
                cps.append(remote(src, to, ws.at[n, k], wr.at[n, k], d, f ^ k))
            else:
                c = pltpu.make_async_copy(src, to, wl.at[n])
                c.start()
                cps.append(c)
        at = stop
    for k in range(1, 8):
        c = pltpu.make_async_remote_copy(
            src_ref=dyo.at[:, rows_of(k), :], dst_ref=dst, send_sem=ds_.at[k], recv_sem=dr_.at[k],
            device_id=(d, f ^ k), device_id_type=MESH,
        )
        c.wait()
    pltpu.make_async_copy(dyo.at[:, rows_of(0), :], dst, dl).wait()
    for c in gathers:
        c.finish()
    for c in cps:
        c.wait()

    def sent(t, _):
        @pl.when(outer)
        def _():
            to_inner(t).wait_send()

        @pl.when(jnp.logical_not(outer))
        def _():
            across(t).wait_send()
            to_outer(t).wait_send()

        return 0

    lax.fori_loop(0, taps, sent, 0)


def branches_back(d, y, key, k, pooled, dr, sizes, steps):
    Q, h, W3 = d.shape
    TT, w = y.shape[1:]
    W = W3 // 3
    T = 8 * h
    b16, f32 = jnp.bfloat16, jnp.float32
    V = pltpu.VMEM
    return pl.pallas_call(
        functools.partial(branches_back_kernel, steps),
        out_shape=[jax.ShapeDtypeStruct((Q, h, 8 * w), b16), jax.ShapeDtypeStruct((18, W // 8, 8 * w), b16),
            jax.ShapeDtypeStruct((10, W, w), b16),
        ],
        in_specs=[VM] + [ANY] * 3 + [VM] * 3,
        out_specs=[ANY] * 2 + [VM],
        scratch_shapes=[
            V((Q, TT, W3), b16), V((W3, Q * T), b16), V((18, W, w), b16), V((18, W, w), b16),
            V((18, W, w), b16), V((18, W, w), b16), V((Q, T, w), b16),
            V((Q * h, w), f32), V((8, w), f32), V(y.shape, b16), V(key.shape, b16), V(k.shape, b16), DMA((3,)),
        ]
        + gather_sems() * 3
        + [DMA((4, 8)), DMA((4, 8)), DMA((4,)), DMA((8,)), DMA((8,)), DMA(())]
        + [DMA((9,))] * 6,
        compiler_params=pltpu.CompilerParams(collective_id=10, has_side_effects=True, vmem_limit_bytes=VLIM),
        name="branches_back",
    )(d, y, key, k, pooled, dr, sizes)


class Sum:
    def __init__(self, bufs, d, f):
        self.b1, self.b2, self.s1, self.r1, self.s2, self.r2 = bufs
        self.d, self.f = d, f

    def start(self, rows):
        b1, d, f = self.b1, self.d, self.f
        for n, row in enumerate(rows):
            b1[f, n : n + 1, :] = row
        self.cps = [remote(b1.at[f], b1.at[f], self.s1.at[k], self.r1.at[k], d, f ^ k) for k in (6, 2, 4, 7, 3, 5, 1)]

    def turn(self):
        b1, b2, d, f = self.b1, self.b2, self.d, self.f
        for c in self.cps:
            c.wait()
        tot = b1[0]
        for k in range(1, 8):
            tot = tot + b1[k]
        b2[d] = tot
        self.cps = [remote(b2.at[d], b2.at[d], self.s2.at[k], self.r2.at[k], d ^ k, f) for k in (3, 2, 1)]

    def result(self):
        for c in self.cps:
            c.wait()
        tot = self.b2[0]
        for k in range(1, 4):
            tot = tot + self.b2[k]
        return tot


class Reduce:
    def __init__(self, full, part, half, near, far, corner, tot, zin, zo, out, sems, d, f):
        self.half, self.corner = half, corner
        self.full, self.part, self.near, self.fars, self.tot, self.out = full, part, near, far, tot, out
        self.zin, self.zo, self.d, self.f = zin, zo, d, f
        self.sems = sems
        self.c0 = f % 2
        self.me = f // 2

    def pair(self):
        ps, pr = self.sems[:2]
        self.cps = [
            remote(self.full.at[self.part(2 * g + 1 - self.c0)], self.near.at[g], ps.at[g], pr.at[g], self.d, self.f ^ 1)
            for g in range(4)
        ]

    def far(self):
        ss, rs = self.sems[2:4]
        for c in self.cps:
            c.wait()
        self.cps = []
        for k in (3, 1, 2, 0):
            g = self.me ^ k
            val = self.full[self.part(2 * g + self.c0)].astype(jnp.float32) + self.near[g].astype(jnp.float32)
            self.near[g] = val.astype(self.near.dtype)
            if k == 3:
                for a in (0, 1):
                    self.cps.append(
                        remote(
                            self.near.at[(g,) + self.half(a)], self.corner.at[self.half(a)], ss.at[a], rs.at[a],
                            self.d, self.f ^ (2 + 2 * a),
                        )
                    )

    def beside(self):
        ss, rs = self.sems[2:4]
        for c in self.cps:
            c.wait()
        self.cps = []
        for k in (1, 2):
            g = self.me ^ k
            a = self.half(2 - k)
            val = self.near[(g,) + a].astype(jnp.float32) + self.corner[a].astype(jnp.float32)
            self.near[(g,) + a] = val.astype(self.near.dtype)
            self.cps.append(
                remote(
                    self.near.at[g], self.fars.at[k - 1], ss.at[k + 1], rs.at[k + 1], self.d, self.f ^ (2 * k)
                )
            )

    def to_inner(self):
        ss, rs = self.sems[4:6]
        return pltpu.make_async_remote_copy(
            src_ref=self.tot, dst_ref=self.zin, send_sem=ss.at[0], recv_sem=rs.at[0],
            device_id=(self.d ^ 1, self.f), device_id_type=MESH,
        )

    def across(self):
        ss, rs = self.sems[4:6]
        return pltpu.make_async_remote_copy(
            src_ref=self.tot, dst_ref=self.zo, send_sem=ss.at[1], recv_sem=rs.at[1],
            device_id=(self.d ^ 3, self.f), device_id_type=MESH,
        )

    def to_outer(self):
        ss, rs = self.sems[4:6]
        return pltpu.make_async_remote_copy(
            src_ref=self.out, dst_ref=self.out, send_sem=ss.at[2], recv_sem=rs.at[2],
            device_id=(self.d ^ 1, self.f), device_id_type=MESH,
        )

    def tiles(self):
        for c in self.cps:
            c.wait()
        val = self.near[self.me].astype(jnp.float32)
        for k in (1, 2):
            val = val + self.fars[k - 1].astype(jnp.float32)
        self.tot[...] = val.astype(self.tot.dtype)

        @pl.when(self.d % 3 == 0)
        def _():
            self.to_inner().start()

    def middle(self):
        @pl.when(self.d % 3 > 0)
        def _():
            self.to_inner().wait_recv()
            val = self.tot[...].astype(jnp.float32) + self.zin[...].astype(jnp.float32)
            self.tot[...] = val.astype(self.tot.dtype)
            self.across().start()

    def last(self):
        @pl.when(self.d % 3 > 0)
        def _():
            self.across().wait_recv()
            val = self.tot[...].astype(jnp.float32) + self.zo[...].astype(jnp.float32)
            self.out[...] = val.astype(self.out.dtype)
            self.to_outer().start()

    def done(self):
        @pl.when(self.d % 3 == 0)
        def _():
            self.to_inner().wait_send()
            self.to_outer().wait_recv()

        @pl.when(self.d % 3 > 0)
        def _():
            self.across().wait_send()
            self.to_outer().wait_send()


def reduce_scratch(block):
    V, b16 = pltpu.VMEM, jnp.bfloat16
    return [V((4,) + block, b16), V((2,) + block, b16), V(block, b16), V(block, b16), V(block, b16), V(block, b16)] + [DMA((4,))] * 6


def wide(row, n):
    return jnp.concatenate([row] * n, axis=1)


def bottleneck_back_kernel(
    x_any, ins_ref, st_ref, gr, gd, ge, dy_any, dpt, y_any, pm_in, wp_any, n3_any, l3_any, we_any, n2_any, l2_any, h2_any,
    wd_any, ext_any, n1_any, l1_any, wr_any, key_any, tail_any,
    gf_o, pm_o, ex_o, di_o, re_o, s3_o, s2_o, s1_o, tk_o,
    pm, ex, di, dp3, acc, ext2, d1n, key, gf, pick, in1, in2,
    x_ref, dy, y_ref, wp, n3, l3, we, n2, l2, h2, wd, ext, n1, l1, wr, tail, lsem, ksem, hs, hr, gs, s1, r1, s2, r2, s3, r3, ws, wrs, wl,
    *sems,
):
    sems = list(sems)

    def take(n):
        got = sems[:n]
        del sems[:n]
        return got

    load = Load(
        lsem, tail=(tail_any, tail), y=(y_any, y_ref), wp=(wp_any, wp), dy=(dy_any, dy), l3=(l3_any, l3), n3=(n3_any, n3),
        we=(we_any, we), l2=(l2_any, l2), n2=(n2_any, n2), h2=(h2_any, h2), ext=(ext_any, ext), wd=(wd_any, wd),
        l1=(l1_any, l1), n1=(n1_any, n1), x=(x_any, x_ref), wr=(wr_any, wr),
    )
    f, d = greet(range(1, 8), range(1, 4))
    N, C = x_ref.shape
    Q, h = ext2.shape[0], ext2.shape[1] // 2
    e = h // 2
    rows = h // 4
    neck = acc.shape[1]
    nb = neck // 8
    nw = pm.shape[0] // 8
    W = dpt.shape[1]

    def ds(i, n):
        return pl.ds(pl.multiple_of(n * i, n), n)

    def reducer(full, part, half, out):
        near, far, corner, tot, zin, zo = take(6)
        return Reduce(full, part, half, near, far, corner, tot, zin, zo, out, take(6), d, f)

    def half_rows(n):
        return lambda a: (pl.ds(a * n, n),)

    r_pm = reducer(pm, lambda g: (ds(g, nw),), half_rows(nw // 2), pm_o)
    r_ex = reducer(ex, lambda g: (slice(None), ds(g, C // 8)), half_rows(neck // 2), ex_o)
    r_di = [
        reducer(
            di.at[pl.ds(3 * i, 3)], lambda g: (slice(None), ds(g, nb)),
            lambda a: (slice(None), pl.ds(a * (nb // 2), nb // 2)), di_o.at[pl.ds(3 * i, 3)],
        )
        for i in range(3)
    ]
    re_ = ex
    d3 = dy
    r_re = reducer(re_, lambda g: (ds(g, nb),), half_rows(nb // 2), re_o)
    sum3, sum2, sum1 = (Sum(take(6), d, f) for _ in range(3))

    outer = d % 3 == 0
    o = in1.shape[1] // 8
    lanes = in1.shape[2]
    kout = []

    def move(src, dst, ss, rs, t, other):
        two = pl.ds(2 * t, 2)
        return pltpu.make_async_remote_copy(
            src_ref=src.at[two], dst_ref=dst.at[two], send_sem=ss.at[t], recv_sem=rs.at[t],
            device_id=(d ^ other, f), device_id_type=MESH,
        )

    def to_inner(t):
        return move(tail, in1, s1, r1, t, 1)

    def across(t):
        return move(in1, in2, s2, r2, t, 3)

    def to_outer(t):
        return move(in1, in1, s3, r3, t, 1)

    def hand(t):
        @pl.when(outer)
        def _():
            to_inner(t).start()

    def first(t):
        @pl.when(jnp.logical_not(outer))
        def _():
            to_inner(t).wait_recv()
            for n in (2 * t, 2 * t + 1):
                in1[n] = (in1[n].astype(jnp.float32) + tail[n].astype(jnp.float32)).astype(in1.dtype)
            across(t).start()

    def second(t):
        @pl.when(jnp.logical_not(outer))
        def _():
            across(t).wait()
            for n in (2 * t, 2 * t + 1):
                in1[n] = (in1[n].astype(jnp.float32) + in2[n].astype(jnp.float32)).astype(in1.dtype)
            to_outer(t).start()

    def keep(n, at, size):
        for t in range(at, at + size):

            @pl.when(outer)
            def _():
                to_outer(t).wait_recv()

        for k in (6, 7, 2, 3, 4, 5, 1, 0):
            src = in1.at[pl.ds(2 * at, 2 * size), pl.ds(pl.multiple_of(o * (f ^ k), 16), o), :]
            to = tk_o.at[pl.ds(2 * at, 2 * size), :, pl.ds(pl.multiple_of(lanes * f, 128), lanes)]
            if k:
                kout.append(remote(src, to, ws.at[n, k], wrs.at[n, k], d, f ^ k))
            else:
                c = pltpu.make_async_copy(src, to, wl.at[n])
                c.start()
                kout.append(c)

    load.need("tail")
    hand(0)
    hand(1)
    kcp = pltpu.make_async_copy(key_any.at[:, pl.ds(pl.multiple_of(PAD - e + h * f, 16), 2 * h), :], key, ksem)
    kcp.start()
    count = st_ref[0:1, 0:1]
    load.need("y")
    for c in range(0, C, 256):
        pm[:, c : c + 256] = tn_dot(dpt[...], y_ref[:, c : c + 256]).astype(jnp.bfloat16)
    pm[:, C:] = pm_in[...]
    r_pm.pair()
    load.need("wp", "dy", "l3", "n3")
    ones, crossed = [], []
    ins = wide(ins_ref[...], 2)
    for c in range(0, C, 256):
        w = slice(c, c + 256)
        if c == C // 2:
            first(0)
        v = dy[:, w].astype(jnp.float32) + nn_dot(dpt[...], wp[:, w])
        v = v * l3[:, w].astype(jnp.float32)
        dp3[:, w] = v.astype(jnp.bfloat16)
        v = v * ins
        ones.append(jnp.sum(v, axis=0, keepdims=True))
        crossed.append(jnp.sum(v * n3[:, w].astype(jnp.float32), axis=0, keepdims=True))
    sum3.start([cat_rows(ones), cat_rows(crossed)])
    order = lax.broadcasted_iota(jnp.int32, (N, N), 1)
    m, r, q = order % 4, (order // 4) % rows, order // h
    hit = (r * (N // rows) + q * 4 + m) == lax.broadcasted_iota(jnp.int32, (N, N), 0)
    pick[...] = hit.astype(jnp.float32).astype(jnp.bfloat16)
    sum3.turn()
    r_pm.far()
    tot = sum3.result()
    s3_o[...] = tot
    second(0)
    first(1)
    hand(2)
    for c in range(0, C, 256):
        w = slice(c, c + 256)
        v = dp3[:, w].astype(jnp.float32) - tot[0:1, w] / count - n3[:, w].astype(jnp.float32) * (tot[1:2, w] / count)
        d3[:, w] = (ins * v * (ge[:, w] * st_ref[3:4, w])).astype(jnp.bfloat16)
    load.need("we", "l2", "n2")
    ones, crossed = [], []
    for c in range(0, neck, 256):
        w = slice(c, c + 256)
        v = nt_dot(d3[...], we[w, :]) * l2[:, w].astype(jnp.float32)
        acc[:, w] = v
        v = v * ins
        ones.append(jnp.sum(v, axis=0, keepdims=True))
        crossed.append(jnp.sum(v * n2[:, w].astype(jnp.float32), axis=0, keepdims=True))
    sum2.start([cat_rows(ones), cat_rows(crossed)])
    load.need("h2")
    for c in range(0, C, 256):
        ex[:, c : c + 256] = tn_dot(h2[...], d3[:, c : c + 256]).astype(jnp.bfloat16)
    sum2.turn()
    r_ex.pair()
    tot = sum2.result()
    s2_o[...] = tot
    for c in range(0, neck, 256):
        w = slice(c, c + 256)
        v = acc[:, w] - tot[0:1, w] / count - n2[:, w].astype(jnp.float32) * (tot[1:2, w] / count)
        v = ins * v * (gd[:, w] * st_ref[2:3, w])
        ext2[:, e : e + h, w] = v.astype(jnp.bfloat16).reshape(Q, h, 256)
    up = remote(ext2.at[:, pl.ds(e, e)], ext2.at[:, pl.ds(e + h, e)], hs.at[0], hr.at[0], d, lax.rem(f + 7, 8))
    down = remote(ext2.at[:, pl.ds(h, e)], ext2.at[:, pl.ds(0, e)], hs.at[1], hr.at[1], d, lax.rem(f + 1, 8))
    second(1)
    hand(3)
    kcp.wait()
    load.need("ext", "wd", "l1", "n1")
    r_pm.beside()
    r_ex.far()
    first(2)
    for i in range(3):
        for j in range(3):
            lo, hi = span(j - 1, Q)
            ok = same_crop(
                key[lo:hi, e : e + h, :], key[lo + j - 1 : hi + j - 1, e * i : e * i + h, :], neck
            )
            v = jnp.where(ok, ext[lo + j - 1 : hi + j - 1, e * i : e * i + h, :], 0).reshape((hi - lo) * h, neck)
            g = ext2[lo:hi, e : e + h, :].reshape((hi - lo) * h, neck)
            di[3 * i + j] = tn_dot(g, v).astype(jnp.bfloat16)
        r_di[i].pair()
        if i == 0:
            hand(4)
            first(3)
            second(2)
        if i == 1:
            r_ex.beside()
    up.wait()
    down.wait()
    r_pm.tiles()
    acc[...] = jnp.zeros_like(acc)
    for i in range(3):
        if i == 1:
            first(4)
            second(3)
        for j in (1, 0, 2):
            lo, hi = span(1 - j, Q)
            ok = same_crop(
                key[lo:hi, e : e + h, :], key[lo + 1 - j : hi + 1 - j, e * (2 - i) : e * (2 - i) + h, :], neck
            )
            v = jnp.where(ok, ext2[lo + 1 - j : hi + 1 - j, e * (2 - i) : e * (2 - i) + h, :], 0)
            v = v.reshape((hi - lo) * h, neck)
            for c in range(0, neck, 256):
                acc[lo * h : hi * h, c : c + 256] += nn_dot(v, wd[3 * i + j, :, c : c + 256])
    ones, crossed = [], []
    for c in range(0, neck, 256):
        w = slice(c, c + 256)
        v = acc[:, w] * l1[:, w].astype(jnp.float32)
        acc[:, w] = v
        v = v * ins
        ones.append(jnp.sum(v, axis=0, keepdims=True))
        crossed.append(jnp.sum(v * n1[:, w].astype(jnp.float32), axis=0, keepdims=True))
    sum1.start([cat_rows(ones), cat_rows(crossed)])
    for r in r_di:
        r.far()
    r_pm.middle()
    sum1.turn()
    r_ex.tiles()
    second(4)
    r_pm.last()
    for r in r_di:
        r.beside()
    tot = sum1.result()
    s1_o[...] = tot
    for c in range(0, neck, 256):
        w = slice(c, c + 256)
        v = acc[:, w] - tot[0:1, w] / count - n1[:, w].astype(jnp.float32) * (tot[1:2, w] / count)
        v = (ins * v * (gr[:, w] * st_ref[1:2, w])).astype(jnp.bfloat16)
        d1n[:, w] = nn_dot(pick[...], v).astype(jnp.bfloat16)
    load.need("x", "wr")
    for c in range(0, C, 256):
        re_[:, c : c + 256] = tn_dot(d1n[...], x_ref[:, c : c + 256]).astype(jnp.bfloat16)
    r_re.pair()
    r_di[0].tiles()
    r_re.far()
    r_ex.middle()
    out = []
    for n, c in enumerate(range(0, C, 256)):
        w = slice(c, c + 256)
        if n >= 2:
            out[n - 2].wait()
        gf[n % 2] = nn_dot(pick[...], dp3[:, w]) + nn_dot(d1n[...], wr[:, w])
        cp = pltpu.make_async_copy(gf.at[n % 2], gf_o.at[:, pl.ds(c, 256)], gs.at[n % 2])
        cp.start()
        out.append(cp)
        if n == 0:
            r_re.beside()
        if n == 1:
            r_di[0].middle()
            r_ex.last()
        if n == 3:
            r_di[1].tiles()
            r_di[0].last()
        if n == 5:
            r_di[1].middle()
        if n == 7:
            r_di[2].tiles()
            r_di[1].last()
    keep(0, 0, 3)
    keep(1, 3, 2)
    r_di[2].middle()
    r_re.tiles()
    r_di[2].last()
    r_re.middle()
    r_re.last()
    out[-2].wait()
    out[-1].wait()
    for t in range(5):

        @pl.when(outer)
        def _():
            to_inner(t).wait_send()

        @pl.when(jnp.logical_not(outer))
        def _():
            to_outer(t).wait_send()

    for c in kout:
        c.wait()
    for r in [r_pm, r_ex, r_re] + r_di:
        r.done()


def bottleneck_back(*args):
    x, st, dpt, pm_in, h2 = args[0], args[2], args[7], args[9], args[16]
    N, C = x.shape
    Q, h2_, neck = args[18].shape
    h = h2_ // 2
    tail = args[23]
    W = dpt.shape[1]
    PM = C + pm_in.shape[1]
    b16, f32 = jnp.bfloat16, jnp.float32
    S, V = jax.ShapeDtypeStruct, pltpu.VMEM
    blocks = [(W // 8, PM), (neck, C // 8), (9, neck // 8, neck), (neck // 8, C)]
    scratch = [
        V((W, PM), b16), V((neck, C), b16), V((9, neck, neck), b16), V((N, C), b16),
        V((N, neck), f32), V((Q, 2 * h, neck), b16), V((N, neck), b16), V((Q, 2 * h, 128), b16), V((2, N, 256), f32),
        V((N, N), b16), V(tail.shape, b16), V(tail.shape, b16),
    ]
    scratch += [V(args[n].shape, args[n].dtype) for n in (0, 6, 8, 10, 11, 12, 13, 14, 15, 16, 17, 18, 19, 20, 21, 23)]
    scratch += [
        DMA((16,)),
        DMA(()), DMA((2,)), DMA((2,)), DMA((2,)),
    ]
    scratch += [DMA((5,))] * 6 + [DMA((2, 8)), DMA((2, 8)), DMA((2,))]
    for n in (0, 1, 2, 2, 2, 3):
        scratch += reduce_scratch((3,) + blocks[2][1:] if n == 2 else blocks[n])
    scratch += sum_sems(2, C) + sum_sems(2, neck) + sum_sems(2, neck)
    return pl.pallas_call(
        bottleneck_back_kernel,
        out_shape=[S((N, C), f32)] + [S(b, b16) for b in blocks] + [S((2, C), f32), S((2, neck), f32), S((2, neck), f32)]
        + [S((10, W // 8, C), b16)],
        in_specs=[VM if n in (1, 2, 3, 4, 5, 7, 9) else ANY for n in range(24)],
        out_specs=[ANY] + [VM] * 7 + [ANY],
        scratch_shapes=scratch,
        compiler_params=pltpu.CompilerParams(collective_id=12, has_side_effects=True, vmem_limit_bytes=VLIM),
        name="bottleneck_back",
    )(*args)


def spaced_taps(src, key, kernels, acc, base, h, steps, sign, first_lane, dot, b):
    Q = key.shape[0]
    s = sign * steps[b]
    W = kernels.shape[1] if sign < 0 else src.shape[2]
    lanes = slice(first_lane, first_lane + W)
    for n, j in enumerate((0, -1, 1)):
        lo, hi = span(s * j, Q)
        here = key[lo:hi, pl.ds(base, h), :]
        got = None
        for i in (-1, 0, 1):
            at = pl.multiple_of(base + 16 * s * i, 16)
            ok = same_crop(here, key[lo + s * j : hi + s * j, pl.ds(at, h), :], W)
            v = jnp.where(ok, src[lo + s * j : hi + s * j, pl.ds(at, h), lanes], 0).reshape((hi - lo) * h, W)
            r = dot(v, kernels[9 * b + 3 * (i + 1) + j + 1])
            got = r if got is None else got + r
        if n == 0 and sign > 0:
            acc[...] = got
        else:
            acc[lo * h : hi * h] += got


def head_kernel(
    steps, yo, key, kern, y_any, wp_any, wm_any, wc, ins_ref, kb, lab, st_ref, gb, bb, gm, bm,
    lo_o, dp_o, dr_o, pm_o, pooled_o, dpool_o, size_o, sb_o, sm_o,
    acc, near, mine, far, corner, ab, nb, lb, joined, nm, lm, merged, pn, ps, pr, ss, rs, y, wp, wm, lsem,
    *sems,
):
    sems = list(sems)
    load = Load(lsem, y=(y_any, y), wp=(wp_any, wp), wm=(wm_any, wm))
    f, d = greet(range(1, 8), range(1, 4))
    sum_b, sum_m, back_m, back_b = (Sum(sems[6 * n : 6 * n + 6], d, f) for n in range(4))
    Q, h = pn.shape[1], pn.shape[2]
    N = Q * h
    w = yo.shape[2]
    W = wp.shape[0]
    T = 8 * h
    c0 = f % 2
    me = f // 2
    f32, b16 = jnp.float32, jnp.bfloat16

    def step(n, _):
        k = 3 - n
        g = me ^ k
        for turn in range(2):
            dest = 2 * g + (1 - c0 if turn == 0 else c0)
            base = pl.multiple_of(PAD + h * dest, 16)
            if turn == 1:
                pltpu.make_async_remote_copy(
                    src_ref=pn.at[k], dst_ref=near.at[k], send_sem=ps.at[k], recv_sem=pr.at[k],
                    device_id=(d, f ^ 1), device_id_type=MESH,
                ).wait_recv()
            for b in range(3):
                lanes = slice(b * W, (b + 1) * W)
                spaced_taps(yo, key, kern, acc, base, h, steps, 1, 0, nt_dot, b)
                if turn == 0:
                    pn[k, :, :, lanes] = acc[...].astype(b16).reshape(Q, h, W)
                else:
                    val = acc[...] + near[k, :, :, lanes].astype(f32).reshape(N, W)
                    mine[k, :, :, lanes] = val.astype(b16).reshape(Q, h, W)
            if turn == 0:
                remote(pn.at[k], near.at[k], ps.at[k], pr.at[k], d, f ^ 1)
            else:

                @pl.when(k == 3)
                def _():
                    for a in (0, 1):
                        by_way(a).start()

        return 0

    def by_way(a):
        two = pl.ds(a * (Q // 2), Q // 2)
        return pltpu.make_async_remote_copy(
            src_ref=mine.at[3, two], dst_ref=corner.at[two], send_sem=ss.at[a], recv_sem=rs.at[a],
            device_id=(d, f ^ (2 + 2 * a)), device_id_type=MESH,
        )

    lax.fori_loop(0, 3, step, 0)
    for a in (0, 1):
        by_way(a).wait()
    out = []
    for k in (1, 2):
        two = slice((2 - k) * (Q // 2), (3 - k) * (Q // 2))
        for b in range(3):
            lanes = slice(b * W, (b + 1) * W)
            val = mine[k, two, :, lanes].astype(f32) + corner[two, :, lanes].astype(f32)
            mine[k, two, :, lanes] = val.astype(b16)
        out.append(remote(mine.at[k], far.at[k - 1], ss.at[k + 1], rs.at[k + 1], d, f ^ (2 * k)))
    lax.fori_loop(3, 4, step, 0)
    load.need("y", "wp", "wm")
    ab[:, :W] = nt_dot(y[...], wp[...])
    crop = (lax.broadcasted_iota(jnp.int32, (T, 128), 1) + 1).astype(f32)

    def crops(q, carry):
        total, size = carry
        one = (key[q, PAD : PAD + T, :].astype(f32) == crop).astype(f32).astype(b16)
        return total + tn_dot(one, yo[q, PAD : PAD + T, :]), size + tn_dot(one, jnp.ones((T, 128), b16))

    total, size = lax.fori_loop(0, Q, crops, (jnp.zeros((128, w), f32), jnp.zeros((128, 128), f32)))
    size = jnp.where(size > 0, size, 1.0)[:8]
    size_o[...] = size
    pooled = (total[:8] / size[:, :1]).astype(b16)
    pooled_o[...] = pooled
    part = nt_dot(pooled, kern[27])
    part = cat_rows([part[c : c + 1] for c in range(CROPS_TILE)])
    ins = wide(ins_ref[...], 2)
    for c in out:
        c.wait()
    ones, squares = [], []
    for b in range(4):
        lanes = slice(b * W, (b + 1) * W)
        if b:
            src = slice((b - 1) * W, b * W)
            v = mine[0, :, :, src].astype(f32)
            for k in (1, 2):
                v = v + far[k - 1, :, :, src].astype(f32)
            ab[:, lanes] = v.reshape(N, W)
        s, t = column_sums(ab[:, lanes], ins_ref[...])
        ones.append(s)
        squares.append(t)
    sum_b.start([cat_rows(ones), cat_rows(squares), part])
    for k in range(4):
        pltpu.make_async_remote_copy(
            src_ref=pn.at[k], dst_ref=near.at[k], send_sem=ps.at[k], recv_sem=pr.at[k],
            device_id=(d, f ^ 1), device_id_type=MESH,
        ).wait_send()
    sum_b.turn()
    pool_act = sum_b.b2[d, 2:3, :]
    pool, pool_lean = bend(pool_act)
    pool = pool.astype(b16).astype(f32)
    here = wide(kb[...].astype(f32), W // 128)
    v = jnp.zeros((N, W), f32)
    for c in range(CROPS_TILE):
        v = jnp.where(here == c + 1.0, pool[:, c * W : (c + 1) * W], v)
    joined[:, 4 * W :] = v.astype(b16)
    tot = sum_b.result()
    count = st_ref[0:1, 0:1]
    mean = tot[0:1] / count
    inv_b = lax.rsqrt(tot[1:2] / count - mean * mean + eps)
    for b in range(4):
        lanes = slice(b * W, (b + 1) * W)
        n = (ab[:, lanes] - mean[:, lanes]) * inv_b[:, lanes]
        act, lean = bend(n * gb[:, lanes] + bb[:, lanes])
        joined[:, lanes] = act.astype(b16)
        nb[:, lanes] = n.astype(b16)
        lb[:, lanes] = lean.astype(b16)
    am = nt_dot(joined[...], wm[...])
    s, t = column_sums(am, ins_ref[...])
    sum_m.start([s, t])
    sum_m.turn()
    tot = sum_m.result()
    mean = tot[0:1] / count
    inv_m = lax.rsqrt(tot[1:2] / count - mean * mean + eps)
    n = (am - mean) * inv_m
    act, lean = bend(n * gm[...] + bm[...])
    merged[...] = act.astype(b16)
    nm[...] = n
    lm[...] = lean
    logits = nn_dot(merged[...], wc[...])
    lane = lax.broadcasted_iota(jnp.int32, (N, 128), 1)
    valid = lane < CLASSES
    top = jnp.max(jnp.where(valid, logits, -jnp.inf), axis=1, keepdims=True)
    ex = jnp.where(valid, jnp.exp(logits - top), 0.0)
    prob = ex / jnp.sum(ex, axis=1, keepdims=True)
    target = (lab[...] == lane.astype(f32)).astype(f32)
    dl = (ins_ref[...] * (prob - target) / count).astype(b16)
    e = nt_dot(dl, wc[...]) * lm[...]
    m = e * ins
    back_m.start([jnp.sum(m, axis=0, keepdims=True), jnp.sum(m * nm[...], axis=0, keepdims=True)])
    order = lax.broadcasted_iota(jnp.int32, (N, N), 1)
    rows = h // 4
    mm, r, q = order % 4, (order // 4) % rows, order // h
    hit = (r * (N // rows) + q * 4 + mm) == lax.broadcasted_iota(jnp.int32, (N, N), 0)
    lo_o[...] = nn_dot(hit.astype(f32).astype(b16), logits.astype(b16)).astype(b16)
    back_m.turn()
    J = joined.shape[1]
    pm_o[:, J : J + 128] = tn_dot(merged[...], dl).astype(b16)
    pm_o[:, J + 128 :] = jnp.zeros((W, pm_o.shape[1] - J - 128), b16)
    tot = back_m.result()
    sm_o[...] = tot
    dm = (ins * gm[...] * inv_m * (e - tot[0:1] / count - nm[...] * (tot[1:2] / count))).astype(b16)
    ones, crossed = [], []
    for b in range(4):
        lanes = slice(b * W, (b + 1) * W)
        v = nn_dot(dm, wm[:, lanes]) * lb[:, lanes].astype(f32)
        ab[:, lanes] = v
        v = v * ins
        ones.append(jnp.sum(v, axis=0, keepdims=True))
        crossed.append(jnp.sum(v * nb[:, lanes].astype(f32), axis=0, keepdims=True))
    v = nn_dot(dm, wm[:, 4 * W :])
    part = cat_rows(
        [jnp.sum(jnp.where(here == c + 1.0, v, 0.0), axis=0, keepdims=True) for c in range(CROPS_TILE)]
    )
    back_b.start([cat_rows(ones), cat_rows(crossed), part])
    pm_o[:, :J] = tn_dot(dm, joined[...]).astype(b16)
    back_b.turn()
    v = (back_b.b2[d, 2:3, :] * pool_lean).astype(b16)
    dpool_o[...] = jnp.zeros_like(dpool_o)
    for c in range(CROPS_TILE):
        dpool_o[c : c + 1, :] = v[:, c * W : (c + 1) * W]
    tot = back_b.result()
    sb_o[...] = tot[:2]
    for b in range(4):
        lanes = slice(b * W, (b + 1) * W)
        v = ab[:, lanes] - tot[0:1, lanes] / count - nb[:, lanes].astype(f32) * (tot[1:2, lanes] / count)
        v = (ins * v * (gb[:, lanes] * inv_b[:, lanes])).astype(b16)
        if b:
            dr_o[:, :, (b - 1) * W : b * W] = v.reshape(Q, h, W)
        else:
            dp_o[...] = v


def head(steps, width, *args):
    yo, key, kern, y, wp, wm = args[:6]
    N, C = y.shape
    Q = yo.shape[0]
    h = N // Q
    W = wp.shape[0]
    J = wm.shape[1]
    b16, f32 = jnp.bfloat16, jnp.float32
    S, V = jax.ShapeDtypeStruct, pltpu.VMEM
    return pl.pallas_call(
        functools.partial(head_kernel, steps),
        out_shape=[
            S((N, 128), b16), S((N, W), b16), S((Q, h, 3 * W), b16), S((W, width), b16), S((8, C // 8), b16),
            S((8, W), b16), S((8, 128), f32), S((2, 4 * W), f32), S((2, W), f32),
        ],
        in_specs=[VM] * 3 + [ANY] * 3 + [VM] * 9,
        out_specs=[VM] * 9,
        scratch_shapes=[V((N, W), f32)]
        + [V((4, Q, h, 3 * W), b16)] * 2 + [V((2, Q, h, 3 * W), b16), V((Q, h, 3 * W), b16)]
        + [
            V((N, 4 * W), f32), V((N, 4 * W), b16), V((N, 4 * W), b16), V((N, J), b16), V((N, W), f32), V((N, W), f32),
            V((N, W), b16), V((4, Q, h, 3 * W), b16), DMA((4,)), DMA((4,)), DMA((4,)), DMA((4,)),
            V(y.shape, b16), V(wp.shape, b16), V(wm.shape, b16), DMA((3,)),
        ]
        + sum_sems(3, 4 * W) + sum_sems(2, W) + sum_sems(2, W) + sum_sems(3, 4 * W),
        compiler_params=pltpu.CompilerParams(collective_id=5, has_side_effects=True, vmem_limit_bytes=VLIM),
        name="head",
    )(*args)


def widen_kernel(gk, tk, pm, ex, di, re_, k0, k1, k2, pool, point, merge, dilated, expand, reduce_):
    for b, o in enumerate((k0, k1, k2)):

        def tap(t, _):
            o[t] = (tk[t] if b == 2 else gk[9 * b + t]).astype(jnp.float32)
            return 0

        lax.fori_loop(0, 9, tap, 0)
    pool[...] = tk[9].astype(jnp.float32)
    C = point.shape[1]
    point[...] = pm[:, :C].astype(jnp.float32)
    merge[...] = pm[:, C : C + merge.shape[1]].astype(jnp.float32)

    def rows(t, _):
        dilated[t] = di[t].astype(jnp.float32)
        return 0

    lax.fori_loop(0, 9, rows, 0)
    expand[...] = ex[...].astype(jnp.float32)
    reduce_[...] = re_[...].astype(jnp.float32)


def widen(gk, tk, pm, ex, di, re_, J):
    _, o, C = gk.shape
    shapes = [(9, o, C)] * 3 + [(o, C), (o, C), (o, J), di.shape, ex.shape, re_.shape]
    return pl.pallas_call(
        widen_kernel,
        out_shape=[jax.ShapeDtypeStruct(v, jnp.float32) for v in shapes],
        in_specs=[VM] * 6,
        out_specs=[VM] * 9,
        compiler_params=pltpu.CompilerParams(vmem_limit_bytes=VLIM),
        name="widen",
    )(gk, tk, pm, ex, di, re_)


def norm_coeffs(totals, squares, count):
    average = totals / count
    return average, lax.rsqrt(squares / count - average * average + eps)


def fast_body(
    features, crop_ids, labels, w_reduce, gain_reduce, bias_reduce, w_dilated, gain_dilated, bias_dilated,
    w_expand, gain_expand, bias_expand, w_point, gain_point, bias_point, w_rate, gain_rate, bias_rate,
    w_rate_double, gain_rate_double, bias_rate_double, w_rate_triple, gain_rate_triple, bias_rate_triple,
    w_pool, w_merge, gain_merge, bias_merge, w_classes,
):
    rows, cols, C = features.shape
    Q = cols // 4
    h = rows * 4
    N = rows * cols
    nf = lax.axis_size("fsdp")
    W = gain_point.shape[0]
    steps = (RATE // 4, 2 * RATE // 4, 3 * RATE // 4)
    place = lax.axis_index("fsdp")

    def perm(a):
        a = a.reshape((rows, Q, 4) + a.shape[2:])
        return jnp.swapaxes(a, 0, 1).reshape((N,) + a.shape[3:])

    def unperm(a):
        a = a.reshape((Q, rows, 4) + a.shape[1:])
        return jnp.swapaxes(a, 0, 1).reshape((rows, cols) + a.shape[3:])

    local_crop = perm(crop_ids) - lax.axis_index("dp") * CROPS_TILE
    in_crop = perm(crop_ids) >= 0
    inside = in_crop.astype(jnp.float32)[:, None]
    key_loc = jnp.where(in_crop, local_crop + 1, 0)
    kb = jnp.broadcast_to(key_loc.astype(jnp.bfloat16)[:, None], (N, 128))
    key_row = jnp.pad(key_loc.astype(jnp.float32).reshape(Q, h), ((0, 0), (0, 128 - h)))
    ins = jnp.broadcast_to(inside, (N, 128))
    rates = [jnp.swapaxes(w.reshape(9, C, -1), 1, 2) for w in (w_rate, w_rate_double, w_rate_triple)]
    vecs = [v[None, :] for v in (gain_reduce, bias_reduce, gain_dilated, bias_dilated, gain_expand, bias_expand)]
    (
        y_own, y, n_three, l_three, n_one, l_one, n_two, l_two, ext, h_two, key, kernel,
        wr, wd, full_expand, wp, wm, wc, count,
    ) = bottleneck(
        features.reshape(N, C), key_row, ins, vecs,
        [
            w_reduce.T, jnp.swapaxes(w_dilated.reshape(9, w_dilated.shape[2], -1), 1, 2), w_expand, w_point.T, w_merge.T,
            jnp.pad(w_classes, ((0, 0), (0, 128 - CLASSES))),
        ],
        rates + [w_pool.T[None]],
    )
    neck = gain_reduce.shape[0]
    stats = count
    count = count[0, 0]
    y = y.reshape(N, C)
    g_br = jnp.concatenate([gain_point, gain_rate, gain_rate_double, gain_rate_triple])[None]
    b_br = jnp.concatenate([bias_point, bias_rate, bias_rate_double, bias_rate_triple])[None]
    lab = jnp.broadcast_to(perm(labels).astype(jnp.float32)[:, None], (N, 128))
    J = wm.shape[1]
    width = J + 128 + -(C + J + 128) % 512
    logits, d_point, d_rates, rest, pooled, d_pool, sizes, st_br, st_m = head(
        steps, width, y_own, key, kernel, y, wp, wm, wc, ins, kb, lab, stats, g_br, b_br,
        gain_merge[None], bias_merge[None],
    )
    class_logits = logits[:, :CLASSES].reshape(rows, cols, CLASSES)
    gb_br, gg_br = st_br[0], st_br[1]
    gb_merge, gg_merge = st_m[0], st_m[1]
    d_y, grad_k, tail = branches_back(d_rates, y_own, key, kernel, pooled, d_pool, sizes, steps)
    grad_features, pm, ex, di, re_, st3, st2, st1, tail = bottleneck_back(
        features.reshape(N, C), ins, stats, vecs[0], vecs[2], vecs[4], d_y.reshape(N, C), d_point, y, rest, wp,
        n_three, l_three, full_expand, n_two, l_two, h_two, wd, ext, n_one, l_one, wr, key, tail,
    )
    grad_classes = pm[:, C + J : C + J + CLASSES].astype(jnp.float32)
    *grad_k, grad_pool, grad_point, grad_merge, grad_dilated, grad_expand, grad_reduce = widen(grad_k, tail, pm, ex, di, re_, J)
    grad_k = [jnp.swapaxes(v.reshape(3, 3, -1, C), 2, 3) for v in grad_k]
    grad_pool, grad_point, grad_merge, grad_reduce = grad_pool.T, grad_point.T, grad_merge.T, grad_reduce.T
    grad_dilated = jnp.swapaxes(grad_dilated, 1, 2).reshape(3, 3, neck, -1)
    grad_features = grad_features.reshape(rows, cols, C)
    gg_expand, gb_expand, gg_dilated, gb_dilated, gg_reduce, gb_reduce = st3[1], st3[0], st2[1], st2[0], st1[1], st1[0]
    return (
        class_logits,
        grad_features,
        grad_reduce, gg_reduce, gb_reduce,
        grad_dilated, gg_dilated, gb_dilated,
        grad_expand, gg_expand, gb_expand,
        grad_point, gg_br[:W], gb_br[:W],
        grad_k[0], gg_br[W : 2 * W], gb_br[W : 2 * W],
        grad_k[1], gg_br[2 * W : 3 * W], gb_br[2 * W : 3 * W],
        grad_k[2], gg_br[3 * W :], gb_br[3 * W :],
        grad_pool,
        grad_merge, gg_merge, gb_merge,
        grad_classes,
    )


def passed_along(value, axis, by):
    count = lax.axis_size(axis)
    pairs = [(i, i + by) for i in range(count) if 0 <= i + by < count]
    return lax.ppermute(value, axis, pairs)


def padded(cells, sides, width):
    for axis, dim in sides:
        count = lax.axis_size(axis)
        ends = count - 1
        head = lax.slice_in_dim(cells, 0, width, axis=dim)
        tail = lax.slice_in_dim(cells, cells.shape[dim] - width, cells.shape[dim], axis=dim)
        cells = jnp.concatenate(
            [
                lax.ppermute(tail, axis, [(i, (i + 1) % count) for i in range(ends)]),
                cells,
                lax.ppermute(head, axis, [((i + 1) % count, i) for i in range(ends)]),
            ],
            axis=dim,
        )
    return cells


def flat_dot(first_op, second_op):
    return jnp.dot(first_op, second_op, preferred_element_type=jnp.float32)


def inner_dot(first_op, second_op):
    return lax.dot_general(
        first_op, second_op, (((0,), (0,)), ((), ())), preferred_element_type=jnp.float32
    )


def outer_dot(first_op, second_op):
    return lax.dot_general(
        first_op, second_op, (((1,), (1,)), ((), ())), preferred_element_type=jnp.float32
    )


def slope(values):
    gate_value = jax.nn.sigmoid(values)
    return gate_value * (1.0 + values * (1.0 - gate_value))


def widen_rows(values, extent, mover):
    row_count = values.shape[0]
    neighbours = -(-extent // row_count)
    above = [mover(values, distance) for distance in range(neighbours, 0, -1)]
    below = [mover(values, -distance) for distance in range(1, neighbours + 1)]
    stacked = jnp.concatenate(above + [values] + below, axis=0)
    start_row = neighbours * row_count - extent
    return stacked[start_row : start_row + row_count + 2 * extent]


def rim_slice(widened, spacing, margin, height):
    return widened[margin - spacing : margin + height + spacing]


def offset_table(broad_key_rows, crop_random_keys, spacing, margin):
    height, breadth = crop_random_keys.shape
    first_row = margin - spacing
    extended = jnp.pad(
        broad_key_rows[first_row : first_row + height + 2 * spacing], ((0, 0), (spacing, spacing))
    )
    tables = []
    for row_tap in range(3):
        for col_tap in range(3):
            nearby = extended[
                row_tap * spacing : row_tap * spacing + height,
                col_tap * spacing : col_tap * spacing + breadth,
            ]
            tables.append(
                ((nearby == crop_random_keys) & (crop_random_keys > 0))
                .astype(jnp.float32)
                .reshape(height * breadth, 1)
            )
    return tables


def spread_offsets(widened, kernel, tables, spacing, height, breadth):
    channels = widened.shape[2]
    extended = jnp.pad(widened, ((0, 0), (spacing, spacing), (0, 0)))
    summed = jnp.zeros((height * breadth, kernel.shape[3]), jnp.float32)
    for row_tap in range(3):
        for col_tap in range(3):
            nearby = extended[
                row_tap * spacing : row_tap * spacing + height,
                col_tap * spacing : col_tap * spacing + breadth,
            ]
            summed = summed + tables[3 * row_tap + col_tap] * flat_dot(
                nearby.reshape(height * breadth, channels), kernel[row_tap, col_tap]
            )
    return summed


def collect_taps(widened, kernel, tables, spacing, height, breadth):
    channels = widened.shape[2]
    extended = jnp.pad(widened, ((0, 0), (spacing, spacing), (0, 0)))
    summed = jnp.zeros((height * breadth, kernel.shape[2]), jnp.float32)
    for row_tap in range(3):
        for col_tap in range(3):
            back_row = 2 - row_tap
            back_col = 2 - col_tap
            nearby = extended[
                back_row * spacing : back_row * spacing + height,
                back_col * spacing : back_col * spacing + breadth,
            ]
            summed = summed + tables[3 * back_row + back_col] * outer_dot(
                nearby.reshape(height * breadth, channels), kernel[row_tap, col_tap]
            )
    return summed


def kernel_offsets(widened, grads_low, tables, spacing, height, breadth):
    channels = widened.shape[2]
    extended = jnp.pad(widened, ((0, 0), (spacing, spacing), (0, 0)))
    pieces = []
    for row_tap in range(3):
        for col_tap in range(3):
            nearby = extended[
                row_tap * spacing : row_tap * spacing + height,
                col_tap * spacing : col_tap * spacing + breadth,
            ]
            masked = (tables[3 * row_tap + col_tap] * grads_low).astype(jnp.bfloat16)
            pieces.append(inner_dot(nearby.reshape(height * breadth, channels), masked))
    return pieces


def statistics(partial_value):
    return lax.psum(partial_value, ("dp", "fsdp"))


def norm_apply(values, totals, squares, pixel_count, factor, offset):
    average = totals / pixel_count
    inverse = lax.rsqrt(squares / pixel_count - average * average + eps)
    normed = (values - average) * inverse
    return (normed * factor + offset, normed, inverse)


def norm_forward(values, inside, pixel_count, factor, offset):
    totals, squares = statistics(
        (jnp.sum(values * inside, axis=0), jnp.sum(values * values * inside, axis=0))
    )
    return norm_apply(values, totals, squares, pixel_count, factor, offset)


def norm_backward(upstream, normed, inverse, factor, inside, pixel_count):
    totals, crossed = lax.psum(
        (jnp.sum(upstream * inside, axis=0), jnp.sum(upstream * normed * inside, axis=0)),
        ("dp", "fsdp"),
    )
    passed = (
        inside
        * factor
        * inverse
        * (upstream - totals / pixel_count - normed * crossed / pixel_count)
    )
    return (passed, crossed, totals)


def body(
    features,
    crop_ids,
    labels,
    w_reduce,
    gain_reduce,
    bias_reduce,
    w_dilated,
    gain_dilated,
    bias_dilated,
    w_expand,
    gain_expand,
    bias_expand,
    w_point,
    gain_point,
    bias_point,
    w_rate,
    gain_rate,
    bias_rate,
    w_rate_double,
    gain_rate_double,
    bias_rate_double,
    w_rate_triple,
    gain_rate_triple,
    bias_rate_triple,
    w_pool,
    w_merge,
    gain_merge,
    bias_merge,
    w_classes,
):
    local_rows, local_columns, channels = features.shape
    pixel_values = local_rows * local_columns
    inputs_flat = features.reshape(pixel_values, channels)
    crop_random_keys = crop_ids + 1
    outer_extent = 3 * RATE
    spacings = (RATE, 2 * RATE, 3 * RATE)
    broad_key_rows = widen_rows(
        crop_random_keys,
        outer_extent,
        lambda piece, distance: passed_along(piece, "fsdp", distance),
    )
    inside = (crop_random_keys > 0).astype(jnp.float32).reshape(pixel_values, 1)
    inner_neck = offset_table(broad_key_rows, crop_random_keys, DILATION_SPAN, outer_extent)
    near_rates = [
        offset_table(broad_key_rows, crop_random_keys, spacing, outer_extent)
        for spacing in spacings
    ]
    (
        full_reduce,
        complete_dilated,
        full_expand,
        full_point,
        full_rate,
        full_double,
        full_triple,
        full_pool,
        full_merge,
        full_classes,
    ) = (
        lax.all_gather(w_reduce, "fsdp", axis=1, tiled=True),
        lax.all_gather(w_dilated, "fsdp", axis=3, tiled=True),
        lax.all_gather(w_expand, "fsdp", axis=1, tiled=True),
        lax.all_gather(w_point, "fsdp", axis=1, tiled=True),
        lax.all_gather(w_rate, "fsdp", axis=3, tiled=True),
        lax.all_gather(w_rate_double, "fsdp", axis=3, tiled=True),
        lax.all_gather(w_rate_triple, "fsdp", axis=3, tiled=True),
        lax.all_gather(w_pool, "fsdp", axis=1, tiled=True),
        lax.all_gather(w_merge, "fsdp", axis=1, tiled=True),
        lax.all_gather(w_classes, "fsdp", axis=0, tiled=True),
    )
    rate_kernels = (full_rate, full_double, full_triple)
    rate_gains = (gain_rate, gain_rate_double, gain_rate_triple)
    rate_biases = (bias_rate, bias_rate_double, bias_rate_triple)
    act_one = flat_dot(inputs_flat, full_reduce)
    totals, squares, pixel_count = statistics(
        (
            jnp.sum(act_one * inside, axis=0),
            jnp.sum(act_one * act_one * inside, axis=0),
            jnp.sum(inside),
        )
    )
    pre_one, normed_one, inverse_one = norm_apply(
        act_one, totals, squares, pixel_count, gain_reduce, bias_reduce
    )
    first_hidden = jax.nn.silu(pre_one).astype(jnp.bfloat16)
    first_broad = padded(
        first_hidden.reshape(local_rows, local_columns, -1), (("fsdp", 0),), DILATION_SPAN
    )
    second_activation = spread_offsets(
        first_broad, complete_dilated, inner_neck, DILATION_SPAN, local_rows, local_columns
    )
    pre_two, normed_two, inverse_two = norm_forward(
        second_activation, inside, pixel_count, gain_dilated, bias_dilated
    )
    hidden_two = jax.nn.silu(pre_two).astype(jnp.bfloat16)
    act_three = flat_dot(hidden_two, full_expand)
    pre_three, normed_three, inverse_three = norm_forward(
        act_three, inside, pixel_count, gain_expand, bias_expand
    )
    pre_three = pre_three + inputs_flat
    block_out = jax.nn.silu(pre_three).astype(jnp.bfloat16)
    wide_block = widen_rows(
        block_out.reshape(local_rows, local_columns, channels),
        outer_extent,
        lambda piece, distance: passed_along(piece, "fsdp", distance),
    )
    point_act = flat_dot(block_out, full_point)
    pre_point, normed_point, inverse_point = norm_forward(
        point_act, inside, pixel_count, gain_point, bias_point
    )
    branch_point = jax.nn.silu(pre_point).astype(jnp.bfloat16)
    rate_states = []
    rate_branches = []
    for kernel, factor, offset, spacing, tables in zip(
        rate_kernels, rate_gains, rate_biases, spacings, near_rates
    ):
        rate_act = spread_offsets(
            rim_slice(wide_block, spacing, outer_extent, local_rows),
            kernel,
            tables,
            spacing,
            local_rows,
            local_columns,
        )
        pre_rate, normed_rate, inverse_rate = norm_forward(
            rate_act, inside, pixel_count, factor, offset
        )
        rate_states.append((pre_rate, normed_rate, inverse_rate))
        rate_branches.append(jax.nn.silu(pre_rate).astype(jnp.bfloat16))
    crop_flat = crop_ids.reshape(pixel_values)
    crop_total = CROPS_TILE
    first_crop = lax.axis_index("dp") * crop_total
    owner_group = lax.axis_size("fsdp")
    owner_place = lax.axis_index("fsdp")
    local_crop = crop_flat - first_crop
    member = local_crop[:, None] == jnp.arange(crop_total)[None, :]
    member_low = member.astype(jnp.bfloat16)
    crop_sums = inner_dot(member_low, block_out)
    crop_sizes = jnp.sum(member.astype(jnp.float32), axis=0)
    crop_sums, crop_sizes = lax.psum((crop_sums, crop_sizes), "fsdp")
    pooled = (crop_sums / crop_sizes[:, None]).astype(jnp.bfloat16)
    pool_act = flat_dot(pooled, full_pool)
    pool_low = jax.nn.silu(pool_act).astype(jnp.bfloat16)
    branch_pool = flat_dot(member_low, pool_low).astype(jnp.bfloat16)
    joined = jnp.concatenate([branch_point] + rate_branches + [branch_pool], axis=1)
    merge_act = flat_dot(joined, full_merge)
    pre_merge, normed_merge, inverse_merge = norm_forward(
        merge_act, inside, pixel_count, gain_merge, bias_merge
    )
    merged = jax.nn.silu(pre_merge).astype(jnp.bfloat16)
    logits_full = flat_dot(merged, full_classes)
    class_logits = logits_full.astype(jnp.bfloat16).reshape(local_rows, local_columns, -1)
    (
        full_reduce,
        complete_dilated,
        full_expand,
        full_point,
        full_rate,
        full_double,
        full_triple,
        full_pool,
        full_merge,
        full_classes,
    ) = (
        lax.all_gather(w_reduce, "fsdp", axis=1, tiled=True),
        lax.all_gather(w_dilated, "fsdp", axis=3, tiled=True),
        lax.all_gather(w_expand, "fsdp", axis=1, tiled=True),
        lax.all_gather(w_point, "fsdp", axis=1, tiled=True),
        lax.all_gather(w_rate, "fsdp", axis=3, tiled=True),
        lax.all_gather(w_rate_double, "fsdp", axis=3, tiled=True),
        lax.all_gather(w_rate_triple, "fsdp", axis=3, tiled=True),
        lax.all_gather(w_pool, "fsdp", axis=1, tiled=True),
        lax.all_gather(w_merge, "fsdp", axis=1, tiled=True),
        lax.all_gather(w_classes, "fsdp", axis=0, tiled=True),
    )
    rate_kernels = (full_rate, full_double, full_triple)
    highest = jnp.max(logits_full, axis=1, keepdims=True)
    shifted = jnp.exp(logits_full - highest)
    probability = shifted / jnp.sum(shifted, axis=1, keepdims=True)
    targets = (labels.reshape(pixel_values, 1) == jnp.arange(CLASSES)[None, :]).astype(jnp.float32)
    grad_logits = (inside * (probability - targets) / pixel_count).astype(jnp.bfloat16)
    grad_classes = inner_dot(merged, grad_logits)
    grad_merged = outer_dot(grad_logits, full_classes)
    passed, grad_gain_merge, grad_bias_merge = norm_backward(
        grad_merged * slope(pre_merge), normed_merge, inverse_merge, gain_merge, inside, pixel_count
    )
    grad_merge_act = passed.astype(jnp.bfloat16)
    grad_merge = inner_dot(joined, grad_merge_act)
    grad_joined = outer_dot(grad_merge_act, full_merge)
    branch_width = full_merge.shape[1]
    passed, grad_gain_point, grad_bias_point = norm_backward(
        grad_joined[:, :branch_width] * slope(pre_point),
        normed_point,
        inverse_point,
        gain_point,
        inside,
        pixel_count,
    )
    grad_point_act = passed.astype(jnp.bfloat16)
    grad_point = inner_dot(block_out, grad_point_act)
    grad_block = outer_dot(grad_point_act, full_point)
    rate_grads = []
    rate_weight_grads = []
    rate_gain_grads = []
    rate_bias_grads = []
    for branch in range(3):
        column = (1 + branch) * branch_width
        pre_rate, normed_rate, inverse_rate = rate_states[branch]
        passed, gain_grad, bias_grad = norm_backward(
            grad_joined[:, column : column + branch_width] * slope(pre_rate),
            normed_rate,
            inverse_rate,
            rate_gains[branch],
            inside,
            pixel_count,
        )
        grad_rate_act = passed.astype(jnp.bfloat16)
        pieces = kernel_offsets(
            rim_slice(wide_block, spacings[branch], outer_extent, local_rows),
            grad_rate_act,
            near_rates[branch],
            spacings[branch],
            local_rows,
            local_columns,
        )
        rate_weight_grads.append(jnp.stack(pieces).reshape(3, 3, channels, branch_width))
        rate_grads.append(grad_rate_act)
        rate_gain_grads.append(gain_grad)
        rate_bias_grads.append(bias_grad)
    rate_grads_low = jnp.concatenate(rate_grads, axis=1).reshape(local_rows, local_columns, -1)
    wide_grad_rate = widen_rows(
        rate_grads_low, outer_extent, lambda piece, distance: passed_along(piece, "fsdp", distance)
    )
    for branch in range(3):
        grad_slab = wide_grad_rate[:, :, branch * branch_width : (branch + 1) * branch_width]
        grad_block = grad_block + collect_taps(
            rim_slice(grad_slab, spacings[branch], outer_extent, local_rows),
            rate_kernels[branch],
            near_rates[branch],
            spacings[branch],
            local_rows,
            local_columns,
        )
    crop_grad = lax.dot_general(
        member.astype(jnp.float32),
        grad_joined[:, 4 * branch_width :],
        (((0,), (0,)), ((), ())),
        precision=lax.Precision.HIGHEST,
        preferred_element_type=jnp.float32,
    )
    crop_grad = lax.psum(crop_grad, "fsdp")
    grad_pool_act = (crop_grad * slope(pool_act)).astype(jnp.bfloat16)
    owned_crops = (jnp.arange(crop_total) % owner_group == owner_place).astype(jnp.float32)[:, None]
    grad_pool = inner_dot(pooled, (grad_pool_act * owned_crops).astype(jnp.bfloat16))
    grad_pooled = outer_dot(grad_pool_act, full_pool) / crop_sizes[:, None]
    grad_block = grad_block + inside * jnp.take(
        grad_pooled, jnp.clip(local_crop, 0, crop_total - 1), axis=0
    )
    grad_pre_three = grad_block * slope(pre_three)
    passed, grad_gain_expand, grad_bias_expand = norm_backward(
        grad_pre_three, normed_three, inverse_three, gain_expand, inside, pixel_count
    )
    grad_three = passed.astype(jnp.bfloat16)
    grad_expand = inner_dot(hidden_two, grad_three)
    grad_hidden_two = outer_dot(grad_three, full_expand)
    passed, grad_gain_dilated, grad_bias_dilated = norm_backward(
        grad_hidden_two * slope(pre_two), normed_two, inverse_two, gain_dilated, inside, pixel_count
    )
    second_gradient = passed.astype(jnp.bfloat16)
    dilated_fragments = kernel_offsets(
        first_broad, second_gradient, inner_neck, DILATION_SPAN, local_rows, local_columns
    )
    grad_dilated = jnp.stack(dilated_fragments).reshape(
        3, 3, second_gradient.shape[1], second_gradient.shape[1]
    )
    broad_neck_gradient = padded(
        second_gradient.reshape(local_rows, local_columns, -1), (("fsdp", 0),), DILATION_SPAN
    )
    grad_hidden_one = collect_taps(
        broad_neck_gradient, complete_dilated, inner_neck, DILATION_SPAN, local_rows, local_columns
    )
    passed, grad_gain_reduce, grad_bias_reduce = norm_backward(
        grad_hidden_one * slope(pre_one), normed_one, inverse_one, gain_reduce, inside, pixel_count
    )
    grad_one = passed.astype(jnp.bfloat16)
    grad_reduce = inner_dot(inputs_flat, grad_one)
    grad_features = (grad_pre_three + outer_dot(grad_one, full_reduce)).reshape(
        local_rows, local_columns, channels
    )
    shards = (
        lax.psum_scatter(grad_reduce, "fsdp", scatter_dimension=1, tiled=True),
        lax.psum_scatter(grad_dilated, "fsdp", scatter_dimension=3, tiled=True),
        lax.psum_scatter(grad_expand, "fsdp", scatter_dimension=1, tiled=True),
        lax.psum_scatter(grad_point, "fsdp", scatter_dimension=1, tiled=True),
        lax.psum_scatter(rate_weight_grads[0], "fsdp", scatter_dimension=3, tiled=True),
        lax.psum_scatter(rate_weight_grads[1], "fsdp", scatter_dimension=3, tiled=True),
        lax.psum_scatter(rate_weight_grads[2], "fsdp", scatter_dimension=3, tiled=True),
        lax.psum_scatter(grad_pool, "fsdp", scatter_dimension=1, tiled=True),
        lax.psum_scatter(grad_merge, "fsdp", scatter_dimension=1, tiled=True),
        lax.psum_scatter(grad_classes, "fsdp", scatter_dimension=0, tiled=True),
    )
    shards = (
        lax.psum(shards[0].astype(jnp.bfloat16), "dp").astype(jnp.float32),
        lax.psum(shards[1].astype(jnp.bfloat16), "dp").astype(jnp.float32),
        lax.psum(shards[2].astype(jnp.bfloat16), "dp").astype(jnp.float32),
        lax.psum(shards[3].astype(jnp.bfloat16), "dp").astype(jnp.float32),
        lax.psum(shards[4].astype(jnp.bfloat16), "dp").astype(jnp.float32),
        lax.psum(shards[5].astype(jnp.bfloat16), "dp").astype(jnp.float32),
        lax.psum(shards[6].astype(jnp.bfloat16), "dp").astype(jnp.float32),
        lax.psum(shards[7].astype(jnp.bfloat16), "dp").astype(jnp.float32),
        lax.psum(shards[8].astype(jnp.bfloat16), "dp").astype(jnp.float32),
        lax.psum(shards[9].astype(jnp.bfloat16), "dp").astype(jnp.float32),
    )
    return (
        class_logits,
        grad_features,
        shards[0],
        grad_gain_reduce,
        grad_bias_reduce,
        shards[1],
        grad_gain_dilated,
        grad_bias_dilated,
        shards[2],
        grad_gain_expand,
        grad_bias_expand,
        shards[3],
        grad_gain_point,
        grad_bias_point,
        shards[4],
        rate_gain_grads[0],
        rate_bias_grads[0],
        shards[5],
        rate_gain_grads[1],
        rate_bias_grads[1],
        shards[6],
        rate_gain_grads[2],
        rate_bias_grads[2],
        shards[7],
        shards[8],
        grad_gain_merge,
        grad_bias_merge,
        shards[9],
    )


def solution(mesh):
    tiled = mesh.shape["fsdp"] == 8 and mesh.shape["dp"] == 4

    return jax.shard_map(
        fast_body if tiled else body,
        mesh=mesh,
        in_specs=(
            P(("dp", "fsdp"), None, None),
            P(("dp", "fsdp"), None),
            P(("dp", "fsdp"), None),
            P(None, "fsdp"),
            P(),
            P(),
            P(None, None, None, "fsdp"),
            P(),
            P(),
            P(None, "fsdp"),
            P(),
            P(),
            P(None, "fsdp"),
            P(),
            P(),
            P(None, None, None, "fsdp"),
            P(),
            P(),
            P(None, None, None, "fsdp"),
            P(),
            P(),
            P(None, None, None, "fsdp"),
            P(),
            P(),
            P(None, "fsdp"),
            P(None, "fsdp"),
            P(),
            P(),
            P("fsdp", None),
        ),
        out_specs=(
            P(("dp", "fsdp"), None, None),
            P(("dp", "fsdp"), None, None),
            P(None, "fsdp"),
            P(),
            P(),
            P(None, None, None, "fsdp"),
            P(),
            P(),
            P(None, "fsdp"),
            P(),
            P(),
            P(None, "fsdp"),
            P(),
            P(),
            P(None, None, None, "fsdp"),
            P(),
            P(),
            P(None, None, None, "fsdp"),
            P(),
            P(),
            P(None, None, None, "fsdp"),
            P(),
            P(),
            P(None, "fsdp"),
            P(None, "fsdp"),
            P(),
            P(),
            P("fsdp", None),
        ),
        check_vma=False,
    )
```
